32 devices in a mesh: dp: 4 (over y, x), ctx: 2 (over core), expert: 4 (over z).
Axes of the slice: x: 2, y: 2, z: 4, core: 2. Of those that a mesh axis runs over, the one named last changes fastest.
Arguments:
- tokens: bfloat16 [32, 1024, 768], P(('dp', 'expert'), 'ctx'), may hold values from -6 to 6
- cotangent: bfloat16 [32, 1024, 768], P(('dp', 'expert'), 'ctx'), may hold values from -6 to 6
- routes: int32 [32, 1024], P(('dp', 'expert'), 'ctx'), may hold values from 0 to 3, as said below
- norm1_gain: float32 [768], replicated, may hold values from 0.1 to 1.9
- query_weight: bfloat16 [768, 768], replicated, may hold values from -0.109375 to 0.109375
- key_weight: bfloat16 [768, 768], replicated, may hold values from -0.109375 to 0.109375
- value_weight: bfloat16 [768, 768], replicated, may hold values from -0.21875 to 0.21875
- output_weight: bfloat16 [768, 768], replicated, may hold values from -0.875 to 0.875
- bias_table: float32 [32, 12], replicated, may hold values from -4 to 4
- norm2_gain: float32 [768], replicated, may hold values from 0.1 to 1.9
- router_weight: bfloat16 [768, 4], replicated, may hold values from -0.15625 to 0.15625
- w_in: bfloat16 [4, 768, 3072], P('expert'), may hold values from -0.21875 to 0.21875
- w_out: bfloat16 [4, 3072, 768], P('expert'), may hold values from -0.4375 to 0.4375
Outputs:
- block_out: bfloat16 [32, 1024, 768], P(('dp', 'expert'), 'ctx')
- d_tokens: float32 [32, 1024, 768], P(('dp', 'expert'), 'ctx')
- d_norm1_gain: float32 [768], replicated
- d_w_query: float32 [768, 768], replicated
- d_w_key: float32 [768, 768], replicated
- d_w_value: float32 [768, 768], replicated
- d_w_output: float32 [768, 768], replicated
- d_bias_table: float32 [32, 12], replicated
- d_norm2_gain: float32 [768], replicated
- d_w_router: float32 [768, 4], replicated
- d_w_in: float32 [4, 768, 3072], P('expert', None, ('dp', 'ctx'))
- d_w_out: float32 [4, 3072, 768], P('expert', ('dp', 'ctx'))
The draws below stay inside these ranges and needn't reach their ends.
Inputs may be any that keep to these rules, and one draw needn't show every extreme that they name: `routes`: within the 512 tokens of one sequence on one device no expert is named more than 256 times; one expert, the same for every such block, is named exactly 256 times in each.
All inputs are finite; a program needn't handle non-finite values.
Results may differ from the reference program's by a relative error of at most 0.018.
Values may be sent and summed in bfloat16 or wider, within the bound.
No kernel may reach another device: no remote copies, remote signals or barrier semaphores. Data moves between devices by JAX's collectives and lax.ppermute only.
A program may use at most 256 MiB of HBM per device.

```python
import jax
import jax.numpy as jnp
from jax import lax

D = 768
H = 12
DH = 64
NB = 32
FF = 3072
EXPERTS = 4
LEN = 1024
CTX_TOK = 512
CAP = 256
SEQS = 32


def draw_routes(key, part):
    key = jax.random.fold_in(key, 7)
    block_count = SEQS * (LEN // CTX_TOK)
    hot_key, order_key, first_key, second_key = jax.random.split(key, 4)
    hot_expert = jax.random.randint(hot_key, (), 0, EXPERTS)
    orders = jax.vmap(lambda sub_key: jax.random.permutation(sub_key, CTX_TOK))(jax.random.split(order_key, block_count))
    first_pick = jax.random.randint(first_key, (block_count, CTX_TOK), 0, EXPERTS - 1)
    second_pick = jax.random.randint(second_key, (block_count, CTX_TOK), 0, EXPERTS - 1)
    offsets = 1 + jnp.minimum(first_pick, second_pick)
    chosen = jnp.where(orders < CAP, hot_expert, (hot_expert + offsets) % EXPERTS)
    return chosen.reshape(SEQS, LEN).astype(jnp.int32)


def steps_of(rng, shape, pieces, smallest, high):
    level = 1.0
    for axis_at, shards_of in pieces:
        steps = jax.random.uniform(jax.random.fold_in(jax.random.fold_in(rng, 6), axis_at), (shards_of,), jnp.float32, smallest / len(pieces), high / len(pieces))
        level = level * jnp.repeat(jnp.exp(steps), shape[axis_at] // shards_of).reshape((-1,) + (1,) * (len(shape) - 1 - axis_at))
    return level


def gaussian(own_key, shape, deviation, reach, pieces=(), kind=jnp.bfloat16):
    drawn = deviation * jax.random.normal(own_key, shape, jnp.float32)
    if pieces:
        drawn = drawn * steps_of(own_key, shape, pieces, -0.22, 0.18)
    return jnp.clip(drawn, -reach, reach).astype(kind)


def setup_inputs(seed: int = 0) -> dict:
    splits = jax.random.split(jax.random.key(seed), 14)
    tokens = gaussian(splits[0], (SEQS, LEN, D), 1.0, 6.0, ((0, 16), (1, 2)))
    cotangent = gaussian(splits[1], (SEQS, LEN, D), 1.0, 6.0, ((0, 16), (1, 2)))
    routes = draw_routes(jax.random.fold_in(splits[13], 71), 0)
    norm1_gain = jnp.clip(1.0 + 0.18 * jax.random.normal(splits[3], (D,), jnp.float32), 0.1, 1.9)
    query_weight = gaussian(splits[4], (D, D), (4 * D) ** -0.5, 0.109375)
    key_weight = gaussian(splits[5], (D, D), (4 * D) ** -0.5, 0.109375)
    value_weight = gaussian(splits[6], (D, D), D ** -0.5, 0.21875)
    output_weight = gaussian(splits[7], (D, D), (max(D // 16, 1)) ** -0.5, 0.875)
    bias_table = gaussian(splits[8], (NB, H), 1.0, 4.0, (), jnp.float32)
    norm2_gain = jnp.clip(1.0 + 0.18 * jax.random.normal(splits[9], (D,), jnp.float32), 0.1, 1.9)
    router_weight = gaussian(splits[10], (D, EXPERTS), (2 * D) ** -0.5, 0.15625)
    w_in = gaussian(splits[11], (EXPERTS, D, FF), D ** -0.5, 0.21875, ((0, 4),))
    w_out = gaussian(splits[12], (EXPERTS, FF, D), (FF // 16) ** -0.5, 0.4375, ((0, 4),))
    return {"tokens": tokens, "cotangent": cotangent, "routes": routes, "norm1_gain": norm1_gain, "query_weight": query_weight, "key_weight": key_weight, "value_weight": value_weight, "output_weight": output_weight, "bias_table": bias_table, "norm2_gain": norm2_gain, "router_weight": router_weight, "w_in": w_in, "w_out": w_out}


bucket_edges = (1, 2, 3, 4, 5, 6, 7, 8, 12, 16, 23, 32, 46, 64, 91)
norm_eps = 1e-06
precise_result = lax.Precision.HIGHEST

@jax.custom_vjp
def low(v):
    return lax.optimization_barrier(v.astype(jnp.bfloat16)).astype(jnp.float32)

@jax.custom_vjp
def low_back(v):
    return v

def low_keep(v):
    return (low(v), None)

def low_pass(kept, grad):
    return (grad,)

def back_keep(v):
    return (v, None)

def back_low(kept, grad):
    return (low(grad),)
low.defvjp(low_keep, low_pass)
low_back.defvjp(back_keep, back_low)

def bucket_of(relative):
    distance = jnp.abs(relative)
    half_bucket = jnp.zeros(relative.shape, jnp.int32)
    for threshold in bucket_edges:
        half_bucket = half_bucket + (distance >= threshold).astype(jnp.int32)
    return half_bucket + 16 * (relative > 0).astype(jnp.int32)

def rms_norm(value_rows, gain_vector):
    inv_scale = lax.rsqrt(lax.optimization_barrier(jnp.mean(value_rows * value_rows, axis=-1, keepdims=True)) + norm_eps)
    return value_rows * inv_scale * gain_vector

def attend_block(query_rows, start_row, key_seq, value_seq, bias_table):
    row_count = query_rows.shape[0]
    seq_len = key_seq.shape[0]
    q_heads = query_rows.reshape(row_count, H, DH)
    k_heads = key_seq.reshape(seq_len, H, DH)
    v_heads = value_seq.reshape(seq_len, H, DH)
    scores = jnp.einsum('qhd,khd->hqk', q_heads, k_heads, precision=precise_result)
    query_pos = start_row + jnp.arange(row_count, dtype=jnp.int32)
    relative = jnp.arange(seq_len, dtype=jnp.int32)[None, :] - query_pos[:, None]
    bias_rows = jnp.transpose(bias_table[bucket_of(relative)], (2, 0, 1))
    scores = low_back(scores + bias_rows)
    row_max = lax.optimization_barrier(jnp.max(scores, axis=-1, keepdims=True))
    log_total = row_max + jnp.log(lax.optimization_barrier(jnp.sum(jnp.exp(scores - row_max), axis=-1, keepdims=True)))
    weights_low = low(jnp.exp(scores - log_total))
    mixed = jnp.einsum('hqk,khd->qhd', weights_low, v_heads, precision=precise_result)
    return mixed.reshape(row_count, H * DH)

def attend_sequence(query_seq, key_seq, value_seq, bias_table):
    seq_len = query_seq.shape[0]
    block_rows = min(seq_len, 512)
    starts = jnp.arange(seq_len // block_rows, dtype=jnp.int32) * block_rows
    query_blocks = query_seq.reshape(seq_len // block_rows, block_rows, query_seq.shape[1])
    checked = jax.checkpoint(attend_block)
    mixed = lax.map(lambda pair: checked(pair[0], pair[1], key_seq, value_seq, bias_table), (query_blocks, starts))
    return mixed.reshape(seq_len, query_seq.shape[1])

def one_expert(input_tokens, valid_rows, weight_in, weight_out):
    pre_act = low_back(jnp.dot(input_tokens * valid_rows, weight_in, preferred_element_type=jnp.float32, precision=precise_result))
    hidden = low_back(low(jax.nn.gelu(pre_act, approximate=True)))
    outputs = low_back(low(jnp.dot(hidden, weight_out, preferred_element_type=jnp.float32, precision=precise_result)))
    return outputs * valid_rows

def experts_apply(token_rows, route_flat, w_in, w_out):
    total_rows = token_rows.shape[0]
    room = min(total_rows, total_rows // CTX_TOK * CAP)
    order = jnp.argsort(route_flat, stable=True).astype(jnp.int32)
    labels = jnp.arange(EXPERTS, dtype=jnp.int32)
    counts = lax.optimization_barrier(jnp.sum((route_flat[:, None] == labels[None, :]).astype(jnp.int32), axis=0)).astype(jnp.int32)
    firsts = (jnp.cumsum(counts) - counts).astype(jnp.int32)
    places = jnp.arange(room, dtype=jnp.int32)
    checked = jax.checkpoint(one_expert)
    result = jnp.zeros(token_rows.shape, jnp.float32)
    for expert_index in range(EXPERTS):
        valid_rows = (places < counts[expert_index]).astype(jnp.float32)[:, None]
        picked = order[jnp.minimum(firsts[expert_index] + places, total_rows - 1).astype(jnp.int32)]
        outputs = checked(token_rows[picked], valid_rows, w_in[expert_index], w_out[expert_index])
        result = result.at[picked].add(outputs)
    return result

def layer(input_tokens, norm1_gain, query_weight, key_weight, value_weight, output_weight, bias_table, norm2_gain, router_weight, w_in, w_out, routes):
    attention_input = low(rms_norm(input_tokens, norm1_gain))
    query_matrix = low_back(low(jnp.einsum('mbw,wx->mbx', attention_input, query_weight, precision=precise_result)))
    key_rows = low_back(low(jnp.einsum('mbw,wx->mbx', attention_input, key_weight, precision=precise_result)))
    value_rows = low_back(low(jnp.einsum('mbw,wx->mbx', attention_input, value_weight, precision=precise_result)))
    mixed = lax.map(lambda triple: attend_sequence(triple[0], triple[1], triple[2], bias_table), (query_matrix, key_rows, value_rows))
    attention_result = low_back(low(mixed))
    first_residual1 = input_tokens + low_back(jnp.einsum('mbw,wx->mbx', attention_result, output_weight, precision=precise_result))
    router_input = low(rms_norm(first_residual1, norm2_gain))
    router_scores = jnp.einsum('mbw,wx->mbx', router_input, router_weight, precision=precise_result)
    expert_onehot = (routes[..., None] == jnp.arange(EXPERTS, dtype=jnp.int32)).astype(jnp.float32)
    gates = lax.optimization_barrier(jnp.sum(jax.nn.softmax(router_scores, axis=-1) * expert_onehot, axis=-1))
    expert_in = low_back(router_input)
    model_width = input_tokens.shape[2]
    expert_tok = experts_apply(expert_in.reshape(-1, model_width), routes.reshape(-1), w_in, w_out).reshape(input_tokens.shape)
    return first_residual1 + gates[..., None] * expert_tok

def reference(tokens, cotangent, routes, norm1_gain, query_weight, key_weight, value_weight, output_weight, bias_table, norm2_gain, router_weight, w_in, w_out):

    def forward(input_tokens, gain_one, query_w, key_w, value_w, output_w, table, gain_two, router_w, in_w, out_w):
        return layer(input_tokens, gain_one, query_w, key_w, value_w, output_w, table, gain_two, router_w, in_w, out_w, routes)
    primals = (tokens.astype(jnp.float32), norm1_gain.astype(jnp.float32), query_weight.astype(jnp.float32), key_weight.astype(jnp.float32), value_weight.astype(jnp.float32), output_weight.astype(jnp.float32), bias_table.astype(jnp.float32), norm2_gain.astype(jnp.float32), router_weight.astype(jnp.float32), w_in.astype(jnp.float32), w_out.astype(jnp.float32))
    result, pullback = jax.vjp(forward, *primals)
    grads = pullback(cotangent.astype(jnp.float32))
    return (result.astype(jnp.bfloat16), grads[0], grads[1], grads[2], grads[3], grads[4], grads[5], grads[6], grads[7], grads[8], grads[9], grads[10])
```

```python
import jax
import jax.numpy as jnp
import numpy as np
from jax import lax
from jax.experimental import pallas as pl
from jax.experimental.pallas import tpu as pltpu
from jax.sharding import PartitionSpec as P

DH = 64
QB = 256

bucket_edges = (1, 2, 3, 4, 5, 6, 7, 8, 12, 16, 23, 32, 46, 64, 91)
norm_eps = 1e-06
precise_result = lax.Precision.HIGHEST


def bucket_of(relative):
    distance = jnp.abs(relative)
    half_bucket = jnp.zeros(relative.shape, jnp.int32)
    for threshold in bucket_edges:
        half_bucket = half_bucket + (distance >= threshold).astype(jnp.int32)
    return half_bucket + 16 * (relative > 0).astype(jnp.int32)


def bucket_grid(row_start, row_count, col_count):
    row_pos = row_start + jnp.arange(row_count, dtype=jnp.int32)
    col_pos = jnp.arange(col_count, dtype=jnp.int32)
    return bucket_of(col_pos[None, :] - row_pos[:, None])


def bias_grid(buckets, table_column, bucket_count):
    result = jnp.zeros(buckets.shape, jnp.float32)
    for label in range(bucket_count):
        result = result + jnp.where(buckets == label, table_column[label], 0.0)
    return result


def fold_buckets(buckets, grad_sum, bucket_count):
    return jnp.stack(
        [jnp.sum(jnp.where(buckets == label, grad_sum, 0.0)) for label in range(bucket_count)]
    )


def head_slice(value_rows, head_index, head_size):
    return lax.dynamic_slice_in_dim(value_rows, head_index * head_size, head_size, 2)


def put_head(target, portion, head_index, head_size):
    return lax.dynamic_update_slice_in_dim(target, portion, head_index * head_size, 2)


def head_scores(q_head, k_head, buckets, bias_table, head_index):
    table_column = lax.dynamic_index_in_dim(bias_table, head_index, 1, keepdims=False)
    scores = jnp.einsum("sqd,skd->sqk", q_head, k_head, preferred_element_type=jnp.float32)
    return scores + bias_grid(buckets, table_column, bias_table.shape[0])[None]


def attend_rows(query_matrix, keys_whole, values_whole, buckets, bias_table, head_size):
    seq_count, row_count, feature_width = query_matrix.shape
    head_count = feature_width // head_size

    def one_head(head_index, running):
        attention_result, log_totals = running
        scores = head_scores(
            head_slice(query_matrix, head_index, head_size),
            head_slice(keys_whole, head_index, head_size),
            buckets,
            bias_table,
            head_index,
        )
        row_max = jnp.max(scores, axis=-1, keepdims=True)
        log_total = row_max + jnp.log(jnp.sum(jnp.exp(scores - row_max), axis=-1, keepdims=True))
        weights_low = jnp.exp(scores - log_total).astype(jnp.bfloat16)
        portion = jnp.einsum(
            "sqk,skd->sqd",
            weights_low,
            head_slice(values_whole, head_index, head_size),
            preferred_element_type=jnp.float32,
        )
        attention_result = put_head(attention_result, portion, head_index, head_size)
        log_totals = lax.dynamic_update_index_in_dim(log_totals, log_total[..., 0], head_index, 0)
        return (attention_result, log_totals)

    initial = (
        jnp.zeros((seq_count, row_count, feature_width), jnp.float32),
        jnp.zeros((head_count, seq_count, row_count), jnp.float32),
    )
    return lax.fori_loop(0, head_count, one_head, initial)


def attend_back_rows(
    query_matrix, keys_whole, values_whole, mixed_grad, log_totals, buckets, bias_table, head_size
):
    seq_count, row_count, feature_width = query_matrix.shape
    col_count = keys_whole.shape[1]
    head_count = feature_width // head_size
    bucket_count = bias_table.shape[0]

    def one_head(head_index, running):
        query_grad, deltas, diag_grad, key_part, value_part = running
        q_head = head_slice(query_matrix, head_index, head_size)
        k_head = head_slice(keys_whole, head_index, head_size)
        v_head = head_slice(values_whole, head_index, head_size)
        g_head = head_slice(mixed_grad, head_index, head_size)
        scores = head_scores(q_head, k_head, buckets, bias_table, head_index)
        weights = jnp.exp(scores - log_totals[head_index][..., None])
        weight_grad = jnp.einsum("sqd,skd->sqk", g_head, v_head, preferred_element_type=jnp.float32)
        delta_row = jnp.sum(weights * weight_grad, axis=-1)
        score_grad = (weights * (weight_grad - delta_row[..., None])).astype(jnp.bfloat16)
        query_grad = put_head(
            query_grad,
            jnp.einsum("sqk,skd->sqd", score_grad, k_head, preferred_element_type=jnp.float32),
            head_index,
            head_size,
        )
        deltas = lax.dynamic_update_index_in_dim(deltas, delta_row, head_index, 0)
        folded = fold_buckets(
            buckets, jnp.sum(score_grad.astype(jnp.float32), axis=0), bucket_count
        )
        diag_grad = lax.dynamic_update_index_in_dim(diag_grad, folded, head_index, 0)
        key_part = put_head(
            key_part,
            jnp.einsum("sqk,sqd->skd", score_grad, q_head, preferred_element_type=jnp.float32),
            head_index,
            head_size,
        )
        value_part = put_head(
            value_part,
            jnp.einsum(
                "sqk,sqd->skd",
                weights.astype(jnp.bfloat16),
                g_head,
                preferred_element_type=jnp.float32,
            ),
            head_index,
            head_size,
        )
        return (query_grad, deltas, diag_grad, key_part, value_part)

    key_shape = (seq_count, col_count, feature_width)
    initial = (
        jnp.zeros((seq_count, row_count, feature_width), jnp.float32),
        jnp.zeros((head_count, seq_count, row_count), jnp.float32),
        jnp.zeros((head_count, bucket_count), jnp.float32),
        jnp.zeros(key_shape, jnp.float32),
        jnp.zeros(key_shape, jnp.float32),
    )
    return lax.fori_loop(0, head_count, one_head, initial)


def bucket_np(relative):
    half_bucket = np.zeros(relative.shape, np.int32)
    for threshold in bucket_edges:
        half_bucket = half_bucket + (np.abs(relative) >= threshold)
    return half_bucket + 16 * (relative > 0)


def bias_lines(bias_table):
    lane = np.arange(4 * QB)
    both = np.stack([lane - 2 * QB, 2 * QB - lane])
    onehot = (bucket_np(both)[..., None] == np.arange(32)).astype(np.float32)
    return jnp.einsum("lcb,bh->hlc", jnp.asarray(onehot), bias_table, precision=lax.Precision.HIGHEST)

def fwd_kernel(lines_ref, q_ref, k_ref, v_ref, o_ref, band_ref):
    n = q_ref.shape[0] // QB
    lane = lax.broadcasted_iota(jnp.int32, (QB, 128), 1)
    for h in range(2):
        line = lines_ref[h, 0:1, :]
        spread = pltpu.roll(jnp.broadcast_to(line, (QB, 4 * QB)), 0, 1, stride=1, stride_axis=0)
        band_ref[h] = spread[:, QB:]
    for i in range(n):
        rows = slice(i * QB, (i + 1) * QB)
        outs = []
        for h in range(2):
            low_bias = lines_ref[h, 0:1, 0:1]
            high_bias = lines_ref[h, 0:1, 4 * QB - 1:]
            q = jnp.where((lane < 64) == (h == 0), q_ref[rows, :], 0)
            s = lax.dot_general(q, k_ref[...], (((1,), (1,)), ((), ())), preferred_element_type=jnp.float32)
            parts = []
            for j in range(n):
                d = j - i
                b = band_ref[h, :, (d + 1) * QB:(d + 2) * QB] if abs(d) <= 1 else (low_bias if d < 0 else high_bias)
                parts.append(s[:, j * QB:(j + 1) * QB] + b)
            s = jnp.concatenate(parts, axis=1)
            m = jnp.max(s, axis=1, keepdims=True)
            p = jnp.exp(s - m)
            l = jnp.sum(p, axis=1, keepdims=True)
            o = jnp.dot(p.astype(jnp.bfloat16), v_ref[...], preferred_element_type=jnp.float32)
            outs.append(o * (1.0 / l))
        o_ref[rows, :] = jnp.where(lane < 64, outs[0], outs[1]).astype(jnp.bfloat16)

def attend(q, k, v, lines):
    length, width = q.shape
    col = pl.BlockSpec((length, 128), lambda h: (0, h))
    return pl.pallas_call(
        fwd_kernel,
        grid=(width // 128,),
        in_specs=[pl.BlockSpec((2, 2, 4 * QB), lambda h: (h, 0, 0)), col, col, col],
        out_specs=col,
        out_shape=jax.ShapeDtypeStruct((length, width), jnp.bfloat16),
        scratch_shapes=[pltpu.VMEM((2, QB, 3 * QB), jnp.float32)],
        compiler_params=pltpu.CompilerParams(vmem_limit_bytes=48 << 20),
        name="attend",
    )(lines, q, k, v)

def bwd_kernel(lines_ref, q_ref, k_ref, v_ref, g_ref, dq_ref, dk_ref, dv_ref, diag_ref, far_ref, band_ref, acc_ref, far_acc, dk_acc, dv_acc):
    n = q_ref.shape[0] // QB
    lane = lax.broadcasted_iota(jnp.int32, (QB, 128), 1)
    for h in range(2):
        for t in range(3):
            start = 2 * QB - (t - 1) * QB - QB
            line = lines_ref[h, 1:2, start:start + 2 * QB]
            spread = pltpu.roll(jnp.broadcast_to(line, (QB, 2 * QB)), QB, 1, stride=1, stride_axis=0)
            band_ref[h, t * QB:(t + 1) * QB, :] = spread[:, :QB]
    acc_ref[...] = jnp.zeros_like(acc_ref)
    far_acc[...] = jnp.zeros_like(far_acc)
    for i in range(n):
        rows = slice(i * QB, (i + 1) * QB)
        grads = []
        for h in range(2):
            keep = (lane < 64) == (h == 0)
            low_bias = lines_ref[h, 0:1, 0:1]
            high_bias = lines_ref[h, 0:1, 4 * QB - 1:]
            q = jnp.where(keep, q_ref[rows, :], 0)
            g = jnp.where(keep, g_ref[rows, :], 0)
            s = lax.dot_general(k_ref[...], q, (((1,), (1,)), ((), ())), preferred_element_type=jnp.float32)
            parts = []
            for j in range(n):
                d = j - i
                b = band_ref[h, (d + 1) * QB:(d + 2) * QB, :] if abs(d) <= 1 else (low_bias if d < 0 else high_bias)
                parts.append(s[j * QB:(j + 1) * QB, :] + b)
            s = jnp.concatenate(parts, axis=0)
            m = jnp.max(s, axis=0, keepdims=True)
            p = jnp.exp(s - m)
            w = p * (1.0 / jnp.sum(p, axis=0, keepdims=True))
            dp = lax.dot_general(v_ref[...], g, (((1,), (1,)), ((), ())), preferred_element_type=jnp.float32)
            delta = jnp.sum(w * dp, axis=0, keepdims=True)
            ds = w * (dp - delta)
            for j in range(n):
                d = j - i
                tile = ds[j * QB:(j + 1) * QB, :]
                if abs(d) <= 1:
                    acc_ref[h, (d + 1) * QB:(d + 2) * QB, :] += tile
                else:
                    far_acc[h, 0 if d < 0 else 1] += jnp.sum(tile.reshape(QB // 8, 8, QB), axis=0)
            low = ds.astype(jnp.bfloat16)
            dv = jnp.dot(w.astype(jnp.bfloat16), g, preferred_element_type=jnp.float32)
            dk = jnp.dot(low, q, preferred_element_type=jnp.float32)
            if i == 0 and h == 0:
                dv_acc[...] = dv
                dk_acc[...] = dk
            else:
                dv_acc[...] += dv
                dk_acc[...] += dk
            grads.append(lax.dot_general(low, k_ref[...], (((0,), (0,)), ((), ())), preferred_element_type=jnp.float32))
        dq_ref[rows, :] = jnp.where(lane < 64, grads[0], grads[1]).astype(jnp.bfloat16)
    dk_ref[...] = dk_acc[...].astype(jnp.bfloat16)
    dv_ref[...] = dv_acc[...].astype(jnp.bfloat16)
    row = lax.broadcasted_iota(jnp.int32, (8, 2 * QB), 0)
    for h in range(2):
        for t in range(3):
            tile = acc_ref[h, t * QB:(t + 1) * QB, :]
            wide = jnp.concatenate([tile, jnp.zeros_like(tile)], axis=1)
            groups = sum(pltpu.roll(wide[8 * e:8 * e + 8], QB - 8 * e, 1) for e in range(QB // 8))
            turned = groups * (row == 0).astype(jnp.float32)
            for e in range(1, 8):
                turned = turned + pltpu.roll(jnp.where(row == e, groups, 0.0), 2 * QB - e, 1)
            diag_ref[h, t:t + 1, :] = jnp.sum(turned, axis=0, keepdims=True)
        far_ref[h, 0:1] = jnp.sum(far_acc[h, 0], axis=0, keepdims=True)
        far_ref[h, 1:2] = jnp.sum(far_acc[h, 1], axis=0, keepdims=True)

def attend_back(q, k, v, g, lines):
    length, width = q.shape
    heads = width // 64
    col = pl.BlockSpec((length, 128), lambda h: (0, h))
    out = jax.ShapeDtypeStruct((length, width), jnp.bfloat16)
    dq, dk, dv, diag, far = pl.pallas_call(
        bwd_kernel,
        grid=(width // 128,),
        in_specs=[pl.BlockSpec((2, 2, 4 * QB), lambda h: (h, 0, 0)), col, col, col, col],
        out_specs=[col, col, col, pl.BlockSpec((2, 3, 2 * QB), lambda h: (h, 0, 0)), pl.BlockSpec((2, 2, QB), lambda h: (h, 0, 0))],
        out_shape=[out, out, out, jax.ShapeDtypeStruct((heads, 3, 2 * QB), jnp.float32), jax.ShapeDtypeStruct((heads, 2, QB), jnp.float32)],
        scratch_shapes=[
            pltpu.VMEM((2, 3 * QB, QB), jnp.float32),
            pltpu.VMEM((2, 3 * QB, QB), jnp.float32),
            pltpu.VMEM((2, 2, 8, QB), jnp.float32),
            pltpu.VMEM((length, 128), jnp.float32),
            pltpu.VMEM((length, 128), jnp.float32),
        ],
        compiler_params=pltpu.CompilerParams(vmem_limit_bytes=48 << 20),
        name="attend_back",
    )(lines, q, k, v, g)
    r = (np.arange(3)[:, None] - 1) * QB - (np.arange(2 * QB)[None] - QB)
    onehot = (bucket_np(r)[..., None] == np.arange(32)).astype(np.float32)
    dbias = jnp.einsum("htx,txb->bh", diag, jnp.asarray(onehot), precision=lax.Precision.HIGHEST)
    far = jnp.sum(far, axis=2)
    dbias = dbias.at[15].add(far[:, 0]).at[31].add(far[:, 1])
    return dq, dk, dv, dbias


def expert_kernel(label_ref, x_ref, u_ref, router_ref, win_ref, wout_ref, rows_ref, back_ref, dw_ref, drouter_ref,
                  xt_ref, g_ref, gt_ref, prob_ref, out_acc, back_acc, hid_ref, pre_ref):
    step = pl.program_id(0)
    count = x_ref.shape[0]
    tile = min(512, count)
    lane = lax.broadcasted_iota(jnp.int32, (tile, 128), 1)
    own = lane == label_ref[0]
    spans = [slice(r * tile, (r + 1) * tile) for r in range(count // tile)]

    @pl.when(step == 0)
    def _():
        for rows in spans:
            logits = jnp.dot(x_ref[rows, :], router_ref[...], preferred_element_type=jnp.float32)
            logits = jnp.where(lane < 4, logits, -jnp.inf)
            raised = jnp.exp(logits - jnp.max(logits, axis=1, keepdims=True))
            prob = raised / jnp.sum(raised, axis=1, keepdims=True)
            prob_ref[rows, :] = prob
            gate = jnp.sum(jnp.where(own, prob, 0.0), axis=1, keepdims=True)
            grad = (gate * u_ref[rows, :].astype(jnp.float32)).astype(jnp.bfloat16)
            g_ref[rows, :] = grad
            gt_ref[:, rows] = grad.T
            xt_ref[:, rows] = x_ref[rows, :].T
        out_acc[...] = jnp.zeros_like(out_acc)
        back_acc[...] = jnp.zeros_like(back_acc)

    for rows in spans:
        pre = jnp.dot(x_ref[rows, :], win_ref[...], preferred_element_type=jnp.float32)
        square = pre * pre
        turn = jnp.tanh(0.7978845608028654 * pre * (1.0 + 0.044715 * square))
        half = 0.5 * (1.0 + turn)
        hidden = (pre * half).astype(jnp.bfloat16)
        slope = half + pre * (0.5 * (1.0 - turn * turn)) * (0.7978845608028654 + 0.1070322243 * square)
        hid_ref[rows, :] = hidden
        out_acc[rows, :] += jnp.dot(hidden, wout_ref[...], preferred_element_type=jnp.float32)
        hidden_grad = lax.dot_general(g_ref[rows, :], wout_ref[...], (((1,), (1,)), ((), ())), preferred_element_type=jnp.float32)
        pre_grad = (hidden_grad * slope).astype(jnp.bfloat16)
        pre_ref[rows, :] = pre_grad
        back_acc[rows, :] += lax.dot_general(pre_grad, win_ref[...], (((1,), (1,)), ((), ())), preferred_element_type=jnp.float32)
    dw_ref[0] = jnp.dot(xt_ref[...], pre_ref[...], preferred_element_type=jnp.float32).astype(dw_ref.dtype)
    dw_ref[1] = jnp.dot(gt_ref[...], hid_ref[...], preferred_element_type=jnp.float32).astype(dw_ref.dtype)

    @pl.when(step == pl.num_programs(0) - 1)
    def _():
        total = jnp.zeros(drouter_ref.shape, jnp.float32)
        for rows in spans:
            prob = prob_ref[rows, :]
            gate = jnp.sum(jnp.where(own, prob, 0.0), axis=1, keepdims=True)
            out = out_acc[rows, :].astype(jnp.bfloat16).astype(jnp.float32)
            rows_ref[rows, :] = (gate * out).astype(jnp.bfloat16)
            gate_grad = jnp.sum(u_ref[rows, :].astype(jnp.float32) * out, axis=1, keepdims=True)
            logit_grad = prob * (jnp.where(own, gate_grad, 0.0) - gate * gate_grad)
            high = logit_grad.astype(jnp.bfloat16)
            low = (logit_grad - high.astype(jnp.float32)).astype(jnp.bfloat16)
            back = back_acc[rows, :].astype(jnp.bfloat16).astype(jnp.float32)
            for part in (high, low):
                back += lax.dot_general(part, router_ref[...], (((1,), (1,)), ((), ())), preferred_element_type=jnp.float32)
                total += jnp.dot(xt_ref[:, rows], part, preferred_element_type=jnp.float32)
            back_ref[rows, :] = back.astype(jnp.bfloat16)
        drouter_ref[...] = total


def run_expert(label, rows_in, upstream_rows, router_weight, w_in, w_out):
    count, width = rows_in.shape
    inner = w_in.shape[1]
    chunk = 256
    once = pl.Buffered(1)
    whole = lambda f, lab: (0, 0)
    router_wide = jnp.pad(router_weight, ((0, 0), (0, 128 - router_weight.shape[1])))
    return pl.pallas_call(
        expert_kernel,
        grid_spec=pltpu.PrefetchScalarGridSpec(
            num_scalar_prefetch=1,
            grid=(inner // chunk,),
            in_specs=[
                pl.BlockSpec((count, width), whole, pipeline_mode=once),
                pl.BlockSpec((count, width), whole, pipeline_mode=once),
                pl.BlockSpec((width, 128), whole, pipeline_mode=once),
                pl.BlockSpec((width, chunk), lambda f, lab: (0, f)),
                pl.BlockSpec((chunk, width), lambda f, lab: (f, 0)),
            ],
            out_specs=[
                pl.BlockSpec((count, width), whole, pipeline_mode=once),
                pl.BlockSpec((count, width), whole, pipeline_mode=once),
                pl.BlockSpec((2, width, chunk), lambda f, lab: (0, 0, f)),
                pl.BlockSpec((width, 128), whole, pipeline_mode=once),
            ],
            scratch_shapes=[
                pltpu.VMEM((width, count), jnp.bfloat16),
                pltpu.VMEM((count, width), jnp.bfloat16),
                pltpu.VMEM((width, count), jnp.bfloat16),
                pltpu.VMEM((count, 128), jnp.float32),
                pltpu.VMEM((count, width), jnp.float32),
                pltpu.VMEM((count, width), jnp.float32),
                pltpu.VMEM((count, chunk), jnp.bfloat16),
                pltpu.VMEM((count, chunk), jnp.bfloat16),
            ],
        ),
        out_shape=[
            jax.ShapeDtypeStruct((count, width), jnp.bfloat16),
            jax.ShapeDtypeStruct((count, width), jnp.bfloat16),
            jax.ShapeDtypeStruct((2, width, inner), jnp.bfloat16),
            jax.ShapeDtypeStruct((width, 128), jnp.float32),
        ],
        compiler_params=pltpu.CompilerParams(vmem_limit_bytes=60 << 20),
        name="experts",
    )(label, rows_in, upstream_rows, router_wide, w_in, w_out)


def make_dispatch(routes, labels, capacity):
    hits = (routes[..., None] == labels).astype(jnp.int32)
    places = jnp.sum((jnp.cumsum(hits, axis=1) - 1) * hits, axis=-1)
    expert_match = routes[None, :, None, :] == labels[:, None, None, None]
    slot_match = places[:, None, :] == jnp.arange(capacity, dtype=jnp.int32)[None, :, None]
    return (expert_match & slot_match[None]).astype(jnp.bfloat16)


def exchange(pieces, axis, sign):
    size = lax.axis_size(axis)
    return [pieces[0]] + [
        lax.ppermute(pieces[turn], axis, [(at, (at + sign * turn) % size) for at in range(size)])
        for turn in range(1, size)
    ]


def trade(blocks):
    at = lax.axis_index("ctx")
    mine = lax.dynamic_index_in_dim(blocks, at, 0, keepdims=False)
    other = lax.dynamic_index_in_dim(blocks, 1 - at, 0, keepdims=False)
    arrived = lax.ppermute(other, "ctx", [(0, 1), (1, 0)])
    return jnp.stack([jnp.where(at == 0, mine, arrived), jnp.where(at == 0, arrived, mine)])


def norm_scale(value_rows):
    return lax.rsqrt(jnp.mean(value_rows * value_rows, axis=-1, keepdims=True) + norm_eps)


def norm_back(value_rows, scale, gain_vector, grad_rows):
    scaled = grad_rows * gain_vector
    shrink = jnp.mean(scaled * value_rows, axis=-1, keepdims=True) * scale * scale * scale
    return scale * scaled - value_rows * shrink, jnp.sum(grad_rows * value_rows * scale, axis=(0, 1))


def wide_dot(rows, weight):
    return jnp.einsum("sxd,de->sxe", rows, weight, preferred_element_type=jnp.float32)


def wide_dot_back(rows, weight):
    return jnp.einsum("sxe,de->sxd", rows, weight, preferred_element_type=jnp.float32)


def weight_dot(left, right):
    return jnp.einsum("sxd,sxe->de", left, right, preferred_element_type=jnp.float32)


def split_rows(flat):
    high = flat.astype(jnp.bfloat16)
    return high, (flat - high.astype(jnp.float32)).astype(jnp.bfloat16)


def sum_all(matrices, smalls):
    width = matrices[0].shape[1]
    flat = jnp.concatenate([jnp.ravel(small) for small in smalls])
    fill = -flat.shape[0] % (8 * width)
    flat = jnp.pad(flat, (0, fill)).reshape(-1, width)
    packed = jnp.concatenate([matrix.astype(jnp.bfloat16) for matrix in matrices] + list(split_rows(flat)))
    packed = lax.psum(packed, ("dp", "ctx", "expert")).astype(jnp.float32)
    outs, at = [], 0
    for matrix in matrices:
        outs.append(packed[at : at + matrix.shape[0]])
        at += matrix.shape[0]
    rows = flat.shape[0]
    flat = (packed[at : at + rows] + packed[at + rows : at + 2 * rows]).reshape(-1)
    at = 0
    for small in smalls:
        outs.append(flat[at : at + small.size].reshape(small.shape))
        at += small.size
    return outs


def per_device(
    tokens,
    cotangent,
    routes,
    norm1_gain,
    query_weight,
    key_weight,
    value_weight,
    output_weight,
    bias_table,
    norm2_gain,
    router_weight,
    w_in,
    w_out,
):
    seq_count, local_len, model_width = tokens.shape
    owners = lax.axis_size("expert")
    capacity = local_len // 2
    whole_seq = seq_count == 2 and lax.axis_size("ctx") == 2 and local_len % QB == 0
    if whole_seq:
        tokens, cotangent, routes = trade(tokens), trade(cotangent), trade(routes)
    label = lax.axis_index("expert")
    labels = (label + jnp.arange(owners, dtype=jnp.int32)) % owners
    dispatch = make_dispatch(routes, labels, capacity)

    def to_owners(rows):
        sent = jnp.einsum("escx,sxd->escd", dispatch, rows, preferred_element_type=jnp.float32)
        sent = sent.astype(jnp.bfloat16)
        return jnp.concatenate(exchange(list(sent), "expert", 1)).reshape(-1, model_width)

    def to_tokens(rows):
        pieces = list(rows.reshape(owners, seq_count, capacity, model_width))
        pieces = jnp.stack(exchange(pieces, "expert", -1))
        return jnp.einsum("escx,escd->sxd", dispatch, pieces, preferred_element_type=jnp.float32)

    upstream_rows = to_owners(cotangent)
    inputs = tokens.astype(jnp.float32)
    scale1 = norm_scale(inputs)
    attn_in = (inputs * scale1 * norm1_gain).astype(jnp.bfloat16)
    queries = wide_dot(attn_in, query_weight).astype(jnp.bfloat16)
    keys = wide_dot(attn_in, key_weight).astype(jnp.bfloat16)
    values = wide_dot(attn_in, value_weight).astype(jnp.bfloat16)
    if whole_seq:
        lines = bias_lines(bias_table)
        flat = (seq_count * local_len, model_width)
        qkv = [rows.reshape(flat) for rows in (queries, keys, values)]
        attended = attend(*qkv, lines).reshape(tokens.shape)
    else:
        first_pos = lax.axis_index("ctx") * local_len
        keys = lax.all_gather(keys, "ctx", axis=1, tiled=True)
        values = lax.all_gather(values, "ctx", axis=1, tiled=True)
        buckets = bucket_grid(first_pos, local_len, keys.shape[1])
        attended, log_totals = attend_rows(queries, keys, values, buckets, bias_table, DH)
        attended = attended.astype(jnp.bfloat16)
    residual1 = inputs + wide_dot(attended, output_weight)
    scale2 = norm_scale(residual1)
    router_in = (residual1 * scale2 * norm2_gain).astype(jnp.bfloat16)
    rows_in = to_owners(router_in)
    rows_out, rows_back, grad_experts, grad_router = run_expert(
        label.astype(jnp.int32).reshape(1), rows_in, upstream_rows, router_weight, w_in[0], w_out[0]
    )
    grad_router = grad_router[:, : router_weight.shape[1]]
    router_in_grad = to_tokens(rows_back)
    block_out = (residual1 + to_tokens(rows_out)).astype(jnp.bfloat16)
    grad_experts = lax.psum_scatter(grad_experts, ("dp", "ctx"), scatter_dimension=2, tiled=True)
    norm2_back, grad_norm2 = norm_back(residual1, scale2, norm2_gain, router_in_grad)
    residual_grad = cotangent.astype(jnp.float32) + norm2_back
    attn_grad = residual_grad.astype(jnp.bfloat16)
    grad_w_output = weight_dot(attended, attn_grad)
    mixed_grad = wide_dot_back(attn_grad, output_weight).astype(jnp.bfloat16)
    grad_w_output, grad_norm2, grad_router = sum_all([grad_w_output], [grad_norm2, grad_router])
    if whole_seq:
        *grads, grad_bias = attend_back(*qkv, mixed_grad.reshape(flat), lines)
        query_low, key_low, value_low = (rows.reshape(tokens.shape) for rows in grads)
    else:
        query_grad, _, diag_grad, key_part, value_part = attend_back_rows(
            queries, keys, values, mixed_grad, log_totals, buckets, bias_table, DH
        )
        grad_bias = diag_grad.T
        query_low = query_grad.astype(jnp.bfloat16)
        key_low = lax.psum_scatter(key_part, "ctx", scatter_dimension=1, tiled=True).astype(jnp.bfloat16)
        value_low = lax.psum_scatter(value_part, "ctx", scatter_dimension=1, tiled=True).astype(jnp.bfloat16)
    norm_in_grad = wide_dot_back(query_low, query_weight)
    norm_in_grad = norm_in_grad + wide_dot_back(key_low, key_weight)
    norm_in_grad = norm_in_grad + wide_dot_back(value_low, value_weight)
    norm1_back, grad_norm1 = norm_back(inputs, scale1, norm1_gain, norm_in_grad)
    d_tokens = residual_grad + norm1_back
    grad_w_query, grad_w_key, grad_w_value, grad_bias, grad_norm1 = sum_all(
        [weight_dot(attn_in, rows) for rows in (query_low, key_low, value_low)], [grad_bias, grad_norm1]
    )
    if whole_seq:
        block_out, d_tokens = trade(block_out), trade(d_tokens)
    grad_experts = grad_experts.astype(jnp.float32)
    return (
        block_out,
        d_tokens,
        grad_norm1,
        grad_w_query,
        grad_w_key,
        grad_w_value,
        grad_w_output,
        grad_bias,
        grad_norm2,
        grad_router,
        grad_experts[0][None],
        grad_experts[1].T[None],
    )


def solution(mesh):
    rows = P(("dp", "expert"), "ctx", None)
    in_specs = (rows, rows, P(("dp", "expert"), "ctx")) + (P(),) * 8 + (P("expert", None, None),) * 2
    out_specs = (rows, rows) + (P(),) * 8 + (P("expert", None, ("dp", "ctx")), P("expert", ("dp", "ctx"), None))
    return jax.shard_map(per_device, mesh=mesh, in_specs=in_specs, out_specs=out_specs, check_vma=False)
```

```python
import jax
import jax.numpy as jnp
import numpy as np
from jax import lax
from jax.experimental import pallas as pl
from jax.experimental.pallas import tpu as pltpu
from jax.sharding import PartitionSpec as P

DH = 64
QB = 256

bucket_edges = (1, 2, 3, 4, 5, 6, 7, 8, 12, 16, 23, 32, 46, 64, 91)
norm_eps = 1e-06
precise_result = lax.Precision.HIGHEST


def bucket_of(relative):
    distance = jnp.abs(relative)
    half_bucket = jnp.zeros(relative.shape, jnp.int32)
    for threshold in bucket_edges:
        half_bucket = half_bucket + (distance >= threshold).astype(jnp.int32)
    return half_bucket + 16 * (relative > 0).astype(jnp.int32)


def bucket_grid(row_start, row_count, col_count):
    row_pos = row_start + jnp.arange(row_count, dtype=jnp.int32)
    col_pos = jnp.arange(col_count, dtype=jnp.int32)
    return bucket_of(col_pos[None, :] - row_pos[:, None])


def bias_grid(buckets, table_column, bucket_count):
    result = jnp.zeros(buckets.shape, jnp.float32)
    for label in range(bucket_count):
        result = result + jnp.where(buckets == label, table_column[label], 0.0)
    return result


def fold_buckets(buckets, grad_sum, bucket_count):
    return jnp.stack(
        [jnp.sum(jnp.where(buckets == label, grad_sum, 0.0)) for label in range(bucket_count)]
    )


def head_slice(value_rows, head_index, head_size):
    return lax.dynamic_slice_in_dim(value_rows, head_index * head_size, head_size, 2)


def put_head(target, portion, head_index, head_size):
    return lax.dynamic_update_slice_in_dim(target, portion, head_index * head_size, 2)


def head_scores(q_head, k_head, buckets, bias_table, head_index):
    table_column = lax.dynamic_index_in_dim(bias_table, head_index, 1, keepdims=False)
    scores = jnp.einsum("sqd,skd->sqk", q_head, k_head, preferred_element_type=jnp.float32)
    return scores + bias_grid(buckets, table_column, bias_table.shape[0])[None]


def attend_rows(query_matrix, keys_whole, values_whole, buckets, bias_table, head_size):
    seq_count, row_count, feature_width = query_matrix.shape
    head_count = feature_width // head_size

    def one_head(head_index, running):
        attention_result, log_totals = running
        scores = head_scores(
            head_slice(query_matrix, head_index, head_size),
            head_slice(keys_whole, head_index, head_size),
            buckets,
            bias_table,
            head_index,
        )
        row_max = jnp.max(scores, axis=-1, keepdims=True)
        log_total = row_max + jnp.log(jnp.sum(jnp.exp(scores - row_max), axis=-1, keepdims=True))
        weights_low = jnp.exp(scores - log_total).astype(jnp.bfloat16)
        portion = jnp.einsum(
            "sqk,skd->sqd",
            weights_low,
            head_slice(values_whole, head_index, head_size),
            preferred_element_type=jnp.float32,
        )
        attention_result = put_head(attention_result, portion, head_index, head_size)
        log_totals = lax.dynamic_update_index_in_dim(log_totals, log_total[..., 0], head_index, 0)
        return (attention_result, log_totals)

    initial = (
        jnp.zeros((seq_count, row_count, feature_width), jnp.float32),
        jnp.zeros((head_count, seq_count, row_count), jnp.float32),
    )
    return lax.fori_loop(0, head_count, one_head, initial)


def attend_back_rows(
    query_matrix, keys_whole, values_whole, mixed_grad, log_totals, buckets, bias_table, head_size
):
    seq_count, row_count, feature_width = query_matrix.shape
    col_count = keys_whole.shape[1]
    head_count = feature_width // head_size
    bucket_count = bias_table.shape[0]

    def one_head(head_index, running):
        query_grad, deltas, diag_grad, key_part, value_part = running
        q_head = head_slice(query_matrix, head_index, head_size)
        k_head = head_slice(keys_whole, head_index, head_size)
        v_head = head_slice(values_whole, head_index, head_size)
        g_head = head_slice(mixed_grad, head_index, head_size)
        scores = head_scores(q_head, k_head, buckets, bias_table, head_index)
        weights = jnp.exp(scores - log_totals[head_index][..., None])
        weight_grad = jnp.einsum("sqd,skd->sqk", g_head, v_head, preferred_element_type=jnp.float32)
        delta_row = jnp.sum(weights * weight_grad, axis=-1)
        score_grad = (weights * (weight_grad - delta_row[..., None])).astype(jnp.bfloat16)
        query_grad = put_head(
            query_grad,
            jnp.einsum("sqk,skd->sqd", score_grad, k_head, preferred_element_type=jnp.float32),
            head_index,
            head_size,
        )
        deltas = lax.dynamic_update_index_in_dim(deltas, delta_row, head_index, 0)
        folded = fold_buckets(
            buckets, jnp.sum(score_grad.astype(jnp.float32), axis=0), bucket_count
        )
        diag_grad = lax.dynamic_update_index_in_dim(diag_grad, folded, head_index, 0)
        key_part = put_head(
            key_part,
            jnp.einsum("sqk,sqd->skd", score_grad, q_head, preferred_element_type=jnp.float32),
            head_index,
            head_size,
        )
        value_part = put_head(
            value_part,
            jnp.einsum(
                "sqk,sqd->skd",
                weights.astype(jnp.bfloat16),
                g_head,
                preferred_element_type=jnp.float32,
            ),
            head_index,
            head_size,
        )
        return (query_grad, deltas, diag_grad, key_part, value_part)

    key_shape = (seq_count, col_count, feature_width)
    initial = (
        jnp.zeros((seq_count, row_count, feature_width), jnp.float32),
        jnp.zeros((head_count, seq_count, row_count), jnp.float32),
        jnp.zeros((head_count, bucket_count), jnp.float32),
        jnp.zeros(key_shape, jnp.float32),
        jnp.zeros(key_shape, jnp.float32),
    )
    return lax.fori_loop(0, head_count, one_head, initial)


def bucket_np(relative):
    half_bucket = np.zeros(relative.shape, np.int32)
    for threshold in bucket_edges:
        half_bucket = half_bucket + (np.abs(relative) >= threshold)
    return half_bucket + 16 * (relative > 0)


def bias_lines(bias_table):
    lane = np.arange(4 * QB)
    both = np.stack([lane - 2 * QB, 2 * QB - lane])
    onehot = (bucket_np(both)[..., None] == np.arange(32)).astype(np.float32)
    return jnp.einsum("lcb,bh->hlc", jnp.asarray(onehot), bias_table, precision=lax.Precision.HIGHEST)

def fwd_kernel(first, lines_ref, q_ref, k_ref, v_ref, o_ref, band_ref):
    n = k_ref.shape[0] // QB
    lane = lax.broadcasted_iota(jnp.int32, (QB, 128), 1)
    for h in range(2):
        line = lines_ref[h, 0:1, :]
        spread = pltpu.roll(jnp.broadcast_to(line, (QB, 4 * QB)), 0, 1, stride=1, stride_axis=0)
        band_ref[h] = spread[:, QB:]
    for i in range(first, first + q_ref.shape[0] // QB):
        rows = slice((i - first) * QB, (i - first + 1) * QB)
        outs = []
        for h in range(2):
            low_bias = lines_ref[h, 0:1, 0:1]
            high_bias = lines_ref[h, 0:1, 4 * QB - 1:]
            q = jnp.where((lane < 64) == (h == 0), q_ref[rows, :], 0)
            s = lax.dot_general(q, k_ref[...], (((1,), (1,)), ((), ())), preferred_element_type=jnp.float32)
            parts = []
            for j in range(n):
                d = j - i
                b = band_ref[h, :, (d + 1) * QB:(d + 2) * QB] if abs(d) <= 1 else (low_bias if d < 0 else high_bias)
                parts.append(s[:, j * QB:(j + 1) * QB] + b)
            s = jnp.concatenate(parts, axis=1)
            m = jnp.max(s, axis=1, keepdims=True)
            p = jnp.exp(s - m)
            l = jnp.sum(p, axis=1, keepdims=True)
            o = jnp.dot(p.astype(jnp.bfloat16), v_ref[...], preferred_element_type=jnp.float32)
            outs.append(o * (1.0 / l))
        o_ref[rows, :] = jnp.where(lane < 64, outs[0], outs[1]).astype(jnp.bfloat16)

def attend(q, k, v, lines, first, count):
    length, width = q.shape
    col = pl.BlockSpec((length, 128), lambda h: (0, h))
    span = pl.BlockSpec((count, 128), lambda h: (first // count, h))
    return pl.pallas_call(
        lambda *refs: fwd_kernel(first // QB, *refs),
        grid=(width // 128,),
        in_specs=[pl.BlockSpec((2, 2, 4 * QB), lambda h: (h, 0, 0)), span, col, col],
        out_specs=pl.BlockSpec((count, 128), lambda h: (0, h)),
        out_shape=jax.ShapeDtypeStruct((count, width), jnp.bfloat16),
        scratch_shapes=[pltpu.VMEM((2, QB, 3 * QB), jnp.float32)],
        compiler_params=pltpu.CompilerParams(vmem_limit_bytes=48 << 20),
        cost_estimate=pl.CostEstimate(flops=40 * count * length * width, bytes_accessed=6 * length * width, transcendentals=count * length * width // 64),
        name="attend",
    )(lines, q, k, v)

def bwd_kernel(lines_ref, q_ref, k_ref, v_ref, g_ref, dq_ref, dk_ref, dv_ref, diag_ref, far_ref, band_ref, acc_ref, far_acc, dk_acc, dv_acc):
    n = q_ref.shape[0] // QB
    lane = lax.broadcasted_iota(jnp.int32, (QB, 128), 1)
    for h in range(2):
        for t in range(3):
            start = 2 * QB - (t - 1) * QB - QB
            line = lines_ref[h, 1:2, start:start + 2 * QB]
            spread = pltpu.roll(jnp.broadcast_to(line, (QB, 2 * QB)), QB, 1, stride=1, stride_axis=0)
            band_ref[h, t * QB:(t + 1) * QB, :] = spread[:, :QB]
    acc_ref[...] = jnp.zeros_like(acc_ref)
    far_acc[...] = jnp.zeros_like(far_acc)
    for i in range(n):
        rows = slice(i * QB, (i + 1) * QB)
        grads = []
        for h in range(2):
            keep = (lane < 64) == (h == 0)
            low_bias = lines_ref[h, 0:1, 0:1]
            high_bias = lines_ref[h, 0:1, 4 * QB - 1:]
            q = jnp.where(keep, q_ref[rows, :], 0)
            g = jnp.where(keep, g_ref[rows, :], 0)
            s = lax.dot_general(k_ref[...], q, (((1,), (1,)), ((), ())), preferred_element_type=jnp.float32)
            parts = []
            for j in range(n):
                d = j - i
                b = band_ref[h, (d + 1) * QB:(d + 2) * QB, :] if abs(d) <= 1 else (low_bias if d < 0 else high_bias)
                parts.append(s[j * QB:(j + 1) * QB, :] + b)
            s = jnp.concatenate(parts, axis=0)
            m = jnp.max(s, axis=0, keepdims=True)
            p = jnp.exp(s - m)
            w = p * (1.0 / jnp.sum(p, axis=0, keepdims=True))
            dp = lax.dot_general(v_ref[...], g, (((1,), (1,)), ((), ())), preferred_element_type=jnp.float32)
            delta = jnp.sum(w * dp, axis=0, keepdims=True)
            ds = w * (dp - delta)
            for j in range(n):
                d = j - i
                tile = ds[j * QB:(j + 1) * QB, :]
                if abs(d) <= 1:
                    acc_ref[h, (d + 1) * QB:(d + 2) * QB, :] += tile
                else:
                    far_acc[h, 0 if d < 0 else 1] += jnp.sum(tile.reshape(QB // 8, 8, QB), axis=0)
            low = ds.astype(jnp.bfloat16)
            dv = jnp.dot(w.astype(jnp.bfloat16), g, preferred_element_type=jnp.float32)
            dk = jnp.dot(low, q, preferred_element_type=jnp.float32)
            if i == 0 and h == 0:
                dv_acc[...] = dv
                dk_acc[...] = dk
            else:
                dv_acc[...] += dv
                dk_acc[...] += dk
            grads.append(lax.dot_general(low, k_ref[...], (((0,), (0,)), ((), ())), preferred_element_type=jnp.float32))
        dq_ref[rows, :] = jnp.where(lane < 64, grads[0], grads[1]).astype(jnp.bfloat16)
    dk_ref[...] = dk_acc[...].astype(jnp.bfloat16)
    dv_ref[...] = dv_acc[...].astype(jnp.bfloat16)
    row = lax.broadcasted_iota(jnp.int32, (8, 2 * QB), 0)
    for h in range(2):
        for t in range(3):
            tile = acc_ref[h, t * QB:(t + 1) * QB, :]
            wide = jnp.concatenate([tile, jnp.zeros_like(tile)], axis=1)
            groups = sum(pltpu.roll(wide[8 * e:8 * e + 8], QB - 8 * e, 1) for e in range(QB // 8))
            turned = groups * (row == 0).astype(jnp.float32)
            for e in range(1, 8):
                turned = turned + pltpu.roll(jnp.where(row == e, groups, 0.0), 2 * QB - e, 1)
            diag_ref[h, t:t + 1, :] = jnp.sum(turned, axis=0, keepdims=True)
        far_ref[h, 0:1] = jnp.sum(far_acc[h, 0], axis=0, keepdims=True)
        far_ref[h, 1:2] = jnp.sum(far_acc[h, 1], axis=0, keepdims=True)

def attend_back(q, k, v, g, lines):
    length, width = q.shape
    heads = width // 64
    col = pl.BlockSpec((length, 128), lambda h: (0, h))
    out = jax.ShapeDtypeStruct((length, width), jnp.bfloat16)
    dq, dk, dv, diag, far = pl.pallas_call(
        bwd_kernel,
        grid=(width // 128,),
        in_specs=[pl.BlockSpec((2, 2, 4 * QB), lambda h: (h, 0, 0)), col, col, col, col],
        out_specs=[col, col, col, pl.BlockSpec((2, 3, 2 * QB), lambda h: (h, 0, 0)), pl.BlockSpec((2, 2, QB), lambda h: (h, 0, 0))],
        out_shape=[out, out, out, jax.ShapeDtypeStruct((heads, 3, 2 * QB), jnp.float32), jax.ShapeDtypeStruct((heads, 2, QB), jnp.float32)],
        scratch_shapes=[
            pltpu.VMEM((2, 3 * QB, QB), jnp.float32),
            pltpu.VMEM((2, 3 * QB, QB), jnp.float32),
            pltpu.VMEM((2, 2, 8, QB), jnp.float32),
            pltpu.VMEM((length, 128), jnp.float32),
            pltpu.VMEM((length, 128), jnp.float32),
        ],
        compiler_params=pltpu.CompilerParams(vmem_limit_bytes=48 << 20),
        cost_estimate=pl.CostEstimate(flops=84 * length * length * width, bytes_accessed=14 * length * width, transcendentals=length * length * width // 64),
        name="attend_back",
    )(lines, q, k, v, g)
    r = (np.arange(3)[:, None] - 1) * QB - (np.arange(2 * QB)[None] - QB)
    onehot = (bucket_np(r)[..., None] == np.arange(32)).astype(np.float32)
    dbias = jnp.einsum("htx,txb->bh", diag, jnp.asarray(onehot), precision=lax.Precision.HIGHEST)
    far = jnp.sum(far, axis=2)
    dbias = dbias.at[15].add(far[:, 0]).at[31].add(far[:, 1])
    return dq, dk, dv, dbias


def expert_kernel(label_ref, *refs):
    count = (len(refs) - 10) // 4
    x_refs, u_refs = refs[:count], refs[count : 2 * count]
    router_ref, win_ref, wout_ref = refs[2 * count : 2 * count + 3]
    rest = refs[2 * count + 3 :]
    rows_refs, back_refs = rest[:count], rest[count : 2 * count]
    g_ref, hid_ref, pre_ref, drouter_ref, prob_ref, out_acc, back_acc = rest[2 * count :]
    step = pl.program_id(0)
    tile = x_refs[0].shape[0]
    lane = lax.broadcasted_iota(jnp.int32, (tile, 128), 1)
    own = lane == label_ref[0]
    spans = [slice(r * tile, (r + 1) * tile) for r in range(count)]

    @pl.when(step == 0)
    def _():
        for piece, rows in enumerate(spans):
            logits = jnp.dot(x_refs[piece][...], router_ref[...], preferred_element_type=jnp.float32)
            logits = jnp.where(lane < 4, logits, -jnp.inf)
            raised = jnp.exp(logits - jnp.max(logits, axis=1, keepdims=True))
            prob = raised / jnp.sum(raised, axis=1, keepdims=True)
            prob_ref[rows, :] = prob
            gate = jnp.sum(jnp.where(own, prob, 0.0), axis=1, keepdims=True)
            g_ref[rows, :] = (gate * u_refs[piece][...].astype(jnp.float32)).astype(jnp.bfloat16)
        out_acc[...] = jnp.zeros_like(out_acc)
        back_acc[...] = jnp.zeros_like(back_acc)

    for piece, rows in enumerate(spans):
        pre = jnp.dot(x_refs[piece][...], win_ref[...], preferred_element_type=jnp.float32)
        square = pre * pre
        turn = jnp.tanh(pre * (0.7978845608028654 + 0.035677408136300125 * square))
        half = 0.5 + 0.5 * turn
        hidden = (pre * half).astype(jnp.bfloat16)
        slope = half + pre * (half - half * half) * (1.5957691216057308 + 0.21406444881780074 * square)
        hid_ref[rows, :] = hidden
        out_acc[rows, :] += jnp.dot(hidden, wout_ref[...], preferred_element_type=jnp.float32)
        hidden_grad = lax.dot_general(g_ref[rows, :], wout_ref[...], (((1,), (1,)), ((), ())), preferred_element_type=jnp.float32)
        pre_grad = (hidden_grad * slope).astype(jnp.bfloat16)
        pre_ref[rows, :] = pre_grad
        back_acc[rows, :] += lax.dot_general(pre_grad, win_ref[...], (((1,), (1,)), ((), ())), preferred_element_type=jnp.float32)

    @pl.when(step == pl.num_programs(0) - 1)
    def _():
        total = jnp.zeros(drouter_ref.shape, jnp.float32)
        for piece, rows in enumerate(spans):
            prob = prob_ref[rows, :]
            gate = jnp.sum(jnp.where(own, prob, 0.0), axis=1, keepdims=True)
            out = out_acc[rows, :].astype(jnp.bfloat16).astype(jnp.float32)
            rows_refs[piece][...] = (gate * out).astype(jnp.bfloat16)
            gate_grad = jnp.sum(u_refs[piece][...].astype(jnp.float32) * out, axis=1, keepdims=True)
            logit_grad = prob * (jnp.where(own, gate_grad, 0.0) - gate * gate_grad)
            high = logit_grad.astype(jnp.bfloat16)
            low = (logit_grad - high.astype(jnp.float32)).astype(jnp.bfloat16)
            back = back_acc[rows, :].astype(jnp.bfloat16).astype(jnp.float32)
            for part in (high, low):
                back += lax.dot_general(part, router_ref[...], (((1,), (1,)), ((), ())), preferred_element_type=jnp.float32)
                total += lax.dot_general(x_refs[piece][...], part, (((0,), (0,)), ((), ())), preferred_element_type=jnp.float32)
            back_refs[piece][...] = back.astype(jnp.bfloat16)
        drouter_ref[...] = total


def run_expert(label, pieces, upstream_pieces, router_wide, w_in, w_out, chunk=768):
    count, (tile, width) = len(pieces), pieces[0].shape
    rows, inner = count * tile, w_in.shape[1]
    once = pl.Buffered(1)
    piece = pl.BlockSpec((tile, width), lambda f, lab: (0, 0), pipeline_mode=once)
    inner_block = pl.BlockSpec((rows, chunk), lambda f, lab: (0, f))
    low = lambda *shape: jax.ShapeDtypeStruct(shape, jnp.bfloat16)
    outs = pl.pallas_call(
        expert_kernel,
        grid_spec=pltpu.PrefetchScalarGridSpec(
            num_scalar_prefetch=1,
            grid=(inner // chunk,),
            in_specs=[piece] * (2 * count) + [
                pl.BlockSpec((width, 128), lambda f, lab: (0, 0), pipeline_mode=once),
                pl.BlockSpec((width, chunk), lambda f, lab: (0, f)),
                pl.BlockSpec((chunk, width), lambda f, lab: (f, 0)),
            ],
            out_specs=[piece] * (2 * count) + [
                pl.BlockSpec((rows, width), lambda f, lab: (0, 0), pipeline_mode=once),
                inner_block,
                inner_block,
                pl.BlockSpec((width, 128), lambda f, lab: (0, 0), pipeline_mode=once),
            ],
            scratch_shapes=[
                pltpu.VMEM((rows, 128), jnp.float32),
                pltpu.VMEM((rows, width), jnp.float32),
                pltpu.VMEM((rows, width), jnp.float32),
            ],
        ),
        out_shape=[low(tile, width)] * (2 * count)
        + [low(rows, width), low(rows, inner), low(rows, inner), jax.ShapeDtypeStruct((width, 128), jnp.float32)],
        compiler_params=pltpu.CompilerParams(vmem_limit_bytes=48 << 20),
        cost_estimate=pl.CostEstimate(flops=16 * rows * width * inner, bytes_accessed=8 * width * inner, transcendentals=rows * inner),
        name="experts",
    )(label, *pieces, *upstream_pieces, router_wide, w_in, w_out)
    return outs[:count], outs[count : 2 * count], outs[2 * count :]


def expert_grads_kernel(groups, count, *refs):
    x_refs, refs = refs[: groups * count], refs[groups * count :]
    g_refs, hid_refs, pre_refs = refs[:groups], refs[groups : 2 * groups], refs[2 * groups : 3 * groups]
    dw_ref, xt_ref, gt_ref = refs[3 * groups :]
    width = xt_ref.shape[0]
    tile = x_refs[0].shape[0]
    rows = g_refs[0].shape[0]

    @pl.when(pl.program_id(0) == 0)
    def _():
        for at in range(groups):
            gt_ref[:, at * rows : (at + 1) * rows] = g_refs[at][...].T
            for piece in range(count):
                start = at * rows + piece * tile
                xt_ref[:, start : start + tile] = x_refs[at * count + piece][...].T

    for side, (left, right) in enumerate(((xt_ref, pre_refs), (gt_ref, hid_refs))):
        total = sum(
            jnp.dot(left[:, at * rows : (at + 1) * rows], right[at][...], preferred_element_type=jnp.float32)
            for at in range(groups)
        )
        dw_ref[:, side * width : (side + 1) * width] = total.astype(jnp.bfloat16).T


def expert_grads(pieces, grads, hiddens, pre_grads, chunk=512):
    groups, count = len(grads), len(pieces) // len(grads)
    (tile, width), (rows, inner) = pieces[0].shape, hiddens[0].shape
    once = pl.Buffered(1)
    inner_block = pl.BlockSpec((rows, chunk), lambda f: (0, f))
    return pl.pallas_call(
        lambda *refs: expert_grads_kernel(groups, count, *refs),
        grid=(inner // chunk,),
        in_specs=[pl.BlockSpec((tile, width), lambda f: (0, 0), pipeline_mode=once)] * (groups * count)
        + [pl.BlockSpec((rows, width), lambda f: (0, 0), pipeline_mode=once)] * groups
        + [inner_block] * (2 * groups),
        out_specs=pl.BlockSpec((chunk, 2 * width), lambda f: (f, 0)),
        out_shape=jax.ShapeDtypeStruct((inner, 2 * width), jnp.bfloat16),
        scratch_shapes=[pltpu.VMEM((width, groups * rows), jnp.bfloat16)] * 2,
        compiler_params=pltpu.CompilerParams(vmem_limit_bytes=48 << 20),
        cost_estimate=pl.CostEstimate(flops=6 * groups * rows * width * inner, bytes_accessed=4 * (groups * rows + width) * inner, transcendentals=0),
        name="expert_grads",
    )(*pieces, *grads, *hiddens, *pre_grads)


def make_dispatch(routes, labels, capacity):
    hits = (routes[..., None] == labels).astype(jnp.int32)
    places = jnp.sum((jnp.cumsum(hits, axis=1) - 1) * hits, axis=-1)
    expert_match = routes[None, :, None, :] == labels[:, None, None, None]
    slot_match = places[:, None, :] == jnp.arange(capacity, dtype=jnp.int32)[None, :, None]
    return (expert_match & slot_match[None]).astype(jnp.bfloat16)


def exchange(pieces, axis, sign):
    size = lax.axis_size(axis)
    return [pieces[0]] + [
        lax.ppermute(pieces[turn], axis, [(at, (at + sign * turn) % size) for at in range(size)])
        for turn in range(1, size)
    ]


def trade(blocks):
    at = lax.axis_index("ctx")
    mine = lax.dynamic_index_in_dim(blocks, at, 0, keepdims=False)
    other = lax.dynamic_index_in_dim(blocks, 1 - at, 0, keepdims=False)
    arrived = lax.ppermute(other, "ctx", [(0, 1), (1, 0)])
    return jnp.stack([jnp.where(at == 0, mine, arrived), jnp.where(at == 0, arrived, mine)])


def norm_scale(value_rows):
    return lax.rsqrt(jnp.mean(value_rows * value_rows, axis=-1, keepdims=True) + norm_eps)


def norm_back(value_rows, scale, gain_vector, grad_rows):
    scaled = grad_rows * gain_vector
    shrink = jnp.mean(scaled * value_rows, axis=-1, keepdims=True) * scale * scale * scale
    return scale * scaled - value_rows * shrink, jnp.sum(grad_rows * value_rows * scale, axis=(0, 1))


def wide_dot(rows, weight):
    return jnp.einsum("sxd,de->sxe", rows, weight, preferred_element_type=jnp.float32)


def wide_dot_back(rows, weight):
    return jnp.einsum("sxe,de->sxd", rows, weight, preferred_element_type=jnp.float32)


def weight_dot(left, right):
    return jnp.einsum("sxd,sxe->de", left, right, preferred_element_type=jnp.float32)


def split_rows(flat):
    high = flat.astype(jnp.bfloat16)
    return high, (flat - high.astype(jnp.float32)).astype(jnp.bfloat16)


def sum_all(matrices, smalls):
    width = matrices[0].shape[1]
    flat = jnp.concatenate([jnp.ravel(small) for small in smalls])
    fill = -flat.shape[0] % (8 * width)
    flat = jnp.pad(flat, (0, fill)).reshape(-1, width)
    packed = jnp.concatenate([matrix.astype(jnp.bfloat16) for matrix in matrices] + list(split_rows(flat)))
    packed = lax.psum(packed, ("dp", "ctx", "expert")).astype(jnp.float32)
    outs, at = [], 0
    for matrix in matrices:
        outs.append(packed[at : at + matrix.shape[0]])
        at += matrix.shape[0]
    rows = flat.shape[0]
    flat = (packed[at : at + rows] + packed[at + rows : at + 2 * rows]).reshape(-1)
    at = 0
    for small in smalls:
        outs.append(flat[at : at + small.size].reshape(small.shape))
        at += small.size
    return outs


def per_device(
    tokens,
    cotangent,
    routes,
    norm1_gain,
    query_weight,
    key_weight,
    value_weight,
    output_weight,
    bias_table,
    norm2_gain,
    router_weight,
    w_in,
    w_out,
):
    seq_count, local_len, model_width = tokens.shape
    owners = lax.axis_size("expert")
    capacity = local_len // 2
    whole_seq = seq_count == 2 and lax.axis_size("ctx") == 2 and local_len % QB == 0
    if whole_seq:
        routes, cotangent, tokens = trade(routes), trade(cotangent), trade(tokens)
    groups = [slice(0, 1), slice(1, 2)] if whole_seq else [slice(0, seq_count)]
    label = lax.axis_index("expert")
    labels = (label + jnp.arange(owners, dtype=jnp.int32)) % owners
    dispatch = make_dispatch(routes, labels, capacity)

    together = lax.optimization_barrier

    def sort_rows(group, rows):
        sent = [
            jnp.einsum("scx,sxd->scd", dispatch[turn, group], rows, preferred_element_type=jnp.float32)
            for turn in range(owners)
        ]
        return [piece.astype(jnp.bfloat16).reshape(-1, model_width) for piece in sent]

    def place_rows(group, pieces):
        pieces = jnp.stack(pieces).reshape(owners, -1, capacity, model_width)
        return jnp.einsum("escx,escd->sxd", dispatch[:, group], pieces, preferred_element_type=jnp.float32)

    inputs = tokens.astype(jnp.float32)
    scale1 = norm_scale(inputs)
    attn_in = (inputs * scale1 * norm1_gain).astype(jnp.bfloat16)
    queries = wide_dot(attn_in, query_weight).astype(jnp.bfloat16)
    keys = wide_dot(attn_in, key_weight).astype(jnp.bfloat16)
    values = wide_dot(attn_in, value_weight).astype(jnp.bfloat16)
    sorted_upstream = [sort_rows(group, cotangent[group]) for group in groups]
    sorted_upstream, queries = together((sorted_upstream, queries))
    upstream = [exchange(rows, "expert", 1) for rows in sorted_upstream]
    if whole_seq:
        lines = bias_lines(bias_table)
        flat = (seq_count * local_len, model_width)
        qkv = [rows.reshape(flat) for rows in (queries, keys, values)]
    else:
        first_pos = lax.axis_index("ctx") * local_len
        keys = lax.all_gather(keys, "ctx", axis=1, tiled=True)
        values = lax.all_gather(values, "ctx", axis=1, tiled=True)
        buckets = bucket_grid(first_pos, local_len, keys.shape[1])
        attended, log_totals = attend_rows(queries, keys, values, buckets, bias_table, DH)
    attended_groups, residual1, scale2, arrived = [], [], [], []
    in_flight, fed = upstream[0], queries.reshape(-1, model_width)
    for at, group in enumerate(groups):
        if whole_seq:
            rows = attend(fed, *qkv[1:], lines, at * local_len, local_len)[None]
        else:
            rows = attended.astype(jnp.bfloat16)
        rows, in_flight = together((rows, in_flight))
        if at == 0:
            upstream[0] = in_flight
        else:
            arrived[-1] = in_flight
        attended_groups.append(rows)
        residual1.append(inputs[group] + wide_dot(rows, output_weight))
        scale2.append(norm_scale(residual1[-1]))
        router_in = (residual1[-1] * scale2[-1] * norm2_gain).astype(jnp.bfloat16)
        sorted_rows, fed = together((sort_rows(group, router_in), fed))
        in_flight = exchange(sorted_rows, "expert", 1)
        arrived.append(in_flight)
    attended = attended_groups
    router_wide = jnp.pad(router_weight, ((0, 0), (0, 128 - router_weight.shape[1])))
    label = label.astype(jnp.int32).reshape(1)
    done, back = [], []
    for rows, grads in zip(arrived, upstream):
        result = run_expert(label, rows, grads, router_wide, w_in[0], w_out[0])
        if back:
            result, back[-1] = together((result, back[-1]))
        done.append(result)
        back.append(exchange(result[1], "expert", -1))
    rows_out = [item[0] for item in done]
    grad_rows, hiddens, pre_grads, grad_router = zip(*[item[2] for item in done])
    grad_router = sum(grad_router)[:, : router_weight.shape[1]]
    grad_experts = expert_grads(sum(arrived, []), grad_rows, hiddens, pre_grads)
    grad_experts, back[-1], rows_out = together((grad_experts, back[-1], rows_out))
    grad_experts = lax.psum_scatter(grad_experts, ("dp", "ctx"), scatter_dimension=0, tiled=True)
    returned = [exchange(list(rows), "expert", -1) for rows in rows_out]
    residual_grad, attn_grad, mixed_grad, grad_norm2 = [], [], [], 0.0
    for group, rows, scale, pieces in zip(groups, residual1, scale2, back):
        norm2_back, gain_part = norm_back(rows, scale, norm2_gain, place_rows(group, pieces))
        grad_norm2 = grad_norm2 + gain_part
        residual_grad.append(cotangent[group].astype(jnp.float32) + norm2_back)
        attn_grad.append(residual_grad[-1].astype(jnp.bfloat16))
        mixed_grad.append(wide_dot_back(attn_grad[-1], output_weight).astype(jnp.bfloat16))
    grad_w_output = sum(weight_dot(left, right) for left, right in zip(attended, attn_grad))
    residual_grad, mixed_grad = jnp.concatenate(residual_grad), jnp.concatenate(mixed_grad)
    early_sums = sum_all([grad_w_output], [grad_norm2, grad_router])
    if whole_seq:
        *grads, grad_bias = attend_back(*qkv, mixed_grad.reshape(flat), lines)
        query_low, key_low, value_low = (rows.reshape(tokens.shape) for rows in grads)
    else:
        query_grad, _, diag_grad, key_part, value_part = attend_back_rows(
            queries, keys, values, mixed_grad, log_totals, buckets, bias_table, DH
        )
        grad_bias = diag_grad.T
        query_low = query_grad.astype(jnp.bfloat16)
        key_low = lax.psum_scatter(key_part, "ctx", scatter_dimension=1, tiled=True).astype(jnp.bfloat16)
        value_low = lax.psum_scatter(value_part, "ctx", scatter_dimension=1, tiled=True).astype(jnp.bfloat16)
    early_sums, returned, query_low, key_low, value_low = together(
        (early_sums, returned, query_low, key_low, value_low)
    )
    block_out = [rows + place_rows(group, pieces) for group, rows, pieces in zip(groups, residual1, returned)]
    block_out = jnp.concatenate(block_out).astype(jnp.bfloat16)
    grad_w_output, grad_norm2, grad_router = early_sums
    norm_in_grad = wide_dot_back(query_low, query_weight)
    norm_in_grad = norm_in_grad + wide_dot_back(key_low, key_weight)
    norm_in_grad = norm_in_grad + wide_dot_back(value_low, value_weight)
    norm1_back, grad_norm1 = norm_back(inputs, scale1, norm1_gain, norm_in_grad)
    d_tokens = residual_grad + norm1_back
    grad_qkv = [weight_dot(attn_in, rows) for rows in (query_low, key_low, value_low)]
    grad_qkv, grad_experts = together((grad_qkv, grad_experts))
    grad_w_query, grad_w_key, grad_w_value, grad_bias, grad_norm1 = sum_all(grad_qkv, [grad_bias, grad_norm1])
    if whole_seq:
        block_out, d_tokens = trade(block_out), trade(d_tokens)
    grad_experts = grad_experts.astype(jnp.float32)
    return (
        block_out,
        d_tokens,
        grad_norm1,
        grad_w_query,
        grad_w_key,
        grad_w_value,
        grad_w_output,
        grad_bias,
        grad_norm2,
        grad_router,
        grad_experts[:, :model_width].T[None],
        grad_experts[:, model_width:][None],
    )


def solution(mesh):
    rows = P(("dp", "expert"), "ctx", None)
    in_specs = (rows, rows, P(("dp", "expert"), "ctx")) + (P(),) * 8 + (P("expert", None, None),) * 2
    out_specs = (rows, rows) + (P(),) * 8 + (P("expert", None, ("dp", "ctx")), P("expert", ("dp", "ctx"), None))
    return jax.shard_map(per_device, mesh=mesh, in_specs=in_specs, out_specs=out_specs, check_vma=False)
```

```python
import jax
import jax.numpy as jnp
import numpy as np
from jax import lax
from jax.experimental import pallas as pl
from jax.experimental.pallas import tpu as pltpu
from jax.sharding import PartitionSpec as P

DH = 64
QB = 256

bucket_edges = (1, 2, 3, 4, 5, 6, 7, 8, 12, 16, 23, 32, 46, 64, 91)
norm_eps = 1e-06
precise_result = lax.Precision.HIGHEST


def bucket_of(relative):
    distance = jnp.abs(relative)
    half_bucket = jnp.zeros(relative.shape, jnp.int32)
    for threshold in bucket_edges:
        half_bucket = half_bucket + (distance >= threshold).astype(jnp.int32)
    return half_bucket + 16 * (relative > 0).astype(jnp.int32)


def bucket_grid(row_start, row_count, col_count):
    row_pos = row_start + jnp.arange(row_count, dtype=jnp.int32)
    col_pos = jnp.arange(col_count, dtype=jnp.int32)
    return bucket_of(col_pos[None, :] - row_pos[:, None])


def bias_grid(buckets, table_column, bucket_count):
    result = jnp.zeros(buckets.shape, jnp.float32)
    for label in range(bucket_count):
        result = result + jnp.where(buckets == label, table_column[label], 0.0)
    return result


def fold_buckets(buckets, grad_sum, bucket_count):
    return jnp.stack(
        [jnp.sum(jnp.where(buckets == label, grad_sum, 0.0)) for label in range(bucket_count)]
    )


def head_slice(value_rows, head_index, head_size):
    return lax.dynamic_slice_in_dim(value_rows, head_index * head_size, head_size, 2)


def put_head(target, portion, head_index, head_size):
    return lax.dynamic_update_slice_in_dim(target, portion, head_index * head_size, 2)


def head_scores(q_head, k_head, buckets, bias_table, head_index):
    table_column = lax.dynamic_index_in_dim(bias_table, head_index, 1, keepdims=False)
    scores = jnp.einsum("sqd,skd->sqk", q_head, k_head, preferred_element_type=jnp.float32)
    return scores + bias_grid(buckets, table_column, bias_table.shape[0])[None]


def attend_rows(query_matrix, keys_whole, values_whole, buckets, bias_table, head_size):
    seq_count, row_count, feature_width = query_matrix.shape
    head_count = feature_width // head_size

    def one_head(head_index, running):
        attention_result, log_totals = running
        scores = head_scores(
            head_slice(query_matrix, head_index, head_size),
            head_slice(keys_whole, head_index, head_size),
            buckets,
            bias_table,
            head_index,
        )
        row_max = jnp.max(scores, axis=-1, keepdims=True)
        log_total = row_max + jnp.log(jnp.sum(jnp.exp(scores - row_max), axis=-1, keepdims=True))
        weights_low = jnp.exp(scores - log_total).astype(jnp.bfloat16)
        portion = jnp.einsum(
            "sqk,skd->sqd",
            weights_low,
            head_slice(values_whole, head_index, head_size),
            preferred_element_type=jnp.float32,
        )
        attention_result = put_head(attention_result, portion, head_index, head_size)
        log_totals = lax.dynamic_update_index_in_dim(log_totals, log_total[..., 0], head_index, 0)
        return (attention_result, log_totals)

    initial = (
        jnp.zeros((seq_count, row_count, feature_width), jnp.float32),
        jnp.zeros((head_count, seq_count, row_count), jnp.float32),
    )
    return lax.fori_loop(0, head_count, one_head, initial)


def attend_back_rows(
    query_matrix, keys_whole, values_whole, mixed_grad, log_totals, buckets, bias_table, head_size
):
    seq_count, row_count, feature_width = query_matrix.shape
    col_count = keys_whole.shape[1]
    head_count = feature_width // head_size
    bucket_count = bias_table.shape[0]

    def one_head(head_index, running):
        query_grad, deltas, diag_grad, key_part, value_part = running
        q_head = head_slice(query_matrix, head_index, head_size)
        k_head = head_slice(keys_whole, head_index, head_size)
        v_head = head_slice(values_whole, head_index, head_size)
        g_head = head_slice(mixed_grad, head_index, head_size)
        scores = head_scores(q_head, k_head, buckets, bias_table, head_index)
        weights = jnp.exp(scores - log_totals[head_index][..., None])
        weight_grad = jnp.einsum("sqd,skd->sqk", g_head, v_head, preferred_element_type=jnp.float32)
        delta_row = jnp.sum(weights * weight_grad, axis=-1)
        score_grad = (weights * (weight_grad - delta_row[..., None])).astype(jnp.bfloat16)
        query_grad = put_head(
            query_grad,
            jnp.einsum("sqk,skd->sqd", score_grad, k_head, preferred_element_type=jnp.float32),
            head_index,
            head_size,
        )
        deltas = lax.dynamic_update_index_in_dim(deltas, delta_row, head_index, 0)
        folded = fold_buckets(
            buckets, jnp.sum(score_grad.astype(jnp.float32), axis=0), bucket_count
        )
        diag_grad = lax.dynamic_update_index_in_dim(diag_grad, folded, head_index, 0)
        key_part = put_head(
            key_part,
            jnp.einsum("sqk,sqd->skd", score_grad, q_head, preferred_element_type=jnp.float32),
            head_index,
            head_size,
        )
        value_part = put_head(
            value_part,
            jnp.einsum(
                "sqk,sqd->skd",
                weights.astype(jnp.bfloat16),
                g_head,
                preferred_element_type=jnp.float32,
            ),
            head_index,
            head_size,
        )
        return (query_grad, deltas, diag_grad, key_part, value_part)

    key_shape = (seq_count, col_count, feature_width)
    initial = (
        jnp.zeros((seq_count, row_count, feature_width), jnp.float32),
        jnp.zeros((head_count, seq_count, row_count), jnp.float32),
        jnp.zeros((head_count, bucket_count), jnp.float32),
        jnp.zeros(key_shape, jnp.float32),
        jnp.zeros(key_shape, jnp.float32),
    )
    return lax.fori_loop(0, head_count, one_head, initial)


def bucket_np(relative):
    half_bucket = np.zeros(relative.shape, np.int32)
    for threshold in bucket_edges:
        half_bucket = half_bucket + (np.abs(relative) >= threshold)
    return half_bucket + 16 * (relative > 0)


def bias_lines(bias_table):
    lane = np.arange(4 * QB)
    both = np.stack([lane - 2 * QB, 2 * QB - lane])
    onehot = (bucket_np(both)[..., None] == np.arange(32)).astype(np.float32)
    return jnp.einsum("lcb,bh->hlc", jnp.asarray(onehot), bias_table, precision=lax.Precision.HIGHEST)

def fwd_kernel(first, lines_ref, q_ref, k_ref, v_ref, o_ref, band_ref):
    n = k_ref.shape[0] // QB
    lane = lax.broadcasted_iota(jnp.int32, (QB, 128), 1)
    for h in range(2):
        line = lines_ref[h, 0:1, :]
        spread = pltpu.roll(jnp.broadcast_to(line, (QB, 4 * QB)), 0, 1, stride=1, stride_axis=0)
        band_ref[h] = spread[:, QB:]
    for i in range(first, first + q_ref.shape[0] // QB):
        rows = slice((i - first) * QB, (i - first + 1) * QB)
        outs = []
        for h in range(2):
            low_bias = lines_ref[h, 0:1, 0:1]
            high_bias = lines_ref[h, 0:1, 4 * QB - 1:]
            q = jnp.where((lane < 64) == (h == 0), q_ref[rows, :], 0)
            s = lax.dot_general(q, k_ref[...], (((1,), (1,)), ((), ())), preferred_element_type=jnp.float32)
            parts = []
            for j in range(n):
                d = j - i
                b = band_ref[h, :, (d + 1) * QB:(d + 2) * QB] if abs(d) <= 1 else (low_bias if d < 0 else high_bias)
                parts.append(s[:, j * QB:(j + 1) * QB] + b)
            s = jnp.concatenate(parts, axis=1)
            m = jnp.max(s, axis=1, keepdims=True)
            p = jnp.exp(s - m)
            l = jnp.sum(p, axis=1, keepdims=True)
            o = jnp.dot(p.astype(jnp.bfloat16), v_ref[...], preferred_element_type=jnp.float32)
            outs.append(o * (1.0 / l))
        o_ref[rows, :] = jnp.where(lane < 64, outs[0], outs[1]).astype(jnp.bfloat16)

def attend(q, k, v, lines, first, count):
    length, width = q.shape
    col = pl.BlockSpec((length, 128), lambda h: (0, h))
    span = pl.BlockSpec((count, 128), lambda h: (first // count, h))
    return pl.pallas_call(
        lambda *refs: fwd_kernel(first // QB, *refs),
        grid=(width // 128,),
        in_specs=[pl.BlockSpec((2, 2, 4 * QB), lambda h: (h, 0, 0)), span, col, col],
        out_specs=pl.BlockSpec((count, 128), lambda h: (0, h)),
        out_shape=jax.ShapeDtypeStruct((count, width), jnp.bfloat16),
        scratch_shapes=[pltpu.VMEM((2, QB, 3 * QB), jnp.float32)],
        compiler_params=pltpu.CompilerParams(vmem_limit_bytes=48 << 20),
        cost_estimate=pl.CostEstimate(flops=40 * count * length * width, bytes_accessed=6 * length * width, transcendentals=count * length * width // 64),
        name="attend",
    )(lines, q, k, v)

def bwd_kernel(lines_ref, fold_ref, q_ref, k_ref, v_ref, g_ref, grad_ref, bias_ref, band_ref, acc_ref, far_acc, dk_acc, dv_acc):
    n = q_ref.shape[0] // QB
    lane = lax.broadcasted_iota(jnp.int32, (QB, 128), 1)
    for h in range(2):
        for t in range(3):
            start = 2 * QB - (t - 1) * QB - QB
            line = lines_ref[h, 1:2, start:start + 2 * QB]
            spread = pltpu.roll(jnp.broadcast_to(line, (QB, 2 * QB)), QB, 1, stride=1, stride_axis=0)
            band_ref[h, t * QB:(t + 1) * QB, :] = spread[:, :QB]
    acc_ref[...] = jnp.zeros_like(acc_ref)
    far_acc[...] = jnp.zeros_like(far_acc)
    for i in range(n):
        rows = slice(i * QB, (i + 1) * QB)
        grads = []
        for h in range(2):
            keep = (lane < 64) == (h == 0)
            low_bias = lines_ref[h, 0:1, 0:1]
            high_bias = lines_ref[h, 0:1, 4 * QB - 1:]
            q = jnp.where(keep, q_ref[rows, :], 0)
            g = jnp.where(keep, g_ref[rows, :], 0)
            s = lax.dot_general(k_ref[...], q, (((1,), (1,)), ((), ())), preferred_element_type=jnp.float32)
            parts = []
            for j in range(n):
                d = j - i
                b = band_ref[h, (d + 1) * QB:(d + 2) * QB, :] if abs(d) <= 1 else (low_bias if d < 0 else high_bias)
                parts.append(s[j * QB:(j + 1) * QB, :] + b)
            s = jnp.concatenate(parts, axis=0)
            m = jnp.max(s, axis=0, keepdims=True)
            p = jnp.exp(s - m)
            w = p * (1.0 / jnp.sum(p, axis=0, keepdims=True))
            dp = lax.dot_general(v_ref[...], g, (((1,), (1,)), ((), ())), preferred_element_type=jnp.float32)
            delta = jnp.sum(w * dp, axis=0, keepdims=True)
            ds = w * (dp - delta)
            for j in range(n):
                d = j - i
                tile = ds[j * QB:(j + 1) * QB, :]
                if abs(d) <= 1:
                    acc_ref[h, (d + 1) * QB:(d + 2) * QB, :] += tile
                else:
                    far_acc[h, 0 if d < 0 else 1] += jnp.sum(tile.reshape(QB // 8, 8, QB), axis=0)
            low = ds.astype(jnp.bfloat16)
            dv = jnp.dot(w.astype(jnp.bfloat16), g, preferred_element_type=jnp.float32)
            dk = jnp.dot(low, q, preferred_element_type=jnp.float32)
            if i == 0 and h == 0:
                dv_acc[...] = dv
                dk_acc[...] = dk
            else:
                dv_acc[...] += dv
                dk_acc[...] += dk
            grads.append(lax.dot_general(low, k_ref[...], (((0,), (0,)), ((), ())), preferred_element_type=jnp.float32))
        grad_ref[0, rows, :] = jnp.where(lane < 64, grads[0], grads[1]).astype(jnp.bfloat16)
    grad_ref[1] = dk_acc[...].astype(jnp.bfloat16)
    grad_ref[2] = dv_acc[...].astype(jnp.bfloat16)
    row = lax.broadcasted_iota(jnp.int32, (8, 2 * QB), 0)
    for h in range(2):
        total = jnp.zeros((8, 128), jnp.float32)
        for t in range(3):
            tile = acc_ref[h, t * QB:(t + 1) * QB, :]
            wide = jnp.concatenate([tile, jnp.zeros_like(tile)], axis=1)
            moved = sum(pltpu.roll(wide[8 * e:8 * e + 8], QB - 8 * e, 1) for e in range(QB // 8))
            turned = jnp.where(row == 0, moved, 0.0)
            for e in range(1, 8):
                turned = turned + pltpu.roll(jnp.where(row == e, moved, 0.0), 2 * QB - e, 1)
            total = total + jnp.dot(turned, fold_ref[t], precision=lax.Precision.HIGHEST, preferred_element_type=jnp.float32)
        total = jnp.sum(total, axis=0, keepdims=True)
        ends = [jnp.sum(jnp.sum(far_acc[h, side], axis=0, keepdims=True), axis=1, keepdims=True) for side in range(2)]
        column = lax.broadcasted_iota(jnp.int32, (1, 128), 1)
        total = total + jnp.where(column == 15, ends[0], 0.0) + jnp.where(column == 31, ends[1], 0.0)
        bias_ref[0, h:h + 1, :] = total


def attend_back(q, k, v, g, lines, first_pair, pairs, total_pairs=None, earlier=None):
    length = q.shape[0]
    r = (np.arange(3)[:, None] - 1) * QB - (np.arange(2 * QB)[None] - QB)
    fold = (bucket_np(r)[..., None] == np.arange(128)).astype(np.float32)
    col = pl.BlockSpec((length, 128), lambda h: (0, h + first_pair))
    offset = first_pair % total_pairs if total_pairs else 0
    kept = [] if earlier is None else [earlier]
    grads, bias = pl.pallas_call(
        lambda *refs: bwd_kernel(*refs[:6], *refs[6 + len(kept):]),
        grid=(pairs,),
        in_specs=[
            pl.BlockSpec((2, 2, 4 * QB), lambda h: (h + first_pair, 0, 0)),
            pl.BlockSpec((3, 2 * QB, 128), lambda h: (0, 0, 0)),
            col, col, col, col,
        ]
        + [pl.BlockSpec(memory_space=pl.ANY)] * len(kept),
        out_specs=[pl.BlockSpec((3, length, 128), lambda h: (0, 0, h + offset)), pl.BlockSpec((1, 2, 128), lambda h: (h, 0, 0))],
        out_shape=[
            jax.ShapeDtypeStruct((3, length, 128 * (total_pairs or pairs)), jnp.bfloat16),
            jax.ShapeDtypeStruct((pairs, 2, 128), jnp.float32),
        ],
        scratch_shapes=[
            pltpu.VMEM((2, 3 * QB, QB), jnp.float32),
            pltpu.VMEM((2, 3 * QB, QB), jnp.float32),
            pltpu.VMEM((2, 2, 8, QB), jnp.float32),
            pltpu.VMEM((length, 128), jnp.float32),
            pltpu.VMEM((length, 128), jnp.float32),
        ],
        compiler_params=pltpu.CompilerParams(vmem_limit_bytes=48 << 20),
        cost_estimate=pl.CostEstimate(
            flops=84 * length * length * 128 * pairs, bytes_accessed=14 * length * 128 * pairs, transcendentals=2 * length * length * pairs
        ),
        input_output_aliases={6: 0} if kept else {},
        name="attend_back",
    )(lines, jnp.asarray(fold), q, k, v, g, *kept)
    return grads, bias.reshape(2 * pairs, 128)


def expert_kernel(count, label_ref, *refs):
    x_refs, u_refs = refs[:count], refs[count : 2 * count]
    router_ref, win_ref, wout_ref = refs[2 * count : 2 * count + 3]
    rest = refs[len(refs) - 7 - 2 * count :]
    rows_refs, back_refs = rest[:count], rest[count : 2 * count]
    g_ref, hid_ref, pre_ref, drouter_ref, prob_ref, out_acc, back_acc = rest[2 * count :]
    step = pl.program_id(0)
    tile = x_refs[0].shape[0]
    lane = lax.broadcasted_iota(jnp.int32, (tile, 128), 1)
    own = lane == label_ref[0]
    spans = [slice(r * tile, (r + 1) * tile) for r in range(count)]

    @pl.when(step == 0)
    def _():
        for piece, rows in enumerate(spans):
            logits = jnp.dot(x_refs[piece][...], router_ref[...], preferred_element_type=jnp.float32)
            logits = jnp.where(lane < 4, logits, -jnp.inf)
            raised = jnp.exp(logits - jnp.max(logits, axis=1, keepdims=True))
            prob = raised / jnp.sum(raised, axis=1, keepdims=True)
            prob_ref[rows, :] = prob
            gate = jnp.sum(jnp.where(own, prob, 0.0), axis=1, keepdims=True)
            g_ref[rows, :] = (gate * u_refs[piece][...].astype(jnp.float32)).astype(jnp.bfloat16)
        out_acc[...] = jnp.zeros_like(out_acc)
        back_acc[...] = jnp.zeros_like(back_acc)

    for piece, rows in enumerate(spans):
        pre = jnp.dot(x_refs[piece][...], win_ref[...], preferred_element_type=jnp.float32)
        square = pre * pre
        turn = jnp.tanh(pre * (0.7978845608028654 + 0.035677408136300125 * square))
        half = 0.5 + 0.5 * turn
        hidden = (pre * half).astype(jnp.bfloat16)
        slope = half + pre * (half - half * half) * (1.5957691216057308 + 0.21406444881780074 * square)
        hid_ref[rows, :] = hidden
        out_acc[rows, :] += jnp.dot(hidden, wout_ref[...], preferred_element_type=jnp.float32)
        hidden_grad = lax.dot_general(g_ref[rows, :], wout_ref[...], (((1,), (1,)), ((), ())), preferred_element_type=jnp.float32)
        pre_grad = (hidden_grad * slope).astype(jnp.bfloat16)
        pre_ref[rows, :] = pre_grad
        back_acc[rows, :] += lax.dot_general(pre_grad, win_ref[...], (((1,), (1,)), ((), ())), preferred_element_type=jnp.float32)

    @pl.when(step == pl.num_programs(0) - 1)
    def _():
        total = jnp.zeros(drouter_ref.shape, jnp.float32)
        for piece, rows in enumerate(spans):
            prob = prob_ref[rows, :]
            gate = jnp.sum(jnp.where(own, prob, 0.0), axis=1, keepdims=True)
            out = out_acc[rows, :].astype(jnp.bfloat16).astype(jnp.float32)
            rows_refs[piece][...] = (gate * out).astype(jnp.bfloat16)
            gate_grad = jnp.sum(u_refs[piece][...].astype(jnp.float32) * out, axis=1, keepdims=True)
            logit_grad = prob * (jnp.where(own, gate_grad, 0.0) - gate * gate_grad)
            high = logit_grad.astype(jnp.bfloat16)
            low = (logit_grad - high.astype(jnp.float32)).astype(jnp.bfloat16)
            back = back_acc[rows, :].astype(jnp.bfloat16).astype(jnp.float32)
            for part in (high, low):
                back += lax.dot_general(part, router_ref[...], (((1,), (1,)), ((), ())), preferred_element_type=jnp.float32)
                total += lax.dot_general(x_refs[piece][...], part, (((0,), (0,)), ((), ())), preferred_element_type=jnp.float32)
            back_refs[piece][...] = back.astype(jnp.bfloat16)
        drouter_ref[...] = total


def run_expert(label, pieces, upstream_pieces, router_wide, w_in, w_out, group, group_count, earlier, chunk=768):
    count, (tile, width) = len(pieces), pieces[0].shape
    rows, inner = count * tile, w_in.shape[1]
    once = pl.Buffered(1)
    piece = pl.BlockSpec((tile, width), lambda f, lab: (0, 0), pipeline_mode=once)
    inner_block = pl.BlockSpec((rows, chunk), lambda f, lab: (0, f))
    low = lambda *shape: jax.ShapeDtypeStruct(shape, jnp.bfloat16)
    outs = pl.pallas_call(
        lambda *refs: expert_kernel(count, *refs),
        grid_spec=pltpu.PrefetchScalarGridSpec(
            num_scalar_prefetch=1,
            grid=(inner // chunk,),
            in_specs=[piece] * (2 * count) + [
                pl.BlockSpec((width, 128), lambda f, lab: (0, 0), pipeline_mode=once),
                pl.BlockSpec((width, chunk), lambda f, lab: (0, f)),
                pl.BlockSpec((chunk, width), lambda f, lab: (f, 0)),
            ]
            + [pl.BlockSpec(memory_space=pl.ANY)] * len(earlier),
            out_specs=[pl.BlockSpec((tile, width), lambda f, lab: (group, 0), pipeline_mode=once)] * count
            + [piece] * count
            + [
                pl.BlockSpec((rows, width), lambda f, lab: (0, 0), pipeline_mode=once),
                inner_block,
                inner_block,
                pl.BlockSpec((width, 128), lambda f, lab: (0, 0), pipeline_mode=once),
            ],
            scratch_shapes=[
                pltpu.VMEM((rows, 128), jnp.float32),
                pltpu.VMEM((rows, width), jnp.float32),
                pltpu.VMEM((rows, width), jnp.float32),
            ],
        ),
        out_shape=[low(group_count * tile, width)] * count
        + [low(tile, width)] * count
        + [low(rows, width), low(rows, inner), low(rows, inner), jax.ShapeDtypeStruct((width, 128), jnp.float32)],
        compiler_params=pltpu.CompilerParams(vmem_limit_bytes=48 << 20),
        cost_estimate=pl.CostEstimate(flops=16 * rows * width * inner, bytes_accessed=8 * width * inner, transcendentals=rows * inner),
        input_output_aliases={2 * count + 4 + at: at for at in range(len(earlier))},
        name="experts",
    )(label, *pieces, *upstream_pieces, router_wide, w_in, w_out, *earlier)
    return outs[:count], outs[count : 2 * count], outs[2 * count :]


def expert_grads_kernel(groups, count, *refs):
    x_refs, refs = refs[: groups * count], refs[groups * count :]
    g_refs, hid_refs, pre_refs = refs[:groups], refs[groups : 2 * groups], refs[2 * groups : 3 * groups]
    dw_ref, xt_ref, gt_ref = refs[3 * groups :]
    width = xt_ref.shape[0]
    tile = x_refs[0].shape[0]
    rows = g_refs[0].shape[0]

    @pl.when(pl.program_id(0) == 0)
    def _():
        for at in range(groups):
            gt_ref[:, at * rows : (at + 1) * rows] = g_refs[at][...].T
            for piece in range(count):
                start = at * rows + piece * tile
                xt_ref[:, start : start + tile] = x_refs[at * count + piece][...].T

    for side, (left, right) in enumerate(((xt_ref, pre_refs), (gt_ref, hid_refs))):
        total = sum(
            jnp.dot(left[:, at * rows : (at + 1) * rows], right[at][...], preferred_element_type=jnp.float32)
            for at in range(groups)
        )
        dw_ref[:, side * width : (side + 1) * width] = total.astype(jnp.bfloat16).T


def expert_grads(pieces, grads, hiddens, pre_grads, chunk=512):
    groups, count = len(grads), len(pieces) // len(grads)
    (tile, width), (rows, inner) = pieces[0].shape, hiddens[0].shape
    once = pl.Buffered(1)
    inner_block = pl.BlockSpec((rows, chunk), lambda f: (0, f))
    return pl.pallas_call(
        lambda *refs: expert_grads_kernel(groups, count, *refs),
        grid=(inner // chunk,),
        in_specs=[pl.BlockSpec((tile, width), lambda f: (0, 0), pipeline_mode=once)] * (groups * count)
        + [pl.BlockSpec((rows, width), lambda f: (0, 0), pipeline_mode=once)] * groups
        + [inner_block] * (2 * groups),
        out_specs=pl.BlockSpec((chunk, 2 * width), lambda f: (f, 0)),
        out_shape=jax.ShapeDtypeStruct((inner, 2 * width), jnp.bfloat16),
        scratch_shapes=[pltpu.VMEM((width, groups * rows), jnp.bfloat16)] * 2,
        compiler_params=pltpu.CompilerParams(vmem_limit_bytes=48 << 20),
        cost_estimate=pl.CostEstimate(
            flops=6 * groups * rows * width * inner, bytes_accessed=4 * (groups * rows + width) * inner, transcendentals=0
        ),
        name="expert_grads",
    )(*pieces, *grads, *hiddens, *pre_grads)


def make_dispatch(routes, labels, capacity):
    hits = (routes[..., None] == labels).astype(jnp.int32)
    places = jnp.sum((jnp.cumsum(hits, axis=1) - 1) * hits, axis=-1)
    expert_match = routes[None, :, None, :] == labels[:, None, None, None]
    slot_match = places[:, None, :] == jnp.arange(capacity, dtype=jnp.int32)[None, :, None]
    return (expert_match & slot_match[None]).astype(jnp.bfloat16)


def exchange(pieces, axis, sign):
    size = lax.axis_size(axis)
    return [pieces[0]] + [
        lax.ppermute(pieces[turn], axis, [(at, (at + sign * turn) % size) for at in range(size)])
        for turn in range(1, size)
    ]


def trade(blocks):
    at = lax.axis_index("ctx")
    mine = lax.dynamic_index_in_dim(blocks, at, 0, keepdims=False)
    other = lax.dynamic_index_in_dim(blocks, 1 - at, 0, keepdims=False)
    arrived = lax.ppermute(other, "ctx", [(0, 1), (1, 0)])
    return jnp.stack([jnp.where(at == 0, mine, arrived), jnp.where(at == 0, arrived, mine)])


def norm_scale(value_rows):
    return lax.rsqrt(jnp.mean(value_rows * value_rows, axis=-1, keepdims=True) + norm_eps)


def norm_back(value_rows, scale, gain_vector, grad_rows):
    scaled = grad_rows * gain_vector
    shrink = jnp.mean(scaled * value_rows, axis=-1, keepdims=True) * scale * scale * scale
    return scale * scaled - value_rows * shrink, jnp.sum(grad_rows * value_rows * scale, axis=(0, 1))


def wide_dot(rows, weight):
    return jnp.einsum("sxd,de->sxe", rows, weight, preferred_element_type=jnp.float32)


def wide_dot_back(rows, weight):
    return jnp.einsum("sxe,de->sxd", rows, weight, preferred_element_type=jnp.float32)


def weight_dot(left, right):
    return jnp.einsum("sxd,sxe->de", left, right, preferred_element_type=jnp.float32)


def pack_sums(matrices, small=None):
    parts = [matrix.astype(jnp.bfloat16) for matrix in matrices]
    if small is not None:
        small = jnp.pad(small, ((0, -small.shape[0] % 64), (0, parts[0].shape[1] - small.shape[1])))
        high = small.astype(jnp.bfloat16)
        parts += [high, (small - high.astype(jnp.float32)).astype(jnp.bfloat16)]
    return jnp.concatenate(parts)


def add_low(*parts):
    return sum(part.astype(jnp.float32) for part in parts).astype(jnp.bfloat16)


def swap(part, axis, turn):
    return lax.ppermute(part, axis, [(to, to ^ turn) for to in range(lax.axis_size(axis))])


class Summing:
    steps = 4

    def __init__(self, packed):
        self.core, self.plane = lax.axis_index("ctx"), lax.axis_index("dp")
        self.planes = lax.axis_size("dp")
        self.part = packed.reshape(self.planes, 2, -1, packed.shape[1])
        self.step = 0

    def sends(self):
        if self.step == 0:
            return [lax.dynamic_index_in_dim(self.part, 1 - self.core, 1, keepdims=False)]
        if self.step == 1:
            return [
                lax.dynamic_index_in_dim(self.part, self.plane ^ turn, 0, keepdims=False)
                for turn in range(1, self.planes)
            ]
        return [self.part]

    def move(self, sent):
        axis, first = (("ctx", 1), ("dp", 1), ("expert", 1), ("expert", 2))[self.step]
        return [swap(part, axis, first + at) for at, part in enumerate(sent)]

    def take(self, arrived):
        if self.step == 0:
            self.part = lax.dynamic_index_in_dim(self.part, self.core, 1, keepdims=False)
        elif self.step == 1:
            self.part = lax.dynamic_index_in_dim(self.part, self.plane, 0, keepdims=False)
        self.part = add_low(self.part, *arrived)
        self.step += 1

    def finish(self):
        return lax.all_gather(self.part, ("dp", "ctx"), axis=0, tiled=True)


def matrix_of(sums, index, rows):
    return sums[index * rows : (index + 1) * rows]


def small_of(sums, start):
    high, low = jnp.split(sums[start:].astype(jnp.float32), 2)
    return high + low


def per_device(
    tokens,
    cotangent,
    routes,
    norm1_gain,
    query_weight,
    key_weight,
    value_weight,
    output_weight,
    bias_table,
    norm2_gain,
    router_weight,
    w_in,
    w_out,
):
    seq_count, local_len, model_width = tokens.shape
    owners = lax.axis_size("expert")
    capacity = local_len // 2
    whole_seq = seq_count == 2 and lax.axis_size("ctx") == 2 and local_len % QB == 0
    if whole_seq:
        routes, cotangent, tokens = trade(routes), trade(cotangent), trade(tokens)
    groups = [slice(0, 1), slice(1, 2)] if whole_seq else [slice(0, seq_count)]
    label = lax.axis_index("expert")
    labels = (label + jnp.arange(owners, dtype=jnp.int32)) % owners
    dispatch = make_dispatch(routes, labels, capacity)

    together = lax.optimization_barrier

    def sort_rows(group, rows):
        sent = [
            jnp.einsum("scx,sxd->scd", dispatch[turn, group], rows, preferred_element_type=jnp.float32)
            for turn in range(owners)
        ]
        return [piece.astype(jnp.bfloat16).reshape(-1, model_width) for piece in sent]

    def place_rows(group, pieces):
        pieces = jnp.stack(pieces).reshape(owners, -1, capacity, model_width)
        return jnp.einsum("escx,escd->sxd", dispatch[:, group], pieces, preferred_element_type=jnp.float32)

    inputs = tokens.astype(jnp.float32)
    scale1 = norm_scale(inputs)
    attn_in = (inputs * scale1 * norm1_gain).astype(jnp.bfloat16)
    queries = wide_dot(attn_in, query_weight).astype(jnp.bfloat16)
    keys = wide_dot(attn_in, key_weight).astype(jnp.bfloat16)
    values = wide_dot(attn_in, value_weight).astype(jnp.bfloat16)
    sorted_upstream = [sort_rows(group, cotangent[group]) for group in groups]
    sorted_upstream, queries = together((sorted_upstream, queries))
    upstream = [exchange(sorted_upstream[0], "expert", 1)]
    if whole_seq:
        lines = bias_lines(bias_table)
        flat = (seq_count * local_len, model_width)
        qkv = [rows.reshape(flat) for rows in (queries, keys, values)]
    else:
        first_pos = lax.axis_index("ctx") * local_len
        keys = lax.all_gather(keys, "ctx", axis=1, tiled=True)
        values = lax.all_gather(values, "ctx", axis=1, tiled=True)
        buckets = bucket_grid(first_pos, local_len, keys.shape[1])
        attended, log_totals = attend_rows(queries, keys, values, buckets, bias_table, DH)
    attended_groups, residual1, scale2, arrived = [], [], [], []
    in_flight, fed = upstream[0], queries.reshape(-1, model_width)
    for at, group in enumerate(groups):
        if whole_seq:
            rows = attend(fed, *qkv[1:], lines, at * local_len, local_len)[None]
        else:
            rows = attended.astype(jnp.bfloat16)
        rows, in_flight = together((rows, in_flight))
        if at == 0:
            upstream[0] = in_flight
        else:
            arrived[-1], sorted_upstream[at] = together((in_flight, sorted_upstream[at]))
            upstream.append(exchange(sorted_upstream[at], "expert", 1))
        attended_groups.append(rows)
        residual1.append(inputs[group] + wide_dot(rows, output_weight))
        scale2.append(norm_scale(residual1[-1]))
        router_in = (residual1[-1] * scale2[-1] * norm2_gain).astype(jnp.bfloat16)
        sorted_rows, fed = together((sort_rows(group, router_in), fed))
        in_flight = exchange(sorted_rows, "expert", 1)
        arrived.append(in_flight)
    attended = attended_groups
    router_wide = jnp.pad(router_weight, ((0, 0), (0, 128 - router_weight.shape[1])))
    label = label.astype(jnp.int32).reshape(1)
    done, back = [], []
    for at, (rows, grads) in enumerate(zip(arrived, upstream)):
        earlier = done[-1][0] if done else []
        result = run_expert(label, rows, grads, router_wide, w_in[0], w_out[0], at, len(groups), earlier)
        if back:
            result, back[-1] = together((result, back[-1]))
        done.append(result)
        back.append(exchange(result[1], "expert", -1))
    rows_out = done[-1][0]
    grad_rows, hiddens, pre_grads, grad_router = zip(*[item[2] for item in done])
    grad_router = sum(grad_router)[:, : router_weight.shape[1]].T
    grad_experts = expert_grads(sum(arrived, []), grad_rows, hiddens, pre_grads)
    grad_experts, back[-1], rows_out = together((grad_experts, back[-1], rows_out))
    grad_experts = lax.psum_scatter(grad_experts, ("dp", "ctx"), scatter_dimension=0, tiled=True)
    returned = exchange(list(rows_out), "expert", -1)
    residual_grad, attn_grad, mixed_grad, grad_norm2 = [], [], [], 0.0
    for group, rows, scale, pieces in zip(groups, residual1, scale2, back):
        norm2_back, gain_part = norm_back(rows, scale, norm2_gain, place_rows(group, pieces))
        grad_norm2 = grad_norm2 + gain_part
        residual_grad.append(cotangent[group].astype(jnp.float32) + norm2_back)
        attn_grad.append(residual_grad[-1].astype(jnp.bfloat16))
        mixed_grad.append(wide_dot_back(attn_grad[-1], output_weight).astype(jnp.bfloat16))
    grad_w_output = sum(weight_dot(left, right) for left, right in zip(attended, attn_grad))
    residual_grad, mixed_grad = jnp.concatenate(residual_grad), jnp.concatenate(mixed_grad)
    early_small = jnp.concatenate([grad_router, grad_norm2[None]])
    projections = (query_weight, key_weight, value_weight)
    if whole_seq:
        rows_in = attn_in.reshape(flat)
        half = model_width // 2
        pairs = half // 128
        mixed_grad = mixed_grad.reshape(flat)

        def weight_grads(grads):
            return [jnp.dot(rows_in.T, part, preferred_element_type=jnp.float32) for part in grads]

        first_grads, first_bias = attend_back(*qkv, mixed_grad, lines, 0, pairs)
        matrices = [grad_w_output[:, :half], grad_w_output[:, half:]] + weight_grads(first_grads)
        early = Summing(pack_sums(matrices, early_small.reshape(-1, half)))
        second_grads, biases = None, [first_bias]
        for at in range(pairs, 2 * pairs):
            sent, mixed_grad = together((early.sends(), mixed_grad))
            moved = early.move(sent)
            second_grads, bias = attend_back(*qkv, mixed_grad, lines, at, 1, pairs, second_grads)
            second_grads, moved = together((second_grads, moved))
            early.take(moved)
            biases.append(bias)
        second_grads, returned, grad_experts = together((second_grads, returned, grad_experts))
        late = Summing(pack_sums(weight_grads(second_grads), jnp.concatenate(biases)))
        early.take(early.move(early.sends()))
        early_sums = early.finish()
        for step in range(late.steps):
            late.take(late.move(late.sends()))
        late.part, early_sums = together((late.part, early_sums))
        sums = [early_sums, late.finish()]
        norm_in_grad = 0.0
        low_parts = (first_grads, second_grads)
        for at, grads in enumerate(low_parts):
            span = slice(at * 128 * pairs, (at + 1) * 128 * pairs)
            for kind in range(3):
                norm_in_grad += jnp.einsum(
                    "xe,de->xd", grads[kind], projections[kind][:, span], preferred_element_type=jnp.float32
                )
        norm_in_grad = norm_in_grad.reshape(tokens.shape)
        grad_qkv = [
            jnp.concatenate(
                [matrix_of(sums[0], 2 + kind, model_width), matrix_of(sums[1], kind, model_width)], axis=1
            ).astype(jnp.float32)
            for kind in range(3)
        ]
        grad_w_output = jnp.concatenate([matrix_of(sums[0], side, model_width) for side in range(2)], axis=1)
        small = small_of(sums[0], 5 * model_width).reshape(-1, model_width)
        grad_bias = small_of(sums[1], 3 * model_width)
    else:
        query_grad, _, diag_grad, key_part, value_part = attend_back_rows(
            queries, keys, values, mixed_grad, log_totals, buckets, bias_table, DH
        )
        low_parts = [query_grad.astype(jnp.bfloat16)] + [
            lax.psum_scatter(part, "ctx", scatter_dimension=1, tiled=True).astype(jnp.bfloat16)
            for part in (key_part, value_part)
        ]
        norm_in_grad = sum(wide_dot_back(*pair) for pair in zip(low_parts, projections))
        sums = lax.psum(
            pack_sums([grad_w_output] + [weight_dot(attn_in, rows) for rows in low_parts], early_small),
            ("dp", "ctx", "expert"),
        )
        grad_bias = lax.psum(diag_grad, ("dp", "ctx", "expert"))
        grad_w_output, *grad_qkv = (matrix_of(sums, kind, model_width).astype(jnp.float32) for kind in range(4))
        small = small_of(sums, 4 * model_width)
    grad_bias = grad_bias[: bias_table.shape[1], : bias_table.shape[0]].T
    grad_norm1 = sum(jnp.sum(grad * weight.astype(jnp.float32), axis=1) for grad, weight in zip(grad_qkv, projections))
    grad_norm1 = grad_norm1 / norm1_gain
    grad_w_query, grad_w_key, grad_w_value = grad_qkv
    grad_w_output = grad_w_output.astype(jnp.float32)
    experts = router_weight.shape[1]
    grad_router, grad_norm2 = small[:experts, :].T, small[experts]
    returned = [piece.reshape(len(groups), -1, model_width) for piece in returned]
    block_out = [
        rows + place_rows(group, [piece[at] for piece in returned])
        for at, (group, rows) in enumerate(zip(groups, residual1))
    ]
    block_out = jnp.concatenate(block_out).astype(jnp.bfloat16)
    norm1_back, _ = norm_back(inputs, scale1, norm1_gain, norm_in_grad)
    d_tokens = residual_grad + norm1_back
    if whole_seq:
        block_out, d_tokens = trade(block_out), trade(d_tokens)
    grad_experts = grad_experts.astype(jnp.float32)
    return (
        block_out,
        d_tokens,
        grad_norm1,
        grad_w_query,
        grad_w_key,
        grad_w_value,
        grad_w_output,
        grad_bias,
        grad_norm2,
        grad_router,
        grad_experts[:, :model_width].T[None],
        grad_experts[:, model_width:][None],
    )


def solution(mesh):
    rows = P(("dp", "expert"), "ctx", None)
    in_specs = (rows, rows, P(("dp", "expert"), "ctx")) + (P(),) * 8 + (P("expert", None, None),) * 2
    out_specs = (rows, rows) + (P(),) * 8 + (P("expert", None, ("dp", "ctx")), P("expert", ("dp", "ctx"), None))
    return jax.shard_map(per_device, mesh=mesh, in_specs=in_specs, out_specs=out_specs, check_vma=False)
```

```python
import jax
import jax.numpy as jnp
import numpy as np
from jax import lax
from jax.experimental import pallas as pl
from jax.experimental.pallas import tpu as pltpu
from jax.sharding import PartitionSpec as P

DH = 64
QB = 256

bucket_edges = (1, 2, 3, 4, 5, 6, 7, 8, 12, 16, 23, 32, 46, 64, 91)
norm_eps = 1e-06
precise_result = lax.Precision.HIGHEST


def bucket_of(relative):
    distance = jnp.abs(relative)
    half_bucket = jnp.zeros(relative.shape, jnp.int32)
    for threshold in bucket_edges:
        half_bucket = half_bucket + (distance >= threshold).astype(jnp.int32)
    return half_bucket + 16 * (relative > 0).astype(jnp.int32)


def bucket_grid(row_start, row_count, col_count):
    row_pos = row_start + jnp.arange(row_count, dtype=jnp.int32)
    col_pos = jnp.arange(col_count, dtype=jnp.int32)
    return bucket_of(col_pos[None, :] - row_pos[:, None])


def bias_grid(buckets, table_column, bucket_count):
    result = jnp.zeros(buckets.shape, jnp.float32)
    for label in range(bucket_count):
        result = result + jnp.where(buckets == label, table_column[label], 0.0)
    return result


def fold_buckets(buckets, grad_sum, bucket_count):
    return jnp.stack(
        [jnp.sum(jnp.where(buckets == label, grad_sum, 0.0)) for label in range(bucket_count)]
    )


def head_slice(value_rows, head_index, head_size):
    return lax.dynamic_slice_in_dim(value_rows, head_index * head_size, head_size, 2)


def put_head(target, portion, head_index, head_size):
    return lax.dynamic_update_slice_in_dim(target, portion, head_index * head_size, 2)


def head_scores(q_head, k_head, buckets, bias_table, head_index):
    table_column = lax.dynamic_index_in_dim(bias_table, head_index, 1, keepdims=False)
    scores = jnp.einsum("sqd,skd->sqk", q_head, k_head, preferred_element_type=jnp.float32)
    return scores + bias_grid(buckets, table_column, bias_table.shape[0])[None]


def attend_rows(query_matrix, keys_whole, values_whole, buckets, bias_table, head_size):
    seq_count, row_count, feature_width = query_matrix.shape
    head_count = feature_width // head_size

    def one_head(head_index, running):
        attention_result, log_totals = running
        scores = head_scores(
            head_slice(query_matrix, head_index, head_size),
            head_slice(keys_whole, head_index, head_size),
            buckets,
            bias_table,
            head_index,
        )
        row_max = jnp.max(scores, axis=-1, keepdims=True)
        log_total = row_max + jnp.log(jnp.sum(jnp.exp(scores - row_max), axis=-1, keepdims=True))
        weights_low = jnp.exp(scores - log_total).astype(jnp.bfloat16)
        portion = jnp.einsum(
            "sqk,skd->sqd",
            weights_low,
            head_slice(values_whole, head_index, head_size),
            preferred_element_type=jnp.float32,
        )
        attention_result = put_head(attention_result, portion, head_index, head_size)
        log_totals = lax.dynamic_update_index_in_dim(log_totals, log_total[..., 0], head_index, 0)
        return (attention_result, log_totals)

    initial = (
        jnp.zeros((seq_count, row_count, feature_width), jnp.float32),
        jnp.zeros((head_count, seq_count, row_count), jnp.float32),
    )
    return lax.fori_loop(0, head_count, one_head, initial)


def attend_back_rows(
    query_matrix, keys_whole, values_whole, mixed_grad, log_totals, buckets, bias_table, head_size
):
    seq_count, row_count, feature_width = query_matrix.shape
    col_count = keys_whole.shape[1]
    head_count = feature_width // head_size
    bucket_count = bias_table.shape[0]

    def one_head(head_index, running):
        query_grad, deltas, diag_grad, key_part, value_part = running
        q_head = head_slice(query_matrix, head_index, head_size)
        k_head = head_slice(keys_whole, head_index, head_size)
        v_head = head_slice(values_whole, head_index, head_size)
        g_head = head_slice(mixed_grad, head_index, head_size)
        scores = head_scores(q_head, k_head, buckets, bias_table, head_index)
        weights = jnp.exp(scores - log_totals[head_index][..., None])
        weight_grad = jnp.einsum("sqd,skd->sqk", g_head, v_head, preferred_element_type=jnp.float32)
        delta_row = jnp.sum(weights * weight_grad, axis=-1)
        score_grad = (weights * (weight_grad - delta_row[..., None])).astype(jnp.bfloat16)
        query_grad = put_head(
            query_grad,
            jnp.einsum("sqk,skd->sqd", score_grad, k_head, preferred_element_type=jnp.float32),
            head_index,
            head_size,
        )
        deltas = lax.dynamic_update_index_in_dim(deltas, delta_row, head_index, 0)
        folded = fold_buckets(
            buckets, jnp.sum(score_grad.astype(jnp.float32), axis=0), bucket_count
        )
        diag_grad = lax.dynamic_update_index_in_dim(diag_grad, folded, head_index, 0)
        key_part = put_head(
            key_part,
            jnp.einsum("sqk,sqd->skd", score_grad, q_head, preferred_element_type=jnp.float32),
            head_index,
            head_size,
        )
        value_part = put_head(
            value_part,
            jnp.einsum(
                "sqk,sqd->skd",
                weights.astype(jnp.bfloat16),
                g_head,
                preferred_element_type=jnp.float32,
            ),
            head_index,
            head_size,
        )
        return (query_grad, deltas, diag_grad, key_part, value_part)

    key_shape = (seq_count, col_count, feature_width)
    initial = (
        jnp.zeros((seq_count, row_count, feature_width), jnp.float32),
        jnp.zeros((head_count, seq_count, row_count), jnp.float32),
        jnp.zeros((head_count, bucket_count), jnp.float32),
        jnp.zeros(key_shape, jnp.float32),
        jnp.zeros(key_shape, jnp.float32),
    )
    return lax.fori_loop(0, head_count, one_head, initial)


def bucket_np(relative):
    half_bucket = np.zeros(relative.shape, np.int32)
    for threshold in bucket_edges:
        half_bucket = half_bucket + (np.abs(relative) >= threshold)
    return half_bucket + 16 * (relative > 0)


def bias_lines(bias_table):
    lane = np.arange(4 * QB)
    both = np.stack([lane - 2 * QB, 2 * QB - lane])
    onehot = (bucket_np(both)[..., None] == np.arange(32)).astype(np.float32)
    return jnp.einsum("lcb,bh->hlc", jnp.asarray(onehot), bias_table, precision=lax.Precision.HIGHEST)

def fwd_kernel(first, lines_ref, q_ref, k_ref, v_ref, o_ref, band_ref):
    n = k_ref.shape[0] // QB
    lane = lax.broadcasted_iota(jnp.int32, (QB, 128), 1)
    for h in range(2):
        line = lines_ref[h, 0:1, :]
        spread = pltpu.roll(jnp.broadcast_to(line, (QB, 4 * QB)), 0, 1, stride=1, stride_axis=0)
        band_ref[h] = spread[:, QB:]
    for i in range(first, first + q_ref.shape[0] // QB):
        rows = slice((i - first) * QB, (i - first + 1) * QB)
        outs = []
        for h in range(2):
            low_bias = lines_ref[h, 0:1, 0:1]
            high_bias = lines_ref[h, 0:1, 4 * QB - 1:]
            q = jnp.where((lane < 64) == (h == 0), q_ref[rows, :], 0)
            s = lax.dot_general(q, k_ref[...], (((1,), (1,)), ((), ())), preferred_element_type=jnp.float32)
            parts = []
            for j in range(n):
                d = j - i
                b = band_ref[h, :, (d + 1) * QB:(d + 2) * QB] if abs(d) <= 1 else (low_bias if d < 0 else high_bias)
                parts.append(s[:, j * QB:(j + 1) * QB] + b)
            s = jnp.concatenate(parts, axis=1)
            m = jnp.max(s, axis=1, keepdims=True)
            p = jnp.exp(s - m)
            l = jnp.sum(p, axis=1, keepdims=True)
            o = jnp.dot(p.astype(jnp.bfloat16), v_ref[...], preferred_element_type=jnp.float32)
            outs.append(o * (1.0 / l))
        o_ref[rows, :] = jnp.where(lane < 64, outs[0], outs[1]).astype(jnp.bfloat16)

def attend(q, k, v, lines, first, count):
    length, width = q.shape
    col = pl.BlockSpec((length, 128), lambda h: (0, h))
    span = pl.BlockSpec((count, 128), lambda h: (first // count, h))
    return pl.pallas_call(
        lambda *refs: fwd_kernel(first // QB, *refs),
        grid=(width // 128,),
        in_specs=[pl.BlockSpec((2, 2, 4 * QB), lambda h: (h, 0, 0)), span, col, col],
        out_specs=pl.BlockSpec((count, 128), lambda h: (0, h)),
        out_shape=jax.ShapeDtypeStruct((count, width), jnp.bfloat16),
        scratch_shapes=[pltpu.VMEM((2, QB, 3 * QB), jnp.float32)],
        compiler_params=pltpu.CompilerParams(vmem_limit_bytes=48 << 20),
        cost_estimate=pl.CostEstimate(flops=count * length * width, bytes_accessed=2 * length * width, transcendentals=0),
        name="attend",
    )(lines, q, k, v)

def bwd_kernel(lines_ref, fold_ref, q_ref, k_ref, v_ref, g_ref, grad_ref, bias_ref, band_ref, acc_ref, far_acc, dk_acc, dv_acc):
    n = q_ref.shape[0] // QB
    lane = lax.broadcasted_iota(jnp.int32, (QB, 128), 1)
    for h in range(2):
        for t in range(3):
            start = 2 * QB - (t - 1) * QB - QB
            line = lines_ref[h, 1:2, start:start + 2 * QB]
            spread = pltpu.roll(jnp.broadcast_to(line, (QB, 2 * QB)), QB, 1, stride=1, stride_axis=0)
            band_ref[h, t * QB:(t + 1) * QB, :] = spread[:, :QB]
    acc_ref[...] = jnp.zeros_like(acc_ref)
    far_acc[...] = jnp.zeros_like(far_acc)
    for i in range(n):
        rows = slice(i * QB, (i + 1) * QB)
        grads = []
        for h in range(2):
            keep = (lane < 64) == (h == 0)
            low_bias = lines_ref[h, 0:1, 0:1]
            high_bias = lines_ref[h, 0:1, 4 * QB - 1:]
            q = jnp.where(keep, q_ref[rows, :], 0)
            g = jnp.where(keep, g_ref[rows, :], 0)
            s = lax.dot_general(k_ref[...], q, (((1,), (1,)), ((), ())), preferred_element_type=jnp.float32)
            parts = []
            for j in range(n):
                d = j - i
                b = band_ref[h, (d + 1) * QB:(d + 2) * QB, :] if abs(d) <= 1 else (low_bias if d < 0 else high_bias)
                parts.append(s[j * QB:(j + 1) * QB, :] + b)
            s = jnp.concatenate(parts, axis=0)
            m = jnp.max(s, axis=0, keepdims=True)
            p = jnp.exp(s - m)
            w = p * (1.0 / jnp.sum(p, axis=0, keepdims=True))
            dp = lax.dot_general(v_ref[...], g, (((1,), (1,)), ((), ())), preferred_element_type=jnp.float32)
            delta = jnp.sum(w * dp, axis=0, keepdims=True)
            ds = w * (dp - delta)
            for j in range(n):
                d = j - i
                tile = ds[j * QB:(j + 1) * QB, :]
                if abs(d) <= 1:
                    acc_ref[h, (d + 1) * QB:(d + 2) * QB, :] += tile
                else:
                    far_acc[h, 0 if d < 0 else 1] += jnp.sum(tile.reshape(QB // 8, 8, QB), axis=0)
            low = ds.astype(jnp.bfloat16)
            dv = jnp.dot(w.astype(jnp.bfloat16), g, preferred_element_type=jnp.float32)
            dk = jnp.dot(low, q, preferred_element_type=jnp.float32)
            if i == 0 and h == 0:
                dv_acc[...] = dv
                dk_acc[...] = dk
            else:
                dv_acc[...] += dv
                dk_acc[...] += dk
            grads.append(lax.dot_general(low, k_ref[...], (((0,), (0,)), ((), ())), preferred_element_type=jnp.float32))
        grad_ref[0, rows, :] = jnp.where(lane < 64, grads[0], grads[1]).astype(jnp.bfloat16)
    grad_ref[1] = dk_acc[...].astype(jnp.bfloat16)
    grad_ref[2] = dv_acc[...].astype(jnp.bfloat16)
    row = lax.broadcasted_iota(jnp.int32, (8, 2 * QB), 0)
    for h in range(2):
        total = jnp.zeros((8, 128), jnp.float32)
        for t in range(3):
            tile = acc_ref[h, t * QB:(t + 1) * QB, :]
            wide = jnp.concatenate([tile, jnp.zeros_like(tile)], axis=1)
            moved = sum(pltpu.roll(wide[8 * e:8 * e + 8], QB - 8 * e, 1) for e in range(QB // 8))
            turned = jnp.where(row == 0, moved, 0.0)
            for e in range(1, 8):
                turned = turned + pltpu.roll(jnp.where(row == e, moved, 0.0), 2 * QB - e, 1)
            total = total + jnp.dot(turned, fold_ref[t], precision=lax.Precision.HIGHEST, preferred_element_type=jnp.float32)
        total = jnp.sum(total, axis=0, keepdims=True)
        ends = [jnp.sum(jnp.sum(far_acc[h, side], axis=0, keepdims=True), axis=1, keepdims=True) for side in range(2)]
        column = lax.broadcasted_iota(jnp.int32, (1, 128), 1)
        total = total + jnp.where(column == 15, ends[0], 0.0) + jnp.where(column == 31, ends[1], 0.0)
        bias_ref[0, h:h + 1, :] = total


def attend_back(q, k, v, g, lines, first_pair, pairs, total_pairs=None, earlier=None):
    length = q.shape[0]
    r = (np.arange(3)[:, None] - 1) * QB - (np.arange(2 * QB)[None] - QB)
    fold = (bucket_np(r)[..., None] == np.arange(128)).astype(np.float32)
    col = pl.BlockSpec((length, 128), lambda h: (0, h + first_pair))
    offset = first_pair % total_pairs if total_pairs else 0
    kept = [] if earlier is None else [earlier]
    grads, bias = pl.pallas_call(
        lambda *refs: bwd_kernel(*refs[:6], *refs[6 + len(kept):]),
        grid=(pairs,),
        in_specs=[
            pl.BlockSpec((2, 2, 4 * QB), lambda h: (h + first_pair, 0, 0)),
            pl.BlockSpec((3, 2 * QB, 128), lambda h: (0, 0, 0)),
            col, col, col, col,
        ]
        + [pl.BlockSpec(memory_space=pl.ANY)] * len(kept),
        out_specs=[pl.BlockSpec((3, length, 128), lambda h: (0, 0, h + offset)), pl.BlockSpec((1, 2, 128), lambda h: (h, 0, 0))],
        out_shape=[
            jax.ShapeDtypeStruct((3, length, 128 * (total_pairs or pairs)), jnp.bfloat16),
            jax.ShapeDtypeStruct((pairs, 2, 128), jnp.float32),
        ],
        scratch_shapes=[
            pltpu.VMEM((2, 3 * QB, QB), jnp.float32),
            pltpu.VMEM((2, 3 * QB, QB), jnp.float32),
            pltpu.VMEM((2, 2, 8, QB), jnp.float32),
            pltpu.VMEM((length, 128), jnp.float32),
            pltpu.VMEM((length, 128), jnp.float32),
        ],
        compiler_params=pltpu.CompilerParams(vmem_limit_bytes=48 << 20),
        cost_estimate=pl.CostEstimate(
            flops=84 * length * length * 128 * pairs, bytes_accessed=14 * length * 128 * pairs, transcendentals=2 * length * length * pairs
        ),
        input_output_aliases={6: 0} if kept else {},
        name="attend_back",
    )(lines, jnp.asarray(fold), q, k, v, g, *kept)
    return grads, bias.reshape(2 * pairs, 128)


def expert_kernel(count, label_ref, *refs):
    x_refs, u_refs = refs[:count], refs[count : 2 * count]
    router_ref, win_ref, wout_ref = refs[2 * count : 2 * count + 3]
    rest = refs[len(refs) - 7 - 2 * count :]
    rows_refs, back_refs = rest[:count], rest[count : 2 * count]
    g_ref, hid_ref, pre_ref, drouter_ref, prob_ref, out_acc, back_acc = rest[2 * count :]
    step = pl.program_id(0)
    tile = x_refs[0].shape[0]
    lane = lax.broadcasted_iota(jnp.int32, (tile, 128), 1)
    own = lane == label_ref[0]
    spans = [slice(r * tile, (r + 1) * tile) for r in range(count)]

    @pl.when(step == 0)
    def _():
        for piece, rows in enumerate(spans):
            logits = jnp.dot(x_refs[piece][...], router_ref[...], preferred_element_type=jnp.float32)
            logits = jnp.where(lane < 4, logits, -jnp.inf)
            raised = jnp.exp(logits - jnp.max(logits, axis=1, keepdims=True))
            prob = raised / jnp.sum(raised, axis=1, keepdims=True)
            prob_ref[rows, :] = prob
            gate = jnp.sum(jnp.where(own, prob, 0.0), axis=1, keepdims=True)
            g_ref[rows, :] = (gate * u_refs[piece][...].astype(jnp.float32)).astype(jnp.bfloat16)
        out_acc[...] = jnp.zeros_like(out_acc)
        back_acc[...] = jnp.zeros_like(back_acc)

    for piece, rows in enumerate(spans):
        pre = jnp.dot(x_refs[piece][...], win_ref[...], preferred_element_type=jnp.float32)
        square = pre * pre
        turn = jnp.tanh(pre * (0.7978845608028654 + 0.035677408136300125 * square))
        half = 0.5 + 0.5 * turn
        hidden = (pre * half).astype(jnp.bfloat16)
        slope = half + pre * (half - half * half) * (1.5957691216057308 + 0.21406444881780074 * square)
        hid_ref[rows, :] = hidden
        out_acc[rows, :] += jnp.dot(hidden, wout_ref[...], preferred_element_type=jnp.float32)
        hidden_grad = lax.dot_general(g_ref[rows, :], wout_ref[...], (((1,), (1,)), ((), ())), preferred_element_type=jnp.float32)
        pre_grad = (hidden_grad * slope).astype(jnp.bfloat16)
        pre_ref[rows, :] = pre_grad
        back_acc[rows, :] += lax.dot_general(pre_grad, win_ref[...], (((1,), (1,)), ((), ())), preferred_element_type=jnp.float32)

    @pl.when(step == pl.num_programs(0) - 1)
    def _():
        total = jnp.zeros(drouter_ref.shape, jnp.float32)
        for piece, rows in enumerate(spans):
            prob = prob_ref[rows, :]
            gate = jnp.sum(jnp.where(own, prob, 0.0), axis=1, keepdims=True)
            out = out_acc[rows, :].astype(jnp.bfloat16).astype(jnp.float32)
            rows_refs[piece][...] = (gate * out).astype(jnp.bfloat16)
            gate_grad = jnp.sum(u_refs[piece][...].astype(jnp.float32) * out, axis=1, keepdims=True)
            logit_grad = prob * (jnp.where(own, gate_grad, 0.0) - gate * gate_grad)
            high = logit_grad.astype(jnp.bfloat16)
            low = (logit_grad - high.astype(jnp.float32)).astype(jnp.bfloat16)
            back = back_acc[rows, :].astype(jnp.bfloat16).astype(jnp.float32)
            for part in (high, low):
                back += lax.dot_general(part, router_ref[...], (((1,), (1,)), ((), ())), preferred_element_type=jnp.float32)
                total += lax.dot_general(x_refs[piece][...], part, (((0,), (0,)), ((), ())), preferred_element_type=jnp.float32)
            back_refs[piece][...] = back.astype(jnp.bfloat16)
        drouter_ref[...] = total


def run_expert(label, pieces, upstream_pieces, router_wide, w_in, w_out, group, group_count, earlier, chunk=768):
    count, (tile, width) = len(pieces), pieces[0].shape
    rows, inner = count * tile, w_in.shape[1]
    once = pl.Buffered(1)
    piece = pl.BlockSpec((tile, width), lambda f, lab: (0, 0), pipeline_mode=once)
    inner_block = pl.BlockSpec((rows, chunk), lambda f, lab: (0, f))
    low = lambda *shape: jax.ShapeDtypeStruct(shape, jnp.bfloat16)
    outs = pl.pallas_call(
        lambda *refs: expert_kernel(count, *refs),
        grid_spec=pltpu.PrefetchScalarGridSpec(
            num_scalar_prefetch=1,
            grid=(inner // chunk,),
            in_specs=[piece] * (2 * count) + [
                pl.BlockSpec((width, 128), lambda f, lab: (0, 0), pipeline_mode=once),
                pl.BlockSpec((width, chunk), lambda f, lab: (0, f)),
                pl.BlockSpec((chunk, width), lambda f, lab: (f, 0)),
            ]
            + [pl.BlockSpec(memory_space=pl.ANY)] * len(earlier),
            out_specs=[pl.BlockSpec((tile, width), lambda f, lab: (group, 0), pipeline_mode=once)] * count
            + [piece] * count
            + [
                pl.BlockSpec((rows, width), lambda f, lab: (0, 0), pipeline_mode=once),
                inner_block,
                inner_block,
                pl.BlockSpec((width, 128), lambda f, lab: (0, 0), pipeline_mode=once),
            ],
            scratch_shapes=[
                pltpu.VMEM((rows, 128), jnp.float32),
                pltpu.VMEM((rows, width), jnp.float32),
                pltpu.VMEM((rows, width), jnp.float32),
            ],
        ),
        out_shape=[low(group_count * tile, width)] * count
        + [low(tile, width)] * count
        + [low(rows, width), low(rows, inner), low(rows, inner), jax.ShapeDtypeStruct((width, 128), jnp.float32)],
        compiler_params=pltpu.CompilerParams(vmem_limit_bytes=48 << 20),
        cost_estimate=pl.CostEstimate(flops=16 * rows * width * inner, bytes_accessed=8 * width * inner, transcendentals=rows * inner),
        input_output_aliases={2 * count + 4 + at: at for at in range(len(earlier))},
        name="experts",
    )(label, *pieces, *upstream_pieces, router_wide, w_in, w_out, *earlier)
    return outs[:count], outs[count : 2 * count], outs[2 * count :]


def expert_grads_kernel(groups, count, *refs):
    x_refs, refs = refs[: groups * count], refs[groups * count :]
    g_refs, hid_refs, pre_refs = refs[:groups], refs[groups : 2 * groups], refs[2 * groups : 3 * groups]
    dw_ref, xt_ref, gt_ref = refs[3 * groups :]
    width = xt_ref.shape[0]
    tile = x_refs[0].shape[0]
    rows = g_refs[0].shape[0]

    @pl.when(pl.program_id(0) == 0)
    def _():
        for at in range(groups):
            gt_ref[:, at * rows : (at + 1) * rows] = g_refs[at][...].T
            for piece in range(count):
                start = at * rows + piece * tile
                xt_ref[:, start : start + tile] = x_refs[at * count + piece][...].T

    for side, (left, right) in enumerate(((xt_ref, pre_refs), (gt_ref, hid_refs))):
        total = sum(
            jnp.dot(left[:, at * rows : (at + 1) * rows], right[at][...], preferred_element_type=jnp.float32)
            for at in range(groups)
        )
        dw_ref[:, side * width : (side + 1) * width] = total.astype(jnp.bfloat16).T


def expert_grads(pieces, grads, hiddens, pre_grads, chunk=512):
    groups, count = len(grads), len(pieces) // len(grads)
    (tile, width), (rows, inner) = pieces[0].shape, hiddens[0].shape
    once = pl.Buffered(1)
    inner_block = pl.BlockSpec((rows, chunk), lambda f: (0, f))
    return pl.pallas_call(
        lambda *refs: expert_grads_kernel(groups, count, *refs),
        grid=(inner // chunk,),
        in_specs=[pl.BlockSpec((tile, width), lambda f: (0, 0), pipeline_mode=once)] * (groups * count)
        + [pl.BlockSpec((rows, width), lambda f: (0, 0), pipeline_mode=once)] * groups
        + [inner_block] * (2 * groups),
        out_specs=pl.BlockSpec((chunk, 2 * width), lambda f: (f, 0)),
        out_shape=jax.ShapeDtypeStruct((inner, 2 * width), jnp.bfloat16),
        scratch_shapes=[pltpu.VMEM((width, groups * rows), jnp.bfloat16)] * 2,
        compiler_params=pltpu.CompilerParams(vmem_limit_bytes=48 << 20),
        cost_estimate=pl.CostEstimate(
            flops=6 * groups * rows * width * inner, bytes_accessed=4 * (groups * rows + width) * inner, transcendentals=0
        ),
        name="expert_grads",
    )(*pieces, *grads, *hiddens, *pre_grads)


def sort_matrix(slot, slots):
    row = lax.broadcasted_iota(jnp.int32, (slots, slot.shape[1]), 0)
    return (row == slot).astype(jnp.float32).astype(jnp.bfloat16)


def sort_into(piece_refs, block, slot, rows):
    capacity = slot.shape[1] // 2
    matrix = sort_matrix(slot, len(piece_refs) * capacity)
    moved = jnp.dot(matrix, rows, preferred_element_type=jnp.float32).astype(jnp.bfloat16)
    for turn, piece_ref in enumerate(piece_refs):
        piece_ref[block * capacity : (block + 1) * capacity, :] = moved[turn * capacity : (turn + 1) * capacity]


def norm_scale_rows(rows):
    return lax.rsqrt(jnp.mean(rows * rows, axis=-1, keepdims=True) + norm_eps)


def sort_kernel(owners, label_ref, routes_ref, rows_ref, *refs):
    piece_refs, slot_ref = refs[:owners], refs[owners]
    blocks, _, length = routes_ref.shape
    first = lax.broadcasted_iota(jnp.int32, (length, length), 0)
    second = lax.broadcasted_iota(jnp.int32, (length, length), 1)
    upto = (first <= second).astype(jnp.float32).astype(jnp.bfloat16)
    for block in range(blocks):
        routes = routes_ref[block]
        hits = (lax.broadcasted_iota(jnp.int32, (8, length), 0) == routes).astype(jnp.float32)
        counts = jnp.dot(hits.astype(jnp.bfloat16), upto, preferred_element_type=jnp.float32)
        place = jnp.sum(hits * counts, axis=0, keepdims=True).astype(jnp.int32) - 1
        turn = routes - label_ref[0]
        turn = jnp.where(turn < 0, turn + owners, turn)
        slot = turn * (length // 2) + place
        slot_ref[block] = slot
        sort_into(piece_refs, block, slot, rows_ref[block])


def sort_upstream(label, routes, rows, owners):
    blocks, length, width = rows.shape
    vmem = pl.BlockSpec(memory_space=pltpu.VMEM)
    piece = jax.ShapeDtypeStruct((blocks * length // 2, width), jnp.bfloat16)
    *pieces, slots = pl.pallas_call(
        lambda *refs: sort_kernel(owners, *refs),
        in_specs=[pl.BlockSpec(memory_space=pltpu.SMEM), vmem, vmem],
        out_specs=[vmem] * (owners + 1),
        out_shape=[piece] * owners + [jax.ShapeDtypeStruct((blocks, 1, length), jnp.int32)],
        compiler_params=pltpu.CompilerParams(vmem_limit_bytes=48 << 20),
        name="sort_upstream",
    )(label, routes.reshape(blocks, 1, length), rows)
    return pieces, slots


def after_attention_kernel(slot_ref, attended_ref, tokens_ref, weight_ref, gain_ref, residual_ref, *piece_refs):
    for block in range(slot_ref.shape[0]):
        mixed = jnp.dot(attended_ref[block], weight_ref[...], preferred_element_type=jnp.float32)
        residual = tokens_ref[block].astype(jnp.float32) + mixed
        residual_ref[block] = residual
        router_in = (residual * norm_scale_rows(residual) * gain_ref[...]).astype(jnp.bfloat16)
        sort_into(piece_refs, block, slot_ref[block], router_in)


def after_attention(slots, attended, tokens, weight, gain, owners):
    blocks, length, width = tokens.shape
    vmem = pl.BlockSpec(memory_space=pltpu.VMEM)
    piece = jax.ShapeDtypeStruct((blocks * length // 2, width), jnp.bfloat16)
    residual, *pieces = pl.pallas_call(
        after_attention_kernel,
        in_specs=[vmem] * 5,
        out_specs=[vmem] * (owners + 1),
        out_shape=[jax.ShapeDtypeStruct(tokens.shape, jnp.float32)] + [piece] * owners,
        compiler_params=pltpu.CompilerParams(vmem_limit_bytes=48 << 20),
        name="after_attention",
    )(slots, attended, tokens, weight, gain[None])
    return residual, pieces


def before_attention_kernel(owners, slot_ref, *refs):
    piece_refs = refs[:owners]
    residual_ref, upstream_ref, attended_ref, weight_ref, gain_ref = refs[owners : owners + 5]
    residual_grad_ref, mixed_grad_ref, weight_grad_ref, gain_grad_ref = refs[owners + 5 :]
    blocks, _, length = slot_ref.shape
    capacity = length // 2
    weight_grad, gain_grad = 0.0, 0.0
    for block in range(blocks):
        matrix = sort_matrix(slot_ref[block], owners * capacity)
        rows = jnp.concatenate([ref[block * capacity : (block + 1) * capacity, :] for ref in piece_refs])
        grad = lax.dot_general(matrix, rows, (((0,), (0,)), ((), ())), preferred_element_type=jnp.float32)
        residual = residual_ref[block]
        scale = norm_scale_rows(residual)
        normed = residual * scale
        scaled = grad * gain_ref[...]
        shrink = jnp.mean(scaled * normed, axis=-1, keepdims=True)
        gain_grad += jnp.sum(grad * normed, axis=0, keepdims=True)
        residual_grad = upstream_ref[block].astype(jnp.float32) + scale * (scaled - normed * shrink)
        residual_grad_ref[block] = residual_grad
        low = residual_grad.astype(jnp.bfloat16)
        mixed_grad = lax.dot_general(low, weight_ref[...], (((1,), (1,)), ((), ())), preferred_element_type=jnp.float32)
        mixed_grad_ref[block] = mixed_grad.astype(jnp.bfloat16)
        weight_grad += lax.dot_general(attended_ref[block], low, (((0,), (0,)), ((), ())), preferred_element_type=jnp.float32)
    weight_grad_ref[...] = weight_grad
    gain_grad_ref[...] = gain_grad


def before_attention(slots, pieces, residual, upstream, attended, weight, gain):
    width = residual.shape[2]
    vmem = pl.BlockSpec(memory_space=pltpu.VMEM)
    return pl.pallas_call(
        lambda *refs: before_attention_kernel(len(pieces), *refs),
        in_specs=[vmem] * (len(pieces) + 6),
        out_specs=[vmem] * 4,
        out_shape=[
            jax.ShapeDtypeStruct(residual.shape, jnp.float32),
            jax.ShapeDtypeStruct(residual.shape, jnp.bfloat16),
            jax.ShapeDtypeStruct((width, width), jnp.float32),
            jax.ShapeDtypeStruct((1, width), jnp.float32),
        ],
        compiler_params=pltpu.CompilerParams(vmem_limit_bytes=56 << 20),
        name="before_attention",
    )(slots, *pieces, residual, upstream, attended, weight, gain[None])


def exchange(pieces, axis, sign):
    size = lax.axis_size(axis)
    return [pieces[0]] + [
        lax.ppermute(pieces[turn], axis, [(at, (at + sign * turn) % size) for at in range(size)])
        for turn in range(1, size)
    ]


def trade(blocks):
    at = lax.axis_index("ctx")
    mine = lax.dynamic_index_in_dim(blocks, at, 0, keepdims=False)
    other = lax.dynamic_index_in_dim(blocks, 1 - at, 0, keepdims=False)
    arrived = lax.ppermute(other, "ctx", [(0, 1), (1, 0)])
    return jnp.stack([jnp.where(at == 0, mine, arrived), jnp.where(at == 0, arrived, mine)])


def place_rows(slots, pieces):
    blocks, _, length = slots.shape
    width = pieces[0].shape[-1]
    rows = jnp.stack(pieces).reshape(len(pieces), blocks, -1, width).swapaxes(0, 1).reshape(blocks, -1, width)
    places = jnp.arange(rows.shape[1], dtype=jnp.int32)
    matrix = (slots == places[None, :, None]).astype(jnp.bfloat16)
    return jnp.einsum("bsx,bsd->bxd", matrix, rows, preferred_element_type=jnp.float32)


def norm_scale(value_rows):
    return lax.rsqrt(jnp.mean(value_rows * value_rows, axis=-1, keepdims=True) + norm_eps)


def norm_back(value_rows, scale, gain_vector, grad_rows):
    scaled = grad_rows * gain_vector
    shrink = jnp.mean(scaled * value_rows, axis=-1, keepdims=True) * scale * scale * scale
    return scale * scaled - value_rows * shrink, jnp.sum(grad_rows * value_rows * scale, axis=(0, 1))


def wide_dot(rows, weight):
    return jnp.einsum("sxd,de->sxe", rows, weight, preferred_element_type=jnp.float32)


def wide_dot_back(rows, weight):
    return jnp.einsum("sxe,de->sxd", rows, weight, preferred_element_type=jnp.float32)


def weight_dot(left, right):
    return jnp.einsum("sxd,sxe->de", left, right, preferred_element_type=jnp.float32)


def pack_sums(matrices, small=None):
    parts = [matrix.astype(jnp.bfloat16) for matrix in matrices]
    if small is not None:
        small = jnp.pad(small, ((0, -small.shape[0] % 64), (0, parts[0].shape[1] - small.shape[1])))
        high = small.astype(jnp.bfloat16)
        parts += [high, (small - high.astype(jnp.float32)).astype(jnp.bfloat16)]
    return jnp.concatenate(parts)


def add_low(*parts):
    return sum(part.astype(jnp.float32) for part in parts).astype(jnp.bfloat16)


def swap(part, axis, turn):
    return lax.ppermute(part, axis, [(to, to ^ turn) for to in range(lax.axis_size(axis))])


class Summing:
    steps = 4

    def __init__(self, packed):
        self.core, self.plane = lax.axis_index("ctx"), lax.axis_index("dp")
        self.planes = lax.axis_size("dp")
        self.part = packed.reshape(self.planes, 2, -1, packed.shape[1])
        self.step = 0

    def sends(self):
        if self.step == 0:
            return [lax.dynamic_index_in_dim(self.part, 1 - self.core, 1, keepdims=False)]
        if self.step == 1:
            return [
                lax.dynamic_index_in_dim(self.part, self.plane ^ turn, 0, keepdims=False)
                for turn in range(1, self.planes)
            ]
        return [self.part]

    def move(self, sent):
        axis, first = (("ctx", 1), ("dp", 1), ("expert", 1), ("expert", 2))[self.step]
        return [swap(part, axis, first + at) for at, part in enumerate(sent)]

    def take(self, arrived):
        if self.step == 0:
            self.part = lax.dynamic_index_in_dim(self.part, self.core, 1, keepdims=False)
        elif self.step == 1:
            self.part = lax.dynamic_index_in_dim(self.part, self.plane, 0, keepdims=False)
        self.part = add_low(self.part, *arrived)
        self.step += 1

    def finish(self):
        return lax.all_gather(self.part, ("dp", "ctx"), axis=0, tiled=True)


def matrix_of(sums, index, rows):
    return sums[index * rows : (index + 1) * rows]


def small_of(sums, start):
    high, low = jnp.split(sums[start:].astype(jnp.float32), 2)
    return high + low


def per_device(
    tokens,
    cotangent,
    routes,
    norm1_gain,
    query_weight,
    key_weight,
    value_weight,
    output_weight,
    bias_table,
    norm2_gain,
    router_weight,
    w_in,
    w_out,
):
    seq_count, local_len, model_width = tokens.shape
    owners = lax.axis_size("expert")
    capacity = local_len // 2
    whole_seq = seq_count == 2 and lax.axis_size("ctx") == 2 and local_len % QB == 0
    if whole_seq:
        routes, cotangent, tokens = trade(routes), trade(cotangent), trade(tokens)
    groups = [slice(0, 1), slice(1, 2)] if whole_seq else [slice(0, seq_count)]
    label = lax.axis_index("expert").astype(jnp.int32).reshape(1)
    together = lax.optimization_barrier

    sorted_upstream, slots = zip(*[sort_upstream(label, routes[group], cotangent[group], owners) for group in groups])
    sorted_upstream = list(sorted_upstream)
    sorted_upstream[0], tokens = together((sorted_upstream[0], tokens))
    upstream = [exchange(sorted_upstream[0], "expert", 1)]
    inputs = tokens.astype(jnp.float32)
    scale1 = norm_scale(inputs)
    attn_in = (inputs * scale1 * norm1_gain).astype(jnp.bfloat16)
    queries = wide_dot(attn_in, query_weight).astype(jnp.bfloat16)
    keys = wide_dot(attn_in, key_weight).astype(jnp.bfloat16)
    values = wide_dot(attn_in, value_weight).astype(jnp.bfloat16)
    if whole_seq:
        lines = bias_lines(bias_table)
        flat = (seq_count * local_len, model_width)
        qkv = [rows.reshape(flat) for rows in (queries, keys, values)]
    else:
        first_pos = lax.axis_index("ctx") * local_len
        keys = lax.all_gather(keys, "ctx", axis=1, tiled=True)
        values = lax.all_gather(values, "ctx", axis=1, tiled=True)
        buckets = bucket_grid(first_pos, local_len, keys.shape[1])
        attended, log_totals = attend_rows(queries, keys, values, buckets, bias_table, DH)
    attended_groups, residual1, arrived = [], [], []
    in_flight, fed = upstream[0], queries.reshape(-1, model_width)
    for at, group in enumerate(groups):
        if whole_seq:
            rows = attend(fed, *qkv[1:], lines, at * local_len, local_len)[None]
        else:
            rows = attended.astype(jnp.bfloat16)
        rows, in_flight = together((rows, in_flight))
        if at == 0:
            upstream[0] = in_flight
        else:
            arrived[-1], sorted_upstream[at] = together((in_flight, sorted_upstream[at]))
            upstream.append(exchange(sorted_upstream[at], "expert", 1))
        attended_groups.append(rows)
        residual, sorted_rows = after_attention(slots[at], rows, tokens[group], output_weight, norm2_gain, owners)
        residual1.append(residual)
        sorted_rows, fed = together((sorted_rows, fed))
        in_flight = exchange(sorted_rows, "expert", 1)
        arrived.append(in_flight)
    router_wide = jnp.pad(router_weight, ((0, 0), (0, 128 - router_weight.shape[1])))
    done, back = [], []
    for at, (rows, grads) in enumerate(zip(arrived, upstream)):
        earlier = done[-1][0] if done else []
        result = run_expert(label, rows, grads, router_wide, w_in[0], w_out[0], at, len(groups), earlier)
        if back:
            result, back[-1] = together((result, back[-1]))
        done.append(result)
        back.append(exchange(result[1], "expert", -1))
    rows_out = done[-1][0]
    grad_rows, hiddens, pre_grads, grad_router = zip(*[item[2] for item in done])
    grad_router = sum(grad_router)[:, : router_weight.shape[1]].T
    grad_experts = expert_grads(sum(arrived, []), grad_rows, hiddens, pre_grads)
    grad_experts, back[-1], rows_out = together((grad_experts, back[-1], rows_out))
    grad_experts = lax.psum_scatter(grad_experts, ("dp", "ctx"), scatter_dimension=0, tiled=True)
    returned = exchange(list(rows_out), "expert", -1)
    residual_grad, mixed_grad, grad_w_output, grad_norm2 = zip(
        *[
            before_attention(slot, pieces, residual, cotangent[group], rows, output_weight, norm2_gain)
            for slot, pieces, residual, group, rows in zip(slots, back, residual1, groups, attended_groups)
        ]
    )
    residual_grad, mixed_grad = jnp.concatenate(residual_grad), jnp.concatenate(mixed_grad)
    grad_w_output, grad_norm2 = sum(grad_w_output), sum(grad_norm2)
    early_small = jnp.concatenate([grad_router, grad_norm2])
    projections = (query_weight, key_weight, value_weight)
    if whole_seq:
        rows_in = attn_in.reshape(flat)
        half = model_width // 2
        pairs = half // 128
        mixed_grad = mixed_grad.reshape(flat)

        def weight_grads(grads):
            return [jnp.dot(rows_in.T, part, preferred_element_type=jnp.float32) for part in grads]

        first_grads, first_bias = attend_back(*qkv, mixed_grad, lines, 0, pairs)
        matrices = [grad_w_output[:, :half], grad_w_output[:, half:]] + weight_grads(first_grads)
        early = Summing(pack_sums(matrices, early_small.reshape(-1, half)))
        second_grads, biases = None, [first_bias]
        for at in range(pairs, 2 * pairs):
            sent, mixed_grad = together((early.sends(), mixed_grad))
            moved = early.move(sent)
            second_grads, bias = attend_back(*qkv, mixed_grad, lines, at, 1, pairs, second_grads)
            second_grads, moved = together((second_grads, moved))
            early.take(moved)
            biases.append(bias)
        second_grads, returned, grad_experts = together((second_grads, returned, grad_experts))
        late = Summing(pack_sums(weight_grads(second_grads), jnp.concatenate(biases)))
        early.take(early.move(early.sends()))
        early_sums = early.finish()
        for step in range(late.steps):
            late.take(late.move(late.sends()))
        late.part, early_sums = together((late.part, early_sums))
        sums = [early_sums, late.finish()]
        norm_in_grad = 0.0
        low_parts = (first_grads, second_grads)
        for at, grads in enumerate(low_parts):
            span = slice(at * 128 * pairs, (at + 1) * 128 * pairs)
            for kind in range(3):
                norm_in_grad += jnp.einsum(
                    "xe,de->xd", grads[kind], projections[kind][:, span], preferred_element_type=jnp.float32
                )
        norm_in_grad = norm_in_grad.reshape(tokens.shape)
        grad_qkv = [
            jnp.concatenate(
                [matrix_of(sums[0], 2 + kind, model_width), matrix_of(sums[1], kind, model_width)], axis=1
            ).astype(jnp.float32)
            for kind in range(3)
        ]
        grad_w_output = jnp.concatenate([matrix_of(sums[0], side, model_width) for side in range(2)], axis=1)
        small = small_of(sums[0], 5 * model_width).reshape(-1, model_width)
        grad_bias = small_of(sums[1], 3 * model_width)
    else:
        query_grad, _, diag_grad, key_part, value_part = attend_back_rows(
            queries, keys, values, mixed_grad, log_totals, buckets, bias_table, DH
        )
        low_parts = [query_grad.astype(jnp.bfloat16)] + [
            lax.psum_scatter(part, "ctx", scatter_dimension=1, tiled=True).astype(jnp.bfloat16)
            for part in (key_part, value_part)
        ]
        norm_in_grad = sum(wide_dot_back(*pair) for pair in zip(low_parts, projections))
        sums = lax.psum(
            pack_sums([grad_w_output] + [weight_dot(attn_in, rows) for rows in low_parts], early_small),
            ("dp", "ctx", "expert"),
        )
        grad_bias = lax.psum(diag_grad, ("dp", "ctx", "expert"))
        grad_w_output, *grad_qkv = (matrix_of(sums, kind, model_width).astype(jnp.float32) for kind in range(4))
        small = small_of(sums, 4 * model_width)
    grad_bias = grad_bias[: bias_table.shape[1], : bias_table.shape[0]].T
    grad_norm1 = sum(jnp.sum(grad * weight.astype(jnp.float32), axis=1) for grad, weight in zip(grad_qkv, projections))
    grad_norm1 = grad_norm1 / norm1_gain
    grad_w_query, grad_w_key, grad_w_value = grad_qkv
    grad_w_output = grad_w_output.astype(jnp.float32)
    experts = router_weight.shape[1]
    grad_router, grad_norm2 = small[:experts, :].T, small[experts]
    returned = [piece.reshape(len(groups), -1, model_width) for piece in returned]
    block_out = [
        rows + place_rows(slot, [piece[at] for piece in returned])
        for at, (slot, rows) in enumerate(zip(slots, residual1))
    ]
    block_out = jnp.concatenate(block_out).astype(jnp.bfloat16)
    norm1_back, _ = norm_back(inputs, scale1, norm1_gain, norm_in_grad)
    d_tokens = residual_grad + norm1_back
    if whole_seq:
        block_out, d_tokens = trade(block_out), trade(d_tokens)
    grad_experts = grad_experts.astype(jnp.float32)
    return (
        block_out,
        d_tokens,
        grad_norm1,
        grad_w_query,
        grad_w_key,
        grad_w_value,
        grad_w_output,
        grad_bias,
        grad_norm2,
        grad_router,
        grad_experts[:, :model_width].T[None],
        grad_experts[:, model_width:][None],
    )


def solution(mesh):
    rows = P(("dp", "expert"), "ctx", None)
    in_specs = (rows, rows, P(("dp", "expert"), "ctx")) + (P(),) * 8 + (P("expert", None, None),) * 2
    out_specs = (rows, rows) + (P(),) * 8 + (P("expert", None, ("dp", "ctx")), P("expert", ("dp", "ctx"), None))
    return jax.shard_map(per_device, mesh=mesh, in_specs=in_specs, out_specs=out_specs, check_vma=False)
```

```python
import jax
import jax.numpy as jnp
import numpy as np
from jax import lax
from jax.experimental import pallas as pl
from jax.experimental.pallas import tpu as pltpu
from jax.sharding import PartitionSpec as P

DH = 64
QB = 256

bucket_edges = (1, 2, 3, 4, 5, 6, 7, 8, 12, 16, 23, 32, 46, 64, 91)
norm_eps = 1e-06
precise_result = lax.Precision.HIGHEST


def bucket_of(relative):
    distance = jnp.abs(relative)
    half_bucket = jnp.zeros(relative.shape, jnp.int32)
    for threshold in bucket_edges:
        half_bucket = half_bucket + (distance >= threshold).astype(jnp.int32)
    return half_bucket + 16 * (relative > 0).astype(jnp.int32)


def bucket_grid(row_start, row_count, col_count):
    row_pos = row_start + jnp.arange(row_count, dtype=jnp.int32)
    col_pos = jnp.arange(col_count, dtype=jnp.int32)
    return bucket_of(col_pos[None, :] - row_pos[:, None])


def bias_grid(buckets, table_column, bucket_count):
    result = jnp.zeros(buckets.shape, jnp.float32)
    for label in range(bucket_count):
        result = result + jnp.where(buckets == label, table_column[label], 0.0)
    return result


def fold_buckets(buckets, grad_sum, bucket_count):
    return jnp.stack(
        [jnp.sum(jnp.where(buckets == label, grad_sum, 0.0)) for label in range(bucket_count)]
    )


def head_slice(value_rows, head_index, head_size):
    return lax.dynamic_slice_in_dim(value_rows, head_index * head_size, head_size, 2)


def put_head(target, portion, head_index, head_size):
    return lax.dynamic_update_slice_in_dim(target, portion, head_index * head_size, 2)


def head_scores(q_head, k_head, buckets, bias_table, head_index):
    table_column = lax.dynamic_index_in_dim(bias_table, head_index, 1, keepdims=False)
    scores = jnp.einsum("sqd,skd->sqk", q_head, k_head, preferred_element_type=jnp.float32)
    return scores + bias_grid(buckets, table_column, bias_table.shape[0])[None]


def attend_rows(query_matrix, keys_whole, values_whole, buckets, bias_table, head_size):
    seq_count, row_count, feature_width = query_matrix.shape
    head_count = feature_width // head_size

    def one_head(head_index, running):
        attention_result, log_totals = running
        scores = head_scores(
            head_slice(query_matrix, head_index, head_size),
            head_slice(keys_whole, head_index, head_size),
            buckets,
            bias_table,
            head_index,
        )
        row_max = jnp.max(scores, axis=-1, keepdims=True)
        log_total = row_max + jnp.log(jnp.sum(jnp.exp(scores - row_max), axis=-1, keepdims=True))
        weights_low = jnp.exp(scores - log_total).astype(jnp.bfloat16)
        portion = jnp.einsum(
            "sqk,skd->sqd",
            weights_low,
            head_slice(values_whole, head_index, head_size),
            preferred_element_type=jnp.float32,
        )
        attention_result = put_head(attention_result, portion, head_index, head_size)
        log_totals = lax.dynamic_update_index_in_dim(log_totals, log_total[..., 0], head_index, 0)
        return (attention_result, log_totals)

    initial = (
        jnp.zeros((seq_count, row_count, feature_width), jnp.float32),
        jnp.zeros((head_count, seq_count, row_count), jnp.float32),
    )
    return lax.fori_loop(0, head_count, one_head, initial)


def attend_back_rows(
    query_matrix, keys_whole, values_whole, mixed_grad, log_totals, buckets, bias_table, head_size
):
    seq_count, row_count, feature_width = query_matrix.shape
    col_count = keys_whole.shape[1]
    head_count = feature_width // head_size
    bucket_count = bias_table.shape[0]

    def one_head(head_index, running):
        query_grad, deltas, diag_grad, key_part, value_part = running
        q_head = head_slice(query_matrix, head_index, head_size)
        k_head = head_slice(keys_whole, head_index, head_size)
        v_head = head_slice(values_whole, head_index, head_size)
        g_head = head_slice(mixed_grad, head_index, head_size)
        scores = head_scores(q_head, k_head, buckets, bias_table, head_index)
        weights = jnp.exp(scores - log_totals[head_index][..., None])
        weight_grad = jnp.einsum("sqd,skd->sqk", g_head, v_head, preferred_element_type=jnp.float32)
        delta_row = jnp.sum(weights * weight_grad, axis=-1)
        score_grad = (weights * (weight_grad - delta_row[..., None])).astype(jnp.bfloat16)
        query_grad = put_head(
            query_grad,
            jnp.einsum("sqk,skd->sqd", score_grad, k_head, preferred_element_type=jnp.float32),
            head_index,
            head_size,
        )
        deltas = lax.dynamic_update_index_in_dim(deltas, delta_row, head_index, 0)
        folded = fold_buckets(
            buckets, jnp.sum(score_grad.astype(jnp.float32), axis=0), bucket_count
        )
        diag_grad = lax.dynamic_update_index_in_dim(diag_grad, folded, head_index, 0)
        key_part = put_head(
            key_part,
            jnp.einsum("sqk,sqd->skd", score_grad, q_head, preferred_element_type=jnp.float32),
            head_index,
            head_size,
        )
        value_part = put_head(
            value_part,
            jnp.einsum(
                "sqk,sqd->skd",
                weights.astype(jnp.bfloat16),
                g_head,
                preferred_element_type=jnp.float32,
            ),
            head_index,
            head_size,
        )
        return (query_grad, deltas, diag_grad, key_part, value_part)

    key_shape = (seq_count, col_count, feature_width)
    initial = (
        jnp.zeros((seq_count, row_count, feature_width), jnp.float32),
        jnp.zeros((head_count, seq_count, row_count), jnp.float32),
        jnp.zeros((head_count, bucket_count), jnp.float32),
        jnp.zeros(key_shape, jnp.float32),
        jnp.zeros(key_shape, jnp.float32),
    )
    return lax.fori_loop(0, head_count, one_head, initial)


def bucket_np(relative):
    half_bucket = np.zeros(relative.shape, np.int32)
    for threshold in bucket_edges:
        half_bucket = half_bucket + (np.abs(relative) >= threshold)
    return half_bucket + 16 * (relative > 0)


def bias_lines(bias_table):
    lane = np.arange(4 * QB)
    both = np.stack([lane - 2 * QB, 2 * QB - lane])
    onehot = (bucket_np(both)[..., None] == np.arange(32)).astype(np.float32)
    return jnp.einsum("lcb,bh->hlc", jnp.asarray(onehot), bias_table, precision=lax.Precision.HIGHEST)

def fwd_kernel(first, lines_ref, q_ref, k_ref, v_ref, o_ref, band_ref):
    n = k_ref.shape[0] // QB
    lane = lax.broadcasted_iota(jnp.int32, (QB, 128), 1)
    for h in range(2):
        line = lines_ref[h, 0:1, :]
        spread = pltpu.roll(jnp.broadcast_to(line, (QB, 4 * QB)), 0, 1, stride=1, stride_axis=0)
        band_ref[h] = spread[:, QB:]
    for i in range(first, first + q_ref.shape[0] // QB):
        rows = slice((i - first) * QB, (i - first + 1) * QB)
        outs = []
        for h in range(2):
            low_bias = lines_ref[h, 0:1, 0:1]
            high_bias = lines_ref[h, 0:1, 4 * QB - 1:]
            q = jnp.where((lane < 64) == (h == 0), q_ref[rows, :], 0)
            s = lax.dot_general(q, k_ref[...], (((1,), (1,)), ((), ())), preferred_element_type=jnp.float32)
            parts = []
            for j in range(n):
                d = j - i
                b = band_ref[h, :, (d + 1) * QB:(d + 2) * QB] if abs(d) <= 1 else (low_bias if d < 0 else high_bias)
                parts.append(s[:, j * QB:(j + 1) * QB] + b)
            s = jnp.concatenate(parts, axis=1)
            m = jnp.max(s, axis=1, keepdims=True)
            p = jnp.exp(s - m)
            l = jnp.sum(p, axis=1, keepdims=True)
            o = jnp.dot(p.astype(jnp.bfloat16), v_ref[...], preferred_element_type=jnp.float32)
            outs.append(o * (1.0 / l))
        o_ref[rows, :] = jnp.where(lane < 64, outs[0], outs[1]).astype(jnp.bfloat16)

def attend(q, k, v, lines, first, count):
    length, width = q.shape
    col = pl.BlockSpec((length, 128), lambda h: (0, h))
    span = pl.BlockSpec((count, 128), lambda h: (first // count, h))
    return pl.pallas_call(
        lambda *refs: fwd_kernel(first // QB, *refs),
        grid=(width // 128,),
        in_specs=[pl.BlockSpec((2, 2, 4 * QB), lambda h: (h, 0, 0)), span, col, col],
        out_specs=pl.BlockSpec((count, 128), lambda h: (0, h)),
        out_shape=jax.ShapeDtypeStruct((count, width), jnp.bfloat16),
        scratch_shapes=[pltpu.VMEM((2, QB, 3 * QB), jnp.float32)],
        compiler_params=pltpu.CompilerParams(vmem_limit_bytes=48 << 20),
        cost_estimate=pl.CostEstimate(flops=count * length * width, bytes_accessed=2 * length * width, transcendentals=0),
        name="attend",
    )(lines, q, k, v)

def bwd_kernel(lines_ref, fold_ref, q_ref, k_ref, v_ref, g_ref, xt_ref, grad_ref, sums_ref, band_ref, acc_ref, far_acc, dk_acc, dv_acc):
    n = q_ref.shape[0] // QB
    lane = lax.broadcasted_iota(jnp.int32, (QB, 128), 1)
    for h in range(2):
        for t in range(3):
            start = 2 * QB - (t - 1) * QB - QB
            line = lines_ref[h, 1:2, start:start + 2 * QB]
            spread = pltpu.roll(jnp.broadcast_to(line, (QB, 2 * QB)), QB, 1, stride=1, stride_axis=0)
            band_ref[h, t * QB:(t + 1) * QB, :] = spread[:, :QB]
    acc_ref[...] = jnp.zeros_like(acc_ref)
    far_acc[...] = jnp.zeros_like(far_acc)
    for i in range(n):
        rows = slice(i * QB, (i + 1) * QB)
        grads = []
        for h in range(2):
            keep = (lane < 64) == (h == 0)
            low_bias = lines_ref[h, 0:1, 0:1]
            high_bias = lines_ref[h, 0:1, 4 * QB - 1:]
            q = jnp.where(keep, q_ref[rows, :], 0)
            g = jnp.where(keep, g_ref[rows, :], 0)
            s = lax.dot_general(k_ref[...], q, (((1,), (1,)), ((), ())), preferred_element_type=jnp.float32)
            parts = []
            for j in range(n):
                d = j - i
                b = band_ref[h, (d + 1) * QB:(d + 2) * QB, :] if abs(d) <= 1 else (low_bias if d < 0 else high_bias)
                parts.append(s[j * QB:(j + 1) * QB, :] + b)
            s = jnp.concatenate(parts, axis=0)
            m = jnp.max(s, axis=0, keepdims=True)
            p = jnp.exp(s - m)
            w = p * (1.0 / jnp.sum(p, axis=0, keepdims=True))
            dp = lax.dot_general(v_ref[...], g, (((1,), (1,)), ((), ())), preferred_element_type=jnp.float32)
            delta = jnp.sum(w * dp, axis=0, keepdims=True)
            ds = w * (dp - delta)
            for j in range(n):
                d = j - i
                tile = ds[j * QB:(j + 1) * QB, :]
                if abs(d) <= 1:
                    acc_ref[h, (d + 1) * QB:(d + 2) * QB, :] += tile
                else:
                    far_acc[h, 0 if d < 0 else 1] += jnp.sum(tile.reshape(QB // 8, 8, QB), axis=0)
            low = ds.astype(jnp.bfloat16)
            dv = jnp.dot(w.astype(jnp.bfloat16), g, preferred_element_type=jnp.float32)
            dk = jnp.dot(low, q, preferred_element_type=jnp.float32)
            if i == 0 and h == 0:
                dv_acc[...] = dv
                dk_acc[...] = dk
            else:
                dv_acc[...] += dv
                dk_acc[...] += dk
            grads.append(lax.dot_general(low, k_ref[...], (((0,), (0,)), ((), ())), preferred_element_type=jnp.float32))
        grad_ref[0, rows, :] = jnp.where(lane < 64, grads[0], grads[1]).astype(jnp.bfloat16)
    grad_ref[1] = dk_acc[...].astype(jnp.bfloat16)
    grad_ref[2] = dv_acc[...].astype(jnp.bfloat16)
    row = lax.broadcasted_iota(jnp.int32, (8, 2 * QB), 0)
    totals = []
    for h in range(2):
        total = jnp.zeros((8, 128), jnp.float32)
        for t in range(3):
            tile = acc_ref[h, t * QB:(t + 1) * QB, :]
            wide = jnp.concatenate([tile, jnp.zeros_like(tile)], axis=1)
            moved = sum(pltpu.roll(wide[8 * e:8 * e + 8], QB - 8 * e, 1) for e in range(QB // 8))
            turned = jnp.where(row == 0, moved, 0.0)
            for e in range(1, 8):
                turned = turned + pltpu.roll(jnp.where(row == e, moved, 0.0), 2 * QB - e, 1)
            total = total + jnp.dot(turned, fold_ref[t], precision=lax.Precision.HIGHEST, preferred_element_type=jnp.float32)
        total = jnp.sum(total, axis=0, keepdims=True)
        ends = [jnp.sum(jnp.sum(far_acc[h, side], axis=0, keepdims=True), axis=1, keepdims=True) for side in range(2)]
        column = lax.broadcasted_iota(jnp.int32, (1, 128), 1)
        total = total + jnp.where(column == 15, ends[0], 0.0) + jnp.where(column == 31, ends[1], 0.0)
        totals.append(total)
    width = xt_ref.shape[0]
    for kind in range(3):
        weight = jnp.dot(xt_ref[...], grad_ref[kind], preferred_element_type=jnp.float32)
        sums_ref[kind * width:(kind + 1) * width, :] = weight.astype(jnp.bfloat16)
    high = [total.astype(jnp.bfloat16).astype(jnp.float32) for total in totals]
    rows = high + [total - part for total, part in zip(totals, high)]
    small = jnp.concatenate(rows + [jnp.zeros((124, 128), jnp.float32)], axis=0)
    sums_ref[3 * width:, :] = small.astype(jnp.bfloat16)


def attend_back(q, k, v, g, xt, lines, first_pair, pairs, total_pairs, earlier=()):
    length, width = q.shape
    rows = 3 * width + 128
    r = (np.arange(3)[:, None] - 1) * QB - (np.arange(2 * QB)[None] - QB)
    fold = (bucket_np(r)[..., None] == np.arange(128)).astype(np.float32)
    col = pl.BlockSpec((length, 128), lambda h: (0, h + first_pair))
    offset = first_pair % total_pairs
    return pl.pallas_call(
        lambda *refs: bwd_kernel(*refs[:7], *refs[7 + len(earlier):]),
        grid=(pairs,),
        in_specs=[
            pl.BlockSpec((2, 2, 4 * QB), lambda h: (h + first_pair, 0, 0)),
            pl.BlockSpec((3, 2 * QB, 128), lambda h: (0, 0, 0)),
            col, col, col, col,
            pl.BlockSpec((width, length), lambda h: (0, 0), pipeline_mode=pl.Buffered(1)),
        ]
        + [pl.BlockSpec(memory_space=pl.ANY)] * len(earlier),
        out_specs=[
            pl.BlockSpec((3, length, 128), lambda h: (0, 0, h + offset)),
            pl.BlockSpec((rows, 128), lambda h: (0, h + offset)),
        ],
        out_shape=[
            jax.ShapeDtypeStruct((3, length, 128 * total_pairs), jnp.bfloat16),
            jax.ShapeDtypeStruct((rows, 128 * total_pairs), jnp.bfloat16),
        ],
        scratch_shapes=[
            pltpu.VMEM((2, 3 * QB, QB), jnp.float32),
            pltpu.VMEM((2, 3 * QB, QB), jnp.float32),
            pltpu.VMEM((2, 2, 8, QB), jnp.float32),
            pltpu.VMEM((length, 128), jnp.float32),
            pltpu.VMEM((length, 128), jnp.float32),
        ],
        compiler_params=pltpu.CompilerParams(vmem_limit_bytes=48 << 20),
        cost_estimate=pl.CostEstimate(
            flops=84 * length * length * 128 * pairs, bytes_accessed=14 * length * 128 * pairs, transcendentals=2 * length * length * pairs
        ),
        input_output_aliases={7: 0, 8: 1} if earlier else {},
        name="attend_back",
    )(lines, jnp.asarray(fold), q, k, v, g, xt, *earlier)


def expert_kernel(count, label_ref, *refs):
    x_refs, u_refs = refs[:count], refs[count : 2 * count]
    router_ref, win_ref, wout_ref = refs[2 * count : 2 * count + 3]
    rest = refs[len(refs) - 7 - 2 * count :]
    rows_refs, back_refs = rest[:count], rest[count : 2 * count]
    g_ref, hid_ref, pre_ref, drouter_ref, prob_ref, out_acc, back_acc = rest[2 * count :]
    step = pl.program_id(0)
    tile = x_refs[0].shape[0]
    lane = lax.broadcasted_iota(jnp.int32, (tile, 128), 1)
    own = lane == label_ref[0]
    spans = [slice(r * tile, (r + 1) * tile) for r in range(count)]

    @pl.when(step == 0)
    def _():
        for piece, rows in enumerate(spans):
            logits = jnp.dot(x_refs[piece][...], router_ref[...], preferred_element_type=jnp.float32)
            logits = jnp.where(lane < 4, logits, -jnp.inf)
            raised = jnp.exp(logits - jnp.max(logits, axis=1, keepdims=True))
            prob = raised / jnp.sum(raised, axis=1, keepdims=True)
            prob_ref[rows, :] = prob
            gate = jnp.sum(jnp.where(own, prob, 0.0), axis=1, keepdims=True)
            g_ref[rows, :] = (gate * u_refs[piece][...].astype(jnp.float32)).astype(jnp.bfloat16)
        out_acc[...] = jnp.zeros_like(out_acc)
        back_acc[...] = jnp.zeros_like(back_acc)

    for piece, rows in enumerate(spans):
        pre = jnp.dot(x_refs[piece][...], win_ref[...], preferred_element_type=jnp.float32)
        square = pre * pre
        turn = jnp.tanh(pre * (0.7978845608028654 + 0.035677408136300125 * square))
        half = 0.5 + 0.5 * turn
        hidden = (pre * half).astype(jnp.bfloat16)
        slope = half + pre * (half - half * half) * (1.5957691216057308 + 0.21406444881780074 * square)
        hid_ref[rows, :] = hidden
        out_acc[rows, :] += jnp.dot(hidden, wout_ref[...], preferred_element_type=jnp.float32)
        hidden_grad = lax.dot_general(g_ref[rows, :], wout_ref[...], (((1,), (1,)), ((), ())), preferred_element_type=jnp.float32)
        pre_grad = (hidden_grad * slope).astype(jnp.bfloat16)
        pre_ref[rows, :] = pre_grad
        back_acc[rows, :] += lax.dot_general(pre_grad, win_ref[...], (((1,), (1,)), ((), ())), preferred_element_type=jnp.float32)

    @pl.when(step == pl.num_programs(0) - 1)
    def _():
        total = jnp.zeros(drouter_ref.shape, jnp.float32)
        for piece, rows in enumerate(spans):
            prob = prob_ref[rows, :]
            gate = jnp.sum(jnp.where(own, prob, 0.0), axis=1, keepdims=True)
            out = out_acc[rows, :].astype(jnp.bfloat16).astype(jnp.float32)
            rows_refs[piece][...] = (gate * out).astype(jnp.bfloat16)
            gate_grad = jnp.sum(u_refs[piece][...].astype(jnp.float32) * out, axis=1, keepdims=True)
            logit_grad = prob * (jnp.where(own, gate_grad, 0.0) - gate * gate_grad)
            high = logit_grad.astype(jnp.bfloat16)
            low = (logit_grad - high.astype(jnp.float32)).astype(jnp.bfloat16)
            back = back_acc[rows, :].astype(jnp.bfloat16).astype(jnp.float32)
            for part in (high, low):
                back += lax.dot_general(part, router_ref[...], (((1,), (1,)), ((), ())), preferred_element_type=jnp.float32)
                total += lax.dot_general(x_refs[piece][...], part, (((0,), (0,)), ((), ())), preferred_element_type=jnp.float32)
            back_refs[piece][...] = back.astype(jnp.bfloat16)
        drouter_ref[...] = total


def run_expert(label, pieces, upstream_pieces, tile, upstream_part, router_wide, w_in, w_out, group, group_count, earlier, chunk=768):
    count, width = len(pieces), pieces[0].shape[1]
    rows, inner = count * tile, w_in.shape[1]
    once = pl.Buffered(1)
    piece = pl.BlockSpec((tile, width), lambda f, lab: (0, 0), pipeline_mode=once)
    inner_block = pl.BlockSpec((rows, chunk), lambda f, lab: (0, f))
    low = lambda *shape: jax.ShapeDtypeStruct(shape, jnp.bfloat16)
    outs = pl.pallas_call(
        lambda *refs: expert_kernel(count, *refs),
        grid_spec=pltpu.PrefetchScalarGridSpec(
            num_scalar_prefetch=1,
            grid=(inner // chunk,),
            in_specs=[piece] * count
            + [pl.BlockSpec((tile, width), lambda f, lab: (upstream_part, 0), pipeline_mode=once)] * count
            + [
                pl.BlockSpec((width, 128), lambda f, lab: (0, 0), pipeline_mode=once),
                pl.BlockSpec((width, chunk), lambda f, lab: (0, f)),
                pl.BlockSpec((chunk, width), lambda f, lab: (f, 0)),
            ]
            + [pl.BlockSpec(memory_space=pl.ANY)] * len(earlier),
            out_specs=[pl.BlockSpec((tile, width), lambda f, lab: (group, 0), pipeline_mode=once)] * count
            + [piece] * count
            + [
                pl.BlockSpec((rows, width), lambda f, lab: (0, 0), pipeline_mode=once),
                inner_block,
                inner_block,
                pl.BlockSpec((width, 128), lambda f, lab: (0, 0), pipeline_mode=once),
            ],
            scratch_shapes=[
                pltpu.VMEM((rows, 128), jnp.float32),
                pltpu.VMEM((rows, width), jnp.float32),
                pltpu.VMEM((rows, width), jnp.float32),
            ],
        ),
        out_shape=[low(group_count * tile, width)] * count
        + [low(tile, width)] * count
        + [low(rows, width), low(rows, inner), low(rows, inner), jax.ShapeDtypeStruct((width, 128), jnp.float32)],
        compiler_params=pltpu.CompilerParams(vmem_limit_bytes=48 << 20),
        cost_estimate=pl.CostEstimate(flops=16 * rows * width * inner, bytes_accessed=8 * width * inner, transcendentals=rows * inner),
        input_output_aliases={2 * count + 4 + at: at for at in range(len(earlier))},
        name="experts",
    )(label, *pieces, *upstream_pieces, router_wide, w_in, w_out, *earlier)
    return outs[:count], outs[count : 2 * count], outs[2 * count :]


def expert_grads_kernel(groups, count, *refs):
    x_refs, refs = refs[: groups * count], refs[groups * count :]
    g_refs, hid_refs, pre_refs = refs[:groups], refs[groups : 2 * groups], refs[2 * groups : 3 * groups]
    dw_ref, xt_ref, gt_ref = refs[3 * groups :]
    width = xt_ref.shape[0]
    rows = g_refs[0].shape[0]
    tile = rows // count

    @pl.when(pl.program_id(0) == 0)
    def _():
        for at in range(groups):
            gt_ref[:, at * rows : (at + 1) * rows] = g_refs[at][...].T
            for piece in range(count):
                start = at * rows + piece * tile
                xt_ref[:, start : start + tile] = x_refs[at * count + piece][...].T

    for side, (left, right) in enumerate(((xt_ref, pre_refs), (gt_ref, hid_refs))):
        total = sum(
            jnp.dot(left[:, at * rows : (at + 1) * rows], right[at][...], preferred_element_type=jnp.float32)
            for at in range(groups)
        )
        dw_ref[:, side * width : (side + 1) * width] = total.astype(jnp.bfloat16).T


def expert_grads(pieces, grads, hiddens, pre_grads, chunk=512):
    groups, count = len(grads), len(pieces) // len(grads)
    width, (rows, inner) = pieces[0].shape[1], hiddens[0].shape
    tile = rows // count
    once = pl.Buffered(1)
    inner_block = pl.BlockSpec((rows, chunk), lambda f: (0, f))
    return pl.pallas_call(
        lambda *refs: expert_grads_kernel(groups, count, *refs),
        grid=(inner // chunk,),
        in_specs=[pl.BlockSpec((tile, width), lambda f: (0, 0), pipeline_mode=once)] * (groups * count)
        + [pl.BlockSpec((rows, width), lambda f: (0, 0), pipeline_mode=once)] * groups
        + [inner_block] * (2 * groups),
        out_specs=pl.BlockSpec((chunk, 2 * width), lambda f: (f, 0)),
        out_shape=jax.ShapeDtypeStruct((inner, 2 * width), jnp.bfloat16),
        scratch_shapes=[pltpu.VMEM((width, groups * rows), jnp.bfloat16)] * 2,
        compiler_params=pltpu.CompilerParams(vmem_limit_bytes=48 << 20),
        cost_estimate=pl.CostEstimate(
            flops=6 * groups * rows * width * inner, bytes_accessed=4 * (groups * rows + width) * inner, transcendentals=0
        ),
        name="expert_grads",
    )(*pieces, *grads, *hiddens, *pre_grads)


def sort_matrix(slot, slots):
    row = lax.broadcasted_iota(jnp.int32, (slots, slot.shape[1]), 0)
    return (row == slot).astype(jnp.float32).astype(jnp.bfloat16)


def sort_into(piece_refs, block, slot, rows):
    capacity = slot.shape[1] // 2
    matrix = sort_matrix(slot, len(piece_refs) * capacity)
    moved = jnp.dot(matrix, rows, preferred_element_type=jnp.float32).astype(jnp.bfloat16)
    for turn, piece_ref in enumerate(piece_refs):
        piece_ref[block * capacity : (block + 1) * capacity, :] = moved[turn * capacity : (turn + 1) * capacity]


def norm_scale_rows(rows):
    return lax.rsqrt(jnp.mean(rows * rows, axis=-1, keepdims=True) + norm_eps)


def sort_kernel(owners, label_ref, routes_ref, rows_ref, *refs):
    piece_refs, slot_ref = refs[:owners], refs[owners]
    blocks, _, length = routes_ref.shape
    first = lax.broadcasted_iota(jnp.int32, (length, length), 0)
    second = lax.broadcasted_iota(jnp.int32, (length, length), 1)
    upto = (first <= second).astype(jnp.float32).astype(jnp.bfloat16)
    for block in range(blocks):
        routes = routes_ref[block]
        hits = (lax.broadcasted_iota(jnp.int32, (8, length), 0) == routes).astype(jnp.float32)
        counts = jnp.dot(hits.astype(jnp.bfloat16), upto, preferred_element_type=jnp.float32)
        place = jnp.sum(hits * counts, axis=0, keepdims=True).astype(jnp.int32) - 1
        turn = routes - label_ref[0]
        turn = jnp.where(turn < 0, turn + owners, turn)
        slot = turn * (length // 2) + place
        slot_ref[block] = slot
        sort_into(piece_refs, block, slot, rows_ref[block])


def one_step(shape):
    return pl.BlockSpec(shape, lambda step: (0,) * len(shape), pipeline_mode=pl.Buffered(1))


def sort_upstream(label, routes, rows, owners, part, parts):
    blocks, length, width = rows.shape
    count = blocks * length // 2
    *pieces, slots = pl.pallas_call(
        lambda *refs: sort_kernel(owners, *refs),
        grid=(1,),
        in_specs=[pl.BlockSpec(memory_space=pltpu.SMEM), one_step((blocks, 1, length)), one_step(rows.shape)],
        out_specs=[pl.BlockSpec((count, width), lambda step: (part, 0), pipeline_mode=pl.Buffered(1))] * owners
        + [one_step((blocks, 1, length))],
        out_shape=[jax.ShapeDtypeStruct((parts * count, width), jnp.bfloat16)] * owners
        + [jax.ShapeDtypeStruct((blocks, 1, length), jnp.int32)],
        compiler_params=pltpu.CompilerParams(vmem_limit_bytes=48 << 20),
        name="sort_upstream",
    )(label, routes.reshape(blocks, 1, length), rows)
    return pieces, slots


def after_attention_kernel(slot_ref, attended_ref, tokens_ref, weight_ref, gain_ref, residual_ref, *piece_refs):
    for block in range(slot_ref.shape[0]):
        mixed = jnp.dot(attended_ref[block], weight_ref[...], preferred_element_type=jnp.float32)
        residual = tokens_ref[block].astype(jnp.float32) + mixed
        residual_ref[block] = residual
        router_in = (residual * norm_scale_rows(residual) * gain_ref[...]).astype(jnp.bfloat16)
        sort_into(piece_refs, block, slot_ref[block], router_in)


def after_attention(slots, attended, tokens, weight, gain, owners, earlier):
    blocks, length, width = tokens.shape
    count = blocks * length // 2
    parts = 2 if earlier else 1
    residual, *pieces = pl.pallas_call(
        lambda *refs: after_attention_kernel(*refs[:5], *refs[5 + len(earlier) :]),
        grid=(1,),
        in_specs=[
            one_step(slots.shape), one_step(tokens.shape), one_step(tokens.shape), one_step(weight.shape), one_step((1, width))
        ]
        + [pl.BlockSpec(memory_space=pl.ANY)] * len(earlier),
        out_specs=[one_step(tokens.shape)] + [one_step((count, width))] * owners,
        out_shape=[jax.ShapeDtypeStruct(tokens.shape, jnp.float32)]
        + [jax.ShapeDtypeStruct((parts * count, width), jnp.bfloat16)] * owners,
        input_output_aliases={5 + at: 1 + at for at in range(len(earlier))},
        compiler_params=pltpu.CompilerParams(vmem_limit_bytes=48 << 20),
        name="after_attention",
    )(slots, attended, tokens, weight, gain[None], *earlier)
    return residual, pieces


def before_attention_kernel(owners, slot_ref, *refs):
    piece_refs = refs[:owners]
    residual_ref, upstream_ref, attended_ref, weight_ref, gain_ref = refs[owners : owners + 5]
    residual_grad_ref, mixed_grad_ref, weight_grad_ref, gain_grad_ref = refs[owners + 5 :]
    blocks, _, length = slot_ref.shape
    capacity = length // 2
    weight_grad, gain_grad = 0.0, 0.0
    for block in range(blocks):
        matrix = sort_matrix(slot_ref[block], owners * capacity)
        rows = jnp.concatenate([ref[block * capacity : (block + 1) * capacity, :] for ref in piece_refs])
        grad = lax.dot_general(matrix, rows, (((0,), (0,)), ((), ())), preferred_element_type=jnp.float32)
        residual = residual_ref[block]
        scale = norm_scale_rows(residual)
        normed = residual * scale
        scaled = grad * gain_ref[...]
        shrink = jnp.mean(scaled * normed, axis=-1, keepdims=True)
        gain_grad += jnp.sum(grad * normed, axis=0, keepdims=True)
        residual_grad = upstream_ref[block].astype(jnp.float32) + scale * (scaled - normed * shrink)
        residual_grad_ref[block] = residual_grad
        low = residual_grad.astype(jnp.bfloat16)
        mixed_grad = lax.dot_general(low, weight_ref[...], (((1,), (1,)), ((), ())), preferred_element_type=jnp.float32)
        mixed_grad_ref[block] = mixed_grad.astype(jnp.bfloat16)
        weight_grad += lax.dot_general(attended_ref[block], low, (((0,), (0,)), ((), ())), preferred_element_type=jnp.float32)
    weight_grad_ref[...] = weight_grad
    gain_grad_ref[...] = gain_grad


def before_attention(slots, pieces, residual, upstream, attended, weight, gain):
    width = residual.shape[2]
    vmem = pl.BlockSpec(memory_space=pltpu.VMEM)
    return pl.pallas_call(
        lambda *refs: before_attention_kernel(len(pieces), *refs),
        in_specs=[vmem] * (len(pieces) + 6),
        out_specs=[vmem] * 4,
        out_shape=[
            jax.ShapeDtypeStruct(residual.shape, jnp.float32),
            jax.ShapeDtypeStruct(residual.shape, jnp.bfloat16),
            jax.ShapeDtypeStruct((width, width), jnp.float32),
            jax.ShapeDtypeStruct((1, width), jnp.float32),
        ],
        compiler_params=pltpu.CompilerParams(vmem_limit_bytes=56 << 20),
        name="before_attention",
    )(slots, *pieces, residual, upstream, attended, weight, gain[None])


def exchange(pieces, axis, sign, size=None, skipped=0):
    size = size or lax.axis_size(axis)
    return [pieces[0]] + [
        lax.ppermute(piece, axis, [(at, (at + sign * turn) % size) for at in range(size)])
        for turn, piece in enumerate(pieces[1:], 1 + skipped)
    ]


def trade(blocks):
    at = lax.axis_index("ctx")
    mine = lax.dynamic_index_in_dim(blocks, at, 0, keepdims=False)
    other = lax.dynamic_index_in_dim(blocks, 1 - at, 0, keepdims=False)
    arrived = lax.ppermute(other, "ctx", [(0, 1), (1, 0)])
    return jnp.stack([jnp.where(at == 0, mine, arrived), jnp.where(at == 0, arrived, mine)])


def token_grads_kernel(first_ref, second_ref, *refs):
    weight_refs, (tokens_ref, residual_grad_ref, gain_ref, out_ref) = refs[:3], refs[3:]
    grad = 0.0
    for kind in range(3):
        low = jnp.concatenate([first_ref[kind], second_ref[kind]], axis=1)
        grad += lax.dot_general(low, weight_refs[kind][...], (((1,), (1,)), ((), ())), preferred_element_type=jnp.float32)
    rows = tokens_ref[...].astype(jnp.float32)
    scale = norm_scale_rows(rows)
    normed = rows * scale
    scaled = grad * gain_ref[...]
    shrink = jnp.mean(scaled * normed, axis=-1, keepdims=True)
    out_ref[...] = residual_grad_ref[...] + scale * (scaled - normed * shrink)


def token_grads(first, second, weights, tokens, residual_grad, gain):
    length, width = tokens.shape
    half = pl.BlockSpec((3, QB, width // 2), lambda step: (0, step, 0))
    rows = pl.BlockSpec((QB, width), lambda step: (step, 0))
    return pl.pallas_call(
        token_grads_kernel,
        grid=(length // QB,),
        in_specs=[half, half] + [one_step((width, width))] * 3 + [rows, rows, one_step((1, width))],
        out_specs=rows,
        out_shape=jax.ShapeDtypeStruct((length, width), jnp.float32),
        compiler_params=pltpu.CompilerParams(vmem_limit_bytes=48 << 20),
        cost_estimate=pl.CostEstimate(flops=6 * length * width * width, bytes_accessed=14 * length * width, transcendentals=0),
        name="token_grads",
    )(first, second, *weights, tokens, residual_grad, gain[None])


def layer_output_kernel(groups, owners, *refs):
    slot_refs, residual_refs = refs[:groups], refs[groups : 2 * groups]
    piece_refs, out_ref = refs[2 * groups : 2 * groups + owners], refs[-1]
    blocks, _, length = slot_refs[0].shape
    capacity = length // 2
    for group in range(groups):
        for block in range(blocks):
            at = group * blocks + block
            matrix = sort_matrix(slot_refs[group][block], owners * capacity)
            rows = jnp.concatenate([ref[at * capacity : (at + 1) * capacity, :] for ref in piece_refs])
            moved = lax.dot_general(matrix, rows, (((0,), (0,)), ((), ())), preferred_element_type=jnp.float32)
            out_ref[at] = (residual_refs[group][block] + moved).astype(jnp.bfloat16)


def layer_output(slots, residuals, pieces):
    blocks, length, width = residuals[0].shape
    vmem = pl.BlockSpec(memory_space=pltpu.VMEM)
    return pl.pallas_call(
        lambda *refs: layer_output_kernel(len(slots), len(pieces), *refs),
        in_specs=[vmem] * (2 * len(slots) + len(pieces)),
        out_specs=vmem,
        out_shape=jax.ShapeDtypeStruct((len(slots) * blocks, length, width), jnp.bfloat16),
        compiler_params=pltpu.CompilerParams(vmem_limit_bytes=48 << 20),
        name="layer_output",
    )(*slots, *residuals, *pieces)


def weight_outputs_kernel(first_ref, second_ref, *refs):
    weight_refs, gain_ref, out_refs, gain_grad_ref = refs[:3], refs[3], refs[4:7], refs[7]
    width = gain_ref.shape[1]
    half = width // 2
    total = 0.0
    for kind in range(3):
        for side, ref in enumerate((first_ref, second_ref)):
            columns = slice(side * half, (side + 1) * half)
            grad = ref[kind * width : (kind + 1) * width, :].astype(jnp.float32)
            out_refs[kind][:, columns] = grad
            total += jnp.sum(grad * weight_refs[kind][:, columns].astype(jnp.float32), axis=1, keepdims=True)
    total = jnp.broadcast_to(total, (width, 128)).T
    gain_grad_ref[...] = total[:1] / gain_ref[...]


def weight_outputs(first, second, weights, gain):
    width = gain.shape[0]
    vmem = pl.BlockSpec(memory_space=pltpu.VMEM)
    return pl.pallas_call(
        weight_outputs_kernel,
        in_specs=[vmem] * 6,
        out_specs=[vmem] * 4,
        out_shape=[jax.ShapeDtypeStruct((width, width), jnp.float32)] * 3 + [jax.ShapeDtypeStruct((1, width), jnp.float32)],
        compiler_params=pltpu.CompilerParams(vmem_limit_bytes=48 << 20),
        name="weight_outputs",
    )(first, second, *weights, gain[None])


def token_grads_kernel(first_ref, second_ref, *refs):
    weight_refs, (tokens_ref, residual_grad_ref, gain_ref, out_ref) = refs[:3], refs[3:]
    grad = 0.0
    for kind in range(3):
        low = jnp.concatenate([first_ref[kind], second_ref[kind]], axis=1)
        grad += lax.dot_general(low, weight_refs[kind][...], (((1,), (1,)), ((), ())), preferred_element_type=jnp.float32)
    rows = tokens_ref[...].astype(jnp.float32)
    scale = norm_scale_rows(rows)
    normed = rows * scale
    scaled = grad * gain_ref[...]
    shrink = jnp.mean(scaled * normed, axis=-1, keepdims=True)
    out_ref[...] = residual_grad_ref[...] + scale * (scaled - normed * shrink)


def token_grads(first, second, weights, tokens, residual_grad, gain):
    length, width = tokens.shape
    half = pl.BlockSpec((3, QB, width // 2), lambda step: (0, step, 0))
    rows = pl.BlockSpec((QB, width), lambda step: (step, 0))
    return pl.pallas_call(
        token_grads_kernel,
        grid=(length // QB,),
        in_specs=[half, half] + [one_step((width, width))] * 3 + [rows, rows, one_step((1, width))],
        out_specs=rows,
        out_shape=jax.ShapeDtypeStruct((length, width), jnp.float32),
        compiler_params=pltpu.CompilerParams(vmem_limit_bytes=48 << 20),
        cost_estimate=pl.CostEstimate(flops=6 * length * width * width, bytes_accessed=14 * length * width, transcendentals=0),
        name="token_grads",
    )(first, second, *weights, tokens, residual_grad, gain[None])


def place_rows(slots, pieces):
    blocks, _, length = slots.shape
    width = pieces[0].shape[-1]
    rows = jnp.stack(pieces).reshape(len(pieces), blocks, -1, width).swapaxes(0, 1).reshape(blocks, -1, width)
    places = jnp.arange(rows.shape[1], dtype=jnp.int32)
    matrix = (slots == places[None, :, None]).astype(jnp.bfloat16)
    return jnp.einsum("bsx,bsd->bxd", matrix, rows, preferred_element_type=jnp.float32)


def norm_scale(value_rows):
    return lax.rsqrt(jnp.mean(value_rows * value_rows, axis=-1, keepdims=True) + norm_eps)


def norm_back(value_rows, scale, gain_vector, grad_rows):
    scaled = grad_rows * gain_vector
    shrink = jnp.mean(scaled * value_rows, axis=-1, keepdims=True) * scale * scale * scale
    return scale * scaled - value_rows * shrink, jnp.sum(grad_rows * value_rows * scale, axis=(0, 1))


def wide_dot(rows, weight):
    return jnp.einsum("sxd,de->sxe", rows, weight, preferred_element_type=jnp.float32)


def wide_dot_back(rows, weight):
    return jnp.einsum("sxe,de->sxd", rows, weight, preferred_element_type=jnp.float32)


def weight_dot(left, right):
    return jnp.einsum("sxd,sxe->de", left, right, preferred_element_type=jnp.float32)


def pack_sums(matrices, small=None):
    parts = [matrix.astype(jnp.bfloat16) for matrix in matrices]
    if small is not None:
        small = jnp.pad(small, ((0, -small.shape[0] % 64), (0, parts[0].shape[1] - small.shape[1])))
        high = small.astype(jnp.bfloat16)
        parts += [high, (small - high.astype(jnp.float32)).astype(jnp.bfloat16)]
    return jnp.concatenate(parts)


def add_low(*parts):
    return sum(part.astype(jnp.float32) for part in parts).astype(jnp.bfloat16)


def swap(part, axis, turn):
    return lax.ppermute(part, axis, [(to, to ^ turn) for to in range(lax.axis_size(axis))])


class Summing:
    steps = 4

    def __init__(self, packed):
        self.core, self.plane = lax.axis_index("ctx"), lax.axis_index("dp")
        self.planes = lax.axis_size("dp")
        self.part = packed.reshape(self.planes, 2, -1, packed.shape[1])
        self.step = 0

    def sends(self):
        if self.step == 0:
            return [lax.dynamic_index_in_dim(self.part, 1 - self.core, 1, keepdims=False)]
        if self.step == 1:
            return [
                lax.dynamic_index_in_dim(self.part, self.plane ^ turn, 0, keepdims=False)
                for turn in range(1, self.planes)
            ]
        return [self.part]

    def move(self, sent):
        axis, first = (("ctx", 1), ("dp", 1), ("expert", 1), ("expert", 2))[self.step]
        return [swap(part, axis, first + at) for at, part in enumerate(sent)]

    def take(self, arrived):
        if self.step == 0:
            self.part = lax.dynamic_index_in_dim(self.part, self.core, 1, keepdims=False)
        elif self.step == 1:
            self.part = lax.dynamic_index_in_dim(self.part, self.plane, 0, keepdims=False)
        self.part = add_low(self.part, *arrived)
        self.step += 1

    def finish(self):
        return lax.all_gather(self.part, ("dp", "ctx"), axis=0, tiled=True)


def matrix_of(sums, index, rows):
    return sums[index * rows : (index + 1) * rows]


def small_of(sums, start):
    high, low = jnp.split(sums[start:].astype(jnp.float32), 2)
    return high + low


def per_device(
    tokens,
    cotangent,
    routes,
    norm1_gain,
    query_weight,
    key_weight,
    value_weight,
    output_weight,
    bias_table,
    norm2_gain,
    router_weight,
    w_in,
    w_out,
):
    seq_count, local_len, model_width = tokens.shape
    owners = lax.axis_size("expert")
    capacity = local_len // 2
    whole_seq = seq_count == 2 and lax.axis_size("ctx") == 2 and local_len % QB == 0
    if whole_seq:
        routes, cotangent, tokens = trade(routes), trade(cotangent), trade(tokens)
    groups = [slice(0, 1), slice(1, 2)] if whole_seq else [slice(0, seq_count)]
    label = lax.axis_index("expert").astype(jnp.int32).reshape(1)
    together = lax.optimization_barrier

    sorted_upstream, slots = zip(
        *[
            sort_upstream(label, routes[group], cotangent[group], owners, at, 1 + at)
            for at, group in enumerate(groups)
        ]
    )
    sorted_first, tokens = together((sorted_upstream[0], tokens))
    upstream = [exchange(sorted_first, "expert", 1)]
    inputs = tokens.astype(jnp.float32)
    scale1 = norm_scale(inputs)
    attn_in = (inputs * scale1 * norm1_gain).astype(jnp.bfloat16)
    queries = wide_dot(attn_in, query_weight).astype(jnp.bfloat16)
    keys = wide_dot(attn_in, key_weight).astype(jnp.bfloat16)
    values = wide_dot(attn_in, value_weight).astype(jnp.bfloat16)
    if whole_seq:
        lines = bias_lines(bias_table)
        flat = (seq_count * local_len, model_width)
        qkv = [rows.reshape(flat) for rows in (queries, keys, values)]
    else:
        first_pos = lax.axis_index("ctx") * local_len
        keys = lax.all_gather(keys, "ctx", axis=1, tiled=True)
        values = lax.all_gather(values, "ctx", axis=1, tiled=True)
        buckets = bucket_grid(first_pos, local_len, keys.shape[1])
        attended, log_totals = attend_rows(queries, keys, values, buckets, bias_table, DH)
    attended_groups, residual1, arrived = [], [], []
    in_flight, fed = upstream[0], queries.reshape(-1, model_width)
    for at, group in enumerate(groups):
        if whole_seq:
            rows = attend(fed, *qkv[1:], lines, at * local_len, local_len)[None]
        else:
            rows = attended.astype(jnp.bfloat16)
        rows, in_flight = together((rows, in_flight))
        if at == 0:
            upstream[0] = in_flight
        else:
            arrived[-1] = in_flight
        attended_groups.append(rows)
        earlier = sorted_upstream[at] if at else []
        residual, sorted_rows = after_attention(
            slots[at], rows, tokens[group], output_weight, norm2_gain, owners, earlier
        )
        residual1.append(residual)
        sorted_rows, fed = together((sorted_rows, fed))
        in_flight = exchange(sorted_rows, "expert", 1)
        arrived.append(in_flight)
    router_wide = jnp.pad(router_weight, ((0, 0), (0, 128 - router_weight.shape[1])))
    done, back = [], []
    upstream += arrived[1:]
    tile = seq_count // len(groups) * local_len // 2
    for at, (rows, grads) in enumerate(zip(arrived, upstream)):
        earlier = done[-1][0] if done else []
        result = run_expert(
            label, rows, grads, tile, min(at, 1), router_wide, w_in[0], w_out[0], at, len(groups), earlier
        )
        if back:
            result, back[-1] = together((result, back[-1]))
        done.append(result)
        back.append(exchange(result[1], "expert", -1))
    rows_out = done[-1][0]
    grad_rows, hiddens, pre_grads, grad_router = zip(*[item[2] for item in done])
    grad_router = sum(grad_router)[:, : router_weight.shape[1]].T
    grad_experts = expert_grads(sum(arrived, []), grad_rows, hiddens, pre_grads)
    grad_experts, back[-1], rows_out = together((grad_experts, back[-1], rows_out))
    grad_experts = lax.psum_scatter(grad_experts, ("dp", "ctx"), scatter_dimension=0, tiled=True)
    if not whole_seq:
        returned = exchange(list(rows_out), "expert", -1)
    residual_grad, mixed_grad, grad_w_output, grad_norm2 = zip(
        *[
            before_attention(slot, pieces, residual, cotangent[group], rows, output_weight, norm2_gain)
            for slot, pieces, residual, group, rows in zip(slots, back, residual1, groups, attended_groups)
        ]
    )
    residual_grad, mixed_grad = jnp.concatenate(residual_grad), jnp.concatenate(mixed_grad)
    grad_w_output, grad_norm2 = sum(grad_w_output), sum(grad_norm2)
    early_small = jnp.concatenate([grad_router, grad_norm2])
    projections = (query_weight, key_weight, value_weight)
    if whole_seq:
        half = model_width // 2
        pairs = half // 128
        mixed_grad = mixed_grad.reshape(flat)
        turned = attn_in.reshape(flat).T
        returned = exchange(list(rows_out[:-1]), "expert", -1, owners)
        first = attend_back(*qkv, mixed_grad, turned, lines, 0, pairs, pairs)
        first, returned, last_rows = together((first, returned, rows_out[-1]))
        returned.append(exchange([None, last_rows], "expert", -1, owners, owners - 2)[1])
        first_grads, first_sums = first
        matrices = [first_sums, grad_w_output[:, :half], grad_w_output[:, half:]]
        early = Summing(pack_sums(matrices, early_small.reshape(-1, half)))
        second = ()
        for at in range(pairs, 2 * pairs):
            sent, mixed_grad = together((early.sends(), mixed_grad))
            moved = early.move(sent)
            second = attend_back(*qkv, mixed_grad, turned, lines, at, 1, pairs, second)
            if at == pairs + 1:
                second, moved, returned = together((second, moved, returned))
            else:
                second, moved = together((second, moved))
            early.take(moved)
        (second_grads, second_sums), grad_experts = together((second, grad_experts))
        late = Summing(second_sums)
        sent, sent_late, returned = together((early.sends(), late.sends(), returned))
        moved, moved_late = early.move(sent), late.move(sent_late)
        block_out = layer_output(slots, residual1, returned)
        moved, moved_late, block_out = together((moved, moved_late, block_out))
        early.take(moved)
        late.take(moved_late)
        early_sums = early.finish()
        sent_late, second_grads = together((late.sends(), second_grads))
        moved_late = late.move(sent_late)
        d_tokens = token_grads(
            first_grads, second_grads, projections, tokens.reshape(flat), residual_grad.reshape(flat), norm1_gain
        ).reshape(tokens.shape)
        moved_late, d_tokens = together((moved_late, d_tokens))
        late.take(moved_late)
        for step in range(2):
            late.take(late.move(late.sends()))
        late.part, early_sums = together((late.part, early_sums))
        sums = [early_sums, late.finish()]
        *grad_qkv, grad_norm1 = weight_outputs(*sums, projections, norm1_gain)
        grad_norm1 = grad_norm1[0]
        start = 3 * model_width + 128
        grad_w_output = jnp.concatenate(
            [matrix_of(sums[0][start:], side, model_width) for side in range(2)], axis=1
        )
        small = small_of(sums[0], start + 2 * model_width).reshape(-1, model_width)
        grad_bias = jnp.concatenate([part[start - 128 : start - 124] for part in sums], axis=1).astype(jnp.float32)
        grad_bias = (grad_bias[:2] + grad_bias[2:]).reshape(2, -1, 128).swapaxes(0, 1).reshape(-1, 128)
    else:
        query_grad, _, diag_grad, key_part, value_part = attend_back_rows(
            queries, keys, values, mixed_grad, log_totals, buckets, bias_table, DH
        )
        low_parts = [query_grad.astype(jnp.bfloat16)] + [
            lax.psum_scatter(part, "ctx", scatter_dimension=1, tiled=True).astype(jnp.bfloat16)
            for part in (key_part, value_part)
        ]
        norm_in_grad = sum(wide_dot_back(*pair) for pair in zip(low_parts, projections))
        sums = lax.psum(
            pack_sums([grad_w_output] + [weight_dot(attn_in, rows) for rows in low_parts], early_small),
            ("dp", "ctx", "expert"),
        )
        grad_bias = lax.psum(diag_grad, ("dp", "ctx", "expert"))
        grad_w_output, *grad_qkv = (matrix_of(sums, kind, model_width).astype(jnp.float32) for kind in range(4))
        small = small_of(sums, 4 * model_width)
        norm1_back, grad_norm1 = norm_back(inputs, scale1, norm1_gain, norm_in_grad)
        grad_norm1 = lax.psum(grad_norm1, ("dp", "ctx", "expert"))
    grad_bias = grad_bias[: bias_table.shape[1], : bias_table.shape[0]].T
    grad_w_query, grad_w_key, grad_w_value = grad_qkv
    grad_w_output = grad_w_output.astype(jnp.float32)
    experts = router_weight.shape[1]
    grad_router, grad_norm2 = small[:experts, :].T, small[experts]
    if not whole_seq:
        block_out = layer_output(slots, residual1, returned)
        d_tokens = residual_grad + norm1_back
    if whole_seq:
        block_out, d_tokens = trade(block_out), trade(d_tokens)
    grad_experts = grad_experts.astype(jnp.float32)
    return (
        block_out,
        d_tokens,
        grad_norm1,
        grad_w_query,
        grad_w_key,
        grad_w_value,
        grad_w_output,
        grad_bias,
        grad_norm2,
        grad_router,
        grad_experts[:, :model_width].T[None],
        grad_experts[:, model_width:][None],
    )


def solution(mesh):
    rows = P(("dp", "expert"), "ctx", None)
    in_specs = (rows, rows, P(("dp", "expert"), "ctx")) + (P(),) * 8 + (P("expert", None, None),) * 2
    out_specs = (rows, rows) + (P(),) * 8 + (P("expert", None, ("dp", "ctx")), P("expert", ("dp", "ctx"), None))
    return jax.shard_map(per_device, mesh=mesh, in_specs=in_specs, out_specs=out_specs, check_vma=False)
```

```python
import jax
import jax.numpy as jnp
import numpy as np
from jax import lax
from jax.experimental import pallas as pl
from jax.experimental.pallas import tpu as pltpu
from jax.sharding import PartitionSpec as P

DH = 64
QB = 256

bucket_edges = (1, 2, 3, 4, 5, 6, 7, 8, 12, 16, 23, 32, 46, 64, 91)
norm_eps = 1e-06
precise_result = lax.Precision.HIGHEST


def bucket_of(relative):
    distance = jnp.abs(relative)
    half_bucket = jnp.zeros(relative.shape, jnp.int32)
    for threshold in bucket_edges:
        half_bucket = half_bucket + (distance >= threshold).astype(jnp.int32)
    return half_bucket + 16 * (relative > 0).astype(jnp.int32)


def bucket_grid(row_start, row_count, col_count):
    row_pos = row_start + jnp.arange(row_count, dtype=jnp.int32)
    col_pos = jnp.arange(col_count, dtype=jnp.int32)
    return bucket_of(col_pos[None, :] - row_pos[:, None])


def bias_grid(buckets, table_column, bucket_count):
    result = jnp.zeros(buckets.shape, jnp.float32)
    for label in range(bucket_count):
        result = result + jnp.where(buckets == label, table_column[label], 0.0)
    return result


def fold_buckets(buckets, grad_sum, bucket_count):
    return jnp.stack(
        [jnp.sum(jnp.where(buckets == label, grad_sum, 0.0)) for label in range(bucket_count)]
    )


def head_slice(value_rows, head_index, head_size):
    return lax.dynamic_slice_in_dim(value_rows, head_index * head_size, head_size, 2)


def put_head(target, portion, head_index, head_size):
    return lax.dynamic_update_slice_in_dim(target, portion, head_index * head_size, 2)


def head_scores(q_head, k_head, buckets, bias_table, head_index):
    table_column = lax.dynamic_index_in_dim(bias_table, head_index, 1, keepdims=False)
    scores = jnp.einsum("sqd,skd->sqk", q_head, k_head, preferred_element_type=jnp.float32)
    return scores + bias_grid(buckets, table_column, bias_table.shape[0])[None]


def attend_rows(query_matrix, keys_whole, values_whole, buckets, bias_table, head_size):
    seq_count, row_count, feature_width = query_matrix.shape
    head_count = feature_width // head_size

    def one_head(head_index, running):
        attention_result, log_totals = running
        scores = head_scores(
            head_slice(query_matrix, head_index, head_size),
            head_slice(keys_whole, head_index, head_size),
            buckets,
            bias_table,
            head_index,
        )
        row_max = jnp.max(scores, axis=-1, keepdims=True)
        log_total = row_max + jnp.log(jnp.sum(jnp.exp(scores - row_max), axis=-1, keepdims=True))
        weights_low = jnp.exp(scores - log_total).astype(jnp.bfloat16)
        portion = jnp.einsum(
            "sqk,skd->sqd",
            weights_low,
            head_slice(values_whole, head_index, head_size),
            preferred_element_type=jnp.float32,
        )
        attention_result = put_head(attention_result, portion, head_index, head_size)
        log_totals = lax.dynamic_update_index_in_dim(log_totals, log_total[..., 0], head_index, 0)
        return (attention_result, log_totals)

    initial = (
        jnp.zeros((seq_count, row_count, feature_width), jnp.float32),
        jnp.zeros((head_count, seq_count, row_count), jnp.float32),
    )
    return lax.fori_loop(0, head_count, one_head, initial)


def attend_back_rows(
    query_matrix, keys_whole, values_whole, mixed_grad, log_totals, buckets, bias_table, head_size
):
    seq_count, row_count, feature_width = query_matrix.shape
    col_count = keys_whole.shape[1]
    head_count = feature_width // head_size
    bucket_count = bias_table.shape[0]

    def one_head(head_index, running):
        query_grad, deltas, diag_grad, key_part, value_part = running
        q_head = head_slice(query_matrix, head_index, head_size)
        k_head = head_slice(keys_whole, head_index, head_size)
        v_head = head_slice(values_whole, head_index, head_size)
        g_head = head_slice(mixed_grad, head_index, head_size)
        scores = head_scores(q_head, k_head, buckets, bias_table, head_index)
        weights = jnp.exp(scores - log_totals[head_index][..., None])
        weight_grad = jnp.einsum("sqd,skd->sqk", g_head, v_head, preferred_element_type=jnp.float32)
        delta_row = jnp.sum(weights * weight_grad, axis=-1)
        score_grad = (weights * (weight_grad - delta_row[..., None])).astype(jnp.bfloat16)
        query_grad = put_head(
            query_grad,
            jnp.einsum("sqk,skd->sqd", score_grad, k_head, preferred_element_type=jnp.float32),
            head_index,
            head_size,
        )
        deltas = lax.dynamic_update_index_in_dim(deltas, delta_row, head_index, 0)
        folded = fold_buckets(
            buckets, jnp.sum(score_grad.astype(jnp.float32), axis=0), bucket_count
        )
        diag_grad = lax.dynamic_update_index_in_dim(diag_grad, folded, head_index, 0)
        key_part = put_head(
            key_part,
            jnp.einsum("sqk,sqd->skd", score_grad, q_head, preferred_element_type=jnp.float32),
            head_index,
            head_size,
        )
        value_part = put_head(
            value_part,
            jnp.einsum(
                "sqk,sqd->skd",
                weights.astype(jnp.bfloat16),
                g_head,
                preferred_element_type=jnp.float32,
            ),
            head_index,
            head_size,
        )
        return (query_grad, deltas, diag_grad, key_part, value_part)

    key_shape = (seq_count, col_count, feature_width)
    initial = (
        jnp.zeros((seq_count, row_count, feature_width), jnp.float32),
        jnp.zeros((head_count, seq_count, row_count), jnp.float32),
        jnp.zeros((head_count, bucket_count), jnp.float32),
        jnp.zeros(key_shape, jnp.float32),
        jnp.zeros(key_shape, jnp.float32),
    )
    return lax.fori_loop(0, head_count, one_head, initial)


def bucket_np(relative):
    half_bucket = np.zeros(relative.shape, np.int32)
    for threshold in bucket_edges:
        half_bucket = half_bucket + (np.abs(relative) >= threshold)
    return half_bucket + 16 * (relative > 0)


def bias_lines(bias_table):
    lane = np.arange(4 * QB)
    both = np.stack([lane - 2 * QB, 2 * QB - lane])
    onehot = (bucket_np(both)[..., None] == np.arange(32)).astype(np.float32)
    return jnp.einsum("lcb,bh->hlc", jnp.asarray(onehot), bias_table, precision=lax.Precision.HIGHEST)

def tile_index(i, j, n, core):
    half = n // 2
    if i // half == j // half:
        return max(-2, min(2, j - i)) + 2
    return jnp.clip(j - i - n * core * (1 if i < j else -1), -2, 2) + 2


def fwd_kernel(first, core_ref, lines_ref, q_ref, k_ref, v_ref, o_ref, total_ref, band_ref):
    n = k_ref.shape[0] // QB
    lane = lax.broadcasted_iota(jnp.int32, (QB, 128), 1)
    for h in range(2):
        line = lines_ref[h, 0:1, :]
        spread = pltpu.roll(jnp.broadcast_to(line, (QB, 4 * QB)), 0, 1, stride=1, stride_axis=0)
        band_ref[h, 0] = jnp.broadcast_to(line[:, :1], (QB, QB))
        for t in range(3):
            band_ref[h, 1 + t] = spread[:, (1 + t) * QB:(2 + t) * QB]
        band_ref[h, 4] = jnp.broadcast_to(line[:, 4 * QB - 1:], (QB, QB))
    for i in range(first, first + q_ref.shape[0] // QB):
        rows = slice((i - first) * QB, (i - first + 1) * QB)
        outs = []
        for h in range(2):
            q = jnp.where((lane < 64) == (h == 0), q_ref[rows, :], 0)
            s = lax.dot_general(q, k_ref[...], (((1,), (1,)), ((), ())), preferred_element_type=jnp.float32)
            parts = []
            for j in range(n):
                parts.append(s[:, j * QB:(j + 1) * QB] + band_ref[h, tile_index(i, j, n, core_ref[0])])
            s = jnp.concatenate(parts, axis=1)
            m = jnp.max(s, axis=1, keepdims=True)
            p = jnp.exp(s - m)
            l = jnp.sum(p, axis=1, keepdims=True)
            o = jnp.dot(p.astype(jnp.bfloat16), v_ref[...], preferred_element_type=jnp.float32)
            outs.append(o * (1.0 / l))
            total = jnp.broadcast_to(m + jnp.log(l), (QB, 128)).T
            total_ref[0, h:h + 1, rows] = total[:1]
        o_ref[rows, :] = jnp.where(lane < 64, outs[0], outs[1]).astype(jnp.bfloat16)

def attend(core, q, k, v, lines, first, count):
    length, width = q.shape
    col = pl.BlockSpec((length, 128), lambda h: (0, h))
    span = pl.BlockSpec((count, 128), lambda h: (first // count, h))
    return pl.pallas_call(
        lambda *refs: fwd_kernel(first // QB, *refs),
        grid=(width // 128,),
        in_specs=[pl.BlockSpec(memory_space=pltpu.SMEM), pl.BlockSpec((2, 2, 4 * QB), lambda h: (h, 0, 0)), span, col, col],
        out_specs=[pl.BlockSpec((count, 128), lambda h: (0, h)), pl.BlockSpec((1, 2, count), lambda h: (h, 0, 0))],
        out_shape=[
            jax.ShapeDtypeStruct((count, width), jnp.bfloat16),
            jax.ShapeDtypeStruct((width // 128, 2, count), jnp.float32),
        ],
        scratch_shapes=[pltpu.VMEM((2, 5, QB, QB), jnp.float32)],
        compiler_params=pltpu.CompilerParams(vmem_limit_bytes=48 << 20),
        cost_estimate=pl.CostEstimate(flops=count * length * width, bytes_accessed=2 * length * width, transcendentals=0),
        name="attend",
    )(core, lines, q, k, v)

def bwd_kernel(core_ref, lines_ref, fold_ref, q_ref, k_ref, v_ref, g_ref, o_ref, total_ref, xt_ref, grad_ref, sums_ref, band_ref, acc_ref, dk_acc, dv_acc):
    n = q_ref.shape[0] // QB
    lane = lax.broadcasted_iota(jnp.int32, (QB, 128), 1)
    for h in range(2):
        for t in range(3):
            start = 2 * QB - (t - 1) * QB - QB
            line = lines_ref[h, 1:2, start:start + 2 * QB]
            spread = pltpu.roll(jnp.broadcast_to(line, (QB, 2 * QB)), QB, 1, stride=1, stride_axis=0)
            band_ref[h, 1 + t] = spread[:, :QB]
        band_ref[h, 0] = jnp.broadcast_to(lines_ref[h, 0:1, 0:1], (QB, QB))
        band_ref[h, 4] = jnp.broadcast_to(lines_ref[h, 0:1, 4 * QB - 1:], (QB, QB))
    acc_ref[...] = jnp.zeros_like(acc_ref)
    for i in range(n):
        rows = slice(i * QB, (i + 1) * QB)
        grads = []
        for h in range(2):
            keep = (lane < 64) == (h == 0)
            q = jnp.where(keep, q_ref[rows, :], 0)
            g = jnp.where(keep, g_ref[rows, :], 0)
            s = lax.dot_general(k_ref[...], q, (((1,), (1,)), ((), ())), preferred_element_type=jnp.float32)
            parts = []
            for j in range(n):
                parts.append(s[j * QB:(j + 1) * QB, :] + band_ref[h, tile_index(i, j, n, core_ref[0])])
            s = jnp.concatenate(parts, axis=0)
            w = jnp.exp(s - total_ref[0, h:h + 1, rows])
            dp = lax.dot_general(v_ref[...], g, (((1,), (1,)), ((), ())), preferred_element_type=jnp.float32)
            delta = jnp.sum((g.astype(jnp.float32) * o_ref[rows, :].astype(jnp.float32)).T, axis=0, keepdims=True)
            ds = w * (dp - delta)
            for j in range(n):
                acc_ref[h, tile_index(i, j, n, core_ref[0])] += ds[j * QB:(j + 1) * QB, :]
            low = ds.astype(jnp.bfloat16)
            dv = jnp.dot(w.astype(jnp.bfloat16), g, preferred_element_type=jnp.float32)
            dk = jnp.dot(low, q, preferred_element_type=jnp.float32)
            if i == 0 and h == 0:
                dv_acc[...] = dv
                dk_acc[...] = dk
            else:
                dv_acc[...] += dv
                dk_acc[...] += dk
            grads.append(lax.dot_general(low, k_ref[...], (((0,), (0,)), ((), ())), preferred_element_type=jnp.float32))
        grad_ref[0, rows, :] = jnp.where(lane < 64, grads[0], grads[1]).astype(jnp.bfloat16)
    grad_ref[1] = dk_acc[...].astype(jnp.bfloat16)
    grad_ref[2] = dv_acc[...].astype(jnp.bfloat16)
    row = lax.broadcasted_iota(jnp.int32, (8, 2 * QB), 0)
    totals = []
    for h in range(2):
        total = jnp.zeros((8, 128), jnp.float32)
        for t in range(3):
            tile = acc_ref[h, 1 + t]
            wide = jnp.concatenate([tile, jnp.zeros_like(tile)], axis=1)
            moved = sum(pltpu.roll(wide[8 * e:8 * e + 8], QB - 8 * e, 1) for e in range(QB // 8))
            turned = jnp.where(row == 0, moved, 0.0)
            for e in range(1, 8):
                turned = turned + pltpu.roll(jnp.where(row == e, moved, 0.0), 2 * QB - e, 1)
            total = total + jnp.dot(turned, fold_ref[t], precision=lax.Precision.HIGHEST, preferred_element_type=jnp.float32)
        total = jnp.sum(total, axis=0, keepdims=True)
        ends = [jnp.sum(jnp.sum(acc_ref[h, side], axis=0, keepdims=True), axis=1, keepdims=True) for side in (0, 4)]
        column = lax.broadcasted_iota(jnp.int32, (1, 128), 1)
        total = total + jnp.where(column == 15, ends[0], 0.0) + jnp.where(column == 31, ends[1], 0.0)
        totals.append(total)
    width = xt_ref.shape[0]
    for kind in range(3):
        weight = jnp.dot(xt_ref[...], grad_ref[kind], preferred_element_type=jnp.float32)
        sums_ref[kind * width:(kind + 1) * width, :] = weight.astype(jnp.bfloat16)
    high = [total.astype(jnp.bfloat16).astype(jnp.float32) for total in totals]
    rows = high + [total - part for total, part in zip(totals, high)]
    small = jnp.concatenate(rows + [jnp.zeros((124, 128), jnp.float32)], axis=0)
    sums_ref[3 * width:, :] = small.astype(jnp.bfloat16)


def attend_back(core, q, k, v, g, o, totals, xt, lines, first_pair, pairs, total_pairs, earlier=()):
    length, width = q.shape
    rows = 3 * width + 128
    r = (np.arange(3)[:, None] - 1) * QB - (np.arange(2 * QB)[None] - QB)
    fold = (bucket_np(r)[..., None] == np.arange(128)).astype(np.float32)
    col = pl.BlockSpec((length, 128), lambda h: (0, h + first_pair))
    offset = first_pair % total_pairs
    return pl.pallas_call(
        lambda *refs: bwd_kernel(*refs[:10], *refs[10 + len(earlier):]),
        grid=(pairs,),
        in_specs=[
            pl.BlockSpec(memory_space=pltpu.SMEM),
            pl.BlockSpec((2, 2, 4 * QB), lambda h: (h + first_pair, 0, 0)),
            pl.BlockSpec((3, 2 * QB, 128), lambda h: (0, 0, 0)),
            col, col, col, col, col,
            pl.BlockSpec((1, 2, length), lambda h: (h + first_pair, 0, 0)),
            pl.BlockSpec((width, length), lambda h: (0, 0), pipeline_mode=pl.Buffered(1)),
        ]
        + [pl.BlockSpec(memory_space=pl.ANY)] * len(earlier),
        out_specs=[
            pl.BlockSpec((3, length, 128), lambda h: (0, 0, h + offset)),
            pl.BlockSpec((rows, 128), lambda h: (0, h + offset)),
        ],
        out_shape=[
            jax.ShapeDtypeStruct((3, length, 128 * total_pairs), jnp.bfloat16),
            jax.ShapeDtypeStruct((rows, 128 * total_pairs), jnp.bfloat16),
        ],
        scratch_shapes=[
            pltpu.VMEM((2, 5, QB, QB), jnp.float32),
            pltpu.VMEM((2, 5, QB, QB), jnp.float32),
            pltpu.VMEM((length, 128), jnp.float32),
            pltpu.VMEM((length, 128), jnp.float32),
        ],
        compiler_params=pltpu.CompilerParams(vmem_limit_bytes=48 << 20),
        cost_estimate=pl.CostEstimate(
            flops=84 * length * length * 128 * pairs, bytes_accessed=14 * length * 128 * pairs, transcendentals=2 * length * length * pairs
        ),
        input_output_aliases={10: 0, 11: 1} if earlier else {},
        name="attend_back",
    )(core, lines, jnp.asarray(fold), q, k, v, g, o, totals, xt, *earlier)


def expert_kernel(count, label_ref, *refs):
    x_refs, u_refs = refs[:count], refs[count : 2 * count]
    router_ref, win_ref, wout_ref = refs[2 * count : 2 * count + 3]
    rest = refs[len(refs) - 7 - 2 * count :]
    rows_refs, back_refs = rest[:count], rest[count : 2 * count]
    g_ref, hid_ref, pre_ref, drouter_ref, prob_ref, out_acc, back_acc = rest[2 * count :]
    step = pl.program_id(0)
    tile = x_refs[0].shape[0]
    lane = lax.broadcasted_iota(jnp.int32, (tile, 128), 1)
    own = lane == label_ref[0]
    spans = [slice(r * tile, (r + 1) * tile) for r in range(count)]

    @pl.when(step == 0)
    def _():
        for piece, rows in enumerate(spans):
            logits = jnp.dot(x_refs[piece][...], router_ref[...], preferred_element_type=jnp.float32)
            logits = jnp.where(lane < 4, logits, -jnp.inf)
            raised = jnp.exp(logits - jnp.max(logits, axis=1, keepdims=True))
            prob = raised / jnp.sum(raised, axis=1, keepdims=True)
            prob_ref[rows, :] = prob
            gate = jnp.sum(jnp.where(own, prob, 0.0), axis=1, keepdims=True)
            g_ref[rows, :] = (gate * u_refs[piece][...].astype(jnp.float32)).astype(jnp.bfloat16)
        out_acc[...] = jnp.zeros_like(out_acc)
        back_acc[...] = jnp.zeros_like(back_acc)

    for piece, rows in enumerate(spans):
        pre = jnp.dot(x_refs[piece][...], win_ref[...], preferred_element_type=jnp.float32)
        square = pre * pre
        turn = jnp.tanh(pre * (0.7978845608028654 + 0.035677408136300125 * square))
        half = 0.5 + 0.5 * turn
        hidden = (pre * half).astype(jnp.bfloat16)
        slope = half + pre * (half - half * half) * (1.5957691216057308 + 0.21406444881780074 * square)
        hid_ref[rows, :] = hidden
        out_acc[rows, :] += jnp.dot(hidden, wout_ref[...], preferred_element_type=jnp.float32)
        hidden_grad = lax.dot_general(g_ref[rows, :], wout_ref[...], (((1,), (1,)), ((), ())), preferred_element_type=jnp.float32)
        pre_grad = (hidden_grad * slope).astype(jnp.bfloat16)
        pre_ref[rows, :] = pre_grad
        back_acc[rows, :] += lax.dot_general(pre_grad, win_ref[...], (((1,), (1,)), ((), ())), preferred_element_type=jnp.float32)

    @pl.when(step == pl.num_programs(0) - 1)
    def _():
        total = jnp.zeros(drouter_ref.shape, jnp.float32)
        for piece, rows in enumerate(spans):
            prob = prob_ref[rows, :]
            gate = jnp.sum(jnp.where(own, prob, 0.0), axis=1, keepdims=True)
            out = out_acc[rows, :].astype(jnp.bfloat16).astype(jnp.float32)
            rows_refs[piece][...] = (gate * out).astype(jnp.bfloat16)
            gate_grad = jnp.sum(u_refs[piece][...].astype(jnp.float32) * out, axis=1, keepdims=True)
            logit_grad = prob * (jnp.where(own, gate_grad, 0.0) - gate * gate_grad)
            high = logit_grad.astype(jnp.bfloat16)
            low = (logit_grad - high.astype(jnp.float32)).astype(jnp.bfloat16)
            back = back_acc[rows, :].astype(jnp.bfloat16).astype(jnp.float32)
            for part in (high, low):
                back += lax.dot_general(part, router_ref[...], (((1,), (1,)), ((), ())), preferred_element_type=jnp.float32)
                total += lax.dot_general(x_refs[piece][...], part, (((0,), (0,)), ((), ())), preferred_element_type=jnp.float32)
            back_refs[piece][...] = back.astype(jnp.bfloat16)
        drouter_ref[...] = total


def run_expert(label, pieces, upstream_pieces, tile, upstream_part, router_wide, w_in, w_out, group, group_count, earlier, chunk=768):
    count, width = len(pieces), pieces[0].shape[1]
    rows, inner = count * tile, w_in.shape[1]
    once = pl.Buffered(1)
    piece = pl.BlockSpec((tile, width), lambda f, lab: (0, 0), pipeline_mode=once)
    inner_block = pl.BlockSpec((rows, chunk), lambda f, lab: (0, f))
    low = lambda *shape: jax.ShapeDtypeStruct(shape, jnp.bfloat16)
    outs = pl.pallas_call(
        lambda *refs: expert_kernel(count, *refs),
        grid_spec=pltpu.PrefetchScalarGridSpec(
            num_scalar_prefetch=1,
            grid=(inner // chunk,),
            in_specs=[piece] * count
            + [pl.BlockSpec((tile, width), lambda f, lab: (upstream_part, 0), pipeline_mode=once)] * count
            + [
                pl.BlockSpec((width, 128), lambda f, lab: (0, 0), pipeline_mode=once),
                pl.BlockSpec((width, chunk), lambda f, lab: (0, f)),
                pl.BlockSpec((chunk, width), lambda f, lab: (f, 0)),
            ]
            + [pl.BlockSpec(memory_space=pl.ANY)] * len(earlier),
            out_specs=[pl.BlockSpec((tile, width), lambda f, lab: (group, 0), pipeline_mode=once)] * count
            + [piece] * count
            + [
                pl.BlockSpec((rows, width), lambda f, lab: (0, 0), pipeline_mode=once),
                inner_block,
                inner_block,
                pl.BlockSpec((width, 128), lambda f, lab: (0, 0), pipeline_mode=once),
            ],
            scratch_shapes=[
                pltpu.VMEM((rows, 128), jnp.float32),
                pltpu.VMEM((rows, width), jnp.float32),
                pltpu.VMEM((rows, width), jnp.float32),
            ],
        ),
        out_shape=[low(group_count * tile, width)] * count
        + [low(tile, width)] * count
        + [low(rows, width), low(rows, inner), low(rows, inner), jax.ShapeDtypeStruct((width, 128), jnp.float32)],
        compiler_params=pltpu.CompilerParams(vmem_limit_bytes=48 << 20),
        cost_estimate=pl.CostEstimate(flops=16 * rows * width * inner, bytes_accessed=8 * width * inner, transcendentals=rows * inner),
        input_output_aliases={2 * count + 4 + at: at for at in range(len(earlier))},
        name="experts",
    )(label, *pieces, *upstream_pieces, router_wide, w_in, w_out, *earlier)
    return outs[:count], outs[count : 2 * count], outs[2 * count :]


def expert_grads_kernel(groups, count, *refs):
    x_refs, refs = refs[: groups * count], refs[groups * count :]
    g_refs, hid_refs, pre_refs = refs[:groups], refs[groups : 2 * groups], refs[2 * groups : 3 * groups]
    dw_ref, xt_ref, gt_ref = refs[3 * groups :]
    width = xt_ref.shape[0]
    rows = g_refs[0].shape[0]
    tile = rows // count

    @pl.when(pl.program_id(0) == 0)
    def _():
        for at in range(groups):
            gt_ref[:, at * rows : (at + 1) * rows] = g_refs[at][...].T
            for piece in range(count):
                start = at * rows + piece * tile
                xt_ref[:, start : start + tile] = x_refs[at * count + piece][...].T

    for side, (left, right) in enumerate(((xt_ref, pre_refs), (gt_ref, hid_refs))):
        total = sum(
            jnp.dot(left[:, at * rows : (at + 1) * rows], right[at][...], preferred_element_type=jnp.float32)
            for at in range(groups)
        )
        dw_ref[:, side * width : (side + 1) * width] = total.astype(jnp.bfloat16).T


def expert_grads(pieces, grads, hiddens, pre_grads, chunk=512):
    groups, count = len(grads), len(pieces) // len(grads)
    width, (rows, inner) = pieces[0].shape[1], hiddens[0].shape
    tile = rows // count
    once = pl.Buffered(1)
    inner_block = pl.BlockSpec((rows, chunk), lambda f: (0, f))
    return pl.pallas_call(
        lambda *refs: expert_grads_kernel(groups, count, *refs),
        grid=(inner // chunk,),
        in_specs=[pl.BlockSpec((tile, width), lambda f: (0, 0), pipeline_mode=once)] * (groups * count)
        + [pl.BlockSpec((rows, width), lambda f: (0, 0), pipeline_mode=once)] * groups
        + [inner_block] * (2 * groups),
        out_specs=pl.BlockSpec((chunk, 2 * width), lambda f: (f, 0)),
        out_shape=jax.ShapeDtypeStruct((inner, 2 * width), jnp.bfloat16),
        scratch_shapes=[pltpu.VMEM((width, groups * rows), jnp.bfloat16)] * 2,
        compiler_params=pltpu.CompilerParams(vmem_limit_bytes=48 << 20),
        cost_estimate=pl.CostEstimate(
            flops=6 * groups * rows * width * inner, bytes_accessed=4 * (groups * rows + width) * inner, transcendentals=0
        ),
        name="expert_grads",
    )(*pieces, *grads, *hiddens, *pre_grads)


def sort_matrix(slot, slots):
    row = lax.broadcasted_iota(jnp.int32, (slots, slot.shape[1]), 0)
    return (row == slot).astype(jnp.float32).astype(jnp.bfloat16)


def sort_into(piece_refs, block, slot, rows):
    capacity = slot.shape[1] // 2
    matrix = sort_matrix(slot, len(piece_refs) * capacity)
    moved = jnp.dot(matrix, rows, preferred_element_type=jnp.float32).astype(jnp.bfloat16)
    for turn, piece_ref in enumerate(piece_refs):
        piece_ref[block * capacity : (block + 1) * capacity, :] = moved[turn * capacity : (turn + 1) * capacity]


def norm_scale_rows(rows):
    return lax.rsqrt(jnp.mean(rows * rows, axis=-1, keepdims=True) + norm_eps)


def sort_kernel(owners, label_ref, routes_ref, rows_ref, *refs):
    piece_refs, slot_ref = refs[:owners], refs[owners]
    blocks, _, length = routes_ref.shape
    first = lax.broadcasted_iota(jnp.int32, (length, length), 0)
    second = lax.broadcasted_iota(jnp.int32, (length, length), 1)
    upto = (first <= second).astype(jnp.float32).astype(jnp.bfloat16)
    for block in range(blocks):
        routes = routes_ref[block]
        hits = (lax.broadcasted_iota(jnp.int32, (8, length), 0) == routes).astype(jnp.float32)
        counts = jnp.dot(hits.astype(jnp.bfloat16), upto, preferred_element_type=jnp.float32)
        place = jnp.sum(hits * counts, axis=0, keepdims=True).astype(jnp.int32) - 1
        turn = routes - label_ref[0]
        turn = jnp.where(turn < 0, turn + owners, turn)
        slot = turn * (length // 2) + place
        slot_ref[block] = slot
        sort_into(piece_refs, block, slot, rows_ref[block])


def one_step(shape):
    return pl.BlockSpec(shape, lambda step: (0,) * len(shape), pipeline_mode=pl.Buffered(1))


def sort_upstream(label, routes, rows, owners, part, parts):
    blocks, length, width = rows.shape
    count = blocks * length // 2
    *pieces, slots = pl.pallas_call(
        lambda *refs: sort_kernel(owners, *refs),
        grid=(1,),
        in_specs=[pl.BlockSpec(memory_space=pltpu.SMEM), one_step((blocks, 1, length)), one_step(rows.shape)],
        out_specs=[pl.BlockSpec((count, width), lambda step: (part, 0), pipeline_mode=pl.Buffered(1))] * owners
        + [one_step((blocks, 1, length))],
        out_shape=[jax.ShapeDtypeStruct((parts * count, width), jnp.bfloat16)] * owners
        + [jax.ShapeDtypeStruct((blocks, 1, length), jnp.int32)],
        compiler_params=pltpu.CompilerParams(vmem_limit_bytes=48 << 20),
        name="sort_upstream",
    )(label, routes.reshape(blocks, 1, length), rows)
    return pieces, slots


def after_attention_kernel(slot_ref, attended_ref, tokens_ref, weight_ref, gain_ref, residual_ref, *piece_refs):
    for block in range(slot_ref.shape[0]):
        mixed = jnp.dot(attended_ref[block], weight_ref[...], preferred_element_type=jnp.float32)
        residual = tokens_ref[block].astype(jnp.float32) + mixed
        residual_ref[block] = residual
        router_in = (residual * norm_scale_rows(residual) * gain_ref[...]).astype(jnp.bfloat16)
        sort_into(piece_refs, block, slot_ref[block], router_in)


def after_attention(slots, attended, tokens, weight, gain, owners, earlier):
    blocks, length, width = tokens.shape
    count = blocks * length // 2
    parts = 2 if earlier else 1
    residual, *pieces = pl.pallas_call(
        lambda *refs: after_attention_kernel(*refs[:5], *refs[5 + len(earlier) :]),
        grid=(1,),
        in_specs=[
            one_step(slots.shape), one_step(tokens.shape), one_step(tokens.shape), one_step(weight.shape), one_step((1, width))
        ]
        + [pl.BlockSpec(memory_space=pl.ANY)] * len(earlier),
        out_specs=[one_step(tokens.shape)] + [one_step((count, width))] * owners,
        out_shape=[jax.ShapeDtypeStruct(tokens.shape, jnp.float32)]
        + [jax.ShapeDtypeStruct((parts * count, width), jnp.bfloat16)] * owners,
        input_output_aliases={5 + at: 1 + at for at in range(len(earlier))},
        compiler_params=pltpu.CompilerParams(vmem_limit_bytes=48 << 20),
        name="after_attention",
    )(slots, attended, tokens, weight, gain[None], *earlier)
    return residual, pieces


def before_attention_kernel(owners, earlier, slot_ref, *refs):
    piece_refs = refs[:owners]
    residual_ref, upstream_ref, attended_ref, weight_ref, gain_ref = refs[owners : owners + 5]
    residual_grad_ref, mixed_grad_ref, weight_grad_ref, gain_grad_ref = refs[-4:]
    blocks, _, length = slot_ref.shape
    capacity = length // 2
    weight_grad, gain_grad = (refs[-6][...], refs[-5][...]) if earlier else (0.0, 0.0)
    for block in range(blocks):
        slot = jnp.broadcast_to(slot_ref[block].astype(jnp.float32), (128, length)).T[:, :1].astype(jnp.int32)
        place = lax.broadcasted_iota(jnp.int32, (length, owners * capacity), 1)
        matrix = (place == slot).astype(jnp.float32).astype(jnp.bfloat16)
        rows = jnp.concatenate([ref[block * capacity : (block + 1) * capacity, :] for ref in piece_refs])
        grad = jnp.dot(matrix, rows, preferred_element_type=jnp.float32)
        residual = residual_ref[block]
        scale = norm_scale_rows(residual)
        normed = residual * scale
        scaled = grad * gain_ref[...]
        shrink = jnp.mean(scaled * normed, axis=-1, keepdims=True)
        gain_grad += jnp.sum(grad * normed, axis=0, keepdims=True)
        residual_grad = upstream_ref[block].astype(jnp.float32) + scale * (scaled - normed * shrink)
        residual_grad_ref[block] = residual_grad
        low = residual_grad.astype(jnp.bfloat16)
        mixed_grad = lax.dot_general(low, weight_ref[...], (((1,), (1,)), ((), ())), preferred_element_type=jnp.float32)
        mixed_grad_ref[block] = mixed_grad.astype(jnp.bfloat16)
        weight_grad += lax.dot_general(attended_ref[block], low, (((0,), (0,)), ((), ())), preferred_element_type=jnp.float32)
    weight_grad_ref[...] = weight_grad
    gain_grad_ref[...] = gain_grad


def before_attention(slots, pieces, residual, upstream, attended, weight, gain, group, group_count, earlier):
    blocks, length, width = residual.shape
    owners = len(pieces)
    rows = one_step(residual.shape)
    out_rows = pl.BlockSpec(residual.shape, lambda step: (group, 0, 0), pipeline_mode=pl.Buffered(1))
    sums = [one_step((width, width)), one_step((1, width))]
    shape = (group_count * blocks, length, width)
    return pl.pallas_call(
        lambda *refs: before_attention_kernel(owners, bool(earlier), *refs),
        grid=(1,),
        in_specs=[one_step(slots.shape)] + [one_step(pieces[0].shape)] * owners
        + [rows, rows, rows, one_step((width, width)), one_step((1, width))]
        + ([pl.BlockSpec(memory_space=pl.ANY)] * 2 + sums if earlier else []),
        out_specs=[out_rows, out_rows] + sums,
        out_shape=[
            jax.ShapeDtypeStruct(shape, jnp.float32),
            jax.ShapeDtypeStruct(shape, jnp.bfloat16),
            jax.ShapeDtypeStruct((width, width), jnp.float32),
            jax.ShapeDtypeStruct((1, width), jnp.float32),
        ],
        input_output_aliases={owners + 6: 0, owners + 7: 1} if earlier else {},
        compiler_params=pltpu.CompilerParams(vmem_limit_bytes=56 << 20),
        name="before_attention",
    )(slots, *pieces, residual, upstream, attended, weight, gain[None], *earlier)


def exchange(pieces, axis, sign, size=None, skipped=0):
    size = size or lax.axis_size(axis)
    return [pieces[0]] + [
        lax.ppermute(piece, axis, [(at, (at + sign * turn) % size) for at in range(size)])
        for turn, piece in enumerate(pieces[1:], 1 + skipped)
    ]


def own_and_other(blocks):
    at = lax.axis_index("ctx")
    own = lax.dynamic_index_in_dim(blocks, at, 0)
    other = lax.dynamic_index_in_dim(blocks, 1 - at, 0)
    return [own, lax.ppermute(other, "ctx", [(0, 1), (1, 0)])]


def hand_back(own, other):
    at = lax.axis_index("ctx")
    arrived = lax.ppermute(other, "ctx", [(0, 1), (1, 0)])
    return jnp.concatenate([jnp.where(at == 0, own, arrived), jnp.where(at == 0, arrived, own)])


def layer_output_kernel(groups, owners, *refs):
    slot_refs, residual_refs = refs[:groups], refs[groups : 2 * groups]
    piece_refs = refs[2 * groups : 2 * groups + owners]
    blocks, _, length = slot_refs[0].shape
    capacity = length // 2
    for group in range(groups):
        for block in range(blocks):
            at = group * blocks + block
            matrix = sort_matrix(slot_refs[group][block], owners * capacity)
            rows = jnp.concatenate([ref[at * capacity : (at + 1) * capacity, :] for ref in piece_refs])
            moved = lax.dot_general(matrix, rows, (((0,), (0,)), ((), ())), preferred_element_type=jnp.float32)
            refs[len(refs) - groups + group][block] = (residual_refs[group][block] + moved).astype(jnp.bfloat16)


def layer_output(slots, residuals, pieces):
    blocks, length, width = residuals[0].shape
    vmem = pl.BlockSpec(memory_space=pltpu.VMEM)
    return pl.pallas_call(
        lambda *refs: layer_output_kernel(len(slots), len(pieces), *refs),
        in_specs=[vmem] * (2 * len(slots) + len(pieces)),
        out_specs=[vmem] * len(slots),
        out_shape=[jax.ShapeDtypeStruct((blocks, length, width), jnp.bfloat16)] * len(slots),
        compiler_params=pltpu.CompilerParams(vmem_limit_bytes=48 << 20),
        name="layer_output",
    )(*slots, *residuals, *pieces)


def weight_outputs_kernel(first_ref, second_ref, *refs):
    weight_refs, gain_ref, out_refs, gain_grad_ref = refs[:3], refs[3], refs[4:7], refs[7]
    width = gain_ref.shape[1]
    half = width // 2
    total = 0.0
    for kind in range(3):
        for side, ref in enumerate((first_ref, second_ref)):
            columns = slice(side * half, (side + 1) * half)
            grad = ref[kind * width : (kind + 1) * width, :].astype(jnp.float32)
            out_refs[kind][:, columns] = grad
            total += jnp.sum(grad * weight_refs[kind][:, columns].astype(jnp.float32), axis=1, keepdims=True)
    total = jnp.broadcast_to(total, (width, 128)).T
    gain_grad_ref[...] = total[:1] / gain_ref[...]


def weight_outputs(first, second, weights, gain):
    width = gain.shape[0]
    vmem = pl.BlockSpec(memory_space=pltpu.VMEM)
    return pl.pallas_call(
        weight_outputs_kernel,
        in_specs=[vmem] * 6,
        out_specs=[vmem] * 4,
        out_shape=[jax.ShapeDtypeStruct((width, width), jnp.float32)] * 3 + [jax.ShapeDtypeStruct((1, width), jnp.float32)],
        compiler_params=pltpu.CompilerParams(vmem_limit_bytes=48 << 20),
        name="weight_outputs",
    )(first, second, *weights, gain[None])


def token_grads_kernel(first_ref, second_ref, *refs):
    weight_refs, (tokens_ref, residual_grad_ref, gain_ref, out_ref) = refs[:3], refs[3:]
    grad = 0.0
    for kind in range(3):
        low = jnp.concatenate([first_ref[kind], second_ref[kind]], axis=1)
        grad += lax.dot_general(low, weight_refs[kind][...], (((1,), (1,)), ((), ())), preferred_element_type=jnp.float32)
    rows = tokens_ref[...].astype(jnp.float32)
    scale = norm_scale_rows(rows)
    normed = rows * scale
    scaled = grad * gain_ref[...]
    shrink = jnp.mean(scaled * normed, axis=-1, keepdims=True)
    out_ref[...] = residual_grad_ref[...] + scale * (scaled - normed * shrink)


def token_grads(first, second, weights, tokens, residual_grad, gain):
    length, width = tokens.shape
    half = pl.BlockSpec((3, QB, width // 2), lambda step: (0, step, 0))
    rows = pl.BlockSpec((QB, width), lambda step: (step, 0))
    return pl.pallas_call(
        token_grads_kernel,
        grid=(length // QB,),
        in_specs=[half, half] + [one_step((width, width))] * 3 + [rows, rows, one_step((1, width))],
        out_specs=rows,
        out_shape=jax.ShapeDtypeStruct((length, width), jnp.float32),
        compiler_params=pltpu.CompilerParams(vmem_limit_bytes=48 << 20),
        cost_estimate=pl.CostEstimate(flops=6 * length * width * width, bytes_accessed=14 * length * width, transcendentals=0),
        name="token_grads",
    )(first, second, *weights, tokens, residual_grad, gain[None])


def place_rows(slots, pieces):
    blocks, _, length = slots.shape
    width = pieces[0].shape[-1]
    rows = jnp.stack(pieces).reshape(len(pieces), blocks, -1, width).swapaxes(0, 1).reshape(blocks, -1, width)
    places = jnp.arange(rows.shape[1], dtype=jnp.int32)
    matrix = (slots == places[None, :, None]).astype(jnp.bfloat16)
    return jnp.einsum("bsx,bsd->bxd", matrix, rows, preferred_element_type=jnp.float32)


def norm_scale(value_rows):
    return lax.rsqrt(jnp.mean(value_rows * value_rows, axis=-1, keepdims=True) + norm_eps)


def norm_back(value_rows, scale, gain_vector, grad_rows):
    scaled = grad_rows * gain_vector
    shrink = jnp.mean(scaled * value_rows, axis=-1, keepdims=True) * scale * scale * scale
    return scale * scaled - value_rows * shrink, jnp.sum(grad_rows * value_rows * scale, axis=(0, 1))


def wide_dot(rows, weight):
    return jnp.einsum("sxd,de->sxe", rows, weight, preferred_element_type=jnp.float32)


def wide_dot_back(rows, weight):
    return jnp.einsum("sxe,de->sxd", rows, weight, preferred_element_type=jnp.float32)


def weight_dot(left, right):
    return jnp.einsum("sxd,sxe->de", left, right, preferred_element_type=jnp.float32)


def pack_sums(matrices, small=None):
    parts = [matrix.astype(jnp.bfloat16) for matrix in matrices]
    if small is not None:
        small = jnp.pad(small, ((0, -small.shape[0] % 64), (0, parts[0].shape[1] - small.shape[1])))
        high = small.astype(jnp.bfloat16)
        parts += [high, (small - high.astype(jnp.float32)).astype(jnp.bfloat16)]
    return jnp.concatenate(parts)


def add_low(*parts):
    return sum(part.astype(jnp.float32) for part in parts).astype(jnp.bfloat16)


def swap(part, axis, turn):
    return lax.ppermute(part, axis, [(to, to ^ turn) for to in range(lax.axis_size(axis))])


class Summing:
    steps = 4

    def __init__(self, packed):
        self.core, self.plane = lax.axis_index("ctx"), lax.axis_index("dp")
        self.planes = lax.axis_size("dp")
        self.part = packed.reshape(self.planes, 2, -1, packed.shape[1])
        self.step = 0

    def sends(self):
        if self.step == 0:
            return [lax.dynamic_index_in_dim(self.part, 1 - self.core, 1, keepdims=False)]
        if self.step == 1:
            return [
                lax.dynamic_index_in_dim(self.part, self.plane ^ turn, 0, keepdims=False)
                for turn in range(1, self.planes)
            ]
        return [self.part]

    def move(self, sent):
        axis, first = (("ctx", 1), ("dp", 1), ("expert", 1), ("expert", 2))[self.step]
        return [swap(part, axis, first + at) for at, part in enumerate(sent)]

    def take(self, arrived):
        if self.step == 0:
            self.part = lax.dynamic_index_in_dim(self.part, self.core, 1, keepdims=False)
        elif self.step == 1:
            self.part = lax.dynamic_index_in_dim(self.part, self.plane, 0, keepdims=False)
        self.part = add_low(self.part, *arrived)
        self.step += 1

    def finish(self):
        return lax.all_gather(self.part, ("dp", "ctx"), axis=0, tiled=True)


def matrix_of(sums, index, rows):
    return sums[index * rows : (index + 1) * rows]


def small_of(sums, start):
    high, low = jnp.split(sums[start:].astype(jnp.float32), 2)
    return high + low


def per_device(
    tokens,
    cotangent,
    routes,
    norm1_gain,
    query_weight,
    key_weight,
    value_weight,
    output_weight,
    bias_table,
    norm2_gain,
    router_weight,
    w_in,
    w_out,
):
    seq_count, local_len, model_width = tokens.shape
    owners = lax.axis_size("expert")
    capacity = local_len // 2
    whole_seq = seq_count == 2 and lax.axis_size("ctx") == 2 and local_len % QB == 0
    split = own_and_other if whole_seq else lambda blocks: [blocks]
    routes, cotangent, token_groups = split(routes), split(cotangent), split(tokens)
    groups = range(len(routes))
    core = lax.axis_index("ctx").astype(jnp.int32).reshape(1)
    label = lax.axis_index("expert").astype(jnp.int32).reshape(1)
    together = lax.optimization_barrier

    sorted_upstream, slots = zip(
        *[
            sort_upstream(label, routes[group], cotangent[group], owners, group, 1 + group)
            for group in groups
        ]
    )
    sorted_first, token_groups = together((sorted_upstream[0], token_groups))
    tokens = jnp.concatenate(token_groups)
    upstream = [exchange(sorted_first, "expert", 1)]
    inputs = tokens.astype(jnp.float32)
    scale1 = norm_scale(inputs)
    attn_in = (inputs * scale1 * norm1_gain).astype(jnp.bfloat16)
    queries = wide_dot(attn_in, query_weight).astype(jnp.bfloat16)
    keys = wide_dot(attn_in, key_weight).astype(jnp.bfloat16)
    values = wide_dot(attn_in, value_weight).astype(jnp.bfloat16)
    if whole_seq:
        lines = bias_lines(bias_table)
        flat = (seq_count * local_len, model_width)
        qkv = [rows.reshape(flat) for rows in (queries, keys, values)]
    else:
        first_pos = lax.axis_index("ctx") * local_len
        keys = lax.all_gather(keys, "ctx", axis=1, tiled=True)
        values = lax.all_gather(values, "ctx", axis=1, tiled=True)
        buckets = bucket_grid(first_pos, local_len, keys.shape[1])
        attended, log_totals = attend_rows(queries, keys, values, buckets, bias_table, DH)
    attended_groups, residual1, arrived = [], [], []
    if whole_seq:
        log_totals = []
    in_flight, fed = upstream[0], queries.reshape(-1, model_width)
    for at, group in enumerate(groups):
        if whole_seq:
            rows, totals = attend(core, fed, *qkv[1:], lines, at * local_len, local_len)
            rows = rows[None]
            log_totals.append(totals)
        else:
            rows = attended.astype(jnp.bfloat16)
        rows, in_flight = together((rows, in_flight))
        if at == 0:
            upstream[0] = in_flight
        else:
            arrived[-1] = in_flight
        attended_groups.append(rows)
        earlier = sorted_upstream[at] if at else []
        residual, sorted_rows = after_attention(
            slots[at], rows, token_groups[at], output_weight, norm2_gain, owners, earlier
        )
        residual1.append(residual)
        sorted_rows, fed = together((sorted_rows, fed))
        in_flight = exchange(sorted_rows, "expert", 1)
        arrived.append(in_flight)
    router_wide = jnp.pad(router_weight, ((0, 0), (0, 128 - router_weight.shape[1])))
    done, back = [], []
    tile = seq_count // len(groups) * local_len // 2
    for at in groups:
        rows, grads = arrived[at], upstream[0] if at == 0 else arrived[at]
        earlier = done[-1][0] if done else []
        result = run_expert(
            label, rows, grads, tile, min(at, 1), router_wide, w_in[0], w_out[0], at, len(groups), earlier
        )
        if back:
            result, back[-1] = together((result, back[-1]))
        if at + 1 < len(arrived):
            result, arrived[at + 1] = together((result, arrived[at + 1]))
        done.append(result)
        back.append(exchange(result[1], "expert", -1))
    rows_out = done[-1][0]
    grad_rows, hiddens, pre_grads, grad_router = zip(*[item[2] for item in done])
    grad_router = sum(grad_router)[:, : router_weight.shape[1]].T
    grad_experts = expert_grads(sum(arrived, []), grad_rows, hiddens, pre_grads)
    grad_experts, back[-1], rows_out = together((grad_experts, back[-1], rows_out))
    grad_experts = lax.psum_scatter(grad_experts, ("dp", "ctx"), scatter_dimension=0, tiled=True)
    if not whole_seq:
        returned = exchange(list(rows_out), "expert", -1)
    backward = ()
    for group in groups:
        backward = before_attention(
            slots[group], back[group], residual1[group], cotangent[group], attended_groups[group],
            output_weight, norm2_gain, group, len(groups), backward,
        )
    residual_grad, mixed_grad, grad_w_output, grad_norm2 = backward
    early_small = jnp.concatenate([grad_router, grad_norm2])
    projections = (query_weight, key_weight, value_weight)
    if whole_seq:
        half = model_width // 2
        pairs = half // 128
        mixed_grad = mixed_grad.reshape(flat)
        turned = attn_in.reshape(flat).T
        seen = (jnp.concatenate(attended_groups).reshape(flat), jnp.concatenate(log_totals, axis=2), turned)
        returned = exchange(list(rows_out[:-1]), "expert", -1, owners)
        first = attend_back(core, *qkv, mixed_grad, *seen, lines, 0, pairs, pairs)
        first, returned, last_rows = together((first, returned, rows_out[-1]))
        returned.append(exchange([None, last_rows], "expert", -1, owners, owners - 2)[1])
        first_grads, first_sums = first
        matrices = [first_sums, grad_w_output[:, :half], grad_w_output[:, half:]]
        early = Summing(pack_sums(matrices, early_small.reshape(-1, half)))
        second = ()
        for at in range(pairs, 2 * pairs):
            sent, mixed_grad = together((early.sends(), mixed_grad))
            moved = early.move(sent)
            second = attend_back(core, *qkv, mixed_grad, *seen, lines, at, 1, pairs, second)
            if at == pairs + 1:
                second, moved, returned = together((second, moved, returned))
            else:
                second, moved = together((second, moved))
            early.take(moved)
        (second_grads, second_sums), grad_experts = together((second, grad_experts))
        late = Summing(second_sums)
        sent, sent_late, returned = together((early.sends(), late.sends(), returned))
        moved, moved_late = early.move(sent), late.move(sent_late)
        block_out = layer_output(slots, residual1, returned)
        moved, moved_late, block_out = together((moved, moved_late, block_out))
        early.take(moved)
        late.take(moved_late)
        early_sums = early.finish()
        sent_late, second_grads = together((late.sends(), second_grads))
        moved_late = late.move(sent_late)
        d_tokens = token_grads(
            first_grads, second_grads, projections, tokens.reshape(flat), residual_grad.reshape(flat), norm1_gain
        ).reshape(tokens.shape)
        moved_late, d_tokens = together((moved_late, d_tokens))
        late.take(moved_late)
        for step in range(2):
            late.take(late.move(late.sends()))
        late.part, early_sums = together((late.part, early_sums))
        sums = [early_sums, late.finish()]
        *grad_qkv, grad_norm1 = weight_outputs(*sums, projections, norm1_gain)
        grad_norm1 = grad_norm1[0]
        start = 3 * model_width + 128
        grad_w_output = jnp.concatenate(
            [matrix_of(sums[0][start:], side, model_width) for side in range(2)], axis=1
        )
        small = small_of(sums[0], start + 2 * model_width).reshape(-1, model_width)
        grad_bias = jnp.concatenate([part[start - 128 : start - 124] for part in sums], axis=1).astype(jnp.float32)
        grad_bias = (grad_bias[:2] + grad_bias[2:]).reshape(2, -1, 128).swapaxes(0, 1).reshape(-1, 128)
    else:
        query_grad, _, diag_grad, key_part, value_part = attend_back_rows(
            queries, keys, values, mixed_grad, log_totals, buckets, bias_table, DH
        )
        low_parts = [query_grad.astype(jnp.bfloat16)] + [
            lax.psum_scatter(part, "ctx", scatter_dimension=1, tiled=True).astype(jnp.bfloat16)
            for part in (key_part, value_part)
        ]
        norm_in_grad = sum(wide_dot_back(*pair) for pair in zip(low_parts, projections))
        sums = lax.psum(
            pack_sums([grad_w_output] + [weight_dot(attn_in, rows) for rows in low_parts], early_small),
            ("dp", "ctx", "expert"),
        )
        grad_bias = lax.psum(diag_grad, ("dp", "ctx", "expert"))
        grad_w_output, *grad_qkv = (matrix_of(sums, kind, model_width).astype(jnp.float32) for kind in range(4))
        small = small_of(sums, 4 * model_width)
        norm1_back, grad_norm1 = norm_back(inputs, scale1, norm1_gain, norm_in_grad)
        grad_norm1 = lax.psum(grad_norm1, ("dp", "ctx", "expert"))
    grad_bias = grad_bias[: bias_table.shape[1], : bias_table.shape[0]].T
    grad_w_query, grad_w_key, grad_w_value = grad_qkv
    grad_w_output = grad_w_output.astype(jnp.float32)
    experts = router_weight.shape[1]
    grad_router, grad_norm2 = small[:experts, :].T, small[experts]
    if not whole_seq:
        block_out = layer_output(slots, residual1, returned)[0]
        d_tokens = residual_grad + norm1_back
    if whole_seq:
        block_out, d_tokens = hand_back(*block_out), hand_back(d_tokens[:1], d_tokens[1:])
    grad_experts = grad_experts.astype(jnp.float32)
    return (
        block_out,
        d_tokens,
        grad_norm1,
        grad_w_query,
        grad_w_key,
        grad_w_value,
        grad_w_output,
        grad_bias,
        grad_norm2,
        grad_router,
        grad_experts[:, :model_width].T[None],
        grad_experts[:, model_width:][None],
    )


def solution(mesh):
    rows = P(("dp", "expert"), "ctx", None)
    in_specs = (rows, rows, P(("dp", "expert"), "ctx")) + (P(),) * 8 + (P("expert", None, None),) * 2
    out_specs = (rows, rows) + (P(),) * 8 + (P("expert", None, ("dp", "ctx")), P("expert", ("dp", "ctx"), None))
    return jax.shard_map(per_device, mesh=mesh, in_specs=in_specs, out_specs=out_specs, check_vma=False)
```

```python
import jax
import jax.numpy as jnp
import numpy as np
from jax import lax
from jax.experimental import pallas as pl
from jax.experimental.pallas import tpu as pltpu
from jax.sharding import PartitionSpec as P

DH = 64
QB = 256

bucket_edges = (1, 2, 3, 4, 5, 6, 7, 8, 12, 16, 23, 32, 46, 64, 91)
norm_eps = 1e-06
precise_result = lax.Precision.HIGHEST


def bucket_of(relative):
    distance = jnp.abs(relative)
    half_bucket = jnp.zeros(relative.shape, jnp.int32)
    for threshold in bucket_edges:
        half_bucket = half_bucket + (distance >= threshold).astype(jnp.int32)
    return half_bucket + 16 * (relative > 0).astype(jnp.int32)


def bucket_grid(row_start, row_count, col_count):
    row_pos = row_start + jnp.arange(row_count, dtype=jnp.int32)
    col_pos = jnp.arange(col_count, dtype=jnp.int32)
    return bucket_of(col_pos[None, :] - row_pos[:, None])


def bias_grid(buckets, table_column, bucket_count):
    result = jnp.zeros(buckets.shape, jnp.float32)
    for label in range(bucket_count):
        result = result + jnp.where(buckets == label, table_column[label], 0.0)
    return result


def fold_buckets(buckets, grad_sum, bucket_count):
    return jnp.stack(
        [jnp.sum(jnp.where(buckets == label, grad_sum, 0.0)) for label in range(bucket_count)]
    )


def head_slice(value_rows, head_index, head_size):
    return lax.dynamic_slice_in_dim(value_rows, head_index * head_size, head_size, 2)


def put_head(target, portion, head_index, head_size):
    return lax.dynamic_update_slice_in_dim(target, portion, head_index * head_size, 2)


def head_scores(q_head, k_head, buckets, bias_table, head_index):
    table_column = lax.dynamic_index_in_dim(bias_table, head_index, 1, keepdims=False)
    scores = jnp.einsum("sqd,skd->sqk", q_head, k_head, preferred_element_type=jnp.float32)
    return scores + bias_grid(buckets, table_column, bias_table.shape[0])[None]


def attend_rows(query_matrix, keys_whole, values_whole, buckets, bias_table, head_size):
    seq_count, row_count, feature_width = query_matrix.shape
    head_count = feature_width // head_size

    def one_head(head_index, running):
        attention_result, log_totals = running
        scores = head_scores(
            head_slice(query_matrix, head_index, head_size),
            head_slice(keys_whole, head_index, head_size),
            buckets,
            bias_table,
            head_index,
        )
        row_max = jnp.max(scores, axis=-1, keepdims=True)
        log_total = row_max + jnp.log(jnp.sum(jnp.exp(scores - row_max), axis=-1, keepdims=True))
        weights_low = jnp.exp(scores - log_total).astype(jnp.bfloat16)
        portion = jnp.einsum(
            "sqk,skd->sqd",
            weights_low,
            head_slice(values_whole, head_index, head_size),
            preferred_element_type=jnp.float32,
        )
        attention_result = put_head(attention_result, portion, head_index, head_size)
        log_totals = lax.dynamic_update_index_in_dim(log_totals, log_total[..., 0], head_index, 0)
        return (attention_result, log_totals)

    initial = (
        jnp.zeros((seq_count, row_count, feature_width), jnp.float32),
        jnp.zeros((head_count, seq_count, row_count), jnp.float32),
    )
    return lax.fori_loop(0, head_count, one_head, initial)


def attend_back_rows(
    query_matrix, keys_whole, values_whole, mixed_grad, log_totals, buckets, bias_table, head_size
):
    seq_count, row_count, feature_width = query_matrix.shape
    col_count = keys_whole.shape[1]
    head_count = feature_width // head_size
    bucket_count = bias_table.shape[0]

    def one_head(head_index, running):
        query_grad, deltas, diag_grad, key_part, value_part = running
        q_head = head_slice(query_matrix, head_index, head_size)
        k_head = head_slice(keys_whole, head_index, head_size)
        v_head = head_slice(values_whole, head_index, head_size)
        g_head = head_slice(mixed_grad, head_index, head_size)
        scores = head_scores(q_head, k_head, buckets, bias_table, head_index)
        weights = jnp.exp(scores - log_totals[head_index][..., None])
        weight_grad = jnp.einsum("sqd,skd->sqk", g_head, v_head, preferred_element_type=jnp.float32)
        delta_row = jnp.sum(weights * weight_grad, axis=-1)
        score_grad = (weights * (weight_grad - delta_row[..., None])).astype(jnp.bfloat16)
        query_grad = put_head(
            query_grad,
            jnp.einsum("sqk,skd->sqd", score_grad, k_head, preferred_element_type=jnp.float32),
            head_index,
            head_size,
        )
        deltas = lax.dynamic_update_index_in_dim(deltas, delta_row, head_index, 0)
        folded = fold_buckets(
            buckets, jnp.sum(score_grad.astype(jnp.float32), axis=0), bucket_count
        )
        diag_grad = lax.dynamic_update_index_in_dim(diag_grad, folded, head_index, 0)
        key_part = put_head(
            key_part,
            jnp.einsum("sqk,sqd->skd", score_grad, q_head, preferred_element_type=jnp.float32),
            head_index,
            head_size,
        )
        value_part = put_head(
            value_part,
            jnp.einsum(
                "sqk,sqd->skd",
                weights.astype(jnp.bfloat16),
                g_head,
                preferred_element_type=jnp.float32,
            ),
            head_index,
            head_size,
        )
        return (query_grad, deltas, diag_grad, key_part, value_part)

    key_shape = (seq_count, col_count, feature_width)
    initial = (
        jnp.zeros((seq_count, row_count, feature_width), jnp.float32),
        jnp.zeros((head_count, seq_count, row_count), jnp.float32),
        jnp.zeros((head_count, bucket_count), jnp.float32),
        jnp.zeros(key_shape, jnp.float32),
        jnp.zeros(key_shape, jnp.float32),
    )
    return lax.fori_loop(0, head_count, one_head, initial)


def bucket_np(relative):
    half_bucket = np.zeros(relative.shape, np.int32)
    for threshold in bucket_edges:
        half_bucket = half_bucket + (np.abs(relative) >= threshold)
    return half_bucket + 16 * (relative > 0)


def bias_lines(bias_table):
    lane = np.arange(4 * QB)
    both = np.stack([lane - 2 * QB, 2 * QB - lane])
    onehot = (bucket_np(both)[..., None] == np.arange(32)).astype(np.float32)
    return jnp.einsum("lcb,bh->hlc", jnp.asarray(onehot), bias_table, precision=lax.Precision.HIGHEST)

def tile_index(i, j, n, core):
    half = n // 2
    if i // half == j // half:
        return max(-2, min(2, j - i)) + 2
    return jnp.clip(j - i - n * core * (1 if i < j else -1), -2, 2) + 2


def fwd_kernel(first, core_ref, lines_ref, q_ref, k_ref, v_ref, o_ref, total_ref, band_ref):
    n = k_ref.shape[0] // QB
    lane = lax.broadcasted_iota(jnp.int32, (QB, 128), 1)
    for h in range(2):
        line = lines_ref[h, 0:1, :]
        spread = pltpu.roll(jnp.broadcast_to(line, (QB, 4 * QB)), 0, 1, stride=1, stride_axis=0)
        band_ref[h, 0] = jnp.broadcast_to(line[:, :1], (QB, QB))
        for t in range(3):
            band_ref[h, 1 + t] = spread[:, (1 + t) * QB:(2 + t) * QB]
        band_ref[h, 4] = jnp.broadcast_to(line[:, 4 * QB - 1:], (QB, QB))
    for i in range(first, first + q_ref.shape[0] // QB):
        rows = slice((i - first) * QB, (i - first + 1) * QB)
        outs = []
        for h in range(2):
            q = jnp.where((lane < 64) == (h == 0), q_ref[rows, :], 0)
            s = lax.dot_general(q, k_ref[...], (((1,), (1,)), ((), ())), preferred_element_type=jnp.float32)
            parts = []
            for j in range(n):
                parts.append(s[:, j * QB:(j + 1) * QB] + band_ref[h, tile_index(i, j, n, core_ref[0])])
            s = jnp.concatenate(parts, axis=1)
            m = jnp.max(s, axis=1, keepdims=True)
            p = jnp.exp(s - m)
            l = jnp.sum(p, axis=1, keepdims=True)
            o = jnp.dot(p.astype(jnp.bfloat16), v_ref[...], preferred_element_type=jnp.float32)
            outs.append(o * (1.0 / l))
            total = jnp.broadcast_to(m + jnp.log(l), (QB, 128)).T
            total_ref[0, h:h + 1, rows] = total[:1]
        o_ref[rows, :] = jnp.where(lane < 64, outs[0], outs[1]).astype(jnp.bfloat16)

def attend(core, q, k, v, lines, first, count):
    length, width = q.shape
    col = pl.BlockSpec((length, 128), lambda h: (0, h))
    span = pl.BlockSpec((count, 128), lambda h: (first // count, h))
    return pl.pallas_call(
        lambda *refs: fwd_kernel(first // QB, *refs),
        grid=(width // 128,),
        in_specs=[pl.BlockSpec(memory_space=pltpu.SMEM), pl.BlockSpec((2, 2, 4 * QB), lambda h: (h, 0, 0)), span, col, col],
        out_specs=[pl.BlockSpec((count, 128), lambda h: (0, h)), pl.BlockSpec((1, 2, count), lambda h: (h, 0, 0))],
        out_shape=[
            jax.ShapeDtypeStruct((count, width), jnp.bfloat16),
            jax.ShapeDtypeStruct((width // 128, 2, count), jnp.float32),
        ],
        scratch_shapes=[pltpu.VMEM((2, 5, QB, QB), jnp.float32)],
        compiler_params=pltpu.CompilerParams(vmem_limit_bytes=48 << 20),
        cost_estimate=pl.CostEstimate(flops=count * length * width, bytes_accessed=2 * length * width, transcendentals=0),
        name="attend",
    )(core, lines, q, k, v)

def bwd_kernel(core_ref, lines_ref, fold_ref, q_ref, k_ref, v_ref, g_ref, o_ref, total_ref, xt_ref, grad_ref, sums_ref, band_ref, acc_ref, dk_acc, dv_acc):
    n = q_ref.shape[0] // QB
    lane = lax.broadcasted_iota(jnp.int32, (QB, 128), 1)
    for h in range(2):
        for t in range(3):
            start = 2 * QB - (t - 1) * QB - QB
            line = lines_ref[h, 1:2, start:start + 2 * QB]
            spread = pltpu.roll(jnp.broadcast_to(line, (QB, 2 * QB)), QB, 1, stride=1, stride_axis=0)
            band_ref[h, 1 + t] = spread[:, :QB]
        band_ref[h, 0] = jnp.broadcast_to(lines_ref[h, 0:1, 0:1], (QB, QB))
        band_ref[h, 4] = jnp.broadcast_to(lines_ref[h, 0:1, 4 * QB - 1:], (QB, QB))
    acc_ref[...] = jnp.zeros_like(acc_ref)
    for i in range(n):
        rows = slice(i * QB, (i + 1) * QB)
        grads = []
        for h in range(2):
            keep = (lane < 64) == (h == 0)
            q = jnp.where(keep, q_ref[rows, :], 0)
            g = jnp.where(keep, g_ref[rows, :], 0)
            s = lax.dot_general(k_ref[...], q, (((1,), (1,)), ((), ())), preferred_element_type=jnp.float32)
            parts = []
            for j in range(n):
                parts.append(s[j * QB:(j + 1) * QB, :] + band_ref[h, tile_index(i, j, n, core_ref[0])])
            s = jnp.concatenate(parts, axis=0)
            w = jnp.exp(s - total_ref[0, h:h + 1, rows])
            dp = lax.dot_general(v_ref[...], g, (((1,), (1,)), ((), ())), preferred_element_type=jnp.float32)
            delta = jnp.sum((g.astype(jnp.float32) * o_ref[rows, :].astype(jnp.float32)).T, axis=0, keepdims=True)
            ds = w * (dp - delta)
            for j in range(n):
                acc_ref[h, tile_index(i, j, n, core_ref[0])] += ds[j * QB:(j + 1) * QB, :]
            low = ds.astype(jnp.bfloat16)
            dv = jnp.dot(w.astype(jnp.bfloat16), g, preferred_element_type=jnp.float32)
            dk = jnp.dot(low, q, preferred_element_type=jnp.float32)
            if i == 0 and h == 0:
                dv_acc[...] = dv
                dk_acc[...] = dk
            else:
                dv_acc[...] += dv
                dk_acc[...] += dk
            grads.append(lax.dot_general(low, k_ref[...], (((0,), (0,)), ((), ())), preferred_element_type=jnp.float32))
        grad_ref[0, rows, :] = jnp.where(lane < 64, grads[0], grads[1]).astype(jnp.bfloat16)
    grad_ref[1] = dk_acc[...].astype(jnp.bfloat16)
    grad_ref[2] = dv_acc[...].astype(jnp.bfloat16)
    row = lax.broadcasted_iota(jnp.int32, (8, 2 * QB), 0)
    totals = []
    for h in range(2):
        total = jnp.zeros((8, 128), jnp.float32)
        for t in range(3):
            tile = acc_ref[h, 1 + t]
            wide = jnp.concatenate([tile, jnp.zeros_like(tile)], axis=1)
            moved = sum(pltpu.roll(wide[8 * e:8 * e + 8], QB - 8 * e, 1) for e in range(QB // 8))
            turned = jnp.where(row == 0, moved, 0.0)
            for e in range(1, 8):
                turned = turned + pltpu.roll(jnp.where(row == e, moved, 0.0), 2 * QB - e, 1)
            total = total + jnp.dot(turned, fold_ref[t], precision=lax.Precision.HIGHEST, preferred_element_type=jnp.float32)
        total = jnp.sum(total, axis=0, keepdims=True)
        ends = [jnp.sum(jnp.sum(acc_ref[h, side], axis=0, keepdims=True), axis=1, keepdims=True) for side in (0, 4)]
        column = lax.broadcasted_iota(jnp.int32, (1, 128), 1)
        total = total + jnp.where(column == 15, ends[0], 0.0) + jnp.where(column == 31, ends[1], 0.0)
        totals.append(total)
    width = xt_ref.shape[0]
    grads = jnp.concatenate([grad_ref[kind] for kind in range(3)], axis=1)
    weight = jnp.dot(xt_ref[...], grads, preferred_element_type=jnp.float32).astype(jnp.bfloat16)
    for kind in range(3):
        sums_ref[kind * width:(kind + 1) * width, :] = weight[:, kind * 128:(kind + 1) * 128]
    high = [total.astype(jnp.bfloat16).astype(jnp.float32) for total in totals]
    rows = high + [total - part for total, part in zip(totals, high)]
    small = jnp.concatenate(rows + [jnp.zeros((124, 128), jnp.float32)], axis=0)
    sums_ref[3 * width:, :] = small.astype(jnp.bfloat16)


def attend_back(core, q, k, v, g, o, totals, xt, lines, first_pair, pairs, total_pairs, earlier=()):
    length, width = q.shape
    rows = 3 * width + 128
    r = (np.arange(3)[:, None] - 1) * QB - (np.arange(2 * QB)[None] - QB)
    fold = (bucket_np(r)[..., None] == np.arange(128)).astype(np.float32)
    col = pl.BlockSpec((length, 128), lambda h: (0, h + first_pair))
    offset = first_pair % total_pairs
    return pl.pallas_call(
        lambda *refs: bwd_kernel(*refs[:10], *refs[10 + len(earlier):]),
        grid=(pairs,),
        in_specs=[
            pl.BlockSpec(memory_space=pltpu.SMEM),
            pl.BlockSpec((2, 2, 4 * QB), lambda h: (h + first_pair, 0, 0)),
            pl.BlockSpec((3, 2 * QB, 128), lambda h: (0, 0, 0)),
            col, col, col, col, col,
            pl.BlockSpec((1, 2, length), lambda h: (h + first_pair, 0, 0)),
            pl.BlockSpec((width, length), lambda h: (0, 0), pipeline_mode=pl.Buffered(1)),
        ]
        + [pl.BlockSpec(memory_space=pl.ANY)] * len(earlier),
        out_specs=[
            pl.BlockSpec((3, length, 128), lambda h: (0, 0, h + offset)),
            pl.BlockSpec((rows, 128), lambda h: (0, h + offset)),
        ],
        out_shape=[
            jax.ShapeDtypeStruct((3, length, 128 * total_pairs), jnp.bfloat16),
            jax.ShapeDtypeStruct((rows, 128 * total_pairs), jnp.bfloat16),
        ],
        scratch_shapes=[
            pltpu.VMEM((2, 5, QB, QB), jnp.float32),
            pltpu.VMEM((2, 5, QB, QB), jnp.float32),
            pltpu.VMEM((length, 128), jnp.float32),
            pltpu.VMEM((length, 128), jnp.float32),
        ],
        compiler_params=pltpu.CompilerParams(vmem_limit_bytes=48 << 20),
        cost_estimate=pl.CostEstimate(
            flops=84 * length * length * 128 * pairs, bytes_accessed=14 * length * 128 * pairs, transcendentals=2 * length * length * pairs
        ),
        input_output_aliases={10: 0, 11: 1} if earlier else {},
        name="attend_back",
    )(core, lines, jnp.asarray(fold), q, k, v, g, o, totals, xt, *earlier)


def expert_kernel(count, label_ref, *refs):
    x_refs, u_refs = refs[:count], refs[count : 2 * count]
    router_ref, win_ref, wout_ref = refs[2 * count : 2 * count + 3]
    rest = refs[len(refs) - 7 - 2 * count :]
    rows_refs, back_refs = rest[:count], rest[count : 2 * count]
    g_ref, hid_ref, pre_ref, drouter_ref, prob_ref, out_acc, back_acc = rest[2 * count :]
    step = pl.program_id(0)
    tile = x_refs[0].shape[0]
    lane = lax.broadcasted_iota(jnp.int32, (tile, 128), 1)
    own = lane == label_ref[0]
    spans = [slice(r * tile, (r + 1) * tile) for r in range(count)]

    @pl.when(step == 0)
    def _():
        for piece, rows in enumerate(spans):
            logits = jnp.dot(x_refs[piece][...], router_ref[...], preferred_element_type=jnp.float32)
            logits = jnp.where(lane < 4, logits, -jnp.inf)
            raised = jnp.exp(logits - jnp.max(logits, axis=1, keepdims=True))
            prob = raised / jnp.sum(raised, axis=1, keepdims=True)
            prob_ref[rows, :] = prob
            gate = jnp.sum(jnp.where(own, prob, 0.0), axis=1, keepdims=True)
            g_ref[rows, :] = (gate * u_refs[piece][...].astype(jnp.float32)).astype(jnp.bfloat16)
        out_acc[...] = jnp.zeros_like(out_acc)
        back_acc[...] = jnp.zeros_like(back_acc)

    for piece, rows in enumerate(spans):
        pre = jnp.dot(x_refs[piece][...], win_ref[...], preferred_element_type=jnp.float32)
        square = pre * pre
        turn = jnp.tanh(pre * (0.7978845608028654 + 0.035677408136300125 * square))
        half = 0.5 + 0.5 * turn
        hidden = (pre * half).astype(jnp.bfloat16)
        slope = half + pre * (half - half * half) * (1.5957691216057308 + 0.21406444881780074 * square)
        hid_ref[rows, :] = hidden
        out_acc[rows, :] += jnp.dot(hidden, wout_ref[...], preferred_element_type=jnp.float32)
        hidden_grad = lax.dot_general(g_ref[rows, :], wout_ref[...], (((1,), (1,)), ((), ())), preferred_element_type=jnp.float32)
        pre_grad = (hidden_grad * slope).astype(jnp.bfloat16)
        pre_ref[rows, :] = pre_grad
        back_acc[rows, :] += lax.dot_general(pre_grad, win_ref[...], (((1,), (1,)), ((), ())), preferred_element_type=jnp.float32)

    @pl.when(step == pl.num_programs(0) - 1)
    def _():
        total = jnp.zeros(drouter_ref.shape, jnp.float32)
        for piece, rows in enumerate(spans):
            prob = prob_ref[rows, :]
            gate = jnp.sum(jnp.where(own, prob, 0.0), axis=1, keepdims=True)
            out = out_acc[rows, :].astype(jnp.bfloat16).astype(jnp.float32)
            rows_refs[piece][...] = (gate * out).astype(jnp.bfloat16)
            gate_grad = jnp.sum(u_refs[piece][...].astype(jnp.float32) * out, axis=1, keepdims=True)
            logit_grad = prob * (jnp.where(own, gate_grad, 0.0) - gate * gate_grad)
            high = logit_grad.astype(jnp.bfloat16)
            low = (logit_grad - high.astype(jnp.float32)).astype(jnp.bfloat16)
            back = back_acc[rows, :].astype(jnp.bfloat16).astype(jnp.float32)
            for part in (high, low):
                back += lax.dot_general(part, router_ref[...], (((1,), (1,)), ((), ())), preferred_element_type=jnp.float32)
                total += lax.dot_general(x_refs[piece][...], part, (((0,), (0,)), ((), ())), preferred_element_type=jnp.float32)
            back_refs[piece][...] = back.astype(jnp.bfloat16)
        drouter_ref[...] = total


def run_expert(label, pieces, upstream_pieces, tile, upstream_part, router_wide, w_in, w_out, group, group_count, earlier, chunk=768):
    count, width = len(pieces), pieces[0].shape[1]
    rows, inner = count * tile, w_in.shape[1]
    once = pl.Buffered(1)
    piece = pl.BlockSpec((tile, width), lambda f, lab: (0, 0), pipeline_mode=once)
    inner_block = pl.BlockSpec((rows, chunk), lambda f, lab: (0, f))
    low = lambda *shape: jax.ShapeDtypeStruct(shape, jnp.bfloat16)
    outs = pl.pallas_call(
        lambda *refs: expert_kernel(count, *refs),
        grid_spec=pltpu.PrefetchScalarGridSpec(
            num_scalar_prefetch=1,
            grid=(inner // chunk,),
            in_specs=[piece] * count
            + [pl.BlockSpec((tile, width), lambda f, lab: (upstream_part, 0), pipeline_mode=once)] * count
            + [
                pl.BlockSpec((width, 128), lambda f, lab: (0, 0), pipeline_mode=once),
                pl.BlockSpec((width, chunk), lambda f, lab: (0, f)),
                pl.BlockSpec((chunk, width), lambda f, lab: (f, 0)),
            ]
            + [pl.BlockSpec(memory_space=pl.ANY)] * len(earlier),
            out_specs=[pl.BlockSpec((tile, width), lambda f, lab: (group, 0), pipeline_mode=once)] * count
            + [piece] * count
            + [
                pl.BlockSpec((rows, width), lambda f, lab: (0, 0), pipeline_mode=once),
                inner_block,
                inner_block,
                pl.BlockSpec((width, 128), lambda f, lab: (0, 0), pipeline_mode=once),
            ],
            scratch_shapes=[
                pltpu.VMEM((rows, 128), jnp.float32),
                pltpu.VMEM((rows, width), jnp.float32),
                pltpu.VMEM((rows, width), jnp.float32),
            ],
        ),
        out_shape=[low(group_count * tile, width)] * count
        + [low(tile, width)] * count
        + [low(rows, width), low(rows, inner), low(rows, inner), jax.ShapeDtypeStruct((width, 128), jnp.float32)],
        compiler_params=pltpu.CompilerParams(vmem_limit_bytes=48 << 20),
        cost_estimate=pl.CostEstimate(flops=16 * rows * width * inner, bytes_accessed=8 * width * inner, transcendentals=rows * inner),
        input_output_aliases={2 * count + 4 + at: at for at in range(len(earlier))},
        name="experts",
    )(label, *pieces, *upstream_pieces, router_wide, w_in, w_out, *earlier)
    return outs[:count], outs[count : 2 * count], outs[2 * count :]


def expert_grads_kernel(groups, count, *refs):
    x_refs, refs = refs[: groups * count], refs[groups * count :]
    g_refs, hid_refs, pre_refs = refs[:groups], refs[groups : 2 * groups], refs[2 * groups : 3 * groups]
    dw_ref, xt_ref, gt_ref = refs[3 * groups :]
    width = xt_ref.shape[0]
    rows = g_refs[0].shape[0]
    tile = rows // count

    @pl.when(pl.program_id(0) == 0)
    def _():
        for at in range(groups):
            gt_ref[:, at * rows : (at + 1) * rows] = g_refs[at][...].T
            for piece in range(count):
                start = at * rows + piece * tile
                xt_ref[:, start : start + tile] = x_refs[at * count + piece][...].T

    for side, (left, right) in enumerate(((xt_ref, pre_refs), (gt_ref, hid_refs))):
        total = sum(
            jnp.dot(left[:, at * rows : (at + 1) * rows], right[at][...], preferred_element_type=jnp.float32)
            for at in range(groups)
        )
        dw_ref[:, side * width : (side + 1) * width] = total.astype(jnp.bfloat16).T


def expert_grads(pieces, grads, hiddens, pre_grads, chunk=512):
    groups, count = len(grads), len(pieces) // len(grads)
    width, (rows, inner) = pieces[0].shape[1], hiddens[0].shape
    tile = rows // count
    once = pl.Buffered(1)
    inner_block = pl.BlockSpec((rows, chunk), lambda f: (0, f))
    return pl.pallas_call(
        lambda *refs: expert_grads_kernel(groups, count, *refs),
        grid=(inner // chunk,),
        in_specs=[pl.BlockSpec((tile, width), lambda f: (0, 0), pipeline_mode=once)] * (groups * count)
        + [pl.BlockSpec((rows, width), lambda f: (0, 0), pipeline_mode=once)] * groups
        + [inner_block] * (2 * groups),
        out_specs=pl.BlockSpec((chunk, 2 * width), lambda f: (f, 0)),
        out_shape=jax.ShapeDtypeStruct((inner, 2 * width), jnp.bfloat16),
        scratch_shapes=[pltpu.VMEM((width, groups * rows), jnp.bfloat16)] * 2,
        compiler_params=pltpu.CompilerParams(vmem_limit_bytes=48 << 20),
        cost_estimate=pl.CostEstimate(flops=rows * width, bytes_accessed=rows * width, transcendentals=0),
        name="expert_grads",
    )(*pieces, *grads, *hiddens, *pre_grads)


def sort_matrix(slot, slots):
    row = lax.broadcasted_iota(jnp.int32, (slots, slot.shape[1]), 0)
    return (row == slot).astype(jnp.float32).astype(jnp.bfloat16)


def sort_into(piece_refs, block, slot, rows):
    capacity = slot.shape[1] // 2
    matrix = sort_matrix(slot, len(piece_refs) * capacity)
    moved = jnp.dot(matrix, rows, preferred_element_type=jnp.float32).astype(jnp.bfloat16)
    for turn, piece_ref in enumerate(piece_refs):
        piece_ref[block * capacity : (block + 1) * capacity, :] = moved[turn * capacity : (turn + 1) * capacity]


def norm_scale_rows(rows):
    return lax.rsqrt(jnp.mean(rows * rows, axis=-1, keepdims=True) + norm_eps)


def sort_kernel(owners, label_ref, routes_ref, rows_ref, *refs):
    piece_refs, slot_ref = refs[:owners], refs[owners]
    blocks, _, length = routes_ref.shape
    first = lax.broadcasted_iota(jnp.int32, (length, length), 0)
    second = lax.broadcasted_iota(jnp.int32, (length, length), 1)
    upto = (first <= second).astype(jnp.float32).astype(jnp.bfloat16)
    for block in range(blocks):
        routes = routes_ref[block]
        hits = (lax.broadcasted_iota(jnp.int32, (8, length), 0) == routes).astype(jnp.float32)
        counts = jnp.dot(hits.astype(jnp.bfloat16), upto, preferred_element_type=jnp.float32)
        place = jnp.sum(hits * counts, axis=0, keepdims=True).astype(jnp.int32) - 1
        turn = routes - label_ref[0]
        turn = jnp.where(turn < 0, turn + owners, turn)
        slot = turn * (length // 2) + place
        slot_ref[block] = slot
        sort_into(piece_refs, block, slot, rows_ref[block])


def one_step(shape):
    return pl.BlockSpec(shape, lambda step: (0,) * len(shape), pipeline_mode=pl.Buffered(1))


def sort_upstream(label, routes, rows, owners, part, parts):
    blocks, length, width = rows.shape
    count = blocks * length // 2
    *pieces, slots = pl.pallas_call(
        lambda *refs: sort_kernel(owners, *refs),
        grid=(1,),
        in_specs=[pl.BlockSpec(memory_space=pltpu.SMEM), one_step((blocks, 1, length)), one_step(rows.shape)],
        out_specs=[pl.BlockSpec((count, width), lambda step: (part, 0), pipeline_mode=pl.Buffered(1))] * owners
        + [one_step((blocks, 1, length))],
        out_shape=[jax.ShapeDtypeStruct((parts * count, width), jnp.bfloat16)] * owners
        + [jax.ShapeDtypeStruct((blocks, 1, length), jnp.int32)],
        compiler_params=pltpu.CompilerParams(vmem_limit_bytes=48 << 20),
        name="sort_upstream",
    )(label, routes.reshape(blocks, 1, length), rows)
    return pieces, slots


def after_attention_kernel(slot_ref, attended_ref, tokens_ref, weight_ref, gain_ref, residual_ref, *piece_refs):
    for block in range(slot_ref.shape[0]):
        mixed = jnp.dot(attended_ref[block], weight_ref[...], preferred_element_type=jnp.float32)
        residual = tokens_ref[block].astype(jnp.float32) + mixed
        residual_ref[block] = residual
        router_in = (residual * norm_scale_rows(residual) * gain_ref[...]).astype(jnp.bfloat16)
        sort_into(piece_refs, block, slot_ref[block], router_in)


def after_attention(slots, attended, tokens, weight, gain, owners, earlier):
    blocks, length, width = tokens.shape
    count = blocks * length // 2
    parts = 2 if earlier else 1
    residual, *pieces = pl.pallas_call(
        lambda *refs: after_attention_kernel(*refs[:5], *refs[5 + len(earlier) :]),
        grid=(1,),
        in_specs=[
            one_step(slots.shape), one_step(tokens.shape), one_step(tokens.shape), one_step(weight.shape), one_step((1, width))
        ]
        + [pl.BlockSpec(memory_space=pl.ANY)] * len(earlier),
        out_specs=[one_step(tokens.shape)] + [one_step((count, width))] * owners,
        out_shape=[jax.ShapeDtypeStruct(tokens.shape, jnp.float32)]
        + [jax.ShapeDtypeStruct((parts * count, width), jnp.bfloat16)] * owners,
        input_output_aliases={5 + at: 1 + at for at in range(len(earlier))},
        compiler_params=pltpu.CompilerParams(vmem_limit_bytes=48 << 20),
        name="after_attention",
    )(slots, attended, tokens, weight, gain[None], *earlier)
    return residual, pieces


def before_attention_kernel(owners, earlier, slot_ref, *refs):
    piece_refs = refs[:owners]
    residual_ref, upstream_ref, attended_ref, weight_ref, gain_ref = refs[owners : owners + 5]
    residual_grad_ref, mixed_grad_ref, weight_grad_ref, gain_grad_ref = refs[-4:]
    blocks, _, length = slot_ref.shape
    capacity = length // 2
    weight_grad, gain_grad = (refs[-6][...], refs[-5][...]) if earlier else (0.0, 0.0)
    for block in range(blocks):
        slot = jnp.broadcast_to(slot_ref[block].astype(jnp.float32), (128, length)).T[:, :1].astype(jnp.int32)
        place = lax.broadcasted_iota(jnp.int32, (length, owners * capacity), 1)
        matrix = (place == slot).astype(jnp.float32).astype(jnp.bfloat16)
        rows = jnp.concatenate([ref[block * capacity : (block + 1) * capacity, :] for ref in piece_refs])
        grad = jnp.dot(matrix, rows, preferred_element_type=jnp.float32)
        residual = residual_ref[block]
        scale = norm_scale_rows(residual)
        normed = residual * scale
        scaled = grad * gain_ref[...]
        shrink = jnp.mean(scaled * normed, axis=-1, keepdims=True)
        gain_grad += jnp.sum(grad * normed, axis=0, keepdims=True)
        residual_grad = upstream_ref[block].astype(jnp.float32) + scale * (scaled - normed * shrink)
        residual_grad_ref[block] = residual_grad
        low = residual_grad.astype(jnp.bfloat16)
        mixed_grad = lax.dot_general(low, weight_ref[...], (((1,), (1,)), ((), ())), preferred_element_type=jnp.float32)
        mixed_grad_ref[block] = mixed_grad.astype(jnp.bfloat16)
        weight_grad += lax.dot_general(attended_ref[block], low, (((0,), (0,)), ((), ())), preferred_element_type=jnp.float32)
    weight_grad_ref[...] = weight_grad
    gain_grad_ref[...] = gain_grad


def before_attention(slots, pieces, residual, upstream, attended, weight, gain, group, group_count, earlier):
    blocks, length, width = residual.shape
    owners = len(pieces)
    rows = one_step(residual.shape)
    out_rows = pl.BlockSpec(residual.shape, lambda step: (group, 0, 0), pipeline_mode=pl.Buffered(1))
    sums = [one_step((width, width)), one_step((1, width))]
    shape = (group_count * blocks, length, width)
    return pl.pallas_call(
        lambda *refs: before_attention_kernel(owners, bool(earlier), *refs),
        grid=(1,),
        in_specs=[one_step(slots.shape)] + [one_step(pieces[0].shape)] * owners
        + [rows, rows, rows, one_step((width, width)), one_step((1, width))]
        + ([pl.BlockSpec(memory_space=pl.ANY)] * 2 + sums if earlier else []),
        out_specs=[out_rows, out_rows] + sums,
        out_shape=[
            jax.ShapeDtypeStruct(shape, jnp.float32),
            jax.ShapeDtypeStruct(shape, jnp.bfloat16),
            jax.ShapeDtypeStruct((width, width), jnp.float32),
            jax.ShapeDtypeStruct((1, width), jnp.float32),
        ],
        input_output_aliases={owners + 6: 0, owners + 7: 1} if earlier else {},
        compiler_params=pltpu.CompilerParams(vmem_limit_bytes=56 << 20),
        name="before_attention",
    )(slots, *pieces, residual, upstream, attended, weight, gain[None], *earlier)


def exchange(pieces, axis, sign, size=None, skipped=0):
    size = size or lax.axis_size(axis)
    return [pieces[0]] + [
        lax.ppermute(piece, axis, [(at, (at + sign * turn) % size) for at in range(size)])
        for turn, piece in enumerate(pieces[1:], 1 + skipped)
    ]


def own_and_other(blocks):
    at = lax.axis_index("ctx")
    own = lax.dynamic_index_in_dim(blocks, at, 0)
    other = lax.dynamic_index_in_dim(blocks, 1 - at, 0)
    return [own, lax.ppermute(other, "ctx", [(0, 1), (1, 0)])]


def hand_back(own, other):
    at = lax.axis_index("ctx")
    arrived = lax.ppermute(other, "ctx", [(0, 1), (1, 0)])
    return jnp.concatenate([jnp.where(at == 0, own, arrived), jnp.where(at == 0, arrived, own)])


def layer_output_kernel(groups, owners, *refs):
    slot_refs, residual_refs = refs[:groups], refs[groups : 2 * groups]
    piece_refs = refs[2 * groups : 2 * groups + owners]
    blocks, _, length = slot_refs[0].shape
    capacity = length // 2
    for group in range(groups):
        for block in range(blocks):
            at = group * blocks + block
            matrix = sort_matrix(slot_refs[group][block], owners * capacity)
            rows = jnp.concatenate([ref[at * capacity : (at + 1) * capacity, :] for ref in piece_refs])
            moved = lax.dot_general(matrix, rows, (((0,), (0,)), ((), ())), preferred_element_type=jnp.float32)
            refs[len(refs) - groups + group][block] = (residual_refs[group][block] + moved).astype(jnp.bfloat16)


def layer_output(slots, residuals, pieces):
    blocks, length, width = residuals[0].shape
    vmem = pl.BlockSpec(memory_space=pltpu.VMEM)
    return pl.pallas_call(
        lambda *refs: layer_output_kernel(len(slots), len(pieces), *refs),
        in_specs=[vmem] * (2 * len(slots) + len(pieces)),
        out_specs=[vmem] * len(slots),
        out_shape=[jax.ShapeDtypeStruct((blocks, length, width), jnp.bfloat16)] * len(slots),
        compiler_params=pltpu.CompilerParams(vmem_limit_bytes=48 << 20),
        name="layer_output",
    )(*slots, *residuals, *pieces)


def weight_outputs_kernel(place_ref, *refs):
    shard_refs, weight_refs, gain_ref = refs[:4], refs[4:7], refs[7]
    out_refs, output_ref, gain_grad_ref, small_ref = refs[8:11], refs[11], refs[12], refs[13]
    whole_refs = refs[14:]
    width = gain_ref.shape[1]
    half = width // 2
    for side in range(2):
        planes, rows, _ = shard_refs[2 * side].shape
        for turn in range(planes):
            for other in range(2):
                shard = (place_ref[0] ^ turn) * 2 + (place_ref[1] ^ other)
                start = pl.multiple_of(shard * rows, 16)
                whole_refs[side][pl.ds(start, rows), :] = shard_refs[2 * side + other][turn]
    total = 0.0
    for kind in range(3):
        for side, ref in enumerate(whole_refs):
            columns = slice(side * half, (side + 1) * half)
            grad = ref[kind * width : (kind + 1) * width, :].astype(jnp.float32)
            out_refs[kind][:, columns] = grad
            total += jnp.sum(grad * weight_refs[kind][:, columns].astype(jnp.float32), axis=1, keepdims=True)
    total = jnp.broadcast_to(total, (width, 128)).T
    gain_grad_ref[...] = total[:1] / gain_ref[...]
    start = 3 * width + 128
    for side in range(2):
        rows = slice(start + side * width, start + (side + 1) * width)
        output_ref[:, side * half : (side + 1) * half] = whole_refs[0][rows, :].astype(jnp.float32)
    for at, (ref, first) in enumerate(((whole_refs[0], 3 * width), (whole_refs[1], 3 * width), (whole_refs[0], start + 2 * width))):
        small_ref[at] = ref[first : first + 128, :].astype(jnp.float32)


def weight_outputs(shards, weights, gain):
    width = gain.shape[0]
    vmem = pl.BlockSpec(memory_space=pltpu.VMEM)
    place = jnp.stack([lax.axis_index("dp"), lax.axis_index("ctx")]).astype(jnp.int32)
    matrix = jax.ShapeDtypeStruct((width, width), jnp.float32)
    return pl.pallas_call(
        weight_outputs_kernel,
        in_specs=[pl.BlockSpec(memory_space=pltpu.SMEM)] + [vmem] * 8,
        out_specs=[vmem] * 6,
        out_shape=[matrix] * 4
        + [jax.ShapeDtypeStruct((1, width), jnp.float32), jax.ShapeDtypeStruct((3, 128, width // 2), jnp.float32)],
        scratch_shapes=[
            pltpu.VMEM((2 * part.shape[0] * part.shape[1], width // 2), jnp.bfloat16) for part in (shards[0], shards[2])
        ],
        compiler_params=pltpu.CompilerParams(vmem_limit_bytes=56 << 20),
        name="weight_outputs",
    )(place, *shards, *weights, gain[None])


def token_grads_kernel(first_ref, second_ref, *refs):
    weight_refs, (tokens_ref, residual_grad_ref, gain_ref, out_ref) = refs[:3], refs[3:]
    grad = 0.0
    for kind in range(3):
        low = jnp.concatenate([first_ref[kind], second_ref[kind]], axis=1)
        grad += lax.dot_general(low, weight_refs[kind][...], (((1,), (1,)), ((), ())), preferred_element_type=jnp.float32)
    rows = tokens_ref[...].astype(jnp.float32)
    scale = norm_scale_rows(rows)
    normed = rows * scale
    scaled = grad * gain_ref[...]
    shrink = jnp.mean(scaled * normed, axis=-1, keepdims=True)
    out_ref[...] = residual_grad_ref[...] + scale * (scaled - normed * shrink)


def token_grads(first, second, weights, tokens, residual_grad, gain):
    length, width = tokens.shape
    half = pl.BlockSpec((3, QB, width // 2), lambda step: (0, step, 0))
    rows = pl.BlockSpec((QB, width), lambda step: (step, 0))
    return pl.pallas_call(
        token_grads_kernel,
        grid=(length // QB,),
        in_specs=[half, half] + [one_step((width, width))] * 3 + [rows, rows, one_step((1, width))],
        out_specs=rows,
        out_shape=jax.ShapeDtypeStruct((length, width), jnp.float32),
        compiler_params=pltpu.CompilerParams(vmem_limit_bytes=48 << 20),
        cost_estimate=pl.CostEstimate(flops=6 * length * width * width, bytes_accessed=14 * length * width, transcendentals=0),
        name="token_grads",
    )(first, second, *weights, tokens, residual_grad, gain[None])


def place_rows(slots, pieces):
    blocks, _, length = slots.shape
    width = pieces[0].shape[-1]
    rows = jnp.stack(pieces).reshape(len(pieces), blocks, -1, width).swapaxes(0, 1).reshape(blocks, -1, width)
    places = jnp.arange(rows.shape[1], dtype=jnp.int32)
    matrix = (slots == places[None, :, None]).astype(jnp.bfloat16)
    return jnp.einsum("bsx,bsd->bxd", matrix, rows, preferred_element_type=jnp.float32)


def norm_scale(value_rows):
    return lax.rsqrt(jnp.mean(value_rows * value_rows, axis=-1, keepdims=True) + norm_eps)


def norm_back(value_rows, scale, gain_vector, grad_rows):
    scaled = grad_rows * gain_vector
    shrink = jnp.mean(scaled * value_rows, axis=-1, keepdims=True) * scale * scale * scale
    return scale * scaled - value_rows * shrink, jnp.sum(grad_rows * value_rows * scale, axis=(0, 1))


def wide_dot(rows, weight):
    return jnp.einsum("sxd,de->sxe", rows, weight, preferred_element_type=jnp.float32)


def wide_dot_back(rows, weight):
    return jnp.einsum("sxe,de->sxd", rows, weight, preferred_element_type=jnp.float32)


def weight_dot(left, right):
    return jnp.einsum("sxd,sxe->de", left, right, preferred_element_type=jnp.float32)


def pack_sums(matrices, small=None):
    parts = [matrix.astype(jnp.bfloat16) for matrix in matrices]
    if small is not None:
        small = jnp.pad(small, ((0, -small.shape[0] % 64), (0, parts[0].shape[1] - small.shape[1])))
        high = small.astype(jnp.bfloat16)
        parts += [high, (small - high.astype(jnp.float32)).astype(jnp.bfloat16)]
    return jnp.concatenate(parts)


def add_low(*parts):
    return sum(part.astype(jnp.float32) for part in parts).astype(jnp.bfloat16)


def swap(part, axis, turn):
    return lax.ppermute(part, axis, [(to, to ^ turn) for to in range(lax.axis_size(axis))])


class Summing:
    def __init__(self, packed):
        self.core, self.plane = lax.axis_index("ctx"), lax.axis_index("dp")
        self.planes = lax.axis_size("dp")
        self.part = packed.reshape(self.planes, 2, -1, packed.shape[1])
        self.step = 0

    def sends(self):
        if self.step == 0:
            return [lax.dynamic_index_in_dim(self.part, 1 - self.core, 1, keepdims=False)]
        if self.step == 1:
            return [
                lax.dynamic_index_in_dim(self.part, self.plane ^ turn, 0, keepdims=False)
                for turn in range(1, self.planes)
            ]
        return [self.part] * (self.planes - 1 if self.step == 4 else 1)

    def move(self, sent):
        axis, first = (("ctx", 1), ("dp", 1), ("expert", 1), ("expert", 2), ("dp", 1), ("ctx", 1))[self.step]
        return [swap(part, axis, first + at) for at, part in enumerate(sent)]

    def take(self, arrived):
        if self.step == 0:
            self.part = lax.dynamic_index_in_dim(self.part, self.core, 1, keepdims=False)
        elif self.step == 1:
            self.part = lax.dynamic_index_in_dim(self.part, self.plane, 0, keepdims=False)
        if self.step < 4:
            self.part = add_low(self.part, *arrived)
        elif self.step == 4:
            self.part = jnp.stack([self.part] + arrived)
        else:
            self.part = (self.part, arrived[0])
        self.step += 1


def matrix_of(sums, index, rows):
    return sums[index * rows : (index + 1) * rows]


def small_of(sums, start):
    high, low = jnp.split(sums[start:].astype(jnp.float32), 2)
    return high + low


def per_device(
    tokens,
    cotangent,
    routes,
    norm1_gain,
    query_weight,
    key_weight,
    value_weight,
    output_weight,
    bias_table,
    norm2_gain,
    router_weight,
    w_in,
    w_out,
):
    seq_count, local_len, model_width = tokens.shape
    owners = lax.axis_size("expert")
    capacity = local_len // 2
    whole_seq = seq_count == 2 and lax.axis_size("ctx") == 2 and local_len % QB == 0
    split = own_and_other if whole_seq else lambda blocks: [blocks]
    routes, cotangent, token_groups = split(routes), split(cotangent), split(tokens)
    groups = range(len(routes))
    core = lax.axis_index("ctx").astype(jnp.int32).reshape(1)
    label = lax.axis_index("expert").astype(jnp.int32).reshape(1)
    together = lax.optimization_barrier

    sorted_upstream, slots = zip(
        *[
            sort_upstream(label, routes[group], cotangent[group], owners, group, 1 + group)
            for group in groups
        ]
    )
    sorted_first, token_groups = together((sorted_upstream[0], token_groups))
    tokens = jnp.concatenate(token_groups)
    upstream = [exchange(sorted_first, "expert", 1)]
    inputs = tokens.astype(jnp.float32)
    scale1 = norm_scale(inputs)
    attn_in = (inputs * scale1 * norm1_gain).astype(jnp.bfloat16)
    queries = wide_dot(attn_in, query_weight).astype(jnp.bfloat16)
    keys = wide_dot(attn_in, key_weight).astype(jnp.bfloat16)
    values = wide_dot(attn_in, value_weight).astype(jnp.bfloat16)
    if whole_seq:
        lines = bias_lines(bias_table)
        flat = (seq_count * local_len, model_width)
        qkv = [rows.reshape(flat) for rows in (queries, keys, values)]
    else:
        first_pos = lax.axis_index("ctx") * local_len
        keys = lax.all_gather(keys, "ctx", axis=1, tiled=True)
        values = lax.all_gather(values, "ctx", axis=1, tiled=True)
        buckets = bucket_grid(first_pos, local_len, keys.shape[1])
        attended, log_totals = attend_rows(queries, keys, values, buckets, bias_table, DH)
    attended_groups, residual1, arrived = [], [], []
    if whole_seq:
        log_totals = []
    in_flight, fed = upstream[0], queries.reshape(-1, model_width)
    for at, group in enumerate(groups):
        if whole_seq:
            rows, totals = attend(core, fed, *qkv[1:], lines, at * local_len, local_len)
            rows = rows[None]
            log_totals.append(totals)
        else:
            rows = attended.astype(jnp.bfloat16)
        attended_groups.append(rows)
        earlier = sorted_upstream[at] if at else []
        residual, sorted_rows = after_attention(
            slots[at], rows, token_groups[at], output_weight, norm2_gain, owners, earlier
        )
        residual1.append(residual)
        sorted_rows, fed, in_flight = together((sorted_rows, fed, in_flight))
        if at == 0:
            upstream[0] = in_flight
        else:
            arrived[-1] = in_flight
        in_flight = exchange(sorted_rows, "expert", 1)
        arrived.append(in_flight)
    router_wide = jnp.pad(router_weight, ((0, 0), (0, 128 - router_weight.shape[1])))
    done, back = [], []
    tile = seq_count // len(groups) * local_len // 2
    for at in groups:
        rows, grads = arrived[at], upstream[0] if at == 0 else arrived[at]
        earlier = done[-1][0] if done else []
        result = run_expert(
            label, rows, grads, tile, min(at, 1), router_wide, w_in[0], w_out[0], at, len(groups), earlier
        )
        if at + 1 < len(arrived):
            result, arrived[at + 1] = together((result, arrived[at + 1]))
        leaving = result[1]
        if back:
            result, back[-1] = together((result, back[-1]))
        done.append(result)
        back.append(exchange(leaving, "expert", -1))
    rows_out = done[-1][0]
    grad_rows, hiddens, pre_grads, grad_router = zip(*[item[2] for item in done])
    grad_router = sum(grad_router)[:, : router_weight.shape[1]].T
    grad_experts = expert_grads(sum(arrived, []), grad_rows, hiddens, pre_grads)
    grad_experts, back, rows_out = together((grad_experts, back, rows_out))
    grad_experts = lax.psum_scatter(grad_experts, ("dp", "ctx"), scatter_dimension=0, tiled=True)
    if not whole_seq:
        returned = exchange(list(rows_out), "expert", -1)
    backward = ()
    for group in groups:
        backward = before_attention(
            slots[group], back[group], residual1[group], cotangent[group], attended_groups[group],
            output_weight, norm2_gain, group, len(groups), backward,
        )
    residual_grad, mixed_grad, grad_w_output, grad_norm2 = backward
    early_small = jnp.concatenate([grad_router, grad_norm2])
    projections = (query_weight, key_weight, value_weight)
    if whole_seq:
        half = model_width // 2
        pairs = half // 128
        mixed_grad = mixed_grad.reshape(flat)
        turned = attn_in.reshape(flat).T
        seen = (jnp.concatenate(attended_groups).reshape(flat), jnp.concatenate(log_totals, axis=2), turned)
        returned = exchange(list(rows_out[:-1]), "expert", -1, owners)
        first = attend_back(core, *qkv, mixed_grad, *seen, lines, 0, pairs, pairs)
        first, returned, last_rows = together((first, returned, rows_out[-1]))
        returned.append(exchange([None, last_rows], "expert", -1, owners, owners - 2)[1])
        first_grads, first_sums = first
        matrices = [first_sums, grad_w_output[:, :half], grad_w_output[:, half:]]
        early = Summing(pack_sums(matrices, early_small.reshape(-1, half)))
        second = ()
        for at in range(pairs, 2 * pairs):
            sent, mixed_grad = together((early.sends(), mixed_grad))
            moved = early.move(sent)
            second = attend_back(core, *qkv, mixed_grad, *seen, lines, at, 1, pairs, second)
            if at == pairs + 1:
                second, moved, returned = together((second, moved, returned))
            else:
                second, moved = together((second, moved))
            early.take(moved)
        (second_grads, second_sums), grad_experts = together((second, grad_experts))
        late = Summing(second_sums)
        sent, sent_late, returned = together((early.sends(), late.sends(), returned))
        moved, moved_late = early.move(sent), late.move(sent_late)
        block_out = layer_output(slots, residual1, returned)
        moved_late, block_out = together((moved_late, block_out))
        late.take(moved_late)
        sent_late, second_grads = together((late.sends(), second_grads))
        moved_late = late.move(sent_late)
        d_tokens = token_grads(
            first_grads, second_grads, projections, tokens.reshape(flat), residual_grad.reshape(flat), norm1_gain
        ).reshape(tokens.shape)
        moved, moved_late, d_tokens = together((moved, moved_late, d_tokens))
        early.take(moved)
        late.take(moved_late)
        sent, sent_late = together((early.sends(), late.sends()))
        moved = early.move(sent)
        late.take(late.move(sent_late))
        moved, moved_late = together((moved, late.move(late.sends())))
        early.take(moved)
        late.take(moved_late)
        sent, sent_late = together((early.sends(), late.sends()))
        moved, moved_late = together((early.move(sent), late.move(sent_late)))
        early.take(moved)
        late.take(moved_late)
        late.take(late.move(late.sends()))
        *grad_qkv, grad_w_output, grad_norm1, smalls = weight_outputs(early.part + late.part, projections, norm1_gain)
        grad_norm1 = grad_norm1[0]
        small = (smalls[2, :64] + smalls[2, 64:]).reshape(-1, model_width)
        grad_bias = jnp.concatenate([smalls[0, :4], smalls[1, :4]], axis=1)
        grad_bias = (grad_bias[:2] + grad_bias[2:]).reshape(2, -1, 128).swapaxes(0, 1).reshape(-1, 128)
    else:
        query_grad, _, diag_grad, key_part, value_part = attend_back_rows(
            queries, keys, values, mixed_grad, log_totals, buckets, bias_table, DH
        )
        low_parts = [query_grad.astype(jnp.bfloat16)] + [
            lax.psum_scatter(part, "ctx", scatter_dimension=1, tiled=True).astype(jnp.bfloat16)
            for part in (key_part, value_part)
        ]
        norm_in_grad = sum(wide_dot_back(*pair) for pair in zip(low_parts, projections))
        sums = lax.psum(
            pack_sums([grad_w_output] + [weight_dot(attn_in, rows) for rows in low_parts], early_small),
            ("dp", "ctx", "expert"),
        )
        grad_bias = lax.psum(diag_grad, ("dp", "ctx", "expert"))
        grad_w_output, *grad_qkv = (matrix_of(sums, kind, model_width).astype(jnp.float32) for kind in range(4))
        small = small_of(sums, 4 * model_width)
        norm1_back, grad_norm1 = norm_back(inputs, scale1, norm1_gain, norm_in_grad)
        grad_norm1 = lax.psum(grad_norm1, ("dp", "ctx", "expert"))
    grad_bias = grad_bias[: bias_table.shape[1], : bias_table.shape[0]].T
    grad_w_query, grad_w_key, grad_w_value = grad_qkv
    grad_w_output = grad_w_output.astype(jnp.float32)
    experts = router_weight.shape[1]
    grad_router, grad_norm2 = small[:experts, :].T, small[experts]
    if not whole_seq:
        block_out = layer_output(slots, residual1, returned)[0]
        d_tokens = residual_grad + norm1_back
    if whole_seq:
        block_out, d_tokens = hand_back(*block_out), hand_back(d_tokens[:1], d_tokens[1:])
    grad_experts = grad_experts.astype(jnp.float32)
    return (
        block_out,
        d_tokens,
        grad_norm1,
        grad_w_query,
        grad_w_key,
        grad_w_value,
        grad_w_output,
        grad_bias,
        grad_norm2,
        grad_router,
        grad_experts[:, :model_width].T[None],
        grad_experts[:, model_width:][None],
    )


def solution(mesh):
    rows = P(("dp", "expert"), "ctx", None)
    in_specs = (rows, rows, P(("dp", "expert"), "ctx")) + (P(),) * 8 + (P("expert", None, None),) * 2
    out_specs = (rows, rows) + (P(),) * 8 + (P("expert", None, ("dp", "ctx")), P("expert", ("dp", "ctx"), None))
    return jax.shard_map(per_device, mesh=mesh, in_specs=in_specs, out_specs=out_specs, check_vma=False)
```

```python
import jax
import jax.numpy as jnp
import numpy as np
from jax import lax
from jax.experimental import pallas as pl
from jax.experimental.pallas import tpu as pltpu
from jax.sharding import PartitionSpec as P

DH = 64
QB = 256

bucket_edges = (1, 2, 3, 4, 5, 6, 7, 8, 12, 16, 23, 32, 46, 64, 91)
norm_eps = 1e-06
precise_result = lax.Precision.HIGHEST


def bucket_of(relative):
    distance = jnp.abs(relative)
    half_bucket = jnp.zeros(relative.shape, jnp.int32)
    for threshold in bucket_edges:
        half_bucket = half_bucket + (distance >= threshold).astype(jnp.int32)
    return half_bucket + 16 * (relative > 0).astype(jnp.int32)


def bucket_grid(row_start, row_count, col_count):
    row_pos = row_start + jnp.arange(row_count, dtype=jnp.int32)
    col_pos = jnp.arange(col_count, dtype=jnp.int32)
    return bucket_of(col_pos[None, :] - row_pos[:, None])


def bias_grid(buckets, table_column, bucket_count):
    result = jnp.zeros(buckets.shape, jnp.float32)
    for label in range(bucket_count):
        result = result + jnp.where(buckets == label, table_column[label], 0.0)
    return result


def fold_buckets(buckets, grad_sum, bucket_count):
    return jnp.stack(
        [jnp.sum(jnp.where(buckets == label, grad_sum, 0.0)) for label in range(bucket_count)]
    )


def head_slice(value_rows, head_index, head_size):
    return lax.dynamic_slice_in_dim(value_rows, head_index * head_size, head_size, 2)


def put_head(target, portion, head_index, head_size):
    return lax.dynamic_update_slice_in_dim(target, portion, head_index * head_size, 2)


def head_scores(q_head, k_head, buckets, bias_table, head_index):
    table_column = lax.dynamic_index_in_dim(bias_table, head_index, 1, keepdims=False)
    scores = jnp.einsum("sqd,skd->sqk", q_head, k_head, preferred_element_type=jnp.float32)
    return scores + bias_grid(buckets, table_column, bias_table.shape[0])[None]


def attend_rows(query_matrix, keys_whole, values_whole, buckets, bias_table, head_size):
    seq_count, row_count, feature_width = query_matrix.shape
    head_count = feature_width // head_size

    def one_head(head_index, running):
        attention_result, log_totals = running
        scores = head_scores(
            head_slice(query_matrix, head_index, head_size),
            head_slice(keys_whole, head_index, head_size),
            buckets,
            bias_table,
            head_index,
        )
        row_max = jnp.max(scores, axis=-1, keepdims=True)
        log_total = row_max + jnp.log(jnp.sum(jnp.exp(scores - row_max), axis=-1, keepdims=True))
        weights_low = jnp.exp(scores - log_total).astype(jnp.bfloat16)
        portion = jnp.einsum(
            "sqk,skd->sqd",
            weights_low,
            head_slice(values_whole, head_index, head_size),
            preferred_element_type=jnp.float32,
        )
        attention_result = put_head(attention_result, portion, head_index, head_size)
        log_totals = lax.dynamic_update_index_in_dim(log_totals, log_total[..., 0], head_index, 0)
        return (attention_result, log_totals)

    initial = (
        jnp.zeros((seq_count, row_count, feature_width), jnp.float32),
        jnp.zeros((head_count, seq_count, row_count), jnp.float32),
    )
    return lax.fori_loop(0, head_count, one_head, initial)


def attend_back_rows(
    query_matrix, keys_whole, values_whole, mixed_grad, log_totals, buckets, bias_table, head_size
):
    seq_count, row_count, feature_width = query_matrix.shape
    col_count = keys_whole.shape[1]
    head_count = feature_width // head_size
    bucket_count = bias_table.shape[0]

    def one_head(head_index, running):
        query_grad, deltas, diag_grad, key_part, value_part = running
        q_head = head_slice(query_matrix, head_index, head_size)
        k_head = head_slice(keys_whole, head_index, head_size)
        v_head = head_slice(values_whole, head_index, head_size)
        g_head = head_slice(mixed_grad, head_index, head_size)
        scores = head_scores(q_head, k_head, buckets, bias_table, head_index)
        weights = jnp.exp(scores - log_totals[head_index][..., None])
        weight_grad = jnp.einsum("sqd,skd->sqk", g_head, v_head, preferred_element_type=jnp.float32)
        delta_row = jnp.sum(weights * weight_grad, axis=-1)
        score_grad = (weights * (weight_grad - delta_row[..., None])).astype(jnp.bfloat16)
        query_grad = put_head(
            query_grad,
            jnp.einsum("sqk,skd->sqd", score_grad, k_head, preferred_element_type=jnp.float32),
            head_index,
            head_size,
        )
        deltas = lax.dynamic_update_index_in_dim(deltas, delta_row, head_index, 0)
        folded = fold_buckets(
            buckets, jnp.sum(score_grad.astype(jnp.float32), axis=0), bucket_count
        )
        diag_grad = lax.dynamic_update_index_in_dim(diag_grad, folded, head_index, 0)
        key_part = put_head(
            key_part,
            jnp.einsum("sqk,sqd->skd", score_grad, q_head, preferred_element_type=jnp.float32),
            head_index,
            head_size,
        )
        value_part = put_head(
            value_part,
            jnp.einsum(
                "sqk,sqd->skd",
                weights.astype(jnp.bfloat16),
                g_head,
                preferred_element_type=jnp.float32,
            ),
            head_index,
            head_size,
        )
        return (query_grad, deltas, diag_grad, key_part, value_part)

    key_shape = (seq_count, col_count, feature_width)
    initial = (
        jnp.zeros((seq_count, row_count, feature_width), jnp.float32),
        jnp.zeros((head_count, seq_count, row_count), jnp.float32),
        jnp.zeros((head_count, bucket_count), jnp.float32),
        jnp.zeros(key_shape, jnp.float32),
        jnp.zeros(key_shape, jnp.float32),
    )
    return lax.fori_loop(0, head_count, one_head, initial)


def bucket_np(relative):
    half_bucket = np.zeros(relative.shape, np.int32)
    for threshold in bucket_edges:
        half_bucket = half_bucket + (np.abs(relative) >= threshold)
    return half_bucket + 16 * (relative > 0)


def bias_lines(bias_table):
    lane = np.arange(4 * QB)
    both = np.stack([lane - 2 * QB, 2 * QB - lane])
    onehot = (bucket_np(both)[..., None] == np.arange(32)).astype(np.float32)
    return jnp.einsum("lcb,bh->hlc", jnp.asarray(onehot), bias_table, precision=lax.Precision.HIGHEST)

def tile_index(i, j, n, core):
    half = n // 2
    if i // half == j // half:
        return max(-2, min(2, j - i)) + 2
    return jnp.clip(j - i - n * core * (1 if i < j else -1), -2, 2) + 2


def fwd_kernel(first, core_ref, lines_ref, q_ref, k_ref, v_ref, o_ref, total_ref, band_ref):
    n = k_ref.shape[0] // QB
    lane = lax.broadcasted_iota(jnp.int32, (QB, 128), 1)
    for h in range(2):
        line = lines_ref[h, 0:1, :]
        spread = pltpu.roll(jnp.broadcast_to(line, (QB, 4 * QB)), 0, 1, stride=1, stride_axis=0)
        band_ref[h, 0] = jnp.broadcast_to(line[:, :1], (QB, QB))
        for t in range(3):
            band_ref[h, 1 + t] = spread[:, (1 + t) * QB:(2 + t) * QB]
        band_ref[h, 4] = jnp.broadcast_to(line[:, 4 * QB - 1:], (QB, QB))
    for i in range(first, first + q_ref.shape[0] // QB):
        rows = slice((i - first) * QB, (i - first + 1) * QB)
        outs = []
        for h in range(2):
            q = jnp.where((lane < 64) == (h == 0), q_ref[rows, :], 0)
            s = lax.dot_general(q, k_ref[...], (((1,), (1,)), ((), ())), preferred_element_type=jnp.float32)
            parts = []
            for j in range(n):
                parts.append(s[:, j * QB:(j + 1) * QB] + band_ref[h, tile_index(i, j, n, core_ref[0])])
            s = jnp.concatenate(parts, axis=1)
            m = jnp.max(s, axis=1, keepdims=True)
            p = jnp.exp(s - m)
            l = jnp.sum(p, axis=1, keepdims=True)
            o = jnp.dot(p.astype(jnp.bfloat16), v_ref[...], preferred_element_type=jnp.float32)
            outs.append(o * (1.0 / l))
            total = jnp.broadcast_to(m + jnp.log(l), (QB, 128)).T
            total_ref[0, h:h + 1, rows] = total[:1]
        o_ref[rows, :] = jnp.where(lane < 64, outs[0], outs[1]).astype(jnp.bfloat16)

def attend(core, q, k, v, lines, first, count):
    length, width = q.shape
    col = pl.BlockSpec((length, 128), lambda h: (0, h))
    span = pl.BlockSpec((count, 128), lambda h: (first // count, h))
    return pl.pallas_call(
        lambda *refs: fwd_kernel(first // QB, *refs),
        grid=(width // 128,),
        in_specs=[pl.BlockSpec(memory_space=pltpu.SMEM), pl.BlockSpec((2, 2, 4 * QB), lambda h: (h, 0, 0)), span, col, col],
        out_specs=[pl.BlockSpec((count, 128), lambda h: (0, h)), pl.BlockSpec((1, 2, count), lambda h: (h, 0, 0))],
        out_shape=[
            jax.ShapeDtypeStruct((count, width), jnp.bfloat16),
            jax.ShapeDtypeStruct((width // 128, 2, count), jnp.float32),
        ],
        scratch_shapes=[pltpu.VMEM((2, 5, QB, QB), jnp.float32)],
        compiler_params=pltpu.CompilerParams(vmem_limit_bytes=48 << 20),
        cost_estimate=pl.CostEstimate(flops=count * length * width, bytes_accessed=2 * length * width, transcendentals=0),
        name="attend",
    )(core, lines, q, k, v)

def bwd_kernel(core_ref, lines_ref, fold_ref, q_ref, k_ref, v_ref, g_ref, o_ref, total_ref, xt_ref, grad_ref, sums_ref, band_ref, acc_ref, dk_acc, dv_acc):
    n = q_ref.shape[0] // QB
    lane = lax.broadcasted_iota(jnp.int32, (QB, 128), 1)
    for h in range(2):
        for t in range(3):
            start = 2 * QB - (t - 1) * QB - QB
            line = lines_ref[h, 1:2, start:start + 2 * QB]
            spread = pltpu.roll(jnp.broadcast_to(line, (QB, 2 * QB)), QB, 1, stride=1, stride_axis=0)
            band_ref[h, 1 + t] = spread[:, :QB]
        band_ref[h, 0] = jnp.broadcast_to(lines_ref[h, 0:1, 0:1], (QB, QB))
        band_ref[h, 4] = jnp.broadcast_to(lines_ref[h, 0:1, 4 * QB - 1:], (QB, QB))
    acc_ref[...] = jnp.zeros_like(acc_ref)
    for i in range(n):
        rows = slice(i * QB, (i + 1) * QB)
        grads = []
        for h in range(2):
            keep = (lane < 64) == (h == 0)
            q = jnp.where(keep, q_ref[rows, :], 0)
            g = jnp.where(keep, g_ref[rows, :], 0)
            s = lax.dot_general(k_ref[...], q, (((1,), (1,)), ((), ())), preferred_element_type=jnp.float32)
            parts = []
            for j in range(n):
                parts.append(s[j * QB:(j + 1) * QB, :] + band_ref[h, tile_index(i, j, n, core_ref[0])])
            s = jnp.concatenate(parts, axis=0)
            w = jnp.exp(s - total_ref[0, h:h + 1, rows])
            dp = lax.dot_general(v_ref[...], g, (((1,), (1,)), ((), ())), preferred_element_type=jnp.float32)
            delta = jnp.sum((g.astype(jnp.float32) * o_ref[rows, :].astype(jnp.float32)).T, axis=0, keepdims=True)
            ds = w * (dp - delta)
            for j in range(n):
                acc_ref[h, tile_index(i, j, n, core_ref[0])] += ds[j * QB:(j + 1) * QB, :]
            low = ds.astype(jnp.bfloat16)
            dv = jnp.dot(w.astype(jnp.bfloat16), g, preferred_element_type=jnp.float32)
            dk = jnp.dot(low, q, preferred_element_type=jnp.float32)
            if i == 0 and h == 0:
                dv_acc[...] = dv
                dk_acc[...] = dk
            else:
                dv_acc[...] += dv
                dk_acc[...] += dk
            grads.append(lax.dot_general(low, k_ref[...], (((0,), (0,)), ((), ())), preferred_element_type=jnp.float32))
        grad_ref[0, rows, :] = jnp.where(lane < 64, grads[0], grads[1]).astype(jnp.bfloat16)
    grad_ref[1] = dk_acc[...].astype(jnp.bfloat16)
    grad_ref[2] = dv_acc[...].astype(jnp.bfloat16)
    row = lax.broadcasted_iota(jnp.int32, (8, 2 * QB), 0)
    totals = []
    for h in range(2):
        total = jnp.zeros((8, 128), jnp.float32)
        for t in range(3):
            tile = acc_ref[h, 1 + t]
            wide = jnp.concatenate([tile, jnp.zeros_like(tile)], axis=1)
            moved = sum(pltpu.roll(wide[8 * e:8 * e + 8], QB - 8 * e, 1) for e in range(QB // 8))
            turned = jnp.where(row == 0, moved, 0.0)
            for e in range(1, 8):
                turned = turned + pltpu.roll(jnp.where(row == e, moved, 0.0), 2 * QB - e, 1)
            total = total + jnp.dot(turned, fold_ref[t], precision=lax.Precision.HIGHEST, preferred_element_type=jnp.float32)
        total = jnp.sum(total, axis=0, keepdims=True)
        ends = [jnp.sum(jnp.sum(acc_ref[h, side], axis=0, keepdims=True), axis=1, keepdims=True) for side in (0, 4)]
        column = lax.broadcasted_iota(jnp.int32, (1, 128), 1)
        total = total + jnp.where(column == 15, ends[0], 0.0) + jnp.where(column == 31, ends[1], 0.0)
        totals.append(total)
    width = xt_ref.shape[0]
    grads = jnp.concatenate([grad_ref[kind] for kind in range(3)], axis=1)
    weight = jnp.dot(xt_ref[...], grads, preferred_element_type=jnp.float32).astype(jnp.bfloat16)
    for kind in range(3):
        sums_ref[kind * width:(kind + 1) * width, :] = weight[:, kind * 128:(kind + 1) * 128]
    high = [total.astype(jnp.bfloat16).astype(jnp.float32) for total in totals]
    rows = high + [total - part for total, part in zip(totals, high)]
    small = jnp.concatenate(rows + [jnp.zeros((124, 128), jnp.float32)], axis=0)
    sums_ref[3 * width:, :] = small.astype(jnp.bfloat16)


def attend_back(core, q, k, v, g, o, totals, xt, lines, first_pair, pairs, total_pairs, earlier=()):
    length, width = q.shape
    rows = 3 * width + 128
    r = (np.arange(3)[:, None] - 1) * QB - (np.arange(2 * QB)[None] - QB)
    fold = (bucket_np(r)[..., None] == np.arange(128)).astype(np.float32)
    col = pl.BlockSpec((length, 128), lambda h: (0, h + first_pair))
    offset = first_pair % total_pairs
    return pl.pallas_call(
        lambda *refs: bwd_kernel(*refs[:10], *refs[10 + len(earlier):]),
        grid=(pairs,),
        in_specs=[
            pl.BlockSpec(memory_space=pltpu.SMEM),
            pl.BlockSpec((2, 2, 4 * QB), lambda h: (h + first_pair, 0, 0)),
            pl.BlockSpec((3, 2 * QB, 128), lambda h: (0, 0, 0)),
            col, col, col, col, col,
            pl.BlockSpec((1, 2, length), lambda h: (h + first_pair, 0, 0)),
            pl.BlockSpec((width, length), lambda h: (0, 0), pipeline_mode=pl.Buffered(1)),
        ]
        + [pl.BlockSpec(memory_space=pl.ANY)] * len(earlier),
        out_specs=[
            pl.BlockSpec((3, length, 128), lambda h: (0, 0, h + offset)),
            pl.BlockSpec((rows, 128), lambda h: (0, h + offset)),
        ],
        out_shape=[
            jax.ShapeDtypeStruct((3, length, 128 * total_pairs), jnp.bfloat16),
            jax.ShapeDtypeStruct((rows, 128 * total_pairs), jnp.bfloat16),
        ],
        scratch_shapes=[
            pltpu.VMEM((2, 5, QB, QB), jnp.float32),
            pltpu.VMEM((2, 5, QB, QB), jnp.float32),
            pltpu.VMEM((length, 128), jnp.float32),
            pltpu.VMEM((length, 128), jnp.float32),
        ],
        compiler_params=pltpu.CompilerParams(vmem_limit_bytes=48 << 20),
        cost_estimate=pl.CostEstimate(
            flops=84 * length * length * 128 * pairs, bytes_accessed=14 * length * 128 * pairs, transcendentals=2 * length * length * pairs
        ),
        input_output_aliases={10: 0, 11: 1} if earlier else {},
        name="attend_back",
    )(core, lines, jnp.asarray(fold), q, k, v, g, o, totals, xt, *earlier)


def expert_kernel(count, label_ref, *refs):
    x_refs, u_refs = refs[:count], refs[count : 2 * count]
    router_ref, win_ref, wout_ref = refs[2 * count : 2 * count + 3]
    rest = refs[len(refs) - 7 - 2 * count :]
    rows_refs, back_refs = rest[:count], rest[count : 2 * count]
    g_ref, hid_ref, pre_ref, drouter_ref, prob_ref, out_acc, back_acc = rest[2 * count :]
    step = pl.program_id(0)
    tile = x_refs[0].shape[0]
    lane = lax.broadcasted_iota(jnp.int32, (tile, 128), 1)
    own = lane == label_ref[0]
    spans = [slice(r * tile, (r + 1) * tile) for r in range(count)]

    @pl.when(step == 0)
    def _():
        for piece, rows in enumerate(spans):
            logits = jnp.dot(x_refs[piece][...], router_ref[...], preferred_element_type=jnp.float32)
            logits = jnp.where(lane < 4, logits, -jnp.inf)
            raised = jnp.exp(logits - jnp.max(logits, axis=1, keepdims=True))
            prob = raised / jnp.sum(raised, axis=1, keepdims=True)
            prob_ref[rows, :] = prob
            gate = jnp.sum(jnp.where(own, prob, 0.0), axis=1, keepdims=True)
            g_ref[rows, :] = (gate * u_refs[piece][...].astype(jnp.float32)).astype(jnp.bfloat16)
        out_acc[...] = jnp.zeros_like(out_acc)
        back_acc[...] = jnp.zeros_like(back_acc)

    for piece, rows in enumerate(spans):
        pre = jnp.dot(x_refs[piece][...], win_ref[...], preferred_element_type=jnp.float32)
        square = pre * pre
        turn = jnp.tanh(pre * (0.7978845608028654 + 0.035677408136300125 * square))
        half = 0.5 + 0.5 * turn
        hidden = (pre * half).astype(jnp.bfloat16)
        slope = half + pre * (half - half * half) * (1.5957691216057308 + 0.21406444881780074 * square)
        hid_ref[rows, :] = hidden
        out_acc[rows, :] += jnp.dot(hidden, wout_ref[...], preferred_element_type=jnp.float32)
        hidden_grad = lax.dot_general(g_ref[rows, :], wout_ref[...], (((1,), (1,)), ((), ())), preferred_element_type=jnp.float32)
        pre_grad = (hidden_grad * slope).astype(jnp.bfloat16)
        pre_ref[rows, :] = pre_grad
        back_acc[rows, :] += lax.dot_general(pre_grad, win_ref[...], (((1,), (1,)), ((), ())), preferred_element_type=jnp.float32)

    @pl.when(step == pl.num_programs(0) - 1)
    def _():
        total = jnp.zeros(drouter_ref.shape, jnp.float32)
        for piece, rows in enumerate(spans):
            prob = prob_ref[rows, :]
            gate = jnp.sum(jnp.where(own, prob, 0.0), axis=1, keepdims=True)
            out = out_acc[rows, :].astype(jnp.bfloat16).astype(jnp.float32)
            rows_refs[piece][...] = (gate * out).astype(jnp.bfloat16)
            gate_grad = jnp.sum(u_refs[piece][...].astype(jnp.float32) * out, axis=1, keepdims=True)
            logit_grad = prob * (jnp.where(own, gate_grad, 0.0) - gate * gate_grad)
            high = logit_grad.astype(jnp.bfloat16)
            low = (logit_grad - high.astype(jnp.float32)).astype(jnp.bfloat16)
            back = back_acc[rows, :].astype(jnp.bfloat16).astype(jnp.float32)
            for part in (high, low):
                back += lax.dot_general(part, router_ref[...], (((1,), (1,)), ((), ())), preferred_element_type=jnp.float32)
                total += lax.dot_general(x_refs[piece][...], part, (((0,), (0,)), ((), ())), preferred_element_type=jnp.float32)
            back_refs[piece][...] = back.astype(jnp.bfloat16)
        drouter_ref[...] = total


def run_expert(label, pieces, upstream_pieces, tile, upstream_part, router_wide, w_in, w_out, group, group_count, earlier, chunk=768):
    count, width = len(pieces), pieces[0].shape[1]
    rows, inner = count * tile, w_in.shape[1]
    once = pl.Buffered(1)
    piece = pl.BlockSpec((tile, width), lambda f, lab: (0, 0), pipeline_mode=once)
    inner_block = pl.BlockSpec((rows, chunk), lambda f, lab: (0, f))
    low = lambda *shape: jax.ShapeDtypeStruct(shape, jnp.bfloat16)
    outs = pl.pallas_call(
        lambda *refs: expert_kernel(count, *refs),
        grid_spec=pltpu.PrefetchScalarGridSpec(
            num_scalar_prefetch=1,
            grid=(inner // chunk,),
            in_specs=[piece] * count
            + [pl.BlockSpec((tile, width), lambda f, lab: (upstream_part, 0), pipeline_mode=once)] * count
            + [
                pl.BlockSpec((width, 128), lambda f, lab: (0, 0), pipeline_mode=once),
                pl.BlockSpec((width, chunk), lambda f, lab: (0, f)),
                pl.BlockSpec((chunk, width), lambda f, lab: (f, 0)),
            ]
            + [pl.BlockSpec(memory_space=pl.ANY)] * len(earlier),
            out_specs=[pl.BlockSpec((tile, width), lambda f, lab: (group, 0), pipeline_mode=once)] * count
            + [piece] * count
            + [
                pl.BlockSpec((rows, width), lambda f, lab: (0, 0), pipeline_mode=once),
                inner_block,
                inner_block,
                pl.BlockSpec((width, 128), lambda f, lab: (0, 0), pipeline_mode=once),
            ],
            scratch_shapes=[
                pltpu.VMEM((rows, 128), jnp.float32),
                pltpu.VMEM((rows, width), jnp.float32),
                pltpu.VMEM((rows, width), jnp.float32),
            ],
        ),
        out_shape=[low(group_count * tile, width)] * count
        + [low(tile, width)] * count
        + [low(rows, width), low(rows, inner), low(rows, inner), jax.ShapeDtypeStruct((width, 128), jnp.float32)],
        compiler_params=pltpu.CompilerParams(vmem_limit_bytes=48 << 20),
        cost_estimate=pl.CostEstimate(flops=16 * rows * width * inner, bytes_accessed=8 * width * inner, transcendentals=rows * inner),
        input_output_aliases={2 * count + 4 + at: at for at in range(len(earlier))},
        name="experts",
    )(label, *pieces, *upstream_pieces, router_wide, w_in, w_out, *earlier)
    return outs[:count], outs[count : 2 * count], outs[2 * count :]


def expert_grads_kernel(groups, count, *refs):
    x_refs, refs = refs[: groups * count], refs[groups * count :]
    g_refs, hid_refs, pre_refs = refs[:groups], refs[groups : 2 * groups], refs[2 * groups : 3 * groups]
    dw_ref, xt_ref, gt_ref = refs[3 * groups :]
    width = xt_ref.shape[0]
    rows = g_refs[0].shape[0]
    tile = rows // count

    @pl.when(pl.program_id(0) == 0)
    def _():
        for at in range(groups):
            gt_ref[:, at * rows : (at + 1) * rows] = g_refs[at][...].T
            for piece in range(count):
                start = at * rows + piece * tile
                xt_ref[:, start : start + tile] = x_refs[at * count + piece][...].T

    for side, (left, right) in enumerate(((xt_ref, pre_refs), (gt_ref, hid_refs))):
        total = sum(
            jnp.dot(left[:, at * rows : (at + 1) * rows], right[at][...], preferred_element_type=jnp.float32)
            for at in range(groups)
        )
        dw_ref[:, side * width : (side + 1) * width] = total.astype(jnp.bfloat16).T


def expert_grads(pieces, grads, hiddens, pre_grads, chunk=512):
    groups, count = len(grads), len(pieces) // len(grads)
    width, (rows, inner) = pieces[0].shape[1], hiddens[0].shape
    tile = rows // count
    once = pl.Buffered(1)
    inner_block = pl.BlockSpec((rows, chunk), lambda f: (0, f))
    return pl.pallas_call(
        lambda *refs: expert_grads_kernel(groups, count, *refs),
        grid=(inner // chunk,),
        in_specs=[pl.BlockSpec((tile, width), lambda f: (0, 0), pipeline_mode=once)] * (groups * count)
        + [pl.BlockSpec((rows, width), lambda f: (0, 0), pipeline_mode=once)] * groups
        + [inner_block] * (2 * groups),
        out_specs=pl.BlockSpec((chunk, 2 * width), lambda f: (f, 0)),
        out_shape=jax.ShapeDtypeStruct((inner, 2 * width), jnp.bfloat16),
        scratch_shapes=[pltpu.VMEM((width, groups * rows), jnp.bfloat16)] * 2,
        compiler_params=pltpu.CompilerParams(vmem_limit_bytes=48 << 20),
        cost_estimate=pl.CostEstimate(flops=rows * width, bytes_accessed=rows * width, transcendentals=0),
        name="expert_grads",
    )(*pieces, *grads, *hiddens, *pre_grads)


def sort_matrix(slot, slots):
    row = lax.broadcasted_iota(jnp.int32, (slots, slot.shape[1]), 0)
    return (row == slot).astype(jnp.float32).astype(jnp.bfloat16)


def sort_into(piece_refs, block, slot, rows):
    capacity = slot.shape[1] // 2
    matrix = sort_matrix(slot, len(piece_refs) * capacity)
    moved = jnp.dot(matrix, rows, preferred_element_type=jnp.float32).astype(jnp.bfloat16)
    for turn, piece_ref in enumerate(piece_refs):
        piece_ref[block * capacity : (block + 1) * capacity, :] = moved[turn * capacity : (turn + 1) * capacity]


def norm_scale_rows(rows):
    return lax.rsqrt(jnp.mean(rows * rows, axis=-1, keepdims=True) + norm_eps)


def sort_kernel(owners, label_ref, routes_ref, rows_ref, *refs):
    piece_refs, slot_ref = refs[:owners], refs[owners]
    blocks, _, length = routes_ref.shape
    first = lax.broadcasted_iota(jnp.int32, (length, length), 0)
    second = lax.broadcasted_iota(jnp.int32, (length, length), 1)
    upto = (first <= second).astype(jnp.float32).astype(jnp.bfloat16)
    for block in range(blocks):
        routes = routes_ref[block]
        hits = (lax.broadcasted_iota(jnp.int32, (8, length), 0) == routes).astype(jnp.float32)
        counts = jnp.dot(hits.astype(jnp.bfloat16), upto, preferred_element_type=jnp.float32)
        place = jnp.sum(hits * counts, axis=0, keepdims=True).astype(jnp.int32) - 1
        turn = routes - label_ref[0]
        turn = jnp.where(turn < 0, turn + owners, turn)
        slot = turn * (length // 2) + place
        slot_ref[block] = slot
        sort_into(piece_refs, block, slot, rows_ref[block])


def one_step(shape):
    return pl.BlockSpec(shape, lambda step: (0,) * len(shape), pipeline_mode=pl.Buffered(1))


def sort_upstream(label, routes, rows, owners, part, parts):
    blocks, length, width = rows.shape
    count = blocks * length // 2
    *pieces, slots = pl.pallas_call(
        lambda *refs: sort_kernel(owners, *refs),
        grid=(1,),
        in_specs=[pl.BlockSpec(memory_space=pltpu.SMEM), one_step((blocks, 1, length)), one_step(rows.shape)],
        out_specs=[pl.BlockSpec((count, width), lambda step: (part, 0), pipeline_mode=pl.Buffered(1))] * owners
        + [one_step((blocks, 1, length))],
        out_shape=[jax.ShapeDtypeStruct((parts * count, width), jnp.bfloat16)] * owners
        + [jax.ShapeDtypeStruct((blocks, 1, length), jnp.int32)],
        compiler_params=pltpu.CompilerParams(vmem_limit_bytes=48 << 20),
        name="sort_upstream",
    )(label, routes.reshape(blocks, 1, length), rows)
    return pieces, slots


def after_attention_kernel(slot_ref, attended_ref, tokens_ref, weight_ref, gain_ref, residual_ref, *piece_refs):
    for block in range(slot_ref.shape[0]):
        mixed = jnp.dot(attended_ref[block], weight_ref[...], preferred_element_type=jnp.float32)
        residual = tokens_ref[block].astype(jnp.float32) + mixed
        residual_ref[block] = residual
        router_in = (residual * norm_scale_rows(residual) * gain_ref[...]).astype(jnp.bfloat16)
        sort_into(piece_refs, block, slot_ref[block], router_in)


def after_attention(slots, attended, tokens, weight, gain, owners, earlier):
    blocks, length, width = tokens.shape
    count = blocks * length // 2
    parts = 2 if earlier else 1
    residual, *pieces = pl.pallas_call(
        lambda *refs: after_attention_kernel(*refs[:5], *refs[5 + len(earlier) :]),
        grid=(1,),
        in_specs=[
            one_step(slots.shape), one_step(tokens.shape), one_step(tokens.shape), one_step(weight.shape), one_step((1, width))
        ]
        + [pl.BlockSpec(memory_space=pl.ANY)] * len(earlier),
        out_specs=[one_step(tokens.shape)] + [one_step((count, width))] * owners,
        out_shape=[jax.ShapeDtypeStruct(tokens.shape, jnp.float32)]
        + [jax.ShapeDtypeStruct((parts * count, width), jnp.bfloat16)] * owners,
        input_output_aliases={5 + at: 1 + at for at in range(len(earlier))},
        compiler_params=pltpu.CompilerParams(vmem_limit_bytes=48 << 20),
        name="after_attention",
    )(slots, attended, tokens, weight, gain[None], *earlier)
    return residual, pieces


def before_attention_kernel(owners, earlier, slot_ref, *refs):
    piece_refs = refs[:owners]
    residual_ref, upstream_ref, attended_ref, weight_ref, gain_ref = refs[owners : owners + 5]
    residual_grad_ref, mixed_grad_ref, weight_grad_ref, gain_grad_ref = refs[-4:]
    blocks, _, length = slot_ref.shape
    capacity = length // 2
    weight_grad, gain_grad = (refs[-6][...], refs[-5][...]) if earlier else (0.0, 0.0)
    for block in range(blocks):
        slot = jnp.broadcast_to(slot_ref[block].astype(jnp.float32), (128, length)).T[:, :1].astype(jnp.int32)
        place = lax.broadcasted_iota(jnp.int32, (length, owners * capacity), 1)
        matrix = (place == slot).astype(jnp.float32).astype(jnp.bfloat16)
        rows = jnp.concatenate([ref[block * capacity : (block + 1) * capacity, :] for ref in piece_refs])
        grad = jnp.dot(matrix, rows, preferred_element_type=jnp.float32)
        residual = residual_ref[block]
        scale = norm_scale_rows(residual)
        normed = residual * scale
        scaled = grad * gain_ref[...]
        shrink = jnp.mean(scaled * normed, axis=-1, keepdims=True)
        gain_grad += jnp.sum(grad * normed, axis=0, keepdims=True)
        residual_grad = upstream_ref[block].astype(jnp.float32) + scale * (scaled - normed * shrink)
        residual_grad_ref[block] = residual_grad
        low = residual_grad.astype(jnp.bfloat16)
        mixed_grad = lax.dot_general(low, weight_ref[...], (((1,), (1,)), ((), ())), preferred_element_type=jnp.float32)
        mixed_grad_ref[block] = mixed_grad.astype(jnp.bfloat16)
        weight_grad += lax.dot_general(attended_ref[block], low, (((0,), (0,)), ((), ())), preferred_element_type=jnp.float32)
    weight_grad_ref[...] = weight_grad
    gain_grad_ref[...] = gain_grad


def before_attention(slots, pieces, residual, upstream, attended, weight, gain, group, group_count, earlier):
    blocks, length, width = residual.shape
    owners = len(pieces)
    rows = one_step(residual.shape)
    out_rows = pl.BlockSpec(residual.shape, lambda step: (group, 0, 0), pipeline_mode=pl.Buffered(1))
    sums = [one_step((width, width)), one_step((1, width))]
    shape = (group_count * blocks, length, width)
    return pl.pallas_call(
        lambda *refs: before_attention_kernel(owners, bool(earlier), *refs),
        grid=(1,),
        in_specs=[one_step(slots.shape)] + [one_step(pieces[0].shape)] * owners
        + [rows, rows, rows, one_step((width, width)), one_step((1, width))]
        + ([pl.BlockSpec(memory_space=pl.ANY)] * 2 + sums if earlier else []),
        out_specs=[out_rows, out_rows] + sums,
        out_shape=[
            jax.ShapeDtypeStruct(shape, jnp.float32),
            jax.ShapeDtypeStruct(shape, jnp.bfloat16),
            jax.ShapeDtypeStruct((width, width), jnp.float32),
            jax.ShapeDtypeStruct((1, width), jnp.float32),
        ],
        input_output_aliases={owners + 6: 0, owners + 7: 1} if earlier else {},
        compiler_params=pltpu.CompilerParams(vmem_limit_bytes=56 << 20),
        name="before_attention",
    )(slots, *pieces, residual, upstream, attended, weight, gain[None], *earlier)


def exchange(pieces, axis, sign, size=None, skipped=0):
    size = size or lax.axis_size(axis)
    return [pieces[0]] + [
        lax.ppermute(piece, axis, [(at, (at + sign * turn) % size) for at in range(size)])
        for turn, piece in enumerate(pieces[1:], 1 + skipped)
    ]


def own_and_other(blocks):
    at = lax.axis_index("ctx")
    own = lax.dynamic_index_in_dim(blocks, at, 0)
    other = lax.dynamic_index_in_dim(blocks, 1 - at, 0)
    return [own, lax.ppermute(other, "ctx", [(0, 1), (1, 0)])]


def hand_back_kernel(core_ref, own_ref, arrived_ref, out_ref):
    out_ref[...] = jnp.where(pl.program_id(0) == 0, own_ref[...], arrived_ref[...])


def hand_back(own, other):
    arrived = lax.ppermute(other, "ctx", [(0, 1), (1, 0)])
    core = lax.axis_index("ctx").astype(jnp.int32).reshape(1)
    _, length, width = own.shape
    block = (1, QB, width)
    last = length // QB - 1
    return pl.pallas_call(
        hand_back_kernel,
        grid_spec=pltpu.PrefetchScalarGridSpec(
            num_scalar_prefetch=1,
            grid=(2, length // QB),
            in_specs=[
                pl.BlockSpec(block, lambda side, row, core: (0, jnp.where(side == 0, row, last), 0)),
                pl.BlockSpec(block, lambda side, row, core: (0, jnp.where(side == 0, 0, row), 0)),
            ],
            out_specs=pl.BlockSpec(block, lambda side, row, core: (side ^ core[0], row, 0)),
        ),
        out_shape=jax.ShapeDtypeStruct((2, length, width), own.dtype),
        name="hand_back",
    )(core, own, arrived)


def layer_output_kernel(groups, owners, *refs):
    slot_refs, residual_refs = refs[:groups], refs[groups : 2 * groups]
    piece_refs = refs[2 * groups : 2 * groups + owners]
    blocks, _, length = slot_refs[0].shape
    capacity = length // 2
    for group in range(groups):
        for block in range(blocks):
            at = group * blocks + block
            matrix = sort_matrix(slot_refs[group][block], owners * capacity)
            rows = jnp.concatenate([ref[at * capacity : (at + 1) * capacity, :] for ref in piece_refs])
            moved = lax.dot_general(matrix, rows, (((0,), (0,)), ((), ())), preferred_element_type=jnp.float32)
            refs[len(refs) - groups + group][block] = (residual_refs[group][block] + moved).astype(jnp.bfloat16)


def layer_output(slots, residuals, pieces):
    blocks, length, width = residuals[0].shape
    vmem = pl.BlockSpec(memory_space=pltpu.VMEM)
    return pl.pallas_call(
        lambda *refs: layer_output_kernel(len(slots), len(pieces), *refs),
        in_specs=[vmem] * (2 * len(slots) + len(pieces)),
        out_specs=[vmem] * len(slots),
        out_shape=[jax.ShapeDtypeStruct((blocks, length, width), jnp.bfloat16)] * len(slots),
        compiler_params=pltpu.CompilerParams(vmem_limit_bytes=48 << 20),
        name="layer_output",
    )(*slots, *residuals, *pieces)


def weight_outputs_kernel(place_ref, *refs):
    shard_refs, weight_refs, gain_ref = refs[:4], refs[4:7], refs[7]
    out_refs, output_ref, gain_grad_ref, small_ref = refs[8:11], refs[11], refs[12], refs[13]
    whole_refs = refs[14:]
    width = gain_ref.shape[1]
    half = width // 2
    for side in range(2):
        planes, rows, _ = shard_refs[2 * side].shape
        for turn in range(planes):
            for other in range(2):
                shard = (place_ref[0] ^ turn) * 2 + (place_ref[1] ^ other)
                start = pl.multiple_of(shard * rows, 16)
                whole_refs[side][pl.ds(start, rows), :] = shard_refs[2 * side + other][turn]
    total = 0.0
    for kind in range(3):
        for side, ref in enumerate(whole_refs):
            columns = slice(side * half, (side + 1) * half)
            grad = ref[kind * width : (kind + 1) * width, :].astype(jnp.float32)
            out_refs[kind][:, columns] = grad
            total += jnp.sum(grad * weight_refs[kind][:, columns].astype(jnp.float32), axis=1, keepdims=True)
    total = jnp.broadcast_to(total, (width, 128)).T
    gain_grad_ref[...] = total[:1] / gain_ref[...]
    start = 3 * width + 128
    for side in range(2):
        rows = slice(start + side * width, start + (side + 1) * width)
        output_ref[:, side * half : (side + 1) * half] = whole_refs[0][rows, :].astype(jnp.float32)
    for at, (ref, first) in enumerate(((whole_refs[0], 3 * width), (whole_refs[1], 3 * width), (whole_refs[0], start + 2 * width))):
        small_ref[at] = ref[first : first + 128, :].astype(jnp.float32)


def weight_outputs(shards, weights, gain):
    width = gain.shape[0]
    vmem = pl.BlockSpec(memory_space=pltpu.VMEM)
    place = jnp.stack([lax.axis_index("dp"), lax.axis_index("ctx")]).astype(jnp.int32)
    matrix = jax.ShapeDtypeStruct((width, width), jnp.float32)
    return pl.pallas_call(
        weight_outputs_kernel,
        in_specs=[pl.BlockSpec(memory_space=pltpu.SMEM)] + [vmem] * 8,
        out_specs=[vmem] * 6,
        out_shape=[matrix] * 4
        + [jax.ShapeDtypeStruct((1, width), jnp.float32), jax.ShapeDtypeStruct((3, 128, width // 2), jnp.float32)],
        scratch_shapes=[
            pltpu.VMEM((2 * part.shape[0] * part.shape[1], width // 2), jnp.bfloat16) for part in (shards[0], shards[2])
        ],
        compiler_params=pltpu.CompilerParams(vmem_limit_bytes=56 << 20),
        name="weight_outputs",
    )(place, *shards, *weights, gain[None])


def halves(rows, tile, width):
    steps = rows // tile
    first = pl.BlockSpec((tile, width), lambda step: (jnp.minimum(step, steps - 1), 0))
    second = pl.BlockSpec((tile, width), lambda step: (jnp.maximum(step - steps, 0), 0))
    return [first, second], lambda first_ref, second_ref: jnp.where(pl.program_id(0) < steps, first_ref[...], second_ref[...])


def projections_kernel(choose, first_ref, second_ref, gain_ref, *refs):
    weight_refs, out_refs, turned_ref = refs[:3], refs[3:6], refs[6]
    rows = choose(first_ref, second_ref).astype(jnp.float32)
    low = (rows * norm_scale_rows(rows) * gain_ref[...]).astype(jnp.bfloat16)
    for weight_ref, out_ref in zip(weight_refs, out_refs):
        out_ref[...] = jnp.dot(low, weight_ref[...], preferred_element_type=jnp.float32).astype(jnp.bfloat16)
    turned_ref[...] = low.T


def projections_of(first, second, gain, weights):
    rows, width = first.shape
    tile = min(QB, rows)
    specs, choose = halves(rows, tile, width)
    out = jax.ShapeDtypeStruct((2 * rows, width), jnp.bfloat16)
    return pl.pallas_call(
        lambda *refs: projections_kernel(choose, *refs),
        grid=(2 * rows // tile,),
        in_specs=specs + [one_step((1, width))] + [one_step((width, width))] * 3,
        out_specs=[pl.BlockSpec((tile, width), lambda step: (step, 0))] * 3
        + [pl.BlockSpec((width, tile), lambda step: (0, step))],
        out_shape=[out] * 3 + [jax.ShapeDtypeStruct((width, 2 * rows), jnp.bfloat16)],
        compiler_params=pltpu.CompilerParams(vmem_limit_bytes=48 << 20),
        cost_estimate=pl.CostEstimate(flops=64 * rows * width * width, bytes_accessed=16 * rows * width, transcendentals=0),
        name="projections",
    )(first, second, gain[None], *weights)


def token_grads_kernel(choose, first_ref, second_ref, *refs):
    weight_refs, (own_ref, other_ref, residual_grad_ref, gain_ref, *out_refs) = refs[:3], refs[3:]
    grad = 0.0
    for kind in range(3):
        low = jnp.concatenate([first_ref[kind], second_ref[kind]], axis=1)
        grad += lax.dot_general(low, weight_refs[kind][...], (((1,), (1,)), ((), ())), preferred_element_type=jnp.float32)
    rows = choose(own_ref, other_ref).astype(jnp.float32)
    scale = norm_scale_rows(rows)
    normed = rows * scale
    scaled = grad * gain_ref[...]
    shrink = jnp.mean(scaled * normed, axis=-1, keepdims=True)
    out = residual_grad_ref[...] + scale * (scaled - normed * shrink)
    half = pl.num_programs(0) // 2

    @pl.when(pl.program_id(0) < half)
    def _():
        out_refs[0][...] = out

    @pl.when(pl.program_id(0) >= half)
    def _():
        out_refs[1][...] = out


def token_grads(first, second, weights, token_groups, residual_grad, gain):
    length, width = residual_grad.shape
    half = pl.BlockSpec((3, QB, width // 2), lambda step: (0, step, 0))
    rows = pl.BlockSpec((QB, width), lambda step: (step, 0))
    specs, choose = halves(length // 2, QB, width)
    return pl.pallas_call(
        lambda *refs: token_grads_kernel(choose, *refs),
        grid=(length // QB,),
        in_specs=[half, half] + [one_step((width, width))] * 3 + specs + [rows, one_step((1, width))],
        out_specs=specs,
        out_shape=[jax.ShapeDtypeStruct((length // 2, width), jnp.float32)] * 2,
        compiler_params=pltpu.CompilerParams(vmem_limit_bytes=48 << 20),
        cost_estimate=pl.CostEstimate(flops=6 * length * width * width, bytes_accessed=14 * length * width, transcendentals=0),
        name="token_grads",
    )(first, second, *weights, *token_groups, residual_grad, gain[None])


def norm_scale(value_rows):
    return lax.rsqrt(jnp.mean(value_rows * value_rows, axis=-1, keepdims=True) + norm_eps)


def norm_back(value_rows, scale, gain_vector, grad_rows):
    scaled = grad_rows * gain_vector
    shrink = jnp.mean(scaled * value_rows, axis=-1, keepdims=True) * scale * scale * scale
    return scale * scaled - value_rows * shrink, jnp.sum(grad_rows * value_rows * scale, axis=(0, 1))


def wide_dot(rows, weight):
    return jnp.einsum("sxd,de->sxe", rows, weight, preferred_element_type=jnp.float32)


def wide_dot_back(rows, weight):
    return jnp.einsum("sxe,de->sxd", rows, weight, preferred_element_type=jnp.float32)


def weight_dot(left, right):
    return jnp.einsum("sxd,sxe->de", left, right, preferred_element_type=jnp.float32)


def pack_sums(matrices, small=None):
    parts = [matrix.astype(jnp.bfloat16) for matrix in matrices]
    if small is not None:
        small = jnp.pad(small, ((0, -small.shape[0] % 64), (0, parts[0].shape[1] - small.shape[1])))
        high = small.astype(jnp.bfloat16)
        parts += [high, (small - high.astype(jnp.float32)).astype(jnp.bfloat16)]
    return jnp.concatenate(parts)


def add_low(*parts):
    return sum(part.astype(jnp.float32) for part in parts).astype(jnp.bfloat16)


def swap(part, axis, turn):
    return lax.ppermute(part, axis, [(to, to ^ turn) for to in range(lax.axis_size(axis))])


class Summing:
    def __init__(self, packed):
        self.core, self.plane = lax.axis_index("ctx"), lax.axis_index("dp")
        self.planes = lax.axis_size("dp")
        self.part = packed.reshape(self.planes, 2, -1, packed.shape[1])
        self.step = 0

    def sends(self):
        if self.step == 0:
            return [lax.dynamic_index_in_dim(self.part, 1 - self.core, 1, keepdims=False)]
        if self.step == 1:
            return [
                lax.dynamic_index_in_dim(self.part, self.plane ^ turn, 0, keepdims=False)
                for turn in range(1, self.planes)
            ]
        return [self.part] * (self.planes - 1 if self.step == 4 else 1)

    def move(self, sent):
        axis, first = (("ctx", 1), ("dp", 1), ("expert", 1), ("expert", 2), ("dp", 1), ("ctx", 1))[self.step]
        return [swap(part, axis, first + at) for at, part in enumerate(sent)]

    def take(self, arrived):
        if self.step == 0:
            self.part = lax.dynamic_index_in_dim(self.part, self.core, 1, keepdims=False)
        elif self.step == 1:
            self.part = lax.dynamic_index_in_dim(self.part, self.plane, 0, keepdims=False)
        if self.step < 4:
            self.part = add_low(self.part, *arrived)
        elif self.step == 4:
            self.part = jnp.stack([self.part] + arrived)
        else:
            self.part = (self.part, arrived[0])
        self.step += 1


def matrix_of(sums, index, rows):
    return sums[index * rows : (index + 1) * rows]


def small_of(sums, start):
    high, low = jnp.split(sums[start:].astype(jnp.float32), 2)
    return high + low


def per_device(
    tokens,
    cotangent,
    routes,
    norm1_gain,
    query_weight,
    key_weight,
    value_weight,
    output_weight,
    bias_table,
    norm2_gain,
    router_weight,
    w_in,
    w_out,
):
    seq_count, local_len, model_width = tokens.shape
    owners = lax.axis_size("expert")
    capacity = local_len // 2
    whole_seq = seq_count == 2 and lax.axis_size("ctx") == 2 and local_len % QB == 0
    split = own_and_other if whole_seq else lambda blocks: [blocks]
    routes, cotangent, token_groups = split(routes), split(cotangent), split(tokens)
    groups = range(len(routes))
    core = lax.axis_index("ctx").astype(jnp.int32).reshape(1)
    label = lax.axis_index("expert").astype(jnp.int32).reshape(1)
    together = lax.optimization_barrier

    sorted_upstream, slots = zip(
        *[
            sort_upstream(label, routes[group], cotangent[group], owners, group, 1 + group)
            for group in groups
        ]
    )
    sorted_first, token_groups = together((sorted_upstream[0], token_groups))
    upstream = [exchange(sorted_first, "expert", 1)]
    projections = (query_weight, key_weight, value_weight)
    token_rows = [rows.reshape(-1, model_width) for rows in (token_groups if whole_seq else jnp.split(tokens, 2))]
    queries, keys, values, turned = projections_of(*token_rows, norm1_gain, projections)
    if whole_seq:
        lines = bias_lines(bias_table)
        flat = (seq_count * local_len, model_width)
        qkv = [queries, keys, values]
    else:
        queries, keys, values = (rows.reshape(tokens.shape) for rows in (queries, keys, values))
        first_pos = lax.axis_index("ctx") * local_len
        keys = lax.all_gather(keys, "ctx", axis=1, tiled=True)
        values = lax.all_gather(values, "ctx", axis=1, tiled=True)
        buckets = bucket_grid(first_pos, local_len, keys.shape[1])
        attended, log_totals = attend_rows(queries, keys, values, buckets, bias_table, DH)
    attended_groups, residual1, arrived = [], [], []
    if whole_seq:
        log_totals = []
    in_flight, fed = upstream[0], queries.reshape(-1, model_width)
    for at, group in enumerate(groups):
        if whole_seq:
            rows, totals = attend(core, fed, *qkv[1:], lines, at * local_len, local_len)
            rows = rows[None]
            log_totals.append(totals)
        else:
            rows = attended.astype(jnp.bfloat16)
        attended_groups.append(rows)
        earlier = sorted_upstream[at] if at else []
        residual, sorted_rows = after_attention(
            slots[at], rows, token_groups[at], output_weight, norm2_gain, owners, earlier
        )
        residual1.append(residual)
        sorted_rows, fed, in_flight = together((sorted_rows, fed, in_flight))
        if at == 0:
            upstream[0] = in_flight
        else:
            arrived[-1] = in_flight
        in_flight = exchange(sorted_rows, "expert", 1)
        arrived.append(in_flight)
    router_wide = jnp.pad(router_weight, ((0, 0), (0, 128 - router_weight.shape[1])))
    done, back = [], []
    tile = seq_count // len(groups) * local_len // 2
    for at in groups:
        rows, grads = arrived[at], upstream[0] if at == 0 else arrived[at]
        earlier = done[-1][0] if done else []
        result = run_expert(
            label, rows, grads, tile, min(at, 1), router_wide, w_in[0], w_out[0], at, len(groups), earlier
        )
        if at + 1 < len(arrived):
            result, arrived[at + 1] = together((result, arrived[at + 1]))
        if whole_seq and at == 0:
            seen = (jnp.concatenate(attended_groups).reshape(flat), jnp.concatenate(log_totals, axis=2), turned)
            result, seen = together((result, seen))
        leaving = result[1]
        if back:
            result, back[-1] = together((result, back[-1]))
        done.append(result)
        back.append(exchange(leaving, "expert", -1))
    rows_out = done[-1][0]
    grad_rows, hiddens, pre_grads, grad_router = zip(*[item[2] for item in done])
    grad_router = sum(grad_router)[:, : router_weight.shape[1]].T
    grad_experts = expert_grads(sum(arrived, []), grad_rows, hiddens, pre_grads)

    def back_to_attention(group, earlier):
        return before_attention(
            slots[group], back[group], residual1[group], cotangent[group], attended_groups[group],
            output_weight, norm2_gain, group, len(groups), earlier,
        )

    backward = back_to_attention(0, ())
    grad_experts, back[-1], rows_out, backward = together((grad_experts, back[-1], rows_out, backward))
    grad_experts = lax.psum_scatter(grad_experts, ("dp", "ctx"), scatter_dimension=0, tiled=True)
    if not whole_seq:
        returned = exchange(list(rows_out), "expert", -1)
    for group in groups[1:]:
        backward = back_to_attention(group, backward)
    residual_grad, mixed_grad, grad_w_output, grad_norm2 = backward
    early_small = jnp.concatenate([grad_router, grad_norm2])
    if whole_seq:
        half = model_width // 2
        pairs = half // 128
        mixed_grad = mixed_grad.reshape(flat)
        returned = exchange(list(rows_out[:-1]), "expert", -1, owners)
        first = attend_back(core, *qkv, mixed_grad, *seen, lines, 0, pairs, pairs)
        first, returned, last_rows = together((first, returned, rows_out[-1]))
        returned.append(exchange([None, last_rows], "expert", -1, owners, owners - 2)[1])
        first_grads, first_sums = first
        matrices = [first_sums, grad_w_output[:, :half], grad_w_output[:, half:]]
        early = Summing(pack_sums(matrices, early_small.reshape(-1, half)))
        second = ()
        for at in range(pairs, 2 * pairs):
            sent, mixed_grad = together((early.sends(), mixed_grad))
            moved = early.move(sent)
            second = attend_back(core, *qkv, mixed_grad, *seen, lines, at, 1, pairs, second)
            if at == pairs + 1:
                second, moved, returned = together((second, moved, returned))
            else:
                second, moved = together((second, moved))
            early.take(moved)
        (second_grads, second_sums), grad_experts = together((second, grad_experts))
        late = Summing(second_sums)
        sent, sent_late, returned = together((early.sends(), late.sends(), returned))
        moved, moved_late = early.move(sent), late.move(sent_late)
        block_out = layer_output(slots, residual1, returned)
        moved_late, block_out = together((moved_late, block_out))
        late.take(moved_late)
        sent_late, second_grads = together((late.sends(), second_grads))
        moved_late = late.move(sent_late)
        d_tokens = token_grads(
            first_grads, second_grads, projections, token_rows, residual_grad.reshape(flat), norm1_gain
        )
        moved, moved_late, d_tokens = together((moved, moved_late, d_tokens))
        early.take(moved)
        late.take(moved_late)
        sent, sent_late = together((early.sends(), late.sends()))
        moved = early.move(sent)
        late.take(late.move(sent_late))
        moved, moved_late = together((moved, late.move(late.sends())))
        early.take(moved)
        late.take(moved_late)
        sent, sent_late = together((early.sends(), late.sends()))
        moved, moved_late = together((early.move(sent), late.move(sent_late)))
        early.take(moved)
        late.take(moved_late)
        late.take(late.move(late.sends()))
        *grad_qkv, grad_w_output, grad_norm1, smalls = weight_outputs(early.part + late.part, projections, norm1_gain)
        grad_norm1 = grad_norm1[0]
        small = (smalls[2, :64] + smalls[2, 64:]).reshape(-1, model_width)
        grad_bias = jnp.concatenate([smalls[0, :4], smalls[1, :4]], axis=1)
        grad_bias = (grad_bias[:2] + grad_bias[2:]).reshape(2, -1, 128).swapaxes(0, 1).reshape(-1, 128)
    else:
        query_grad, _, diag_grad, key_part, value_part = attend_back_rows(
            queries, keys, values, mixed_grad, log_totals, buckets, bias_table, DH
        )
        low_parts = [query_grad.astype(jnp.bfloat16)] + [
            lax.psum_scatter(part, "ctx", scatter_dimension=1, tiled=True).astype(jnp.bfloat16)
            for part in (key_part, value_part)
        ]
        inputs = tokens.astype(jnp.float32)
        attn_in = turned.T.reshape(tokens.shape)
        norm_in_grad = sum(wide_dot_back(*pair) for pair in zip(low_parts, projections))
        sums = lax.psum(
            pack_sums([grad_w_output] + [weight_dot(attn_in, rows) for rows in low_parts], early_small),
            ("dp", "ctx", "expert"),
        )
        grad_bias = lax.psum(diag_grad, ("dp", "ctx", "expert"))
        grad_w_output, *grad_qkv = (matrix_of(sums, kind, model_width).astype(jnp.float32) for kind in range(4))
        small = small_of(sums, 4 * model_width)
        norm1_back, grad_norm1 = norm_back(inputs, norm_scale(inputs), norm1_gain, norm_in_grad)
        grad_norm1 = lax.psum(grad_norm1, ("dp", "ctx", "expert"))
    grad_bias = grad_bias[: bias_table.shape[1], : bias_table.shape[0]].T
    grad_w_query, grad_w_key, grad_w_value = grad_qkv
    grad_w_output = grad_w_output.astype(jnp.float32)
    experts = router_weight.shape[1]
    grad_router, grad_norm2 = small[:experts, :].T, small[experts]
    if not whole_seq:
        block_out = layer_output(slots, residual1, returned)[0]
        d_tokens = residual_grad + norm1_back
    if whole_seq:
        block_out, d_tokens = hand_back(*block_out), hand_back(*[rows[None] for rows in d_tokens])
    grad_experts = grad_experts.astype(jnp.float32)
    return (
        block_out,
        d_tokens,
        grad_norm1,
        grad_w_query,
        grad_w_key,
        grad_w_value,
        grad_w_output,
        grad_bias,
        grad_norm2,
        grad_router,
        grad_experts[:, :model_width].T[None],
        grad_experts[:, model_width:][None],
    )


def solution(mesh):
    rows = P(("dp", "expert"), "ctx", None)
    in_specs = (rows, rows, P(("dp", "expert"), "ctx")) + (P(),) * 8 + (P("expert", None, None),) * 2
    out_specs = (rows, rows) + (P(),) * 8 + (P("expert", None, ("dp", "ctx")), P("expert", ("dp", "ctx"), None))
    return jax.shard_map(per_device, mesh=mesh, in_specs=in_specs, out_specs=out_specs, check_vma=False)
```

```python
import jax
import jax.numpy as jnp
import numpy as np
from jax import lax
from jax.experimental import pallas as pl
from jax.experimental.pallas import tpu as pltpu
from jax.sharding import PartitionSpec as P

DH = 64
QB = 256

bucket_edges = (1, 2, 3, 4, 5, 6, 7, 8, 12, 16, 23, 32, 46, 64, 91)
norm_eps = 1e-06
precise_result = lax.Precision.HIGHEST


def bucket_of(relative):
    distance = jnp.abs(relative)
    half_bucket = jnp.zeros(relative.shape, jnp.int32)
    for threshold in bucket_edges:
        half_bucket = half_bucket + (distance >= threshold).astype(jnp.int32)
    return half_bucket + 16 * (relative > 0).astype(jnp.int32)


def bucket_grid(row_start, row_count, col_count):
    row_pos = row_start + jnp.arange(row_count, dtype=jnp.int32)
    col_pos = jnp.arange(col_count, dtype=jnp.int32)
    return bucket_of(col_pos[None, :] - row_pos[:, None])


def bias_grid(buckets, table_column, bucket_count):
    result = jnp.zeros(buckets.shape, jnp.float32)
    for label in range(bucket_count):
        result = result + jnp.where(buckets == label, table_column[label], 0.0)
    return result


def fold_buckets(buckets, grad_sum, bucket_count):
    return jnp.stack(
        [jnp.sum(jnp.where(buckets == label, grad_sum, 0.0)) for label in range(bucket_count)]
    )


def head_slice(value_rows, head_index, head_size):
    return lax.dynamic_slice_in_dim(value_rows, head_index * head_size, head_size, 2)


def put_head(target, portion, head_index, head_size):
    return lax.dynamic_update_slice_in_dim(target, portion, head_index * head_size, 2)


def head_scores(q_head, k_head, buckets, bias_table, head_index):
    table_column = lax.dynamic_index_in_dim(bias_table, head_index, 1, keepdims=False)
    scores = jnp.einsum("sqd,skd->sqk", q_head, k_head, preferred_element_type=jnp.float32)
    return scores + bias_grid(buckets, table_column, bias_table.shape[0])[None]


def attend_rows(query_matrix, keys_whole, values_whole, buckets, bias_table, head_size):
    seq_count, row_count, feature_width = query_matrix.shape
    head_count = feature_width // head_size

    def one_head(head_index, running):
        attention_result, log_totals = running
        scores = head_scores(
            head_slice(query_matrix, head_index, head_size),
            head_slice(keys_whole, head_index, head_size),
            buckets,
            bias_table,
            head_index,
        )
        row_max = jnp.max(scores, axis=-1, keepdims=True)
        log_total = row_max + jnp.log(jnp.sum(jnp.exp(scores - row_max), axis=-1, keepdims=True))
        weights_low = jnp.exp(scores - log_total).astype(jnp.bfloat16)
        portion = jnp.einsum(
            "sqk,skd->sqd",
            weights_low,
            head_slice(values_whole, head_index, head_size),
            preferred_element_type=jnp.float32,
        )
        attention_result = put_head(attention_result, portion, head_index, head_size)
        log_totals = lax.dynamic_update_index_in_dim(log_totals, log_total[..., 0], head_index, 0)
        return (attention_result, log_totals)

    initial = (
        jnp.zeros((seq_count, row_count, feature_width), jnp.float32),
        jnp.zeros((head_count, seq_count, row_count), jnp.float32),
    )
    return lax.fori_loop(0, head_count, one_head, initial)


def attend_back_rows(
    query_matrix, keys_whole, values_whole, mixed_grad, log_totals, buckets, bias_table, head_size
):
    seq_count, row_count, feature_width = query_matrix.shape
    col_count = keys_whole.shape[1]
    head_count = feature_width // head_size
    bucket_count = bias_table.shape[0]

    def one_head(head_index, running):
        query_grad, deltas, diag_grad, key_part, value_part = running
        q_head = head_slice(query_matrix, head_index, head_size)
        k_head = head_slice(keys_whole, head_index, head_size)
        v_head = head_slice(values_whole, head_index, head_size)
        g_head = head_slice(mixed_grad, head_index, head_size)
        scores = head_scores(q_head, k_head, buckets, bias_table, head_index)
        weights = jnp.exp(scores - log_totals[head_index][..., None])
        weight_grad = jnp.einsum("sqd,skd->sqk", g_head, v_head, preferred_element_type=jnp.float32)
        delta_row = jnp.sum(weights * weight_grad, axis=-1)
        score_grad = (weights * (weight_grad - delta_row[..., None])).astype(jnp.bfloat16)
        query_grad = put_head(
            query_grad,
            jnp.einsum("sqk,skd->sqd", score_grad, k_head, preferred_element_type=jnp.float32),
            head_index,
            head_size,
        )
        deltas = lax.dynamic_update_index_in_dim(deltas, delta_row, head_index, 0)
        folded = fold_buckets(
            buckets, jnp.sum(score_grad.astype(jnp.float32), axis=0), bucket_count
        )
        diag_grad = lax.dynamic_update_index_in_dim(diag_grad, folded, head_index, 0)
        key_part = put_head(
            key_part,
            jnp.einsum("sqk,sqd->skd", score_grad, q_head, preferred_element_type=jnp.float32),
            head_index,
            head_size,
        )
        value_part = put_head(
            value_part,
            jnp.einsum(
                "sqk,sqd->skd",
                weights.astype(jnp.bfloat16),
                g_head,
                preferred_element_type=jnp.float32,
            ),
            head_index,
            head_size,
        )
        return (query_grad, deltas, diag_grad, key_part, value_part)

    key_shape = (seq_count, col_count, feature_width)
    initial = (
        jnp.zeros((seq_count, row_count, feature_width), jnp.float32),
        jnp.zeros((head_count, seq_count, row_count), jnp.float32),
        jnp.zeros((head_count, bucket_count), jnp.float32),
        jnp.zeros(key_shape, jnp.float32),
        jnp.zeros(key_shape, jnp.float32),
    )
    return lax.fori_loop(0, head_count, one_head, initial)


def bucket_np(relative):
    half_bucket = np.zeros(relative.shape, np.int32)
    for threshold in bucket_edges:
        half_bucket = half_bucket + (np.abs(relative) >= threshold)
    return half_bucket + 16 * (relative > 0)


def bias_lines(bias_table):
    lane = np.arange(4 * QB)
    both = np.stack([lane - 2 * QB, 2 * QB - lane])
    onehot = (bucket_np(both)[..., None] == np.arange(32)).astype(np.float32)
    return jnp.einsum("lcb,bh->hlc", jnp.asarray(onehot), bias_table, precision=lax.Precision.HIGHEST)

def tile_index(i, j, n, core):
    half = n // 2
    if i // half == j // half:
        return max(-2, min(2, j - i)) + 2
    return jnp.clip(j - i - n * core * (1 if i < j else -1), -2, 2) + 2


def fwd_kernel(first, core_ref, lines_ref, q_ref, k_ref, v_ref, o_ref, total_ref, band_ref):
    n = k_ref.shape[0] // QB
    lane = lax.broadcasted_iota(jnp.int32, (QB, 128), 1)
    for h in range(2):
        line = lines_ref[h, 0:1, :]
        spread = pltpu.roll(jnp.broadcast_to(line, (QB, 4 * QB)), 0, 1, stride=1, stride_axis=0)
        band_ref[h, 0] = jnp.broadcast_to(line[:, :1], (QB, QB))
        for t in range(3):
            band_ref[h, 1 + t] = spread[:, (1 + t) * QB:(2 + t) * QB]
        band_ref[h, 4] = jnp.broadcast_to(line[:, 4 * QB - 1:], (QB, QB))
    for i in range(first, first + q_ref.shape[0] // QB):
        rows = slice((i - first) * QB, (i - first + 1) * QB)
        outs = []
        for h in range(2):
            q = jnp.where((lane < 64) == (h == 0), q_ref[rows, :], 0)
            s = lax.dot_general(q, k_ref[...], (((1,), (1,)), ((), ())), preferred_element_type=jnp.float32)
            parts = []
            for j in range(n):
                parts.append(s[:, j * QB:(j + 1) * QB] + band_ref[h, tile_index(i, j, n, core_ref[0])])
            s = jnp.concatenate(parts, axis=1)
            m = jnp.max(s, axis=1, keepdims=True)
            p = jnp.exp(s - m)
            l = jnp.sum(p, axis=1, keepdims=True)
            o = jnp.dot(p.astype(jnp.bfloat16), v_ref[...], preferred_element_type=jnp.float32)
            outs.append(o * (1.0 / l))
            total = jnp.broadcast_to(m + jnp.log(l), (QB, 128)).T
            total_ref[0, h:h + 1, rows] = total[:1]
        o_ref[rows, :] = jnp.where(lane < 64, outs[0], outs[1]).astype(jnp.bfloat16)

def attend(core, q, k, v, lines, first, count):
    length, width = q.shape
    col = pl.BlockSpec((length, 128), lambda h: (0, h))
    span = pl.BlockSpec((count, 128), lambda h: (first // count, h))
    return pl.pallas_call(
        lambda *refs: fwd_kernel(first // QB, *refs),
        grid=(width // 128,),
        in_specs=[pl.BlockSpec(memory_space=pltpu.SMEM), pl.BlockSpec((2, 2, 4 * QB), lambda h: (h, 0, 0)), span, col, col],
        out_specs=[pl.BlockSpec((count, 128), lambda h: (0, h)), pl.BlockSpec((1, 2, count), lambda h: (h, 0, 0))],
        out_shape=[
            jax.ShapeDtypeStruct((count, width), jnp.bfloat16),
            jax.ShapeDtypeStruct((width // 128, 2, count), jnp.float32),
        ],
        scratch_shapes=[pltpu.VMEM((2, 5, QB, QB), jnp.float32)],
        compiler_params=pltpu.CompilerParams(vmem_limit_bytes=48 << 20),
        cost_estimate=pl.CostEstimate(flops=count * length * width, bytes_accessed=2 * length * width, transcendentals=0),
        name="attend",
    )(core, lines, q, k, v)

def bwd_kernel(core_ref, lines_ref, fold_ref, q_ref, k_ref, v_ref, g_ref, o_ref, total_ref, xt_ref, grad_ref, sums_ref, band_ref, acc_ref, dk_acc, dv_acc):
    n = q_ref.shape[0] // QB
    lane = lax.broadcasted_iota(jnp.int32, (QB, 128), 1)
    for h in range(2):
        for t in range(3):
            start = 2 * QB - (t - 1) * QB - QB
            line = lines_ref[h, 1:2, start:start + 2 * QB]
            spread = pltpu.roll(jnp.broadcast_to(line, (QB, 2 * QB)), QB, 1, stride=1, stride_axis=0)
            band_ref[h, 1 + t] = spread[:, :QB]
        band_ref[h, 0] = jnp.broadcast_to(lines_ref[h, 0:1, 0:1], (QB, QB))
        band_ref[h, 4] = jnp.broadcast_to(lines_ref[h, 0:1, 4 * QB - 1:], (QB, QB))
    acc_ref[...] = jnp.zeros_like(acc_ref)
    for i in range(n):
        rows = slice(i * QB, (i + 1) * QB)
        grads = []
        for h in range(2):
            keep = (lane < 64) == (h == 0)
            q = jnp.where(keep, q_ref[rows, :], 0)
            g = jnp.where(keep, g_ref[rows, :], 0)
            s = lax.dot_general(k_ref[...], q, (((1,), (1,)), ((), ())), preferred_element_type=jnp.float32)
            parts = []
            for j in range(n):
                parts.append(s[j * QB:(j + 1) * QB, :] + band_ref[h, tile_index(i, j, n, core_ref[0])])
            s = jnp.concatenate(parts, axis=0)
            w = jnp.exp(s - total_ref[0, h:h + 1, rows])
            dp = lax.dot_general(v_ref[...], g, (((1,), (1,)), ((), ())), preferred_element_type=jnp.float32)
            delta = jnp.sum((g.astype(jnp.float32) * o_ref[rows, :].astype(jnp.float32)).T, axis=0, keepdims=True)
            ds = w * (dp - delta)
            for j in range(n):
                acc_ref[h, tile_index(i, j, n, core_ref[0])] += ds[j * QB:(j + 1) * QB, :]
            low = ds.astype(jnp.bfloat16)
            dv = jnp.dot(w.astype(jnp.bfloat16), g, preferred_element_type=jnp.float32)
            dk = jnp.dot(low, q, preferred_element_type=jnp.float32)
            if i == 0 and h == 0:
                dv_acc[...] = dv
                dk_acc[...] = dk
            else:
                dv_acc[...] += dv
                dk_acc[...] += dk
            grads.append(lax.dot_general(low, k_ref[...], (((0,), (0,)), ((), ())), preferred_element_type=jnp.float32))
        grad_ref[0, rows, :] = jnp.where(lane < 64, grads[0], grads[1]).astype(jnp.bfloat16)
    grad_ref[1] = dk_acc[...].astype(jnp.bfloat16)
    grad_ref[2] = dv_acc[...].astype(jnp.bfloat16)
    row = lax.broadcasted_iota(jnp.int32, (8, 2 * QB), 0)
    totals = []
    for h in range(2):
        total = jnp.zeros((8, 128), jnp.float32)
        for t in range(3):
            tile = acc_ref[h, 1 + t]
            wide = jnp.concatenate([tile, jnp.zeros_like(tile)], axis=1)
            moved = sum(pltpu.roll(wide[8 * e:8 * e + 8], QB - 8 * e, 1) for e in range(QB // 8))
            turned = jnp.where(row == 0, moved, 0.0)
            for e in range(1, 8):
                turned = turned + pltpu.roll(jnp.where(row == e, moved, 0.0), 2 * QB - e, 1)
            total = total + jnp.dot(turned, fold_ref[t], precision=lax.Precision.HIGHEST, preferred_element_type=jnp.float32)
        total = jnp.sum(total, axis=0, keepdims=True)
        ends = [jnp.sum(jnp.sum(acc_ref[h, side], axis=0, keepdims=True), axis=1, keepdims=True) for side in (0, 4)]
        column = lax.broadcasted_iota(jnp.int32, (1, 128), 1)
        total = total + jnp.where(column == 15, ends[0], 0.0) + jnp.where(column == 31, ends[1], 0.0)
        totals.append(total)
    width = xt_ref.shape[0]
    grads = jnp.concatenate([grad_ref[kind] for kind in range(3)], axis=1)
    weight = jnp.dot(xt_ref[...], grads, preferred_element_type=jnp.float32).astype(jnp.bfloat16)
    for kind in range(3):
        sums_ref[kind * width:(kind + 1) * width, :] = weight[:, kind * 128:(kind + 1) * 128]
    high = [total.astype(jnp.bfloat16).astype(jnp.float32) for total in totals]
    rows = high + [total - part for total, part in zip(totals, high)]
    small = jnp.concatenate(rows + [jnp.zeros((124, 128), jnp.float32)], axis=0)
    sums_ref[3 * width:, :] = small.astype(jnp.bfloat16)


def attend_back(core, q, k, v, g, o, totals, xt, lines, first_pair, pairs, total_pairs, earlier=()):
    length, width = q.shape
    rows = 3 * width + 128
    r = (np.arange(3)[:, None] - 1) * QB - (np.arange(2 * QB)[None] - QB)
    fold = (bucket_np(r)[..., None] == np.arange(128)).astype(np.float32)
    col = pl.BlockSpec((length, 128), lambda h: (0, h + first_pair))
    offset = first_pair % total_pairs
    return pl.pallas_call(
        lambda *refs: bwd_kernel(*refs[:10], *refs[10 + len(earlier):]),
        grid=(pairs,),
        in_specs=[
            pl.BlockSpec(memory_space=pltpu.SMEM),
            pl.BlockSpec((2, 2, 4 * QB), lambda h: (h + first_pair, 0, 0)),
            pl.BlockSpec((3, 2 * QB, 128), lambda h: (0, 0, 0)),
            col, col, col, col, col,
            pl.BlockSpec((1, 2, length), lambda h: (h + first_pair, 0, 0)),
            pl.BlockSpec((width, length), lambda h: (0, 0), pipeline_mode=pl.Buffered(1)),
        ]
        + [pl.BlockSpec(memory_space=pl.ANY)] * len(earlier),
        out_specs=[
            pl.BlockSpec((3, length, 128), lambda h: (0, 0, h + offset)),
            pl.BlockSpec((rows, 128), lambda h: (0, h + offset)),
        ],
        out_shape=[
            jax.ShapeDtypeStruct((3, length, 128 * total_pairs), jnp.bfloat16),
            jax.ShapeDtypeStruct((rows, 128 * total_pairs), jnp.bfloat16),
        ],
        scratch_shapes=[
            pltpu.VMEM((2, 5, QB, QB), jnp.float32),
            pltpu.VMEM((2, 5, QB, QB), jnp.float32),
            pltpu.VMEM((length, 128), jnp.float32),
            pltpu.VMEM((length, 128), jnp.float32),
        ],
        compiler_params=pltpu.CompilerParams(vmem_limit_bytes=60 << 20),
        cost_estimate=pl.CostEstimate(
            flops=84 * length * length * 128 * pairs, bytes_accessed=14 * length * 128 * pairs, transcendentals=2 * length * length * pairs
        ),
        input_output_aliases={10: 0, 11: 1} if earlier else {},
        name="attend_back",
    )(core, lines, jnp.asarray(fold), q, k, v, g, o, totals, xt, *earlier)


def expert_kernel(count, label_ref, *refs):
    x_refs, u_refs = refs[:count], refs[count : 2 * count]
    router_ref, win_ref, wout_ref = refs[2 * count : 2 * count + 3]
    rest = refs[len(refs) - 7 - 2 * count :]
    rows_refs, back_refs = rest[:count], rest[count : 2 * count]
    g_ref, hid_ref, pre_ref, drouter_ref, prob_ref, out_acc, back_acc = rest[2 * count :]
    step = pl.program_id(0)
    tile = x_refs[0].shape[0]
    lane = lax.broadcasted_iota(jnp.int32, (tile, 128), 1)
    own = lane == label_ref[0]
    spans = [slice(r * tile, (r + 1) * tile) for r in range(count)]

    @pl.when(step == 0)
    def _():
        for piece, rows in enumerate(spans):
            logits = jnp.dot(x_refs[piece][...], router_ref[...], preferred_element_type=jnp.float32)
            logits = jnp.where(lane < 4, logits, -jnp.inf)
            raised = jnp.exp(logits - jnp.max(logits, axis=1, keepdims=True))
            prob = raised / jnp.sum(raised, axis=1, keepdims=True)
            prob_ref[rows, :] = prob
            gate = jnp.sum(jnp.where(own, prob, 0.0), axis=1, keepdims=True)
            g_ref[rows, :] = (gate * u_refs[piece][...].astype(jnp.float32)).astype(jnp.bfloat16)
        out_acc[...] = jnp.zeros_like(out_acc)
        back_acc[...] = jnp.zeros_like(back_acc)

    for piece, rows in enumerate(spans):
        pre = jnp.dot(x_refs[piece][...], win_ref[...], preferred_element_type=jnp.float32)
        square = pre * pre
        turn = jnp.tanh(pre * (0.7978845608028654 + 0.035677408136300125 * square))
        half = 0.5 + 0.5 * turn
        hidden = (pre * half).astype(jnp.bfloat16)
        slope = half + pre * (half - half * half) * (1.5957691216057308 + 0.21406444881780074 * square)
        hid_ref[rows, :] = hidden
        out_acc[rows, :] += jnp.dot(hidden, wout_ref[...], preferred_element_type=jnp.float32)
        hidden_grad = lax.dot_general(g_ref[rows, :], wout_ref[...], (((1,), (1,)), ((), ())), preferred_element_type=jnp.float32)
        pre_grad = (hidden_grad * slope).astype(jnp.bfloat16)
        pre_ref[rows, :] = pre_grad
        back_acc[rows, :] += lax.dot_general(pre_grad, win_ref[...], (((1,), (1,)), ((), ())), preferred_element_type=jnp.float32)

    @pl.when(step == pl.num_programs(0) - 1)
    def _():
        total = jnp.zeros(drouter_ref.shape, jnp.float32)
        for piece, rows in enumerate(spans):
            prob = prob_ref[rows, :]
            gate = jnp.sum(jnp.where(own, prob, 0.0), axis=1, keepdims=True)
            out = out_acc[rows, :].astype(jnp.bfloat16).astype(jnp.float32)
            rows_refs[piece][...] = (gate * out).astype(jnp.bfloat16)
            gate_grad = jnp.sum(u_refs[piece][...].astype(jnp.float32) * out, axis=1, keepdims=True)
            logit_grad = prob * (jnp.where(own, gate_grad, 0.0) - gate * gate_grad)
            high = logit_grad.astype(jnp.bfloat16)
            low = (logit_grad - high.astype(jnp.float32)).astype(jnp.bfloat16)
            back = back_acc[rows, :].astype(jnp.bfloat16).astype(jnp.float32)
            for part in (high, low):
                back += lax.dot_general(part, router_ref[...], (((1,), (1,)), ((), ())), preferred_element_type=jnp.float32)
                total += lax.dot_general(x_refs[piece][...], part, (((0,), (0,)), ((), ())), preferred_element_type=jnp.float32)
            back_refs[piece][...] = back.astype(jnp.bfloat16)
        drouter_ref[...] = total


def run_expert(label, pieces, upstream_pieces, tile, upstream_part, router_wide, w_in, w_out, group, group_count, earlier, chunk=768):
    count, width = len(pieces), pieces[0].shape[1]
    rows, inner = count * tile, w_in.shape[1]
    once = pl.Buffered(1)
    piece = pl.BlockSpec((tile, width), lambda f, lab: (0, 0), pipeline_mode=once)
    inner_block = pl.BlockSpec((rows, chunk), lambda f, lab: (0, f))
    low = lambda *shape: jax.ShapeDtypeStruct(shape, jnp.bfloat16)
    outs = pl.pallas_call(
        lambda *refs: expert_kernel(count, *refs),
        grid_spec=pltpu.PrefetchScalarGridSpec(
            num_scalar_prefetch=1,
            grid=(inner // chunk,),
            in_specs=[piece] * count
            + [pl.BlockSpec((tile, width), lambda f, lab: (upstream_part, 0), pipeline_mode=once)] * count
            + [
                pl.BlockSpec((width, 128), lambda f, lab: (0, 0), pipeline_mode=once),
                pl.BlockSpec((width, chunk), lambda f, lab: (0, f)),
                pl.BlockSpec((chunk, width), lambda f, lab: (f, 0)),
            ]
            + [pl.BlockSpec(memory_space=pl.ANY)] * len(earlier),
            out_specs=[pl.BlockSpec((tile, width), lambda f, lab: (group, 0), pipeline_mode=once)] * count
            + [piece] * count
            + [
                pl.BlockSpec((rows, width), lambda f, lab: (0, 0), pipeline_mode=once),
                inner_block,
                inner_block,
                pl.BlockSpec((width, 128), lambda f, lab: (0, 0), pipeline_mode=once),
            ],
            scratch_shapes=[
                pltpu.VMEM((rows, 128), jnp.float32),
                pltpu.VMEM((rows, width), jnp.float32),
                pltpu.VMEM((rows, width), jnp.float32),
            ],
        ),
        out_shape=[low(group_count * tile, width)] * count
        + [low(tile, width)] * count
        + [low(rows, width), low(rows, inner), low(rows, inner), jax.ShapeDtypeStruct((width, 128), jnp.float32)],
        compiler_params=pltpu.CompilerParams(vmem_limit_bytes=60 << 20),
        cost_estimate=pl.CostEstimate(flops=16 * rows * width * inner, bytes_accessed=8 * width * inner, transcendentals=rows * inner),
        input_output_aliases={2 * count + 4 + at: at for at in range(len(earlier))},
        name="experts",
    )(label, *pieces, *upstream_pieces, router_wide, w_in, w_out, *earlier)
    return outs[:count], outs[count : 2 * count], outs[2 * count :]


def expert_grads_kernel(groups, count, *refs):
    x_refs, refs = refs[: groups * count], refs[groups * count :]
    g_refs, hid_refs, pre_refs = refs[:groups], refs[groups : 2 * groups], refs[2 * groups : 3 * groups]
    dw_ref, xt_ref, gt_ref = refs[3 * groups :]
    width = xt_ref.shape[0]
    rows = g_refs[0].shape[0]
    tile = rows // count

    @pl.when(pl.program_id(0) == 0)
    def _():
        for at in range(groups):
            gt_ref[:, at * rows : (at + 1) * rows] = g_refs[at][...].T
            for piece in range(count):
                start = at * rows + piece * tile
                xt_ref[:, start : start + tile] = x_refs[at * count + piece][...].T

    for side, (left, right) in enumerate(((xt_ref, pre_refs), (gt_ref, hid_refs))):
        total = sum(
            jnp.dot(left[:, at * rows : (at + 1) * rows], right[at][...], preferred_element_type=jnp.float32)
            for at in range(groups)
        )
        dw_ref[:, side * width : (side + 1) * width] = total.astype(jnp.bfloat16).T


def expert_grads(pieces, grads, hiddens, pre_grads, chunk=512):
    groups, count = len(grads), len(pieces) // len(grads)
    width, (rows, inner) = pieces[0].shape[1], hiddens[0].shape
    tile = rows // count
    once = pl.Buffered(1)
    inner_block = pl.BlockSpec((rows, chunk), lambda f: (0, f))
    return pl.pallas_call(
        lambda *refs: expert_grads_kernel(groups, count, *refs),
        grid=(inner // chunk,),
        in_specs=[pl.BlockSpec((tile, width), lambda f: (0, 0), pipeline_mode=once)] * (groups * count)
        + [pl.BlockSpec((rows, width), lambda f: (0, 0), pipeline_mode=once)] * groups
        + [inner_block] * (2 * groups),
        out_specs=pl.BlockSpec((chunk, 2 * width), lambda f: (f, 0)),
        out_shape=jax.ShapeDtypeStruct((inner, 2 * width), jnp.bfloat16),
        scratch_shapes=[pltpu.VMEM((width, groups * rows), jnp.bfloat16)] * 2,
        compiler_params=pltpu.CompilerParams(vmem_limit_bytes=60 << 20),
        cost_estimate=pl.CostEstimate(flops=rows * width, bytes_accessed=rows * width, transcendentals=0),
        name="expert_grads",
    )(*pieces, *grads, *hiddens, *pre_grads)


def sort_matrix(slot, slots):
    row = lax.broadcasted_iota(jnp.int32, (slots, slot.shape[1]), 0)
    return (row == slot).astype(jnp.float32).astype(jnp.bfloat16)


def sort_into(piece_refs, block, slot, rows):
    capacity = slot.shape[1] // 2
    matrix = sort_matrix(slot, len(piece_refs) * capacity)
    moved = jnp.dot(matrix, rows, preferred_element_type=jnp.float32).astype(jnp.bfloat16)
    for turn, piece_ref in enumerate(piece_refs):
        piece_ref[block * capacity : (block + 1) * capacity, :] = moved[turn * capacity : (turn + 1) * capacity]


def norm_scale_rows(rows):
    return lax.rsqrt(jnp.mean(rows * rows, axis=-1, keepdims=True) + norm_eps)


def sort_kernel(owners, label_ref, routes_ref, rows_ref, *refs):
    piece_refs, slot_ref = refs[:owners], refs[owners]
    blocks, _, length = routes_ref.shape
    first = lax.broadcasted_iota(jnp.int32, (length, length), 0)
    second = lax.broadcasted_iota(jnp.int32, (length, length), 1)
    upto = (first <= second).astype(jnp.float32).astype(jnp.bfloat16)
    for block in range(blocks):
        routes = routes_ref[block]
        hits = (lax.broadcasted_iota(jnp.int32, (8, length), 0) == routes).astype(jnp.float32)
        counts = jnp.dot(hits.astype(jnp.bfloat16), upto, preferred_element_type=jnp.float32)
        place = jnp.sum(hits * counts, axis=0, keepdims=True).astype(jnp.int32) - 1
        turn = routes - label_ref[0]
        turn = jnp.where(turn < 0, turn + owners, turn)
        slot = turn * (length // 2) + place
        slot_ref[block] = slot
        sort_into(piece_refs, block, slot, rows_ref[block])


def one_step(shape):
    return pl.BlockSpec(shape, lambda step: (0,) * len(shape), pipeline_mode=pl.Buffered(1))


def sort_upstream(label, routes, rows, owners, part, parts):
    blocks, length, width = rows.shape
    count = blocks * length // 2
    *pieces, slots = pl.pallas_call(
        lambda *refs: sort_kernel(owners, *refs),
        grid=(1,),
        in_specs=[pl.BlockSpec(memory_space=pltpu.SMEM), one_step((blocks, 1, length)), one_step(rows.shape)],
        out_specs=[pl.BlockSpec((count, width), lambda step: (part, 0), pipeline_mode=pl.Buffered(1))] * owners
        + [one_step((blocks, 1, length))],
        out_shape=[jax.ShapeDtypeStruct((parts * count, width), jnp.bfloat16)] * owners
        + [jax.ShapeDtypeStruct((blocks, 1, length), jnp.int32)],
        compiler_params=pltpu.CompilerParams(vmem_limit_bytes=48 << 20),
        name="sort_upstream",
    )(label, routes.reshape(blocks, 1, length), rows)
    return pieces, slots


def after_attention_kernel(slot_ref, attended_ref, tokens_ref, weight_ref, gain_ref, residual_ref, *piece_refs):
    for block in range(slot_ref.shape[0]):
        mixed = jnp.dot(attended_ref[block], weight_ref[...], preferred_element_type=jnp.float32)
        residual = tokens_ref[block].astype(jnp.float32) + mixed
        residual_ref[block] = residual
        router_in = (residual * norm_scale_rows(residual) * gain_ref[...]).astype(jnp.bfloat16)
        sort_into(piece_refs, block, slot_ref[block], router_in)


def after_attention(slots, attended, tokens, weight, gain, owners, earlier):
    blocks, length, width = tokens.shape
    count = blocks * length // 2
    parts = 2 if earlier else 1
    residual, *pieces = pl.pallas_call(
        lambda *refs: after_attention_kernel(*refs[:5], *refs[5 + len(earlier) :]),
        grid=(1,),
        in_specs=[
            one_step(slots.shape), one_step(tokens.shape), one_step(tokens.shape), one_step(weight.shape), one_step((1, width))
        ]
        + [pl.BlockSpec(memory_space=pl.ANY)] * len(earlier),
        out_specs=[one_step(tokens.shape)] + [one_step((count, width))] * owners,
        out_shape=[jax.ShapeDtypeStruct(tokens.shape, jnp.float32)]
        + [jax.ShapeDtypeStruct((parts * count, width), jnp.bfloat16)] * owners,
        input_output_aliases={5 + at: 1 + at for at in range(len(earlier))},
        compiler_params=pltpu.CompilerParams(vmem_limit_bytes=48 << 20),
        name="after_attention",
    )(slots, attended, tokens, weight, gain[None], *earlier)
    return residual, pieces


def before_attention_kernel(owners, earlier, slot_ref, *refs):
    piece_refs = refs[:owners]
    residual_ref, upstream_ref, attended_ref, weight_ref, gain_ref = refs[owners : owners + 5]
    residual_grad_ref, mixed_grad_ref, weight_grad_ref, gain_grad_ref = refs[-4:]
    blocks, _, length = slot_ref.shape
    capacity = length // 2
    weight_grad, gain_grad = (refs[-6][...], refs[-5][...]) if earlier else (0.0, 0.0)
    for block in range(blocks):
        slot = jnp.broadcast_to(slot_ref[block].astype(jnp.float32), (128, length)).T[:, :1].astype(jnp.int32)
        place = lax.broadcasted_iota(jnp.int32, (length, owners * capacity), 1)
        matrix = (place == slot).astype(jnp.float32).astype(jnp.bfloat16)
        rows = jnp.concatenate([ref[block * capacity : (block + 1) * capacity, :] for ref in piece_refs])
        grad = jnp.dot(matrix, rows, preferred_element_type=jnp.float32)
        residual = residual_ref[block]
        scale = norm_scale_rows(residual)
        normed = residual * scale
        scaled = grad * gain_ref[...]
        shrink = jnp.mean(scaled * normed, axis=-1, keepdims=True)
        gain_grad += jnp.sum(grad * normed, axis=0, keepdims=True)
        residual_grad = upstream_ref[block].astype(jnp.float32) + scale * (scaled - normed * shrink)
        residual_grad_ref[block] = residual_grad
        low = residual_grad.astype(jnp.bfloat16)
        mixed_grad = lax.dot_general(low, weight_ref[...], (((1,), (1,)), ((), ())), preferred_element_type=jnp.float32)
        mixed_grad_ref[block] = mixed_grad.astype(jnp.bfloat16)
        weight_grad += lax.dot_general(attended_ref[block], low, (((0,), (0,)), ((), ())), preferred_element_type=jnp.float32)
    weight_grad_ref[...] = weight_grad
    gain_grad_ref[...] = gain_grad


def before_attention(slots, pieces, residual, upstream, attended, weight, gain, group, group_count, earlier):
    blocks, length, width = residual.shape
    owners = len(pieces)
    rows = one_step(residual.shape)
    out_rows = pl.BlockSpec(residual.shape, lambda step: (group, 0, 0), pipeline_mode=pl.Buffered(1))
    sums = [one_step((width, width)), one_step((1, width))]
    shape = (group_count * blocks, length, width)
    return pl.pallas_call(
        lambda *refs: before_attention_kernel(owners, bool(earlier), *refs),
        grid=(1,),
        in_specs=[one_step(slots.shape)] + [one_step(pieces[0].shape)] * owners
        + [rows, rows, rows, one_step((width, width)), one_step((1, width))]
        + ([pl.BlockSpec(memory_space=pl.ANY)] * 2 + sums if earlier else []),
        out_specs=[out_rows, out_rows] + sums,
        out_shape=[
            jax.ShapeDtypeStruct(shape, jnp.float32),
            jax.ShapeDtypeStruct(shape, jnp.bfloat16),
            jax.ShapeDtypeStruct((width, width), jnp.float32),
            jax.ShapeDtypeStruct((1, width), jnp.float32),
        ],
        input_output_aliases={owners + 6: 0, owners + 7: 1} if earlier else {},
        compiler_params=pltpu.CompilerParams(vmem_limit_bytes=56 << 20),
        name="before_attention",
    )(slots, *pieces, residual, upstream, attended, weight, gain[None], *earlier)


def exchange(pieces, axis, sign, size=None, skipped=0):
    size = size or lax.axis_size(axis)
    return [pieces[0]] + [
        lax.ppermute(piece, axis, [(at, (at + sign * turn) % size) for at in range(size)])
        for turn, piece in enumerate(pieces[1:], 1 + skipped)
    ]


def own_and_other(blocks):
    at = lax.axis_index("ctx")
    own = lax.dynamic_index_in_dim(blocks, at, 0)
    other = lax.dynamic_index_in_dim(blocks, 1 - at, 0)
    return [own, lax.ppermute(other, "ctx", [(0, 1), (1, 0)])]


def hand_back_kernel(core_ref, own_ref, arrived_ref, out_ref):
    out_ref[...] = jnp.where(pl.program_id(0) == 0, own_ref[...], arrived_ref[...])


def hand_back(own, other):
    arrived = lax.ppermute(other, "ctx", [(0, 1), (1, 0)])
    core = lax.axis_index("ctx").astype(jnp.int32).reshape(1)
    _, length, width = own.shape
    block = (1, QB, width)
    last = length // QB - 1
    return pl.pallas_call(
        hand_back_kernel,
        grid_spec=pltpu.PrefetchScalarGridSpec(
            num_scalar_prefetch=1,
            grid=(2, length // QB),
            in_specs=[
                pl.BlockSpec(block, lambda side, row, core: (0, jnp.where(side == 0, row, last), 0)),
                pl.BlockSpec(block, lambda side, row, core: (0, jnp.where(side == 0, 0, row), 0)),
            ],
            out_specs=pl.BlockSpec(block, lambda side, row, core: (side ^ core[0], row, 0)),
        ),
        out_shape=jax.ShapeDtypeStruct((2, length, width), own.dtype),
        name="hand_back",
    )(core, own, arrived)


def layer_output_kernel(groups, owners, *refs):
    slot_refs, residual_refs = refs[:groups], refs[groups : 2 * groups]
    piece_refs = refs[2 * groups : 2 * groups + owners]
    blocks, _, length = slot_refs[0].shape
    capacity = length // 2
    for group in range(groups):
        for block in range(blocks):
            at = group * blocks + block
            matrix = sort_matrix(slot_refs[group][block], owners * capacity)
            rows = jnp.concatenate([ref[at * capacity : (at + 1) * capacity, :] for ref in piece_refs])
            moved = lax.dot_general(matrix, rows, (((0,), (0,)), ((), ())), preferred_element_type=jnp.float32)
            refs[len(refs) - groups + group][block] = (residual_refs[group][block] + moved).astype(jnp.bfloat16)


def layer_output(slots, residuals, pieces):
    blocks, length, width = residuals[0].shape
    vmem = pl.BlockSpec(memory_space=pltpu.VMEM)
    return pl.pallas_call(
        lambda *refs: layer_output_kernel(len(slots), len(pieces), *refs),
        in_specs=[vmem] * (2 * len(slots) + len(pieces)),
        out_specs=[vmem] * len(slots),
        out_shape=[jax.ShapeDtypeStruct((blocks, length, width), jnp.bfloat16)] * len(slots),
        compiler_params=pltpu.CompilerParams(vmem_limit_bytes=48 << 20),
        name="layer_output",
    )(*slots, *residuals, *pieces)


def weight_outputs_kernel(place_ref, *refs):
    shard_refs, weight_refs, gain_ref = refs[:4], refs[4:7], refs[7]
    out_refs, output_ref, gain_grad_ref, small_ref = refs[8:11], refs[11], refs[12], refs[13]
    whole_refs = refs[14:]
    width = gain_ref.shape[1]
    half = width // 2
    for side in range(2):
        planes, rows, _ = shard_refs[2 * side].shape
        for turn in range(planes):
            for other in range(2):
                shard = (place_ref[0] ^ turn) * 2 + (place_ref[1] ^ other)
                start = pl.multiple_of(shard * rows, 16)
                whole_refs[side][pl.ds(start, rows), :] = shard_refs[2 * side + other][turn]
    total = 0.0
    for kind in range(3):
        for side, ref in enumerate(whole_refs):
            columns = slice(side * half, (side + 1) * half)
            grad = ref[kind * width : (kind + 1) * width, :].astype(jnp.float32)
            out_refs[kind][:, columns] = grad
            total += jnp.sum(grad * weight_refs[kind][:, columns].astype(jnp.float32), axis=1, keepdims=True)
    total = jnp.broadcast_to(total, (width, 128)).T
    gain_grad_ref[...] = total[:1] / gain_ref[...]
    start = 3 * width + 128
    for side in range(2):
        rows = slice(start + side * width, start + (side + 1) * width)
        output_ref[:, side * half : (side + 1) * half] = whole_refs[0][rows, :].astype(jnp.float32)
    for at, (ref, first) in enumerate(((whole_refs[0], 3 * width), (whole_refs[1], 3 * width), (whole_refs[0], start + 2 * width))):
        small_ref[at] = ref[first : first + 128, :].astype(jnp.float32)


def weight_outputs(shards, weights, gain):
    width = gain.shape[0]
    vmem = pl.BlockSpec(memory_space=pltpu.VMEM)
    place = jnp.stack([lax.axis_index("dp"), lax.axis_index("ctx")]).astype(jnp.int32)
    matrix = jax.ShapeDtypeStruct((width, width), jnp.float32)
    return pl.pallas_call(
        weight_outputs_kernel,
        in_specs=[pl.BlockSpec(memory_space=pltpu.SMEM)] + [vmem] * 8,
        out_specs=[vmem] * 6,
        out_shape=[matrix] * 4
        + [jax.ShapeDtypeStruct((1, width), jnp.float32), jax.ShapeDtypeStruct((3, 128, width // 2), jnp.float32)],
        scratch_shapes=[
            pltpu.VMEM((2 * part.shape[0] * part.shape[1], width // 2), jnp.bfloat16) for part in (shards[0], shards[2])
        ],
        compiler_params=pltpu.CompilerParams(vmem_limit_bytes=56 << 20),
        name="weight_outputs",
    )(place, *shards, *weights, gain[None])


def halves(rows, tile, width):
    steps = rows // tile
    first = pl.BlockSpec((tile, width), lambda step: (jnp.minimum(step, steps - 1), 0))
    second = pl.BlockSpec((tile, width), lambda step: (jnp.maximum(step - steps, 0), 0))
    return [first, second], lambda first_ref, second_ref: jnp.where(pl.program_id(0) < steps, first_ref[...], second_ref[...])


def projections_kernel(choose, first_ref, second_ref, gain_ref, *refs):
    weight_refs, out_refs, turned_ref = refs[:3], refs[3:6], refs[6]
    rows = choose(first_ref, second_ref).astype(jnp.float32)
    low = (rows * norm_scale_rows(rows) * gain_ref[...]).astype(jnp.bfloat16)
    for weight_ref, out_ref in zip(weight_refs, out_refs):
        out_ref[...] = jnp.dot(low, weight_ref[...], preferred_element_type=jnp.float32).astype(jnp.bfloat16)
    turned_ref[...] = low.T


def projections_of(first, second, gain, weights):
    rows, width = first.shape
    tile = min(QB, rows)
    specs, choose = halves(rows, tile, width)
    out = jax.ShapeDtypeStruct((2 * rows, width), jnp.bfloat16)
    return pl.pallas_call(
        lambda *refs: projections_kernel(choose, *refs),
        grid=(2 * rows // tile,),
        in_specs=specs + [one_step((1, width))] + [one_step((width, width))] * 3,
        out_specs=[pl.BlockSpec((tile, width), lambda step: (step, 0))] * 3
        + [pl.BlockSpec((width, tile), lambda step: (0, step))],
        out_shape=[out] * 3 + [jax.ShapeDtypeStruct((width, 2 * rows), jnp.bfloat16)],
        compiler_params=pltpu.CompilerParams(vmem_limit_bytes=48 << 20),
        cost_estimate=pl.CostEstimate(flops=64 * rows * width * width, bytes_accessed=16 * rows * width, transcendentals=0),
        name="projections",
    )(first, second, gain[None], *weights)


def token_grads_kernel(choose, first_ref, second_ref, *refs):
    weight_refs, (own_ref, other_ref, residual_grad_ref, gain_ref, *out_refs) = refs[:3], refs[3:]
    grad = 0.0
    for kind in range(3):
        low = jnp.concatenate([first_ref[kind], second_ref[kind]], axis=1)
        grad += lax.dot_general(low, weight_refs[kind][...], (((1,), (1,)), ((), ())), preferred_element_type=jnp.float32)
    rows = choose(own_ref, other_ref).astype(jnp.float32)
    scale = norm_scale_rows(rows)
    normed = rows * scale
    scaled = grad * gain_ref[...]
    shrink = jnp.mean(scaled * normed, axis=-1, keepdims=True)
    out = residual_grad_ref[...] + scale * (scaled - normed * shrink)
    half = pl.num_programs(0) // 2

    @pl.when(pl.program_id(0) < half)
    def _():
        out_refs[0][...] = out

    @pl.when(pl.program_id(0) >= half)
    def _():
        out_refs[1][...] = out


def token_grads(first, second, weights, token_groups, residual_grad, gain):
    length, width = residual_grad.shape
    half = pl.BlockSpec((3, QB, width // 2), lambda step: (0, step, 0))
    rows = pl.BlockSpec((QB, width), lambda step: (step, 0))
    specs, choose = halves(length // 2, QB, width)
    return pl.pallas_call(
        lambda *refs: token_grads_kernel(choose, *refs),
        grid=(length // QB,),
        in_specs=[half, half] + [one_step((width, width))] * 3 + specs + [rows, one_step((1, width))],
        out_specs=specs,
        out_shape=[jax.ShapeDtypeStruct((length // 2, width), jnp.float32)] * 2,
        compiler_params=pltpu.CompilerParams(vmem_limit_bytes=48 << 20),
        cost_estimate=pl.CostEstimate(flops=6 * length * width * width, bytes_accessed=14 * length * width, transcendentals=0),
        name="token_grads",
    )(first, second, *weights, *token_groups, residual_grad, gain[None])


def norm_scale(value_rows):
    return lax.rsqrt(jnp.mean(value_rows * value_rows, axis=-1, keepdims=True) + norm_eps)


def norm_back(value_rows, scale, gain_vector, grad_rows):
    scaled = grad_rows * gain_vector
    shrink = jnp.mean(scaled * value_rows, axis=-1, keepdims=True) * scale * scale * scale
    return scale * scaled - value_rows * shrink, jnp.sum(grad_rows * value_rows * scale, axis=(0, 1))


def wide_dot(rows, weight):
    return jnp.einsum("sxd,de->sxe", rows, weight, preferred_element_type=jnp.float32)


def wide_dot_back(rows, weight):
    return jnp.einsum("sxe,de->sxd", rows, weight, preferred_element_type=jnp.float32)


def weight_dot(left, right):
    return jnp.einsum("sxd,sxe->de", left, right, preferred_element_type=jnp.float32)


def pack_sums(matrices, small=None):
    parts = [matrix.astype(jnp.bfloat16) for matrix in matrices]
    if small is not None:
        small = jnp.pad(small, ((0, -small.shape[0] % 64), (0, parts[0].shape[1] - small.shape[1])))
        high = small.astype(jnp.bfloat16)
        parts += [high, (small - high.astype(jnp.float32)).astype(jnp.bfloat16)]
    return jnp.concatenate(parts)


def add_low(*parts):
    return sum(part.astype(jnp.float32) for part in parts).astype(jnp.bfloat16)


def swap(part, axis, turn):
    return lax.ppermute(part, axis, [(to, to ^ turn) for to in range(lax.axis_size(axis))])


class Summing:
    def __init__(self, packed):
        self.core, self.plane = lax.axis_index("ctx"), lax.axis_index("dp")
        self.planes = lax.axis_size("dp")
        self.part = packed.reshape(self.planes, 2, -1, packed.shape[1])
        self.step = 0

    def sends(self):
        if self.step == 0:
            return [lax.dynamic_index_in_dim(self.part, 1 - self.core, 1, keepdims=False)]
        if self.step == 1:
            return [
                lax.dynamic_index_in_dim(self.part, self.plane ^ turn, 0, keepdims=False)
                for turn in range(1, self.planes)
            ]
        return [self.part] * (self.planes - 1 if self.step == 4 else 1)

    def move(self, sent):
        axis, first = (("ctx", 1), ("dp", 1), ("expert", 1), ("expert", 2), ("dp", 1), ("ctx", 1))[self.step]
        return [swap(part, axis, first + at) for at, part in enumerate(sent)]

    def take(self, arrived):
        if self.step == 0:
            self.part = lax.dynamic_index_in_dim(self.part, self.core, 1, keepdims=False)
        elif self.step == 1:
            self.part = lax.dynamic_index_in_dim(self.part, self.plane, 0, keepdims=False)
        if self.step < 4:
            self.part = add_low(self.part, *arrived)
        elif self.step == 4:
            self.part = jnp.stack([self.part] + arrived)
        else:
            self.part = (self.part, arrived[0])
        self.step += 1


def matrix_of(sums, index, rows):
    return sums[index * rows : (index + 1) * rows]


def small_of(sums, start):
    high, low = jnp.split(sums[start:].astype(jnp.float32), 2)
    return high + low


def per_device(
    tokens,
    cotangent,
    routes,
    norm1_gain,
    query_weight,
    key_weight,
    value_weight,
    output_weight,
    bias_table,
    norm2_gain,
    router_weight,
    w_in,
    w_out,
):
    seq_count, local_len, model_width = tokens.shape
    owners = lax.axis_size("expert")
    capacity = local_len // 2
    whole_seq = seq_count == 2 and lax.axis_size("ctx") == 2 and local_len % QB == 0
    split = own_and_other if whole_seq else lambda blocks: [blocks]
    routes, cotangent, token_groups = split(routes), split(cotangent), split(tokens)
    groups = range(len(routes))
    core = lax.axis_index("ctx").astype(jnp.int32).reshape(1)
    label = lax.axis_index("expert").astype(jnp.int32).reshape(1)
    together = lax.optimization_barrier

    sorted_upstream, slots = zip(
        *[
            sort_upstream(label, routes[group], cotangent[group], owners, group, 1 + group)
            for group in groups
        ]
    )
    sorted_first, token_groups = together((sorted_upstream[0], token_groups))
    upstream = [exchange(sorted_first, "expert", 1)]
    projections = (query_weight, key_weight, value_weight)
    token_rows = [rows.reshape(-1, model_width) for rows in (token_groups if whole_seq else jnp.split(tokens, 2))]
    queries, keys, values, turned = projections_of(*token_rows, norm1_gain, projections)
    if whole_seq:
        lines = bias_lines(bias_table)
        flat = (seq_count * local_len, model_width)
        qkv = [queries, keys, values]
    else:
        queries, keys, values = (rows.reshape(tokens.shape) for rows in (queries, keys, values))
        first_pos = lax.axis_index("ctx") * local_len
        keys = lax.all_gather(keys, "ctx", axis=1, tiled=True)
        values = lax.all_gather(values, "ctx", axis=1, tiled=True)
        buckets = bucket_grid(first_pos, local_len, keys.shape[1])
        attended, log_totals = attend_rows(queries, keys, values, buckets, bias_table, DH)
    attended_groups, residual1, arrived = [], [], []
    if whole_seq:
        log_totals = []
    in_flight, fed = upstream[0], queries.reshape(-1, model_width)
    for at, group in enumerate(groups):
        if whole_seq:
            rows, totals = attend(core, fed, *qkv[1:], lines, at * local_len, local_len)
            rows = rows[None]
            log_totals.append(totals)
        else:
            rows = attended.astype(jnp.bfloat16)
        attended_groups.append(rows)
        earlier = sorted_upstream[at] if at else []
        residual, sorted_rows = after_attention(
            slots[at], rows, token_groups[at], output_weight, norm2_gain, owners, earlier
        )
        residual1.append(residual)
        sorted_rows, fed, in_flight = together((sorted_rows, fed, in_flight))
        if at == 0:
            upstream[0] = in_flight
        else:
            arrived[-1] = in_flight
        in_flight = exchange(sorted_rows, "expert", 1)
        arrived.append(in_flight)
    router_wide = jnp.pad(router_weight, ((0, 0), (0, 128 - router_weight.shape[1])))
    done, back = [], []
    tile = seq_count // len(groups) * local_len // 2
    for at in groups:
        rows, grads = arrived[at], upstream[0] if at == 0 else arrived[at]
        earlier = done[-1][0] if done else []
        result = run_expert(
            label, rows, grads, tile, min(at, 1), router_wide, w_in[0], w_out[0], at, len(groups), earlier
        )
        if at + 1 < len(arrived):
            result, arrived[at + 1] = together((result, arrived[at + 1]))
        if whole_seq and at == 0:
            seen = (jnp.concatenate(attended_groups).reshape(flat), jnp.concatenate(log_totals, axis=2), turned)
            result, seen = together((result, seen))
        leaving = result[1]
        if back:
            result, back[-1] = together((result, back[-1]))
        done.append(result)
        back.append(exchange(leaving, "expert", -1))
    rows_out = done[-1][0]
    grad_rows, hiddens, pre_grads, grad_router = zip(*[item[2] for item in done])
    grad_router = sum(grad_router)[:, : router_weight.shape[1]].T
    grad_experts = expert_grads(sum(arrived, []), grad_rows, hiddens, pre_grads)

    def back_to_attention(group, earlier):
        return before_attention(
            slots[group], back[group], residual1[group], cotangent[group], attended_groups[group],
            output_weight, norm2_gain, group, len(groups), earlier,
        )

    backward = back_to_attention(0, ())
    grad_experts, back[-1], rows_out, backward, grad_router = together(
        (grad_experts, back[-1], rows_out, backward, grad_router)
    )
    grad_experts = lax.psum_scatter(grad_experts, ("dp", "ctx"), scatter_dimension=0, tiled=True)
    if not whole_seq:
        returned = exchange(list(rows_out), "expert", -1)
    for group in groups[1:]:
        backward = back_to_attention(group, backward)
    residual_grad, mixed_grad, grad_w_output, grad_norm2 = backward
    early_small = jnp.concatenate([grad_router, grad_norm2])
    if whole_seq:
        half = model_width // 2
        pairs = half // 128
        mixed_grad = mixed_grad.reshape(flat)
        returned = exchange(list(rows_out[:-1]), "expert", -1, owners)
        first = attend_back(core, *qkv, mixed_grad, *seen, lines, 0, pairs, pairs)
        first, returned, last_rows = together((first, returned, rows_out[-1]))
        returned.append(exchange([None, last_rows], "expert", -1, owners, owners - 2)[1])
        first_grads, first_sums = first
        matrices = [first_sums, grad_w_output[:, :half], grad_w_output[:, half:]]
        early = Summing(pack_sums(matrices, early_small.reshape(-1, half)))
        second = ()
        for at in range(pairs, 2 * pairs):
            sent, mixed_grad = together((early.sends(), mixed_grad))
            moved = early.move(sent)
            second = attend_back(core, *qkv, mixed_grad, *seen, lines, at, 1, pairs, second)
            if at == pairs + 1:
                second, moved, returned = together((second, moved, returned))
            else:
                second, moved = together((second, moved))
            early.take(moved)
        (second_grads, second_sums), grad_experts = together((second, grad_experts))
        late = Summing(second_sums)
        sent, sent_late, returned = together((early.sends(), late.sends(), returned))
        moved, moved_late = early.move(sent), late.move(sent_late)
        block_out = layer_output(slots, residual1, returned)
        moved_late, block_out = together((moved_late, block_out))
        late.take(moved_late)
        sent_late, second_grads = together((late.sends(), second_grads))
        moved_late = late.move(sent_late)
        d_tokens = token_grads(
            first_grads, second_grads, projections, token_rows, residual_grad.reshape(flat), norm1_gain
        )
        moved, moved_late, d_tokens = together((moved, moved_late, d_tokens))
        early.take(moved)
        late.take(moved_late)
        sent, sent_late = together((early.sends(), late.sends()))
        moved = early.move(sent)
        late.take(late.move(sent_late))
        moved, moved_late = together((moved, late.move(late.sends())))
        early.take(moved)
        late.take(moved_late)
        sent, sent_late = together((early.sends(), late.sends()))
        moved, moved_late = together((early.move(sent), late.move(sent_late)))
        early.take(moved)
        late.take(moved_late)
        late.take(late.move(late.sends()))
        *grad_qkv, grad_w_output, grad_norm1, smalls = weight_outputs(early.part + late.part, projections, norm1_gain)
        grad_norm1 = grad_norm1[0]
        small = (smalls[2, :64] + smalls[2, 64:]).reshape(-1, model_width)
        grad_bias = jnp.concatenate([smalls[0, :4], smalls[1, :4]], axis=1)
        grad_bias = (grad_bias[:2] + grad_bias[2:]).reshape(2, -1, 128).swapaxes(0, 1).reshape(-1, 128)
    else:
        query_grad, _, diag_grad, key_part, value_part = attend_back_rows(
            queries, keys, values, mixed_grad, log_totals, buckets, bias_table, DH
        )
        low_parts = [query_grad.astype(jnp.bfloat16)] + [
            lax.psum_scatter(part, "ctx", scatter_dimension=1, tiled=True).astype(jnp.bfloat16)
            for part in (key_part, value_part)
        ]
        inputs = tokens.astype(jnp.float32)
        attn_in = turned.T.reshape(tokens.shape)
        norm_in_grad = sum(wide_dot_back(*pair) for pair in zip(low_parts, projections))
        sums = lax.psum(
            pack_sums([grad_w_output] + [weight_dot(attn_in, rows) for rows in low_parts], early_small),
            ("dp", "ctx", "expert"),
        )
        grad_bias = lax.psum(diag_grad, ("dp", "ctx", "expert"))
        grad_w_output, *grad_qkv = (matrix_of(sums, kind, model_width).astype(jnp.float32) for kind in range(4))
        small = small_of(sums, 4 * model_width)
        norm1_back, grad_norm1 = norm_back(inputs, norm_scale(inputs), norm1_gain, norm_in_grad)
        grad_norm1 = lax.psum(grad_norm1, ("dp", "ctx", "expert"))
    grad_bias = grad_bias[: bias_table.shape[1], : bias_table.shape[0]].T
    grad_w_query, grad_w_key, grad_w_value = grad_qkv
    grad_w_output = grad_w_output.astype(jnp.float32)
    experts = router_weight.shape[1]
    grad_router, grad_norm2 = small[:experts, :].T, small[experts]
    if not whole_seq:
        block_out = layer_output(slots, residual1, returned)[0]
        d_tokens = residual_grad + norm1_back
    if whole_seq:
        block_out, d_tokens = hand_back(*block_out), hand_back(*[rows[None] for rows in d_tokens])
    grad_experts = grad_experts.astype(jnp.float32)
    return (
        block_out,
        d_tokens,
        grad_norm1,
        grad_w_query,
        grad_w_key,
        grad_w_value,
        grad_w_output,
        grad_bias,
        grad_norm2,
        grad_router,
        grad_experts[:, :model_width].T[None],
        grad_experts[:, model_width:][None],
    )


def solution(mesh):
    rows = P(("dp", "expert"), "ctx", None)
    in_specs = (rows, rows, P(("dp", "expert"), "ctx")) + (P(),) * 8 + (P("expert", None, None),) * 2
    out_specs = (rows, rows) + (P(),) * 8 + (P("expert", None, ("dp", "ctx")), P("expert", ("dp", "ctx"), None))
    return jax.shard_map(per_device, mesh=mesh, in_specs=in_specs, out_specs=out_specs, check_vma=False)
```

```python
import jax
import jax.numpy as jnp
import numpy as np
from jax import lax
from jax.experimental import pallas as pl
from jax.experimental.pallas import tpu as pltpu
from jax.sharding import PartitionSpec as P

DH = 64
QB = 256

bucket_edges = (1, 2, 3, 4, 5, 6, 7, 8, 12, 16, 23, 32, 46, 64, 91)
norm_eps = 1e-06
precise_result = lax.Precision.HIGHEST


def bucket_of(relative):
    distance = jnp.abs(relative)
    half_bucket = jnp.zeros(relative.shape, jnp.int32)
    for threshold in bucket_edges:
        half_bucket = half_bucket + (distance >= threshold).astype(jnp.int32)
    return half_bucket + 16 * (relative > 0).astype(jnp.int32)


def bucket_grid(row_start, row_count, col_count):
    row_pos = row_start + jnp.arange(row_count, dtype=jnp.int32)
    col_pos = jnp.arange(col_count, dtype=jnp.int32)
    return bucket_of(col_pos[None, :] - row_pos[:, None])


def bias_grid(buckets, table_column, bucket_count):
    result = jnp.zeros(buckets.shape, jnp.float32)
    for label in range(bucket_count):
        result = result + jnp.where(buckets == label, table_column[label], 0.0)
    return result


def fold_buckets(buckets, grad_sum, bucket_count):
    return jnp.stack(
        [jnp.sum(jnp.where(buckets == label, grad_sum, 0.0)) for label in range(bucket_count)]
    )


def head_slice(value_rows, head_index, head_size):
    return lax.dynamic_slice_in_dim(value_rows, head_index * head_size, head_size, 2)


def put_head(target, portion, head_index, head_size):
    return lax.dynamic_update_slice_in_dim(target, portion, head_index * head_size, 2)


def head_scores(q_head, k_head, buckets, bias_table, head_index):
    table_column = lax.dynamic_index_in_dim(bias_table, head_index, 1, keepdims=False)
    scores = jnp.einsum("sqd,skd->sqk", q_head, k_head, preferred_element_type=jnp.float32)
    return scores + bias_grid(buckets, table_column, bias_table.shape[0])[None]


def attend_rows(query_matrix, keys_whole, values_whole, buckets, bias_table, head_size):
    seq_count, row_count, feature_width = query_matrix.shape
    head_count = feature_width // head_size

    def one_head(head_index, running):
        attention_result, log_totals = running
        scores = head_scores(
            head_slice(query_matrix, head_index, head_size),
            head_slice(keys_whole, head_index, head_size),
            buckets,
            bias_table,
            head_index,
        )
        row_max = jnp.max(scores, axis=-1, keepdims=True)
        log_total = row_max + jnp.log(jnp.sum(jnp.exp(scores - row_max), axis=-1, keepdims=True))
        weights_low = jnp.exp(scores - log_total).astype(jnp.bfloat16)
        portion = jnp.einsum(
            "sqk,skd->sqd",
            weights_low,
            head_slice(values_whole, head_index, head_size),
            preferred_element_type=jnp.float32,
        )
        attention_result = put_head(attention_result, portion, head_index, head_size)
        log_totals = lax.dynamic_update_index_in_dim(log_totals, log_total[..., 0], head_index, 0)
        return (attention_result, log_totals)

    initial = (
        jnp.zeros((seq_count, row_count, feature_width), jnp.float32),
        jnp.zeros((head_count, seq_count, row_count), jnp.float32),
    )
    return lax.fori_loop(0, head_count, one_head, initial)


def attend_back_rows(
    query_matrix, keys_whole, values_whole, mixed_grad, log_totals, buckets, bias_table, head_size
):
    seq_count, row_count, feature_width = query_matrix.shape
    col_count = keys_whole.shape[1]
    head_count = feature_width // head_size
    bucket_count = bias_table.shape[0]

    def one_head(head_index, running):
        query_grad, deltas, diag_grad, key_part, value_part = running
        q_head = head_slice(query_matrix, head_index, head_size)
        k_head = head_slice(keys_whole, head_index, head_size)
        v_head = head_slice(values_whole, head_index, head_size)
        g_head = head_slice(mixed_grad, head_index, head_size)
        scores = head_scores(q_head, k_head, buckets, bias_table, head_index)
        weights = jnp.exp(scores - log_totals[head_index][..., None])
        weight_grad = jnp.einsum("sqd,skd->sqk", g_head, v_head, preferred_element_type=jnp.float32)
        delta_row = jnp.sum(weights * weight_grad, axis=-1)
        score_grad = (weights * (weight_grad - delta_row[..., None])).astype(jnp.bfloat16)
        query_grad = put_head(
            query_grad,
            jnp.einsum("sqk,skd->sqd", score_grad, k_head, preferred_element_type=jnp.float32),
            head_index,
            head_size,
        )
        deltas = lax.dynamic_update_index_in_dim(deltas, delta_row, head_index, 0)
        folded = fold_buckets(
            buckets, jnp.sum(score_grad.astype(jnp.float32), axis=0), bucket_count
        )
        diag_grad = lax.dynamic_update_index_in_dim(diag_grad, folded, head_index, 0)
        key_part = put_head(
            key_part,
            jnp.einsum("sqk,sqd->skd", score_grad, q_head, preferred_element_type=jnp.float32),
            head_index,
            head_size,
        )
        value_part = put_head(
            value_part,
            jnp.einsum(
                "sqk,sqd->skd",
                weights.astype(jnp.bfloat16),
                g_head,
                preferred_element_type=jnp.float32,
            ),
            head_index,
            head_size,
        )
        return (query_grad, deltas, diag_grad, key_part, value_part)

    key_shape = (seq_count, col_count, feature_width)
    initial = (
        jnp.zeros((seq_count, row_count, feature_width), jnp.float32),
        jnp.zeros((head_count, seq_count, row_count), jnp.float32),
        jnp.zeros((head_count, bucket_count), jnp.float32),
        jnp.zeros(key_shape, jnp.float32),
        jnp.zeros(key_shape, jnp.float32),
    )
    return lax.fori_loop(0, head_count, one_head, initial)


def bucket_np(relative):
    half_bucket = np.zeros(relative.shape, np.int32)
    for threshold in bucket_edges:
        half_bucket = half_bucket + (np.abs(relative) >= threshold)
    return half_bucket + 16 * (relative > 0)


def bias_lines(bias_table):
    lane = np.arange(4 * QB)
    both = np.stack([lane - 2 * QB, 2 * QB - lane])
    onehot = (bucket_np(both)[..., None] == np.arange(32)).astype(np.float32)
    return jnp.einsum("lcb,bh->hlc", jnp.asarray(onehot), bias_table, precision=lax.Precision.HIGHEST)

def tile_index(i, j, n, core):
    half = n // 2
    if i // half == j // half:
        return max(-2, min(2, j - i)) + 2
    return jnp.clip(j - i - n * core * (1 if i < j else -1), -2, 2) + 2


def fwd_kernel(first, core_ref, lines_ref, q_ref, k_ref, v_ref, o_ref, total_ref, band_ref):
    n = k_ref.shape[0] // QB
    lane = lax.broadcasted_iota(jnp.int32, (QB, 128), 1)
    for h in range(2):
        line = lines_ref[h, 0:1, :]
        spread = pltpu.roll(jnp.broadcast_to(line, (QB, 4 * QB)), 0, 1, stride=1, stride_axis=0)
        band_ref[h, 0] = jnp.broadcast_to(line[:, :1], (QB, QB))
        for t in range(3):
            band_ref[h, 1 + t] = spread[:, (1 + t) * QB:(2 + t) * QB]
        band_ref[h, 4] = jnp.broadcast_to(line[:, 4 * QB - 1:], (QB, QB))
    for i in range(first, first + q_ref.shape[0] // QB):
        rows = slice((i - first) * QB, (i - first + 1) * QB)
        outs = []
        for h in range(2):
            q = jnp.where((lane < 64) == (h == 0), q_ref[rows, :], 0)
            s = lax.dot_general(q, k_ref[...], (((1,), (1,)), ((), ())), preferred_element_type=jnp.float32)
            parts = []
            for j in range(n):
                parts.append(s[:, j * QB:(j + 1) * QB] + band_ref[h, tile_index(i, j, n, core_ref[0])])
            s = jnp.concatenate(parts, axis=1)
            m = jnp.max(s, axis=1, keepdims=True)
            p = jnp.exp(s - m)
            l = jnp.sum(p, axis=1, keepdims=True)
            o = jnp.dot(p.astype(jnp.bfloat16), v_ref[...], preferred_element_type=jnp.float32)
            outs.append(o * (1.0 / l))
            total = jnp.broadcast_to(m + jnp.log(l), (QB, 128)).T
            total_ref[0, h:h + 1, rows] = total[:1]
        o_ref[rows, :] = jnp.where(lane < 64, outs[0], outs[1]).astype(jnp.bfloat16)

def attend(core, q, k, v, lines, first, count):
    length, width = q.shape
    col = pl.BlockSpec((length, 128), lambda h: (0, h))
    span = pl.BlockSpec((count, 128), lambda h: (first // count, h))
    return pl.pallas_call(
        lambda *refs: fwd_kernel(first // QB, *refs),
        grid=(width // 128,),
        in_specs=[pl.BlockSpec(memory_space=pltpu.SMEM), pl.BlockSpec((2, 2, 4 * QB), lambda h: (h, 0, 0)), span, col, col],
        out_specs=[pl.BlockSpec((count, 128), lambda h: (0, h)), pl.BlockSpec((1, 2, count), lambda h: (h, 0, 0))],
        out_shape=[
            jax.ShapeDtypeStruct((count, width), jnp.bfloat16),
            jax.ShapeDtypeStruct((width // 128, 2, count), jnp.float32),
        ],
        scratch_shapes=[pltpu.VMEM((2, 5, QB, QB), jnp.float32)],
        compiler_params=pltpu.CompilerParams(vmem_limit_bytes=48 << 20),
        cost_estimate=pl.CostEstimate(flops=count * length * width, bytes_accessed=2 * length * width, transcendentals=0),
        name="attend",
    )(core, lines, q, k, v)

def bwd_kernel(core_ref, lines_ref, fold_ref, q_ref, k_ref, v_ref, g_ref, o_ref, total_ref, xt_ref, grad_ref, sums_ref, band_ref, acc_ref, dk_acc, dv_acc):
    n = q_ref.shape[0] // QB
    lane = lax.broadcasted_iota(jnp.int32, (QB, 128), 1)
    for h in range(2):
        for t in range(3):
            start = 2 * QB - (t - 1) * QB - QB
            line = lines_ref[h, 1:2, start:start + 2 * QB]
            spread = pltpu.roll(jnp.broadcast_to(line, (QB, 2 * QB)), QB, 1, stride=1, stride_axis=0)
            band_ref[h, 1 + t] = spread[:, :QB]
        band_ref[h, 0] = jnp.broadcast_to(lines_ref[h, 0:1, 0:1], (QB, QB))
        band_ref[h, 4] = jnp.broadcast_to(lines_ref[h, 0:1, 4 * QB - 1:], (QB, QB))
    acc_ref[...] = jnp.zeros_like(acc_ref)
    for i in range(n):
        rows = slice(i * QB, (i + 1) * QB)
        grads = []
        for h in range(2):
            keep = (lane < 64) == (h == 0)
            q = jnp.where(keep, q_ref[rows, :], 0)
            g = jnp.where(keep, g_ref[rows, :], 0)
            s = lax.dot_general(k_ref[...], q, (((1,), (1,)), ((), ())), preferred_element_type=jnp.float32)
            parts = []
            for j in range(n):
                parts.append(s[j * QB:(j + 1) * QB, :] + band_ref[h, tile_index(i, j, n, core_ref[0])])
            s = jnp.concatenate(parts, axis=0)
            w = jnp.exp(s - total_ref[0, h:h + 1, rows])
            dp = lax.dot_general(v_ref[...], g, (((1,), (1,)), ((), ())), preferred_element_type=jnp.float32)
            delta = jnp.sum((g.astype(jnp.float32) * o_ref[rows, :].astype(jnp.float32)).T, axis=0, keepdims=True)
            ds = w * (dp - delta)
            for j in range(n):
                acc_ref[h, tile_index(i, j, n, core_ref[0])] += ds[j * QB:(j + 1) * QB, :]
            low = ds.astype(jnp.bfloat16)
            dv = jnp.dot(w.astype(jnp.bfloat16), g, preferred_element_type=jnp.float32)
            dk = jnp.dot(low, q, preferred_element_type=jnp.float32)
            if i == 0 and h == 0:
                dv_acc[...] = dv
                dk_acc[...] = dk
            else:
                dv_acc[...] += dv
                dk_acc[...] += dk
            grads.append(lax.dot_general(low, k_ref[...], (((0,), (0,)), ((), ())), preferred_element_type=jnp.float32))
        grad_ref[0, rows, :] = jnp.where(lane < 64, grads[0], grads[1]).astype(jnp.bfloat16)
    grad_ref[1] = dk_acc[...].astype(jnp.bfloat16)
    grad_ref[2] = dv_acc[...].astype(jnp.bfloat16)
    row = lax.broadcasted_iota(jnp.int32, (8, 2 * QB), 0)
    totals = []
    for h in range(2):
        total = jnp.zeros((8, 128), jnp.float32)
        for t in range(3):
            tile = acc_ref[h, 1 + t]
            wide = jnp.concatenate([tile, jnp.zeros_like(tile)], axis=1)
            moved = sum(pltpu.roll(wide[8 * e:8 * e + 8], QB - 8 * e, 1) for e in range(QB // 8))
            turned = jnp.where(row == 0, moved, 0.0)
            for e in range(1, 8):
                turned = turned + pltpu.roll(jnp.where(row == e, moved, 0.0), 2 * QB - e, 1)
            total = total + jnp.dot(turned, fold_ref[t], precision=lax.Precision.HIGHEST, preferred_element_type=jnp.float32)
        total = jnp.sum(total, axis=0, keepdims=True)
        ends = [jnp.sum(jnp.sum(acc_ref[h, side], axis=0, keepdims=True), axis=1, keepdims=True) for side in (0, 4)]
        column = lax.broadcasted_iota(jnp.int32, (1, 128), 1)
        total = total + jnp.where(column == 15, ends[0], 0.0) + jnp.where(column == 31, ends[1], 0.0)
        totals.append(total)
    width = xt_ref.shape[0]
    grads = jnp.concatenate([grad_ref[kind] for kind in range(3)], axis=1)
    weight = jnp.dot(xt_ref[...], grads, preferred_element_type=jnp.float32).astype(jnp.bfloat16)
    for kind in range(3):
        sums_ref[kind * width:(kind + 1) * width, :] = weight[:, kind * 128:(kind + 1) * 128]
    high = [total.astype(jnp.bfloat16).astype(jnp.float32) for total in totals]
    rows = high + [total - part for total, part in zip(totals, high)]
    small = jnp.concatenate(rows + [jnp.zeros((124, 128), jnp.float32)], axis=0)
    sums_ref[3 * width:, :] = small.astype(jnp.bfloat16)


def attend_back(core, q, k, v, g, o, totals, xt, lines, first_pair, pairs, total_pairs, earlier=()):
    length, width = q.shape
    rows = 3 * width + 128
    r = (np.arange(3)[:, None] - 1) * QB - (np.arange(2 * QB)[None] - QB)
    fold = (bucket_np(r)[..., None] == np.arange(128)).astype(np.float32)
    col = pl.BlockSpec((length, 128), lambda h: (0, h + first_pair))
    offset = first_pair % total_pairs
    return pl.pallas_call(
        lambda *refs: bwd_kernel(*refs[:10], *refs[10 + len(earlier):]),
        grid=(pairs,),
        in_specs=[
            pl.BlockSpec(memory_space=pltpu.SMEM),
            pl.BlockSpec((2, 2, 4 * QB), lambda h: (h + first_pair, 0, 0)),
            pl.BlockSpec((3, 2 * QB, 128), lambda h: (0, 0, 0)),
            col, col, col, col, col,
            pl.BlockSpec((1, 2, length), lambda h: (h + first_pair, 0, 0)),
            pl.BlockSpec((width, length), lambda h: (0, 0), pipeline_mode=pl.Buffered(1)),
        ]
        + [pl.BlockSpec(memory_space=pl.ANY)] * len(earlier),
        out_specs=[
            pl.BlockSpec((3, length, 128), lambda h: (0, 0, h + offset)),
            pl.BlockSpec((rows, 128), lambda h: (0, h + offset)),
        ],
        out_shape=[
            jax.ShapeDtypeStruct((3, length, 128 * total_pairs), jnp.bfloat16),
            jax.ShapeDtypeStruct((rows, 128 * total_pairs), jnp.bfloat16),
        ],
        scratch_shapes=[
            pltpu.VMEM((2, 5, QB, QB), jnp.float32),
            pltpu.VMEM((2, 5, QB, QB), jnp.float32),
            pltpu.VMEM((length, 128), jnp.float32),
            pltpu.VMEM((length, 128), jnp.float32),
        ],
        compiler_params=pltpu.CompilerParams(vmem_limit_bytes=60 << 20),
        cost_estimate=pl.CostEstimate(
            flops=84 * length * length * 128 * pairs, bytes_accessed=14 * length * 128 * pairs, transcendentals=2 * length * length * pairs
        ),
        input_output_aliases={10: 0, 11: 1} if earlier else {},
        name="attend_back",
    )(core, lines, jnp.asarray(fold), q, k, v, g, o, totals, xt, *earlier)


def expert_kernel(count, label_ref, *refs):
    x_refs, u_refs = refs[:count], refs[count : 2 * count]
    router_ref, win_ref, wout_ref = refs[2 * count : 2 * count + 3]
    rest = refs[len(refs) - 7 - 2 * count :]
    rows_refs, back_refs = rest[:count], rest[count : 2 * count]
    g_ref, hid_ref, pre_ref, drouter_ref, prob_ref, out_acc, back_acc = rest[2 * count :]
    step = pl.program_id(0)
    tile = x_refs[0].shape[0]
    lane = lax.broadcasted_iota(jnp.int32, (tile, 128), 1)
    own = lane == label_ref[0]
    spans = [slice(r * tile, (r + 1) * tile) for r in range(count)]

    @pl.when(step == 0)
    def _():
        for piece, rows in enumerate(spans):
            logits = jnp.dot(x_refs[piece][...], router_ref[...], preferred_element_type=jnp.float32)
            logits = jnp.where(lane < 4, logits, -jnp.inf)
            raised = jnp.exp(logits - jnp.max(logits, axis=1, keepdims=True))
            prob = raised / jnp.sum(raised, axis=1, keepdims=True)
            prob_ref[rows, :] = prob
            gate = jnp.sum(jnp.where(own, prob, 0.0), axis=1, keepdims=True)
            g_ref[rows, :] = (gate * u_refs[piece][...].astype(jnp.float32)).astype(jnp.bfloat16)
        out_acc[...] = jnp.zeros_like(out_acc)
        back_acc[...] = jnp.zeros_like(back_acc)

    for piece, rows in enumerate(spans):
        pre = jnp.dot(x_refs[piece][...], win_ref[...], preferred_element_type=jnp.float32)
        square = pre * pre
        turn = jnp.tanh(pre * (0.7978845608028654 + 0.035677408136300125 * square))
        half = 0.5 + 0.5 * turn
        hidden = (pre * half).astype(jnp.bfloat16)
        slope = half + pre * (half - half * half) * (1.5957691216057308 + 0.21406444881780074 * square)
        hid_ref[rows, :] = hidden
        out_acc[rows, :] += jnp.dot(hidden, wout_ref[...], preferred_element_type=jnp.float32)
        hidden_grad = lax.dot_general(g_ref[rows, :], wout_ref[...], (((1,), (1,)), ((), ())), preferred_element_type=jnp.float32)
        pre_grad = (hidden_grad * slope).astype(jnp.bfloat16)
        pre_ref[rows, :] = pre_grad
        back_acc[rows, :] += lax.dot_general(pre_grad, win_ref[...], (((1,), (1,)), ((), ())), preferred_element_type=jnp.float32)

    @pl.when(step == pl.num_programs(0) - 1)
    def _():
        total = jnp.zeros(drouter_ref.shape, jnp.float32)
        for piece, rows in enumerate(spans):
            prob = prob_ref[rows, :]
            gate = jnp.sum(jnp.where(own, prob, 0.0), axis=1, keepdims=True)
            out = out_acc[rows, :].astype(jnp.bfloat16).astype(jnp.float32)
            rows_refs[piece][...] = (gate * out).astype(jnp.bfloat16)
            gate_grad = jnp.sum(u_refs[piece][...].astype(jnp.float32) * out, axis=1, keepdims=True)
            logit_grad = prob * (jnp.where(own, gate_grad, 0.0) - gate * gate_grad)
            high = logit_grad.astype(jnp.bfloat16)
            low = (logit_grad - high.astype(jnp.float32)).astype(jnp.bfloat16)
            back = back_acc[rows, :].astype(jnp.bfloat16).astype(jnp.float32)
            for part in (high, low):
                back += lax.dot_general(part, router_ref[...], (((1,), (1,)), ((), ())), preferred_element_type=jnp.float32)
                total += lax.dot_general(x_refs[piece][...], part, (((0,), (0,)), ((), ())), preferred_element_type=jnp.float32)
            back_refs[piece][...] = back.astype(jnp.bfloat16)
        drouter_ref[...] = total


def run_expert(label, pieces, upstream_pieces, tile, upstream_part, router_wide, w_in, w_out, group, group_count, earlier, chunk=768):
    count, width = len(pieces), pieces[0].shape[1]
    rows, inner = count * tile, w_in.shape[1]
    once = pl.Buffered(1)
    piece = pl.BlockSpec((tile, width), lambda f, lab: (0, 0), pipeline_mode=once)
    inner_block = pl.BlockSpec((rows, chunk), lambda f, lab: (0, f))
    low = lambda *shape: jax.ShapeDtypeStruct(shape, jnp.bfloat16)
    outs = pl.pallas_call(
        lambda *refs: expert_kernel(count, *refs),
        grid_spec=pltpu.PrefetchScalarGridSpec(
            num_scalar_prefetch=1,
            grid=(inner // chunk,),
            in_specs=[piece] * count
            + [pl.BlockSpec((tile, width), lambda f, lab: (upstream_part, 0), pipeline_mode=once)] * count
            + [
                pl.BlockSpec((width, 128), lambda f, lab: (0, 0), pipeline_mode=once),
                pl.BlockSpec((width, chunk), lambda f, lab: (0, f)),
                pl.BlockSpec((chunk, width), lambda f, lab: (f, 0)),
            ]
            + [pl.BlockSpec(memory_space=pl.ANY)] * len(earlier),
            out_specs=[pl.BlockSpec((tile, width), lambda f, lab: (group, 0), pipeline_mode=once)] * count
            + [piece] * count
            + [
                pl.BlockSpec((rows, width), lambda f, lab: (0, 0), pipeline_mode=once),
                inner_block,
                inner_block,
                pl.BlockSpec((width, 128), lambda f, lab: (0, 0), pipeline_mode=once),
            ],
            scratch_shapes=[
                pltpu.VMEM((rows, 128), jnp.float32),
                pltpu.VMEM((rows, width), jnp.float32),
                pltpu.VMEM((rows, width), jnp.float32),
            ],
        ),
        out_shape=[low(group_count * tile, width)] * count
        + [low(tile, width)] * count
        + [low(rows, width), low(rows, inner), low(rows, inner), jax.ShapeDtypeStruct((width, 128), jnp.float32)],
        compiler_params=pltpu.CompilerParams(vmem_limit_bytes=60 << 20),
        cost_estimate=pl.CostEstimate(flops=16 * rows * width * inner, bytes_accessed=8 * width * inner, transcendentals=rows * inner),
        input_output_aliases={2 * count + 4 + at: at for at in range(len(earlier))},
        name="experts",
    )(label, *pieces, *upstream_pieces, router_wide, w_in, w_out, *earlier)
    return outs[:count], outs[count : 2 * count], outs[2 * count :]


def expert_grads_kernel(groups, count, *refs):
    x_refs, refs = refs[: groups * count], refs[groups * count :]
    g_refs, hid_refs, pre_refs = refs[:groups], refs[groups : 2 * groups], refs[2 * groups : 3 * groups]
    dw_ref, xt_ref, gt_ref = refs[3 * groups :]
    width = xt_ref.shape[0]
    rows = g_refs[0].shape[0]
    tile = rows // count

    @pl.when(pl.program_id(0) == 0)
    def _():
        for at in range(groups):
            gt_ref[:, at * rows : (at + 1) * rows] = g_refs[at][...].T
            for piece in range(count):
                start = at * rows + piece * tile
                xt_ref[:, start : start + tile] = x_refs[at * count + piece][...].T

    for side, (left, right) in enumerate(((xt_ref, pre_refs), (gt_ref, hid_refs))):
        total = sum(
            jnp.dot(left[:, at * rows : (at + 1) * rows], right[at][...], preferred_element_type=jnp.float32)
            for at in range(groups)
        )
        dw_ref[:, side * width : (side + 1) * width] = total.astype(jnp.bfloat16).T


def expert_grads(pieces, grads, hiddens, pre_grads, chunk=512):
    groups, count = len(grads), len(pieces) // len(grads)
    width, (rows, inner) = pieces[0].shape[1], hiddens[0].shape
    tile = rows // count
    once = pl.Buffered(1)
    inner_block = pl.BlockSpec((rows, chunk), lambda f: (0, f))
    return pl.pallas_call(
        lambda *refs: expert_grads_kernel(groups, count, *refs),
        grid=(inner // chunk,),
        in_specs=[pl.BlockSpec((tile, width), lambda f: (0, 0), pipeline_mode=once)] * (groups * count)
        + [pl.BlockSpec((rows, width), lambda f: (0, 0), pipeline_mode=once)] * groups
        + [inner_block] * (2 * groups),
        out_specs=pl.BlockSpec((chunk, 2 * width), lambda f: (f, 0)),
        out_shape=jax.ShapeDtypeStruct((inner, 2 * width), jnp.bfloat16),
        scratch_shapes=[pltpu.VMEM((width, groups * rows), jnp.bfloat16)] * 2,
        compiler_params=pltpu.CompilerParams(vmem_limit_bytes=60 << 20),
        cost_estimate=pl.CostEstimate(flops=rows * width, bytes_accessed=rows * width, transcendentals=0),
        name="expert_grads",
    )(*pieces, *grads, *hiddens, *pre_grads)


def sort_matrix(slot, slots):
    row = lax.broadcasted_iota(jnp.int32, (slots, slot.shape[1]), 0)
    return (row == slot).astype(jnp.float32).astype(jnp.bfloat16)


def sort_into(piece_refs, block, slot, rows):
    capacity = slot.shape[1] // 2
    matrix = sort_matrix(slot, len(piece_refs) * capacity)
    moved = jnp.dot(matrix, rows, preferred_element_type=jnp.float32).astype(jnp.bfloat16)
    for turn, piece_ref in enumerate(piece_refs):
        piece_ref[block * capacity : (block + 1) * capacity, :] = moved[turn * capacity : (turn + 1) * capacity]


def norm_scale_rows(rows):
    return lax.rsqrt(jnp.mean(rows * rows, axis=-1, keepdims=True) + norm_eps)


def sort_kernel(owners, label_ref, routes_ref, rows_ref, *refs):
    piece_refs, slot_ref = refs[:owners], refs[owners]
    blocks, _, length = routes_ref.shape
    first = lax.broadcasted_iota(jnp.int32, (length, length), 0)
    second = lax.broadcasted_iota(jnp.int32, (length, length), 1)
    upto = (first <= second).astype(jnp.float32).astype(jnp.bfloat16)
    for block in range(blocks):
        routes = routes_ref[block]
        hits = (lax.broadcasted_iota(jnp.int32, (8, length), 0) == routes).astype(jnp.float32)
        counts = jnp.dot(hits.astype(jnp.bfloat16), upto, preferred_element_type=jnp.float32)
        place = jnp.sum(hits * counts, axis=0, keepdims=True).astype(jnp.int32) - 1
        turn = routes - label_ref[0]
        turn = jnp.where(turn < 0, turn + owners, turn)
        slot = turn * (length // 2) + place
        slot_ref[block] = slot
        sort_into(piece_refs, block, slot, rows_ref[block])


def one_step(shape):
    return pl.BlockSpec(shape, lambda step: (0,) * len(shape), pipeline_mode=pl.Buffered(1))


def sort_upstream(label, routes, rows, owners, part, parts):
    blocks, length, width = rows.shape
    count = blocks * length // 2
    *pieces, slots = pl.pallas_call(
        lambda *refs: sort_kernel(owners, *refs),
        grid=(1,),
        in_specs=[pl.BlockSpec(memory_space=pltpu.SMEM), one_step((blocks, 1, length)), one_step(rows.shape)],
        out_specs=[pl.BlockSpec((count, width), lambda step: (part, 0), pipeline_mode=pl.Buffered(1))] * owners
        + [one_step((blocks, 1, length))],
        out_shape=[jax.ShapeDtypeStruct((parts * count, width), jnp.bfloat16)] * owners
        + [jax.ShapeDtypeStruct((blocks, 1, length), jnp.int32)],
        compiler_params=pltpu.CompilerParams(vmem_limit_bytes=48 << 20),
        name="sort_upstream",
    )(label, routes.reshape(blocks, 1, length), rows)
    return pieces, slots


def after_attention_kernel(slot_ref, attended_ref, tokens_ref, weight_ref, gain_ref, residual_ref, *piece_refs):
    for block in range(slot_ref.shape[0]):
        mixed = jnp.dot(attended_ref[block], weight_ref[...], preferred_element_type=jnp.float32)
        residual = tokens_ref[block].astype(jnp.float32) + mixed
        residual_ref[block] = residual
        router_in = (residual * norm_scale_rows(residual) * gain_ref[...]).astype(jnp.bfloat16)
        sort_into(piece_refs, block, slot_ref[block], router_in)


def after_attention(slots, attended, tokens, weight, gain, owners, earlier):
    blocks, length, width = tokens.shape
    count = blocks * length // 2
    parts = 2 if earlier else 1
    residual, *pieces = pl.pallas_call(
        lambda *refs: after_attention_kernel(*refs[:5], *refs[5 + len(earlier) :]),
        grid=(1,),
        in_specs=[
            one_step(slots.shape), one_step(tokens.shape), one_step(tokens.shape), one_step(weight.shape), one_step((1, width))
        ]
        + [pl.BlockSpec(memory_space=pl.ANY)] * len(earlier),
        out_specs=[one_step(tokens.shape)] + [one_step((count, width))] * owners,
        out_shape=[jax.ShapeDtypeStruct(tokens.shape, jnp.float32)]
        + [jax.ShapeDtypeStruct((parts * count, width), jnp.bfloat16)] * owners,
        input_output_aliases={5 + at: 1 + at for at in range(len(earlier))},
        compiler_params=pltpu.CompilerParams(vmem_limit_bytes=48 << 20),
        name="after_attention",
    )(slots, attended, tokens, weight, gain[None], *earlier)
    return residual, pieces


def before_attention_kernel(owners, earlier, slot_ref, *refs):
    piece_refs = refs[:owners]
    residual_ref, upstream_ref, attended_ref, weight_ref, gain_ref = refs[owners : owners + 5]
    residual_grad_ref, mixed_grad_ref, weight_grad_ref, gain_grad_ref = refs[-4:]
    blocks, _, length = slot_ref.shape
    capacity = length // 2
    weight_grad, gain_grad = (refs[-6][...], refs[-5][...]) if earlier else (0.0, 0.0)
    for block in range(blocks):
        slot = jnp.broadcast_to(slot_ref[block].astype(jnp.float32), (128, length)).T[:, :1].astype(jnp.int32)
        place = lax.broadcasted_iota(jnp.int32, (length, owners * capacity), 1)
        matrix = (place == slot).astype(jnp.float32).astype(jnp.bfloat16)
        rows = jnp.concatenate([ref[block * capacity : (block + 1) * capacity, :] for ref in piece_refs])
        grad = jnp.dot(matrix, rows, preferred_element_type=jnp.float32)
        residual = residual_ref[block]
        scale = norm_scale_rows(residual)
        normed = residual * scale
        scaled = grad * gain_ref[...]
        shrink = jnp.mean(scaled * normed, axis=-1, keepdims=True)
        gain_grad += jnp.sum(grad * normed, axis=0, keepdims=True)
        residual_grad = upstream_ref[block].astype(jnp.float32) + scale * (scaled - normed * shrink)
        residual_grad_ref[block] = residual_grad
        low = residual_grad.astype(jnp.bfloat16)
        mixed_grad = lax.dot_general(low, weight_ref[...], (((1,), (1,)), ((), ())), preferred_element_type=jnp.float32)
        mixed_grad_ref[block] = mixed_grad.astype(jnp.bfloat16)
        weight_grad += lax.dot_general(attended_ref[block], low, (((0,), (0,)), ((), ())), preferred_element_type=jnp.float32)
    weight_grad_ref[...] = weight_grad
    gain_grad_ref[...] = gain_grad


def before_attention(slots, pieces, residual, upstream, attended, weight, gain, group, group_count, earlier):
    blocks, length, width = residual.shape
    owners = len(pieces)
    rows = one_step(residual.shape)
    out_rows = pl.BlockSpec(residual.shape, lambda step: (group, 0, 0), pipeline_mode=pl.Buffered(1))
    sums = [one_step((width, width)), one_step((1, width))]
    shape = (group_count * blocks, length, width)
    return pl.pallas_call(
        lambda *refs: before_attention_kernel(owners, bool(earlier), *refs),
        grid=(1,),
        in_specs=[one_step(slots.shape)] + [one_step(pieces[0].shape)] * owners
        + [rows, rows, rows, one_step((width, width)), one_step((1, width))]
        + ([pl.BlockSpec(memory_space=pl.ANY)] * 2 + sums if earlier else []),
        out_specs=[out_rows, out_rows] + sums,
        out_shape=[
            jax.ShapeDtypeStruct(shape, jnp.float32),
            jax.ShapeDtypeStruct(shape, jnp.bfloat16),
            jax.ShapeDtypeStruct((width, width), jnp.float32),
            jax.ShapeDtypeStruct((1, width), jnp.float32),
        ],
        input_output_aliases={owners + 6: 0, owners + 7: 1} if earlier else {},
        compiler_params=pltpu.CompilerParams(vmem_limit_bytes=56 << 20),
        name="before_attention",
    )(slots, *pieces, residual, upstream, attended, weight, gain[None], *earlier)


def exchange(pieces, axis, sign, size=None, skipped=0):
    size = size or lax.axis_size(axis)
    return [pieces[0]] + [
        lax.ppermute(piece, axis, [(at, (at + sign * turn) % size) for at in range(size)])
        for turn, piece in enumerate(pieces[1:], 1 + skipped)
    ]


def own_and_other(blocks):
    at = lax.axis_index("ctx")
    own = lax.dynamic_index_in_dim(blocks, at, 0)
    other = lax.dynamic_index_in_dim(blocks, 1 - at, 0)
    return [own, lax.ppermute(other, "ctx", [(0, 1), (1, 0)])]


def hand_back_kernel(core_ref, own_ref, arrived_ref, out_ref):
    out_ref[...] = jnp.where(pl.program_id(0) == 0, own_ref[...], arrived_ref[...])


def hand_back(own, other):
    arrived = lax.ppermute(other, "ctx", [(0, 1), (1, 0)])
    core = lax.axis_index("ctx").astype(jnp.int32).reshape(1)
    _, length, width = own.shape
    block = (1, QB, width)
    last = length // QB - 1
    return pl.pallas_call(
        hand_back_kernel,
        grid_spec=pltpu.PrefetchScalarGridSpec(
            num_scalar_prefetch=1,
            grid=(2, length // QB),
            in_specs=[
                pl.BlockSpec(block, lambda side, row, core: (0, jnp.where(side == 0, row, last), 0)),
                pl.BlockSpec(block, lambda side, row, core: (0, jnp.where(side == 0, 0, row), 0)),
            ],
            out_specs=pl.BlockSpec(block, lambda side, row, core: (side ^ core[0], row, 0)),
        ),
        out_shape=jax.ShapeDtypeStruct((2, length, width), own.dtype),
        name="hand_back",
    )(core, own, arrived)


def layer_output_kernel(groups, owners, *refs):
    slot_refs, residual_refs = refs[:groups], refs[groups : 2 * groups]
    piece_refs = refs[2 * groups : 2 * groups + owners]
    blocks, _, length = slot_refs[0].shape
    capacity = length // 2
    for group in range(groups):
        for block in range(blocks):
            at = group * blocks + block
            matrix = sort_matrix(slot_refs[group][block], owners * capacity)
            rows = jnp.concatenate([ref[at * capacity : (at + 1) * capacity, :] for ref in piece_refs])
            moved = lax.dot_general(matrix, rows, (((0,), (0,)), ((), ())), preferred_element_type=jnp.float32)
            refs[len(refs) - groups + group][block] = (residual_refs[group][block] + moved).astype(jnp.bfloat16)


def layer_output(slots, residuals, pieces):
    blocks, length, width = residuals[0].shape
    vmem = pl.BlockSpec(memory_space=pltpu.VMEM)
    return pl.pallas_call(
        lambda *refs: layer_output_kernel(len(slots), len(pieces), *refs),
        in_specs=[vmem] * (2 * len(slots) + len(pieces)),
        out_specs=[vmem] * len(slots),
        out_shape=[jax.ShapeDtypeStruct((blocks, length, width), jnp.bfloat16)] * len(slots),
        compiler_params=pltpu.CompilerParams(vmem_limit_bytes=48 << 20),
        name="layer_output",
    )(*slots, *residuals, *pieces)


def weight_outputs_kernel(place_ref, *refs):
    shard_refs, weight_refs, gain_ref = refs[:4], refs[4:7], refs[7]
    out_refs, output_ref, gain_grad_ref, small_ref = refs[8:11], refs[11], refs[12], refs[13]
    whole_refs = refs[14:]
    width = gain_ref.shape[1]
    half = width // 2
    for side in range(2):
        planes, rows, _ = shard_refs[2 * side].shape
        for turn in range(planes):
            for other in range(2):
                shard = (place_ref[0] ^ turn) * 2 + (place_ref[1] ^ other)
                start = pl.multiple_of(shard * rows, 16)
                whole_refs[side][pl.ds(start, rows), :] = shard_refs[2 * side + other][turn]
    total = 0.0
    for kind in range(3):
        for side, ref in enumerate(whole_refs):
            columns = slice(side * half, (side + 1) * half)
            grad = ref[kind * width : (kind + 1) * width, :].astype(jnp.float32)
            out_refs[kind][:, columns] = grad
            total += jnp.sum(grad * weight_refs[kind][:, columns].astype(jnp.float32), axis=1, keepdims=True)
    total = jnp.broadcast_to(total, (width, 128)).T
    gain_grad_ref[...] = total[:1] / gain_ref[...]
    start = 3 * width + 128
    for side in range(2):
        rows = slice(start + side * width, start + (side + 1) * width)
        output_ref[:, side * half : (side + 1) * half] = whole_refs[0][rows, :].astype(jnp.float32)
    for at, (ref, first) in enumerate(((whole_refs[0], 3 * width), (whole_refs[1], 3 * width), (whole_refs[0], start + 2 * width))):
        small_ref[at] = ref[first : first + 128, :].astype(jnp.float32)


def weight_outputs(shards, weights, gain):
    width = gain.shape[0]
    vmem = pl.BlockSpec(memory_space=pltpu.VMEM)
    place = jnp.stack([lax.axis_index("dp"), lax.axis_index("ctx")]).astype(jnp.int32)
    matrix = jax.ShapeDtypeStruct((width, width), jnp.float32)
    return pl.pallas_call(
        weight_outputs_kernel,
        in_specs=[pl.BlockSpec(memory_space=pltpu.SMEM)] + [vmem] * 8,
        out_specs=[vmem] * 6,
        out_shape=[matrix] * 4
        + [jax.ShapeDtypeStruct((1, width), jnp.float32), jax.ShapeDtypeStruct((3, 128, width // 2), jnp.float32)],
        scratch_shapes=[
            pltpu.VMEM((2 * part.shape[0] * part.shape[1], width // 2), jnp.bfloat16) for part in (shards[0], shards[2])
        ],
        compiler_params=pltpu.CompilerParams(vmem_limit_bytes=56 << 20),
        name="weight_outputs",
    )(place, *shards, *weights, gain[None])


def halves(rows, tile, width):
    steps = rows // tile
    first = pl.BlockSpec((tile, width), lambda step: (jnp.minimum(step, steps - 1), 0))
    second = pl.BlockSpec((tile, width), lambda step: (jnp.maximum(step - steps, 0), 0))
    return [first, second], lambda first_ref, second_ref: jnp.where(pl.program_id(0) < steps, first_ref[...], second_ref[...])


def projections_kernel(choose, first_ref, second_ref, gain_ref, *refs):
    weight_refs, out_refs, turned_ref = refs[:3], refs[3:6], refs[6]
    rows = choose(first_ref, second_ref).astype(jnp.float32)
    low = (rows * norm_scale_rows(rows) * gain_ref[...]).astype(jnp.bfloat16)
    for weight_ref, out_ref in zip(weight_refs, out_refs):
        out_ref[...] = jnp.dot(low, weight_ref[...], preferred_element_type=jnp.float32).astype(jnp.bfloat16)
    turned_ref[...] = low.T


def projections_of(first, second, gain, weights):
    rows, width = first.shape
    tile = min(QB, rows)
    specs, choose = halves(rows, tile, width)
    out = jax.ShapeDtypeStruct((2 * rows, width), jnp.bfloat16)
    return pl.pallas_call(
        lambda *refs: projections_kernel(choose, *refs),
        grid=(2 * rows // tile,),
        in_specs=specs + [one_step((1, width))] + [one_step((width, width))] * 3,
        out_specs=[pl.BlockSpec((tile, width), lambda step: (step, 0))] * 3
        + [pl.BlockSpec((width, tile), lambda step: (0, step))],
        out_shape=[out] * 3 + [jax.ShapeDtypeStruct((width, 2 * rows), jnp.bfloat16)],
        compiler_params=pltpu.CompilerParams(vmem_limit_bytes=48 << 20),
        cost_estimate=pl.CostEstimate(flops=64 * rows * width * width, bytes_accessed=16 * rows * width, transcendentals=0),
        name="projections",
    )(first, second, gain[None], *weights)


def token_grads_kernel(choose, first_ref, second_ref, *refs):
    weight_refs, (own_ref, other_ref, residual_grad_ref, gain_ref, *out_refs) = refs[:3], refs[3:]
    grad = 0.0
    for kind in range(3):
        low = jnp.concatenate([first_ref[kind], second_ref[kind]], axis=1)
        grad += lax.dot_general(low, weight_refs[kind][...], (((1,), (1,)), ((), ())), preferred_element_type=jnp.float32)
    rows = choose(own_ref, other_ref).astype(jnp.float32)
    scale = norm_scale_rows(rows)
    normed = rows * scale
    scaled = grad * gain_ref[...]
    shrink = jnp.mean(scaled * normed, axis=-1, keepdims=True)
    out = residual_grad_ref[...] + scale * (scaled - normed * shrink)
    half = pl.num_programs(0) // 2

    @pl.when(pl.program_id(0) < half)
    def _():
        out_refs[0][...] = out

    @pl.when(pl.program_id(0) >= half)
    def _():
        out_refs[1][...] = out


def token_grads(first, second, weights, token_groups, residual_grad, gain):
    length, width = residual_grad.shape
    half = pl.BlockSpec((3, QB, width // 2), lambda step: (0, step, 0))
    rows = pl.BlockSpec((QB, width), lambda step: (step, 0))
    specs, choose = halves(length // 2, QB, width)
    return pl.pallas_call(
        lambda *refs: token_grads_kernel(choose, *refs),
        grid=(length // QB,),
        in_specs=[half, half] + [one_step((width, width))] * 3 + specs + [rows, one_step((1, width))],
        out_specs=specs,
        out_shape=[jax.ShapeDtypeStruct((length // 2, width), jnp.float32)] * 2,
        compiler_params=pltpu.CompilerParams(vmem_limit_bytes=48 << 20),
        cost_estimate=pl.CostEstimate(flops=6 * length * width * width, bytes_accessed=14 * length * width, transcendentals=0),
        name="token_grads",
    )(first, second, *weights, *token_groups, residual_grad, gain[None])


def norm_scale(value_rows):
    return lax.rsqrt(jnp.mean(value_rows * value_rows, axis=-1, keepdims=True) + norm_eps)


def norm_back(value_rows, scale, gain_vector, grad_rows):
    scaled = grad_rows * gain_vector
    shrink = jnp.mean(scaled * value_rows, axis=-1, keepdims=True) * scale * scale * scale
    return scale * scaled - value_rows * shrink, jnp.sum(grad_rows * value_rows * scale, axis=(0, 1))


def wide_dot(rows, weight):
    return jnp.einsum("sxd,de->sxe", rows, weight, preferred_element_type=jnp.float32)


def wide_dot_back(rows, weight):
    return jnp.einsum("sxe,de->sxd", rows, weight, preferred_element_type=jnp.float32)


def weight_dot(left, right):
    return jnp.einsum("sxd,sxe->de", left, right, preferred_element_type=jnp.float32)


def pack_sums(matrices, small=None):
    parts = [matrix.astype(jnp.bfloat16) for matrix in matrices]
    if small is not None:
        small = jnp.pad(small, ((0, -small.shape[0] % 64), (0, parts[0].shape[1] - small.shape[1])))
        high = small.astype(jnp.bfloat16)
        parts += [high, (small - high.astype(jnp.float32)).astype(jnp.bfloat16)]
    return jnp.concatenate(parts)


def add_low(*parts):
    return sum(part.astype(jnp.float32) for part in parts).astype(jnp.bfloat16)


def swap(part, axis, turn):
    return lax.ppermute(part, axis, [(to, to ^ turn) for to in range(lax.axis_size(axis))])


class Summing:
    def __init__(self, packed):
        self.core, self.plane = lax.axis_index("ctx"), lax.axis_index("dp")
        self.planes = lax.axis_size("dp")
        self.part = packed.reshape(self.planes, 2, -1, packed.shape[1])
        self.step = 0

    def sends(self):
        if self.step == 0:
            return [lax.dynamic_index_in_dim(self.part, 1 - self.core, 1, keepdims=False)]
        if self.step == 1:
            return [
                lax.dynamic_index_in_dim(self.part, self.plane ^ turn, 0, keepdims=False)
                for turn in range(1, self.planes)
            ]
        return [self.part] * (self.planes - 1 if self.step == 4 else 1)

    def move(self, sent):
        axis, first = (("ctx", 1), ("dp", 1), ("expert", 1), ("expert", 2), ("dp", 1), ("ctx", 1))[self.step]
        return [swap(part, axis, first + at) for at, part in enumerate(sent)]

    def take(self, arrived):
        if self.step == 0:
            self.part = lax.dynamic_index_in_dim(self.part, self.core, 1, keepdims=False)
        elif self.step == 1:
            self.part = lax.dynamic_index_in_dim(self.part, self.plane, 0, keepdims=False)
        if self.step < 4:
            self.part = add_low(self.part, *arrived)
        elif self.step == 4:
            self.part = jnp.stack([self.part] + arrived)
        else:
            self.part = (self.part, arrived[0])
        self.step += 1


def matrix_of(sums, index, rows):
    return sums[index * rows : (index + 1) * rows]


def small_of(sums, start):
    high, low = jnp.split(sums[start:].astype(jnp.float32), 2)
    return high + low


def per_device(
    tokens,
    cotangent,
    routes,
    norm1_gain,
    query_weight,
    key_weight,
    value_weight,
    output_weight,
    bias_table,
    norm2_gain,
    router_weight,
    w_in,
    w_out,
):
    seq_count, local_len, model_width = tokens.shape
    owners = lax.axis_size("expert")
    capacity = local_len // 2
    whole_seq = seq_count == 2 and lax.axis_size("ctx") == 2 and local_len % QB == 0
    split = own_and_other if whole_seq else lambda blocks: [blocks]
    routes, cotangent, token_groups = split(routes), split(cotangent), split(tokens)
    groups = range(len(routes))
    core = lax.axis_index("ctx").astype(jnp.int32).reshape(1)
    label = lax.axis_index("expert").astype(jnp.int32).reshape(1)
    together = lax.optimization_barrier

    sorted_upstream, slots = zip(
        *[
            sort_upstream(label, routes[group], cotangent[group], owners, group, 1 + group)
            for group in groups
        ]
    )
    sorted_first, token_groups = together((sorted_upstream[0], token_groups))
    upstream = [exchange(sorted_first, "expert", 1)]
    projections = (query_weight, key_weight, value_weight)
    token_rows = [rows.reshape(-1, model_width) for rows in (token_groups if whole_seq else jnp.split(tokens, 2))]
    queries, keys, values, turned = projections_of(*token_rows, norm1_gain, projections)
    if whole_seq:
        lines = bias_lines(bias_table)
        flat = (seq_count * local_len, model_width)
        qkv = [queries, keys, values]
    else:
        queries, keys, values = (rows.reshape(tokens.shape) for rows in (queries, keys, values))
        first_pos = lax.axis_index("ctx") * local_len
        keys = lax.all_gather(keys, "ctx", axis=1, tiled=True)
        values = lax.all_gather(values, "ctx", axis=1, tiled=True)
        buckets = bucket_grid(first_pos, local_len, keys.shape[1])
        attended, log_totals = attend_rows(queries, keys, values, buckets, bias_table, DH)
    attended_groups, residual1, arrived = [], [], []
    if whole_seq:
        log_totals = []
    in_flight, fed = upstream[0], queries.reshape(-1, model_width)
    for at, group in enumerate(groups):
        if whole_seq:
            rows, totals = attend(core, fed, *qkv[1:], lines, at * local_len, local_len)
            rows = rows[None]
            log_totals.append(totals)
        else:
            rows = attended.astype(jnp.bfloat16)
        attended_groups.append(rows)
        earlier = sorted_upstream[at] if at else []
        residual, sorted_rows = after_attention(
            slots[at], rows, token_groups[at], output_weight, norm2_gain, owners, earlier
        )
        residual1.append(residual)
        sorted_rows, fed, in_flight = together((sorted_rows, fed, in_flight))
        if at == 0:
            upstream[0] = in_flight
        else:
            arrived[-1] = in_flight
        in_flight = exchange(sorted_rows, "expert", 1)
        arrived.append(in_flight)
    router_wide = jnp.pad(router_weight, ((0, 0), (0, 128 - router_weight.shape[1])))
    done, back = [], []
    tile = seq_count // len(groups) * local_len // 2
    for at in groups:
        rows, grads = arrived[at], upstream[0] if at == 0 else arrived[at]
        earlier = done[-1][0] if done else []
        result = run_expert(
            label, rows, grads, tile, min(at, 1), router_wide, w_in[0], w_out[0], at, len(groups), earlier
        )
        if at + 1 < len(arrived):
            result, arrived[at + 1] = together((result, arrived[at + 1]))
        if whole_seq and at == 0:
            seen = (jnp.concatenate(attended_groups).reshape(flat), jnp.concatenate(log_totals, axis=2), turned)
            result, seen = together((result, seen))
        leaving = result[1]
        if back:
            result, back[-1] = together((result, back[-1]))
        done.append(result)
        back.append(exchange(leaving, "expert", -1))
    rows_out = done[-1][0]
    grad_rows, hiddens, pre_grads, grad_router = zip(*[item[2] for item in done])
    grad_router = sum(grad_router)[:, : router_weight.shape[1]].T
    grad_experts = expert_grads(sum(arrived, []), grad_rows, hiddens, pre_grads)

    def back_to_attention(group, earlier):
        return before_attention(
            slots[group], back[group], residual1[group], cotangent[group], attended_groups[group],
            output_weight, norm2_gain, group, len(groups), earlier,
        )

    backward = back_to_attention(0, ())
    grad_experts, back[-1], rows_out, backward, grad_router = together(
        (grad_experts, back[-1], rows_out, backward, grad_router)
    )
    grad_experts = lax.psum_scatter(grad_experts, ("dp", "ctx"), scatter_dimension=0, tiled=True)
    if not whole_seq:
        returned = exchange(list(rows_out), "expert", -1)
    for group in groups[1:]:
        backward = back_to_attention(group, backward)
    residual_grad, mixed_grad, grad_w_output, grad_norm2 = backward
    early_small = jnp.concatenate([grad_router, grad_norm2])
    if whole_seq:
        half = model_width // 2
        pairs = half // 128
        mixed_grad = mixed_grad.reshape(flat)
        def send_back(turn):
            return lax.ppermute(rows_out[turn], "expert", [(at, (at - turn) % owners) for at in range(owners)])

        half_turn = owners // 2
        returned = [rows_out[0] if turn in (0, half_turn) else send_back(turn) for turn in range(owners)]
        first = attend_back(core, *qkv, mixed_grad, *seen, lines, 0, pairs, pairs)
        (first_grads, first_sums), returned, rows_out = together((first, returned, rows_out))
        returned[half_turn] = send_back(half_turn)
        matrices = [first_sums, grad_w_output[:, :half], grad_w_output[:, half:]]
        early = Summing(pack_sums(matrices, early_small.reshape(-1, half)))
        second = ()
        for at in range(pairs, 2 * pairs):
            sent, mixed_grad = together((early.sends(), mixed_grad))
            moved = early.move(sent)
            second = attend_back(core, *qkv, mixed_grad, *seen, lines, at, 1, pairs, second)
            if at == pairs + 1:
                second, moved, returned = together((second, moved, returned))
            else:
                second, moved = together((second, moved))
            early.take(moved)
        (second_grads, second_sums), grad_experts = together((second, grad_experts))
        late = Summing(second_sums)
        sent, sent_late, returned = together((early.sends(), late.sends(), returned))
        moved, moved_late = early.move(sent), late.move(sent_late)
        block_out = layer_output(slots, residual1, returned)
        moved_late, block_out = together((moved_late, block_out))
        late.take(moved_late)
        sent_late, second_grads = together((late.sends(), second_grads))
        moved_late = late.move(sent_late)
        d_tokens = token_grads(
            first_grads, second_grads, projections, token_rows, residual_grad.reshape(flat), norm1_gain
        )
        moved, moved_late, d_tokens = together((moved, moved_late, d_tokens))
        early.take(moved)
        late.take(moved_late)
        sent, sent_late = together((early.sends(), late.sends()))
        moved = early.move(sent)
        late.take(late.move(sent_late))
        block_out = hand_back(*block_out)
        moved, moved_late, block_out = together((moved, late.move(late.sends()), block_out))
        early.take(moved)
        late.take(moved_late)
        sent, sent_late = together((early.sends(), late.sends()))
        d_tokens = hand_back(*[rows[None] for rows in d_tokens])
        moved, moved_late, d_tokens = together((early.move(sent), late.move(sent_late), d_tokens))
        early.take(moved)
        late.take(moved_late)
        late.take(late.move(late.sends()))
        *grad_qkv, grad_w_output, grad_norm1, smalls = weight_outputs(early.part + late.part, projections, norm1_gain)
        grad_norm1 = grad_norm1[0]
        small = (smalls[2, :64] + smalls[2, 64:]).reshape(-1, model_width)
        grad_bias = jnp.concatenate([smalls[0, :4], smalls[1, :4]], axis=1)
        grad_bias = (grad_bias[:2] + grad_bias[2:]).reshape(2, -1, 128).swapaxes(0, 1).reshape(-1, 128)
    else:
        query_grad, _, diag_grad, key_part, value_part = attend_back_rows(
            queries, keys, values, mixed_grad, log_totals, buckets, bias_table, DH
        )
        low_parts = [query_grad.astype(jnp.bfloat16)] + [
            lax.psum_scatter(part, "ctx", scatter_dimension=1, tiled=True).astype(jnp.bfloat16)
            for part in (key_part, value_part)
        ]
        inputs = tokens.astype(jnp.float32)
        attn_in = turned.T.reshape(tokens.shape)
        norm_in_grad = sum(wide_dot_back(*pair) for pair in zip(low_parts, projections))
        sums = lax.psum(
            pack_sums([grad_w_output] + [weight_dot(attn_in, rows) for rows in low_parts], early_small),
            ("dp", "ctx", "expert"),
        )
        grad_bias = lax.psum(diag_grad, ("dp", "ctx", "expert"))
        grad_w_output, *grad_qkv = (matrix_of(sums, kind, model_width).astype(jnp.float32) for kind in range(4))
        small = small_of(sums, 4 * model_width)
        norm1_back, grad_norm1 = norm_back(inputs, norm_scale(inputs), norm1_gain, norm_in_grad)
        grad_norm1 = lax.psum(grad_norm1, ("dp", "ctx", "expert"))
    grad_bias = grad_bias[: bias_table.shape[1], : bias_table.shape[0]].T
    grad_w_query, grad_w_key, grad_w_value = grad_qkv
    grad_w_output = grad_w_output.astype(jnp.float32)
    experts = router_weight.shape[1]
    grad_router, grad_norm2 = small[:experts, :].T, small[experts]
    if not whole_seq:
        block_out = layer_output(slots, residual1, returned)[0]
        d_tokens = residual_grad + norm1_back
    grad_experts = grad_experts.astype(jnp.float32)
    return (
        block_out,
        d_tokens,
        grad_norm1,
        grad_w_query,
        grad_w_key,
        grad_w_value,
        grad_w_output,
        grad_bias,
        grad_norm2,
        grad_router,
        grad_experts[:, :model_width].T[None],
        grad_experts[:, model_width:][None],
    )


def solution(mesh):
    rows = P(("dp", "expert"), "ctx", None)
    in_specs = (rows, rows, P(("dp", "expert"), "ctx")) + (P(),) * 8 + (P("expert", None, None),) * 2
    out_specs = (rows, rows) + (P(),) * 8 + (P("expert", None, ("dp", "ctx")), P("expert", ("dp", "ctx"), None))
    return jax.shard_map(per_device, mesh=mesh, in_specs=in_specs, out_specs=out_specs, check_vma=False)
```
